32 devices in a mesh: crop: 4 (over y, x), chan: 8 (over z, core).
Axes of the slice: x: 2, y: 2, z: 4, core: 2. Of those that a mesh axis runs over, the one named last changes fastest.
Arguments:
- features: bfloat16 [4, 2048, 1024], P('crop', 'chan'), may hold values from -6 to 6
- low_in: bfloat16 [4, 256, 128, 128], P('crop', 'chan'), may hold values from -6 to 6
- offsets: int32 [4, 2], P('crop'), may hold values from 0 to 1791, as said below
- d_logits: bfloat16 [4, 21, 128, 128], P('crop'), may hold values from -6 to 6
- w_point: bfloat16 [2048, 256], P('chan'), may hold values from -0.125 to 0.125
- w_atrous: bfloat16 [3, 9, 2048, 256], P(None, None, 'chan'), may hold values from -0.046875 to 0.046875
- w_pool: bfloat16 [2048, 256], P('chan'), may hold values from -0.125 to 0.125
- w_proj: bfloat16 [5, 256, 256], P(None, 'chan'), may hold values from -0.15625 to 0.15625
- w_low: bfloat16 [256, 48], P('chan'), may hold values from -0.375 to 0.375
- w_dec1: bfloat16 [9, 256, 256], P(None, 'chan'), may hold values from -0.109375 to 0.109375
- w_dec1_low: bfloat16 [9, 48, 256], P(None, None, 'chan'), may hold values from -0.109375 to 0.109375
- w_dec2: bfloat16 [9, 256, 256], P(None, 'chan'), may hold values from -0.125 to 0.125
- w_cls: bfloat16 [256, 21], P('chan'), may hold values from -0.375 to 0.375
- b_cls: float32 [21], replicated, may hold values from -3 to 3
- bn_gain: float32 [8, 256], P(None, 'chan'), may hold values from 0.1 to 1.9
- bn_shift: float32 [8, 256], P(None, 'chan'), may hold values from -3 to 3
- low_gain: float32 [48], replicated, may hold values from 0.1 to 1.9
- low_shift: float32 [48], replicated, may hold values from -3 to 3
Outputs:
- logits: float32 [4, 21, 128, 128], P('crop', None, 'chan')
- d_features: float32 [4, 2048, 1024], P('crop', 'chan')
- d_low_in: float32 [4, 256, 128, 128], P('crop', 'chan')
- d_w_point: float32 [2048, 256], P('chan')
- d_w_atrous: float32 [3, 9, 2048, 256], P(None, None, 'chan')
- d_w_pool: float32 [2048, 256], P('chan')
- d_w_proj: float32 [5, 256, 256], P(None, 'chan')
- d_w_low: float32 [256, 48], P('chan')
- d_w_dec1: float32 [9, 256, 256], P(None, 'chan')
- d_w_dec1_low: float32 [9, 48, 256], P(None, None, 'chan')
- d_w_dec2: float32 [9, 256, 256], P(None, 'chan')
- d_w_cls: float32 [256, 21], P('chan')
- d_b_cls: float32 [21], replicated
- d_bn_gain: float32 [8, 256], P(None, 'chan')
- d_bn_shift: float32 [8, 256], P(None, 'chan')
- d_low_gain: float32 [48], replicated
- d_low_shift: float32 [48], replicated
The draws below stay inside these ranges and needn't reach their ends.
Inputs may be any that keep to these rules, and one draw needn't show every extreme that they name: offsets[:, 0] is below 768 and offsets[:, 1] below 1792; some crop's column is the largest allowed.
All inputs are finite; a program needn't handle non-finite values.
Results may differ from the reference program's by a relative error of at most 0.02.
The reference program's roundings to bfloat16 on the way count: a program that leaves them out, or rounds other values in their place, can miss the bound.
Values may be sent and summed in bfloat16 or wider, within the bound.
A program may use at most 320 MiB of HBM per device.

```python
import jax
import jax.numpy as jnp
from jax import lax

CIN = 2048
C = 256
LOW_IN = 256
LOWC = 48
CLASSES = 21
FA = 32
SCENE_H = 1024
SCENE_W = 2048
CROPS = 4
FL = 128
CROP_PX = 512


def draw_offsets(key, part):
    key = jax.random.fold_in(key, 7)
    key_rows, key_cols = jax.random.split(key)
    top_rows = jax.random.randint(key_rows, (CROPS,), 0, SCENE_H - CROP_PX // 2)
    left_cols = jax.random.randint(key_cols, (CROPS,), 0, SCENE_W - CROP_PX // 2)
    left_cols = left_cols.at[0].set(SCENE_W - CROP_PX // 2 - 1)
    return jnp.stack([top_rows, left_cols], axis=1).astype(jnp.int32)


def levels(stream_key, shape, cuts, least, top_value):
    gain, own = 1.0, jax.random.fold_in(stream_key, 6)
    for axis_at, blocks in cuts:
        draws = jnp.exp(jax.random.uniform(jax.random.fold_in(own, axis_at), (blocks,), jnp.float32, least / len(cuts), top_value / len(cuts)))
        gain = gain * jnp.repeat(draws, shape[axis_at] // blocks).reshape([-1 if axis == axis_at else 1 for axis in range(len(shape))])
    return gain


def gaussian(key, shape, scale, limit, cuts=(), held_as=jnp.bfloat16):
    entries = jax.random.normal(key, shape, jnp.float32) * scale
    if len(cuts) > 0:
        entries = levels(key, shape, cuts, -0.22, 0.18) * entries
    return jnp.clip(entries, min=-limit, max=limit).astype(held_as)


def setup_inputs(seed: int = 0) -> dict:
    keys = jax.random.split(jax.random.key(seed), 19)
    return {
        "features": gaussian(keys[0], (CROPS, CIN, FA * FA), 1.0, 6.0, ((0, 4), (1, 8))),
        "low_in": gaussian(keys[1], (CROPS, LOW_IN, FL, FL), 1.0, 6.0, ((0, 4), (1, 8))),
        "offsets": draw_offsets(jax.random.fold_in(keys[18], 71), 0),
        "d_logits": gaussian(keys[3], (CROPS, CLASSES, FL, FL), 1.0, 6.0, ((0, 4),)),
        "w_point": gaussian(keys[4], (CIN, C), CIN ** -0.5, 0.125, ((0, 8),)),
        "w_atrous": gaussian(keys[5], (3, 9, CIN, C), (9 * CIN) ** -0.5, 0.046875, ((2, 8),)),
        "w_pool": gaussian(keys[6], (CIN, C), CIN ** -0.5, 0.125, ((0, 8),)),
        "w_proj": gaussian(keys[7], (5, C, C), (5 * C) ** -0.5, 0.15625, ((1, 8),)),
        "w_low": gaussian(keys[8], (LOW_IN, LOWC), LOW_IN ** -0.5, 0.375, ((0, 8),)),
        "w_dec1": gaussian(keys[9], (9, C, C), (9 * (C + LOWC)) ** -0.5, 0.109375, ((1, 8),)),
        "w_dec1_low": gaussian(keys[10], (9, LOWC, C), (9 * (C + LOWC)) ** -0.5, 0.109375, ((2, 8),)),
        "w_dec2": gaussian(keys[11], (9, C, C), (9 * C) ** -0.5, 0.125, ((1, 8),)),
        "w_cls": gaussian(keys[12], (C, CLASSES), C ** -0.5, 0.375, ((0, 8),)),
        "b_cls": gaussian(keys[13], (CLASSES,), 0.5, 3.0, (), jnp.float32),
        "bn_gain": jnp.clip(1.0 + 0.18 * jax.random.normal(keys[14], (8, C), jnp.float32), 0.1, 1.9),
        "bn_shift": gaussian(keys[15], (8, C), 0.5, 3.0, ((1, 8),), jnp.float32),
        "low_gain": jnp.clip(1.0 + 0.18 * jax.random.normal(keys[16], (LOWC,), jnp.float32), 0.1, 1.9),
        "low_shift": gaussian(keys[17], (LOWC,), 0.5, 3.0, (), jnp.float32),
    }


@jax.custom_vjp
def low(v):
    return lax.optimization_barrier(v.astype(jnp.bfloat16)).astype(jnp.float32)

@jax.custom_vjp
def low_back(v):
    return v

def low_keep(v):
    return (low(v), None)

def low_pass(kept, grad):
    return (grad,)

def back_keep(v):
    return (v, None)

def back_low(kept, grad):
    return (low(grad),)
low.defvjp(low_keep, low_pass)
low_back.defvjp(back_keep, back_low)
epsilon = 1e-05
highest = lax.Precision.HIGHEST
atrous_rates = (6, 12, 18)

def normalize(values, scales, shifts, over_axes):
    average = lax.optimization_barrier(jnp.mean(values, axis=over_axes, keepdims=True))
    spread = lax.optimization_barrier(jnp.mean(jnp.square(values - average), axis=over_axes, keepdims=True))
    return jax.nn.gelu(scales * (values - average) * lax.rsqrt(spread + epsilon) + shifts)

def channel_view(vector):
    return vector[None, :, None, None]

def pointwise(values, weight):
    return jnp.einsum('bchw,co->bohw', values, weight, precision=highest)

def dilated(values, weight, dilation):
    kernel = weight.reshape(3, 3, weight.shape[1], weight.shape[2])
    return lax.conv_general_dilated(values, kernel, (1, 1), ((dilation, dilation), (dilation, dilation)), rhs_dilation=(dilation, dilation), dimension_numbers=('NCHW', 'HWIO', 'NCHW'), precision=highest)

def make_table():
    source_pos = jnp.clip((jnp.arange(FL, dtype=jnp.float32) + 0.5) / 4.0 - 0.5, 0.0, FA - 1.0)
    coarse_cols = jnp.arange(FA, dtype=jnp.float32)[None, :]
    return jnp.maximum(0.0, 1.0 - jnp.abs(source_pos[:, None] - coarse_cols))

def head(features, low_in, w_point, w_atrous, w_pool, w_proj, w_low, w_dec1, w_dec1_low, w_dec2, w_cls, b_cls, bn_gain, bn_shift, low_gain, low_shift, valid_mask):
    features = features.reshape(features.shape[0], features.shape[1], FA, FA)
    over_axes = (0, 2, 3)
    branch_pre = [low_back(pointwise(features, w_point))]
    for branch_no in range(3):
        branch_pre.append(low_back(dilated(features, w_atrous[branch_no], atrous_rates[branch_no])))
    branch_acts = []
    for branch_no in range(4):
        branch_acts.append(low(normalize(branch_pre[branch_no], channel_view(bn_gain[branch_no]), channel_view(bn_shift[branch_no]), over_axes)))
    pooled = low(lax.optimization_barrier(jnp.mean(features, axis=(2, 3))))
    pool_pre = low_back(jnp.dot(pooled, w_pool, precision=highest))
    pool_act = low(normalize(pool_pre, bn_gain[4][None, :], bn_shift[4][None, :], (0,)))
    projected = jnp.dot(pool_act, w_proj[4], precision=highest)[:, :, None, None]
    for branch_no in range(4):
        projected = projected + pointwise(branch_acts[branch_no], w_proj[branch_no])
    projected = low_back(projected)
    merged = normalize(projected, channel_view(bn_gain[5]), channel_view(bn_shift[5]), over_axes)
    up_table = make_table()
    upsampled = low(jnp.einsum('bchw,ih,jw->bcij', merged, up_table, up_table, precision=highest))
    low_pre = low_back(pointwise(low_in, w_low))
    low_act = low(normalize(low_pre, channel_view(low_gain), channel_view(low_shift), over_axes))
    decoded_one = low_back(dilated(upsampled, w_dec1, 1) + dilated(low_act, w_dec1_low, 1))
    first_act = low(normalize(decoded_one, channel_view(bn_gain[6]), channel_view(bn_shift[6]), over_axes))
    decoded_two = low_back(dilated(first_act, w_dec2, 1))
    second_act = low(normalize(decoded_two, channel_view(bn_gain[7]), channel_view(bn_shift[7]), over_axes))
    return valid_mask[:, None] * (pointwise(second_act, w_cls) + channel_view(b_cls))

def reference(features, low_in, offsets, d_logits, w_point, w_atrous, w_pool, w_proj, w_low, w_dec1, w_dec1_low, w_dec2, w_cls, b_cls, bn_gain, bn_shift, low_gain, low_shift):
    row_index = jnp.arange(FL, dtype=jnp.int32)
    rows_valid = offsets[:, 0:1] + 4 * row_index[None, :] < SCENE_H
    cols_valid = offsets[:, 1:2] + 4 * row_index[None, :] < SCENE_W
    valid_mask = (rows_valid[:, :, None] & cols_valid[:, None, :]).astype(jnp.float32)
    as_float = (features.astype(jnp.float32), low_in.astype(jnp.float32), w_point.astype(jnp.float32), w_atrous.astype(jnp.float32), w_pool.astype(jnp.float32), w_proj.astype(jnp.float32), w_low.astype(jnp.float32), w_dec1.astype(jnp.float32), w_dec1_low.astype(jnp.float32), w_dec2.astype(jnp.float32), w_cls.astype(jnp.float32), b_cls.astype(jnp.float32), bn_gain.astype(jnp.float32), bn_shift.astype(jnp.float32), low_gain.astype(jnp.float32), low_shift.astype(jnp.float32))

    def closed(*arrays):
        return head(*arrays, valid_mask)
    logits, pullback = jax.vjp(closed, *as_float)
    gradients = pullback(d_logits.astype(jnp.float32))
    return (logits, gradients[0], gradients[1], gradients[2], gradients[3], gradients[4], gradients[5], gradients[6], gradients[7], gradients[8], gradients[9], gradients[10], gradients[11], gradients[12], gradients[13], gradients[14], gradients[15])
```

```python
import functools

import jax
import jax.numpy as jnp
from jax import lax
from jax.experimental import pallas as pl
from jax.experimental.pallas import tpu as pltpu
from jax.sharding import PartitionSpec as P

FA = 32
SCENE_H = 1024
SCENE_W = 2048

epsilon = 1e-05
highest = lax.Precision.HIGHEST
atrous_rates = (6, 12, 18)
f32 = jnp.float32
bf16 = jnp.bfloat16
BOTH = ("crop", "chan")


MESH = pl.DeviceIdType.MESH


def chip_peers(crops, n):
    my_crop, me = lax.axis_index("crop"), lax.axis_index("chan")
    core = lax.rem(me, 2)
    chips = n // 2
    other = (my_crop, me + 1 - 2 * core)
    far = []
    for i in range(crops):
        for j in range(chips):
            if i or j:
                far.append((lax.rem(my_crop + i, crops), lax.rem(me + 2 * j, n)))
    return other, far


def sum_kernel(crops, n, x_ref, o_ref, pair, slots, pair_sems, send, recv):
    other, far = chip_peers(crops, n)
    my_crop, me = lax.axis_index("crop"), lax.axis_index("chan")
    core = lax.rem(me, 2)
    mine = my_crop * (n // 2) + lax.div(me, 2)
    barrier = pltpu.get_barrier_semaphore()
    for peer in [other] + far:
        pl.semaphore_signal(barrier, inc=1, device_id=peer, device_id_type=MESH)
    pl.semaphore_wait(barrier, 1 + len(far))
    pair[core] = x_ref[...]
    copy = pltpu.make_async_remote_copy(
        src_ref=pair.at[core],
        dst_ref=pair.at[core],
        send_sem=pair_sems.at[0],
        recv_sem=pair_sems.at[1],
        device_id=other,
        device_id_type=MESH,
    )
    copy.start()
    copy.wait()
    slots[mine] = pair[0] + pair[1]
    copies = []
    for k, peer in enumerate(far):
        copy = pltpu.make_async_remote_copy(
            src_ref=slots.at[mine],
            dst_ref=slots.at[mine],
            send_sem=send.at[k],
            recv_sem=recv.at[k],
            device_id=peer,
            device_id_type=MESH,
        )
        copy.start()
        copies.append(copy)
    for copy in copies:
        copy.wait()
    o_ref[...] = jnp.sum(slots[...], axis=0)


def sum_all(values, collective_id):
    crops, n = lax.axis_size("crop"), lax.axis_size("chan")
    chips = crops * n // 2
    flat = jnp.concatenate([v.reshape(-1) for v in values])
    rows = -(-flat.shape[0] // 2048) * 8
    flat = jnp.pad(flat, (0, rows * 256 - flat.shape[0])).reshape(rows, 256)
    total = pl.pallas_call(
        functools.partial(sum_kernel, crops, n),
        out_shape=jax.ShapeDtypeStruct((rows, 256), f32),
        in_specs=[pl.BlockSpec(memory_space=pltpu.VMEM)],
        out_specs=pl.BlockSpec(memory_space=pltpu.VMEM),
        scratch_shapes=[
            pltpu.VMEM((2, rows, 256), f32),
            pltpu.VMEM((chips, rows, 256), f32),
            pltpu.SemaphoreType.DMA((2,)),
            pltpu.SemaphoreType.DMA((chips - 1,)),
            pltpu.SemaphoreType.DMA((chips - 1,)),
        ],
        compiler_params=pltpu.CompilerParams(collective_id=collective_id, has_side_effects=True),
    )(flat).reshape(-1)
    outs, at = [], 0
    for v in values:
        outs.append(total[at : at + v.size].reshape(v.shape))
        at += v.size
    return outs


def conv_forward(values, weight, rate, pad):
    kernel = weight.reshape(3, 3, weight.shape[1], weight.shape[2])
    return lax.conv_general_dilated(
        values[None],
        kernel,
        (1, 1),
        ((pad, pad), (rate, rate)),
        rhs_dilation=(rate, rate),
        dimension_numbers=("NHWC", "HWIO", "NHWC"),
        preferred_element_type=f32,
    )[0]


def conv_back_input(gradient, weight, rate, pad):
    kernel = weight.reshape(3, 3, weight.shape[1], weight.shape[2])[::-1, ::-1]
    return lax.conv_general_dilated(
        gradient[None],
        kernel,
        (1, 1),
        ((pad, pad), (rate, rate)),
        rhs_dilation=(rate, rate),
        dimension_numbers=("NHWC", "HWOI", "NHWC"),
        preferred_element_type=f32,
    )[0]


def conv_back_weight(inputs, gradient, rate, pad):
    out = lax.conv_general_dilated(
        inputs,
        gradient,
        (rate, rate),
        ((pad, pad), (rate, rate)),
        dimension_numbers=("CHWN", "IHWO", "HWNC"),
        preferred_element_type=f32,
    )
    return out.reshape(9, inputs.shape[3], gradient.shape[3])


def neighbours(values_up, values_down):
    n = lax.axis_size("chan")
    from_below = lax.ppermute(values_up, "chan", [(i + 1, i) for i in range(n - 1)])
    from_above = lax.ppermute(values_down, "chan", [(i, i + 1) for i in range(n - 1)])
    return from_below, from_above


def with_halo(values):
    from_below, from_above = neighbours(values[:1], values[-1:])
    return jnp.concatenate([from_above, values, from_below], axis=0)


def act_parts(values, average, inverse, scales, shifts):
    normed = (values - average) * inverse
    return normed, scales * normed + shifts


def gelu_back(before, incoming):
    return jax.vjp(jax.nn.gelu, before)[1](incoming)[0]


def moments(totals, samples):
    average = totals[0] / samples
    return average, lax.rsqrt(totals[1] / samples - average * average + epsilon)


def sums_of(values):
    return jnp.stack([jnp.sum(values, axis=(0, 1)), jnp.sum(values * values, axis=(0, 1))])


def grad_sums(pushed, normed):
    return jnp.stack([jnp.sum(pushed * normed, axis=(0, 1)), jnp.sum(pushed, axis=(0, 1))])


def norm_pull(pushed, normed, inverse, scales, totals, samples):
    return (scales * inverse) * (pushed - totals[1] / samples - normed * (totals[0] / samples))


def up_rows(first, count, coarse_first, coarse_count, fine_side):
    fine = first + jnp.arange(count)
    pos = jnp.clip((fine.astype(f32) + 0.5) / 4.0 - 0.5, 0.0, FA - 1.0)
    coarse = (coarse_first + jnp.arange(coarse_count)).astype(f32)
    table = jnp.maximum(0.0, 1.0 - jnp.abs(pos[:, None] - coarse[None, :]))
    return jnp.where(((fine >= 0) & (fine < fine_side))[:, None], table, 0.0)


def own_rows(values, axis):
    size = values.shape[axis] // lax.axis_size("chan")
    return lax.dynamic_slice_in_dim(values, lax.axis_index("chan") * size, size, axis)


def per_device(
    features,
    low_in,
    offsets,
    d_logits,
    w_point,
    w_atrous,
    w_pool,
    w_proj,
    w_low,
    w_dec1,
    w_dec1_low,
    w_dec2,
    w_cls,
    b_cls,
    bn_gain,
    bn_shift,
    low_gain,
    low_shift,
):
    n = lax.axis_size("chan")
    crops = lax.axis_size("crop")
    me = lax.axis_index("chan")
    my_crop = lax.axis_index("crop")
    fine = low_in.shape[2]
    rows = fine // n
    coarse_rows = FA // n
    channels = w_dec2.shape[2]
    c_in = features.shape[1]
    low_width = w_low.shape[1]
    coarse_samples = FA * FA * crops
    fine_samples = fine * fine * crops

    own = w_dec2.shape[1]
    classes = w_cls.shape[1]
    side = w_dec1_low.transpose(2, 0, 1).reshape(own, 9 * low_width)
    tail = jnp.concatenate([side, w_cls], axis=1)
    tail = jnp.pad(tail, ((0, 0), (0, -tail.shape[1] % channels)))
    tail_rows = tail.shape[1] // channels
    tail = tail.reshape(own, tail_rows, channels).transpose(1, 0, 2)
    packed = lax.all_gather(jnp.concatenate([w_proj, w_dec1, tail, w_dec2]), "chan")
    packed = packed.transpose(1, 0, 2, 3).reshape(-1, channels, channels)
    proj_full, dec1_full = packed[:5], packed[5:14]
    tail_full = packed[14 : 14 + tail_rows].transpose(1, 0, 2).reshape(channels, -1)
    dec2_full = packed[14 + tail_rows :]
    dec1_low_full = tail_full[:, : 9 * low_width].reshape(channels, 9, low_width)
    dec1_low_full = dec1_low_full.transpose(1, 2, 0)
    cls_full = tail_full[:, 9 * low_width : 9 * low_width + classes]
    norms = lax.all_gather(jnp.concatenate([bn_gain, bn_shift]), "chan", axis=1, tiled=True)
    gains, shifts = norms[:8], norms[8:]

    row_index = me * rows + jnp.arange(rows, dtype=jnp.int32)
    col_index = jnp.arange(fine, dtype=jnp.int32)
    rows_valid = offsets[0, 0] + 4 * row_index < SCENE_H
    cols_valid = offsets[0, 1] + 4 * col_index < SCENE_W
    mask = (rows_valid[:, None] & cols_valid[None, :]).astype(f32)

    source = features[0].T.reshape(FA, FA, c_in)
    parts = [jnp.einsum("hwc,co->hwo", source, w_point, preferred_element_type=f32)]
    for k in range(3):
        parts.append(conv_forward(source, w_atrous[k], atrous_rates[k], atrous_rates[k]))
    parts = jnp.concatenate([p.astype(bf16) for p in parts], axis=-1)
    low_terms = jnp.einsum("chw,co->how", low_in[0], w_low, preferred_element_type=f32).astype(bf16)
    low_pre = lax.psum_scatter(low_terms, "chan", scatter_dimension=0, tiled=True).astype(f32)
    low_pre = low_pre.transpose(0, 2, 1)
    branch_pre = lax.psum_scatter(parts, "chan", scatter_dimension=0, tiled=True).astype(f32)

    pooled = jnp.mean(features[0].astype(f32), axis=1).astype(bf16)
    pooled_all = lax.all_gather(pooled, "crop", axis=0)
    pool_part = jnp.einsum("bc,co->bo", pooled_all, w_pool, preferred_element_type=f32)
    low_sums, branch_sums, pool_sums = (sums_of(low_pre), sums_of(branch_pre), pool_part)
    low_sums, branch_sums, pool_pre = sum_all([low_sums, branch_sums, pool_sums / crops], 0)

    branch_average, branch_inverse = moments(branch_sums, coarse_samples)
    branch_gain = gains[0:4].reshape(-1)
    branch_normed, branch_before = act_parts(
        branch_pre, branch_average, branch_inverse, branch_gain, shifts[0:4].reshape(-1)
    )
    branch_bf = jax.nn.gelu(branch_before).astype(bf16)

    pool_average = jnp.mean(pool_pre, axis=0)
    pool_inverse = lax.rsqrt(jnp.mean(jnp.square(pool_pre - pool_average), axis=0) + epsilon)
    pool_normed, pool_before = act_parts(pool_pre, pool_average, pool_inverse, gains[4], shifts[4])
    pool_bf = jax.nn.gelu(pool_before).astype(bf16)
    own_pool = lax.dynamic_slice_in_dim(pool_bf, my_crop, 1, 0)

    proj_flat = proj_full[0:4].reshape(4 * channels, channels)
    projected = jnp.einsum("hwc,co->hwo", branch_bf, proj_flat, preferred_element_type=f32)
    projected = projected + jnp.dot(own_pool, proj_full[4], preferred_element_type=f32)
    (merged_sums,) = sum_all([sums_of(projected)], 1)
    merged_average, merged_inverse = moments(merged_sums, coarse_samples)
    merged_normed, merged_before = act_parts(
        projected, merged_average, merged_inverse, gains[5], shifts[5]
    )
    merged = with_halo(jax.nn.gelu(merged_before))

    row_table = up_rows(me * rows - 1, rows + 2, me * coarse_rows - 1, coarse_rows + 2, fine)
    col_table = up_rows(0, fine, 0, FA, fine)
    wide = jnp.einsum("hwc,jw->hjc", merged, col_table, precision=highest)
    upsampled = jnp.einsum("hjc,ih->ijc", wide, row_table, precision=highest).astype(bf16)

    low_average, low_inverse = moments(low_sums, fine_samples)
    low_normed, low_before = act_parts(low_pre, low_average, low_inverse, low_gain, low_shift)
    low_bf = with_halo(jax.nn.gelu(low_before).astype(bf16))

    both_in = jnp.concatenate([upsampled, low_bf], axis=-1)
    dec1_both = jnp.concatenate([dec1_full, dec1_low_full], axis=1)
    dec1_pre = conv_forward(both_in, dec1_both, 1, 0)
    first_average, first_inverse = moments(sum_all([sums_of(dec1_pre)], 2)[0], fine_samples)
    first_normed, first_before = act_parts(
        dec1_pre, first_average, first_inverse, gains[6], shifts[6]
    )
    first_bf = with_halo(jax.nn.gelu(first_before).astype(bf16))

    dec2_pre = conv_forward(first_bf, dec2_full, 1, 0)
    second_average, second_inverse = moments(sum_all([sums_of(dec2_pre)], 3)[0], fine_samples)
    second_normed, second_before = act_parts(
        dec2_pre, second_average, second_inverse, gains[7], shifts[7]
    )
    second_bf = jax.nn.gelu(second_before).astype(bf16)
    logits = jnp.einsum("hwc,co->ohw", second_bf, cls_full, preferred_element_type=f32)
    logits = (logits + b_cls[:, None, None]) * mask

    my_logits = lax.dynamic_slice_in_dim(d_logits[0], me * rows, rows, 1)
    masked = my_logits * mask.astype(bf16)
    cls_bias_grad = jnp.sum(masked.astype(f32), axis=(1, 2))
    cls_weight_grad = jnp.einsum("hwc,ohw->co", second_bf, masked, preferred_element_type=f32)
    second_grad = jnp.einsum("ohw,co->hwc", masked, cls_full, preferred_element_type=f32)
    second_pushed = gelu_back(second_before, second_grad)
    (second_totals,) = sum_all([grad_sums(second_pushed, second_normed)], 4)
    dec2_bf = norm_pull(
        second_pushed, second_normed, second_inverse, gains[7], second_totals, fine_samples
    ).astype(bf16)
    dec2_halo = with_halo(dec2_bf)

    first_grad = conv_back_input(dec2_halo, dec2_full, 1, 0)
    first_pushed = gelu_back(first_before, first_grad)
    (first_totals,) = sum_all([grad_sums(first_pushed, first_normed)], 5)
    dec2_wgrad = conv_back_weight(first_bf[None], dec2_bf[None], 1, 0)
    dec1_bf = norm_pull(
        first_pushed, first_normed, first_inverse, gains[6], first_totals, fine_samples
    ).astype(bf16)
    dec1_halo = with_halo(dec1_bf)

    both_grad = conv_back_input(dec1_halo, dec1_both, 1, 0)
    up_grad, low_act_grad = both_grad[..., :channels], both_grad[..., channels:]
    dec1_wgrad_both = conv_back_weight(both_in[None], dec1_bf[None], 1, 0)

    narrow = jnp.einsum("ijc,jw->iwc", up_grad, col_table, precision=highest)
    merged_part = jnp.einsum("iwc,ih->hwc", narrow, row_table[1:-1], precision=highest)
    from_below, from_above = neighbours(merged_part[:1], merged_part[-1:])
    merged_grad = merged_part[1:-1]
    merged_grad = merged_grad.at[:1].add(from_above).at[-1:].add(from_below)
    merged_pushed = gelu_back(merged_before, merged_grad)
    low_pushed = gelu_back(low_before, low_act_grad)
    merged_totals, low_totals = sum_all(
        [grad_sums(merged_pushed, merged_normed), grad_sums(low_pushed, low_normed)], 6
    )
    proj_bf = norm_pull(
        merged_pushed, merged_normed, merged_inverse, gains[5], merged_totals, coarse_samples
    ).astype(bf16)
    low_pre_bf = norm_pull(
        low_pushed, low_normed, low_inverse, low_gain, low_totals, fine_samples
    ).astype(bf16)

    branch_act_grad = jnp.einsum("hwo,co->hwc", proj_bf, proj_flat, preferred_element_type=f32)
    proj_wgrad_flat = jnp.einsum("hwc,hwo->co", branch_bf, proj_bf, preferred_element_type=f32)
    branch_pushed = gelu_back(branch_before, branch_act_grad)
    crop_slot = (jnp.arange(crops) == my_crop).astype(f32)
    proj_sums = crop_slot[:, None] * jnp.sum(proj_bf.astype(f32), axis=(0, 1))[None]
    branch_totals, proj_sums, cls_weight_grad, cls_bias_grad = sum_all(
        [grad_sums(branch_pushed, branch_normed), proj_sums, cls_weight_grad, cls_bias_grad], 7
    )
    branch_grad = norm_pull(
        branch_pushed, branch_normed, branch_inverse, branch_gain, branch_totals, coarse_samples
    ).astype(bf16)
    branch_full = lax.all_gather(branch_grad, "chan", axis=0, tiled=True)
    branch_all = lax.all_gather(branch_full, "crop", axis=0)
    source_all = lax.all_gather(source, "crop", axis=0)

    pool_act_grad = jnp.einsum("co,bo->bc", proj_full[4].astype(f32), proj_sums, precision=highest)
    proj_wgrad_pool = jnp.einsum("bc,bo->co", pool_bf.astype(f32), proj_sums, precision=highest)
    pool_pushed = gelu_back(pool_before, pool_act_grad)
    pool_totals = jnp.stack([jnp.sum(pool_pushed * pool_normed, 0), jnp.sum(pool_pushed, 0)])
    pool_grad = norm_pull(
        pool_pushed, pool_normed, pool_inverse, gains[4], pool_totals, crops
    ).astype(bf16)
    own_pool_grad = lax.dynamic_slice_in_dim(pool_grad, my_crop, 1, 0)
    pool_wgrad = jnp.einsum("bc,bo->co", pooled_all, pool_grad, preferred_element_type=f32)

    low_full = lax.all_gather(low_pre_bf.transpose(0, 2, 1), "chan", axis=0, tiled=True)
    low_wgrad = jnp.einsum("chw,how->co", low_in[0], low_full, preferred_element_type=f32)
    early_grad = jnp.einsum("how,co->chw", low_full, w_low, preferred_element_type=f32)

    by_branch = lambda v, k: v[..., k * channels : (k + 1) * channels]
    source_grad = jnp.einsum(
        "hwo,co->hwc", by_branch(branch_full, 0), w_point, preferred_element_type=f32
    )
    point_wgrad = jnp.einsum(
        "bhwc,bhwo->co", source_all, by_branch(branch_all, 0), preferred_element_type=f32
    )
    atrous_wgrad = []
    for k in range(3):
        rate = atrous_rates[k]
        source_grad = source_grad + conv_back_input(
            by_branch(branch_full, k + 1), w_atrous[k], rate, rate
        )
        atrous_wgrad.append(
            conv_back_weight(source_all, by_branch(branch_all, k + 1), rate, rate)
        )
    pooled_grad = jnp.einsum("bo,co->bc", own_pool_grad, w_pool, preferred_element_type=f32)
    source_grad = source_grad + pooled_grad[0] / (FA * FA)

    scatter = lambda v, axis: lax.psum_scatter(v, "chan", scatter_dimension=axis, tiled=True)
    side_part = dec1_wgrad_both[:, channels:].transpose(2, 0, 1).reshape(channels, -1)
    side_size = side_part.shape[1]
    side_part = jnp.pad(side_part, ((0, 0), (0, -side_size % channels)))
    side_part = side_part.reshape(channels, -1, channels).transpose(1, 0, 2)
    blocks = jnp.concatenate(
        [
            dec2_wgrad.astype(bf16),
            dec1_wgrad_both[:, :channels].astype(bf16),
            proj_wgrad_flat.reshape(4, channels, channels).astype(bf16),
            side_part.astype(bf16),
        ]
    )
    blocks = blocks.reshape(-1, n, own, channels).transpose(1, 0, 2, 3)
    blocks = lax.psum_scatter(blocks, "chan", scatter_dimension=0, tiled=False).astype(f32)
    blocks, low_wgrad = lax.psum((blocks, low_wgrad), "crop")
    dec2_wgrad, dec1_wgrad, proj_wgrad = blocks[:9], blocks[9:18], blocks[18:22]
    side_wgrad = blocks[22:].transpose(1, 0, 2).reshape(own, -1)[:, :side_size]
    side_wgrad = side_wgrad.reshape(own, 9, low_width).transpose(1, 2, 0)
    proj_wgrad = jnp.concatenate([proj_wgrad, own_rows(proj_wgrad_pool, 0)[None]], axis=0)

    gain_rows = [branch_totals[0].reshape(4, -1), pool_totals[0:1], merged_totals[0:1]]
    gain_rows += [first_totals[0:1], second_totals[0:1]]
    shift_rows = [branch_totals[1].reshape(4, -1), pool_totals[1:2], merged_totals[1:2]]
    shift_rows += [first_totals[1:2], second_totals[1:2]]
    return (
        logits[None],
        source_grad.reshape(FA * FA, c_in).T[None],
        early_grad[None],
        point_wgrad,
        jnp.stack(atrous_wgrad),
        pool_wgrad,
        proj_wgrad,
        low_wgrad,
        dec1_wgrad,
        side_wgrad,
        dec2_wgrad,
        own_rows(cls_weight_grad, 0),
        cls_bias_grad,
        own_rows(jnp.concatenate(gain_rows), 1),
        own_rows(jnp.concatenate(shift_rows), 1),
        low_totals[0],
        low_totals[1],
    )


def solution(mesh):
    placed = (
        P("crop", "chan", None),
        P("crop", "chan", None, None),
        P("crop", None),
        P("crop", None, None, None),
        P("chan", None),
        P(None, None, "chan", None),
        P("chan", None),
        P(None, "chan", None),
        P("chan", None),
        P(None, "chan", None),
        P(None, None, "chan"),
        P(None, "chan", None),
        P("chan", None),
        P(),
        P(None, "chan"),
        P(None, "chan"),
        P(),
        P(),
    )
    return jax.shard_map(
        per_device,
        mesh=mesh,
        in_specs=placed,
        out_specs=(
            P("crop", None, "chan", None),
            P("crop", "chan", None),
            P("crop", "chan", None, None),
            P("chan", None),
            P(None, None, "chan", None),
            P("chan", None),
            P(None, "chan", None),
            P("chan", None),
            P(None, "chan", None),
            P(None, None, "chan"),
            P(None, "chan", None),
            P("chan", None),
            P(),
            P(None, "chan"),
            P(None, "chan"),
            P(),
            P(),
        ),
        check_vma=False,
    )
```

```python
import functools

import jax
import jax.numpy as jnp
from jax import lax
from jax.experimental import pallas as pl
from jax.experimental.pallas import tpu as pltpu
from jax.sharding import PartitionSpec as P

FA = 32
SCENE_H = 1024
SCENE_W = 2048

epsilon = 1e-05
highest = lax.Precision.HIGHEST
atrous_rates = (6, 12, 18)
f32 = jnp.float32
bf16 = jnp.bfloat16
BOTH = ("crop", "chan")


MESH = pl.DeviceIdType.MESH


def chip_peers(crops, n):
    my_crop, me = lax.axis_index("crop"), lax.axis_index("chan")
    core = lax.rem(me, 2)
    chips = n // 2
    other = (my_crop, me + 1 - 2 * core)
    far = []
    for i in range(crops):
        for j in range(chips):
            if i or j:
                far.append((lax.rem(my_crop + i, crops), lax.rem(me + 2 * j, n)))
    return other, far


GELU_A = 0.7978845608028654
GELU_B = 0.044715


def gelu(x):
    return 0.5 * x * (1.0 + jnp.tanh(GELU_A * (x + GELU_B * x * x * x)))


def gelu_slope(x):
    square = x * x
    t = jnp.tanh(GELU_A * x * (1.0 + GELU_B * square))
    return 0.5 * (1.0 + t) + (0.5 * GELU_A) * x * (1.0 - t * t) * (1.0 + (3.0 * GELU_B) * square)


def dot(a, b):
    return jnp.dot(a, b, preferred_element_type=f32)


def dot_nt(a, b):
    return lax.dot_general(a, b, (((1,), (1,)), ((), ())), preferred_element_type=f32)


def dot_tn(a, b):
    return lax.dot_general(a, b, (((0,), (0,)), ((), ())), preferred_element_type=f32)


def dot_exact(table, values):
    high = values.astype(bf16)
    rest = values - high.astype(f32)
    middle = rest.astype(bf16)
    low = (rest - middle.astype(f32)).astype(bf16)
    return dot(table, high) + (dot(table, middle) + dot(table, low))


def fold(values):
    return jnp.sum(values.reshape(values.shape[0] // 8, 8, values.shape[1]), axis=0)


def row_of(values):
    return jnp.sum(values, axis=0, keepdims=True)


def barrier_with(peers):
    barrier = pltpu.get_barrier_semaphore()
    for peer in peers:
        pl.semaphore_signal(barrier, inc=1, device_id=peer, device_id_type=MESH)
    return lambda: pl.semaphore_wait(barrier, len(peers))


def remote(src, dst, send, recv, peer):
    return pltpu.make_async_remote_copy(
        src_ref=src, dst_ref=dst, send_sem=send, recv_sem=recv, device_id=peer, device_id_type=MESH
    )


class Swap:
    def __init__(self, crops, n, pair, slots, pair_sems, send, recv):
        self.other, self.far = chip_peers(crops, n)
        me = lax.axis_index("chan")
        self.core = lax.rem(me, 2)
        self.mine = lax.axis_index("crop") * (n // 2) + lax.div(me, 2)
        self.pair, self.slots, self.pair_sems = pair, slots, pair_sems
        self.send, self.recv = send, recv

    def start(self):
        here = self.pair.at[self.core]
        copy = remote(here, here, self.pair_sems.at[0], self.pair_sems.at[1], self.other)
        copy.start()
        copy.wait()
        self.slots[self.mine] = self.pair[0] + self.pair[1]
        self.copies = []
        for k, peer in enumerate(self.far):
            slot = self.slots.at[self.mine]
            copy = remote(slot, slot, self.send.at[k], self.recv.at[k], peer)
            copy.start()
            self.copies.append(copy)

    def finish(self):
        for copy in self.copies:
            copy.wait()
        return jnp.sum(self.slots[...], axis=0)


class WideSwap:
    def __init__(self, crops, n, pair, first, second, pair_sems, send, recv):
        my_crop, me = lax.axis_index("crop"), lax.axis_index("chan")
        self.core, self.crop, self.chip = lax.rem(me, 2), my_crop, lax.div(me, 2)
        self.other = (my_crop, me + 1 - 2 * self.core)
        self.over_crops = [(lax.rem(my_crop + i, crops), me) for i in range(1, crops)]
        self.over_chips = [(my_crop, lax.rem(me + 2 * j, n)) for j in range(1, n // 2)]
        self.pair, self.first, self.second = pair, first, second
        self.pair_sems, self.send, self.recv = pair_sems, send, recv

    def run(self):
        here = self.pair.at[self.core]
        copy = remote(here, here, self.pair_sems.at[0], self.pair_sems.at[1], self.other)
        copy.start()
        copy.wait()
        self.first[self.crop] = self.pair[0] + self.pair[1]
        k = 0
        copies = []
        for peer in self.over_crops:
            slot = self.first.at[self.crop]
            copies.append(remote(slot, slot, self.send.at[k], self.recv.at[k], peer))
            copies[-1].start()
            k += 1
        for copy in copies:
            copy.wait()
        self.second[self.chip] = jnp.sum(self.first[...], axis=0)
        copies = []
        for peer in self.over_chips:
            slot = self.second.at[self.chip]
            copies.append(remote(slot, slot, self.send.at[k], self.recv.at[k], peer))
            copies[-1].start()
            k += 1
        for copy in copies:
            copy.wait()
        return jnp.sum(self.second[...], axis=0)


def put_pair(ref, core, a, b):
    ref[core, 0:1] = a[:, :128]
    ref[core, 1:2] = a[:, 128:]
    ref[core, 2:3] = b[:, :128]
    ref[core, 3:4] = b[:, 128:]


def get_pair(total):
    return (
        jnp.concatenate([total[0:1], total[1:2]], axis=1),
        jnp.concatenate([total[2:3], total[3:4]], axis=1),
    )


def spread_row(row):
    return jnp.broadcast_to(row, (128, 128)).T


def up_weights(i, me, n, rows, coarse_rows):
    lower = (2 * i - 3) // 8
    upper_weight = (2 * i - 3 - 8 * lower) / 8.0
    a, b = 1.0 - upper_weight, upper_weight
    if lower < 0:
        top = me == 0
        a, b = jnp.where(top, 0.0, a), jnp.where(top, 1.0, b)
    if lower + 1 >= coarse_rows:
        bottom = me == n - 1
        a, b = jnp.where(bottom, 1.0, a), jnp.where(bottom, 0.0, b)
    if i < 0:
        a, b = jnp.where(me == 0, 0.0, a), jnp.where(me == 0, 0.0, b)
    if i >= rows:
        a, b = jnp.where(me == n - 1, 0.0, a), jnp.where(me == n - 1, 0.0, b)
    return lower + 1, a, b


DECODER_REFS = (
    "branch",
    "low",
    "pool_part",
    "norms",
    "low_gain",
    "low_shift",
    "proj",
    "w1",
    "w1low",
    "w2",
    "cls_t",
    "bias",
    "dlog",
    "mask",
    "up",
    "up_t",
    "logits",
    "branch_out",
    "pool_out",
    "pool_bf",
    "proj_sums",
    "low_out",
    "totals",
    "low_totals",
    "wgrads",
    "low_ext",
    "low_push",
    "lowx",
    "merged_ext",
    "merged_part",
    "dec1",
    "dec2",
    "pushed",
    "pushed1",
    "x1",
    "x2",
    "g2",
    "g1",
    "yt",
    "branch_bf",
    "proj_bf",
    "second",
    "flip",
)


def decoder_kernel(crops, n, samples, *refs):
    names = DECODER_REFS
    ref = dict(zip(names, refs))
    rest = list(refs[len(names) :])
    (wide_pair, wide_first, wide_second, wide_psem, wide_send, wide_recv) = rest[:6]
    (pair, slots, psem, send, recv, halo_send, halo_recv) = rest[6:13]

    coarse_samples, fine_samples = samples
    my_crop, me = lax.axis_index("crop"), lax.axis_index("chan")
    core = lax.rem(me, 2)
    above = (my_crop, lax.rem(me + n - 1, n))
    below = (my_crop, lax.rem(me + 1, n))
    low_width = ref["low"].shape[0]
    fine_cells = ref["low"].shape[1]
    rows = fine_cells // 128
    coarse_cells = ref["branch"].shape[0]
    coarse_rows = coarse_cells // FA
    c = ref["w2"].shape[2]
    own = c // n
    chunk = min(4, rows)

    other, far = chip_peers(crops, n)
    wait_barrier = barrier_with([other, above, below] + far)

    swaps = [
        Swap(crops, n, pair.at[i], slots.at[i], psem.at[i], send.at[i], recv.at[i])
        for i in range(pair.shape[0])
    ]
    wides = [
        WideSwap(
            crops, n, wide_pair.at[i], wide_first.at[i], wide_second.at[i],
            wide_psem.at[i], wide_send.at[i], wide_recv.at[i],
        )
        for i in range(2)
    ]
    for i in range(pair.shape[0]):
        pair[i, core] = jnp.zeros((8, 128), f32)
    for i in range(2):
        wide_pair[i, core] = jnp.zeros(wide_pair.shape[2:], f32)

    def halo(i, first, last, to_above, to_below):
        copies = [
            remote(first, to_above, halo_send.at[i, 0], halo_recv.at[i, 0], above),
            remote(last, to_below, halo_send.at[i, 1], halo_recv.at[i, 1], below),
        ]
        for copy in copies:
            copy.start()
        return copies

    def fine_halo(i, values):
        return halo(
            i,
            values.at[pl.ds(128, 128)],
            values.at[pl.ds(rows * 128, 128)],
            values.at[pl.ds((rows + 1) * 128, 128)],
            values.at[pl.ds(0, 128)],
        )

    def gain(k):
        return ref["norms"][k : k + 1]

    def shift(k):
        return ref["norms"][8 + k : 9 + k]

    def moments(total, square, count):
        average = total * (1.0 / count)
        return average, lax.rsqrt(square * (1.0 / count) - average * average + epsilon)

    column = lax.broadcasted_iota(jnp.int32, (128, c), 0)

    def put_three(target, base, y):
        target[pl.ds(base, 128), 0:c] = jnp.where(column == 0, 0.0, pltpu.roll(y, 1, 0)).astype(bf16)
        target[pl.ds(base, 128), c : 2 * c] = y.astype(bf16)
        target[pl.ds(base, 128), 2 * c : 3 * c] = jnp.where(
            column == 127, 0.0, pltpu.roll(y, 127, 0)
        ).astype(bf16)

    def inside(i):
        at_top = jnp.logical_and(me == 0, i == 0)
        at_bottom = jnp.logical_and(me == n - 1, i == rows + 1)
        return jnp.where(jnp.logical_or(at_top, at_bottom), 0.0, 1.0)

    def each_row(body, first, last, carry):
        def step(i, kept):
            return body(i, pl.multiple_of(i * 128, 128), kept)

        return lax.fori_loop(first, last, step, carry)

    zero = jnp.zeros((8, c), f32)

    low_ext = ref["low_ext"]
    low_ext[:, 128 : 128 + fine_cells] = ref["low"][...]
    wait_barrier()
    low_copies = halo(
        0,
        low_ext.at[:, pl.ds(128, 128)],
        low_ext.at[:, pl.ds(rows * 128, 128)],
        low_ext.at[:, pl.ds((rows + 1) * 128, 128)],
        low_ext.at[:, pl.ds(0, 128)],
    )

    def add_low(i, base, kept):
        v = low_ext[:, pl.ds(base, 128)]
        return kept[0] + v, kept[1] + v * v

    low_zero = jnp.zeros((low_width, 128), f32)
    low_sum, low_square = each_row(add_low, 1, rows + 1, (low_zero, low_zero))

    def lanes_of(values):
        return row_of(values.T)

    wide = wide_pair.at[0]
    for k in range(4):
        v = ref["branch"][:, k * c : (k + 1) * c]
        wide[core, k : k + 1] = row_of(v)
        wide[core, 4 + k : 5 + k] = row_of(v * v)
    wide[core, 8:16] = jnp.where(
        lax.broadcasted_iota(jnp.int32, (8, c), 0) == my_crop, ref["pool_part"][0:1], 0.0
    )
    wide[core, 16:17, 0:low_width] = lanes_of(low_sum)
    wide[core, 17:18, 0:low_width] = lanes_of(low_square)
    total_a = wides[0].run()

    def branch_parts(k):
        average, inverse = moments(total_a[k : k + 1], total_a[4 + k : 5 + k], coarse_samples)
        normed = (ref["branch"][:, k * c : (k + 1) * c] - average) * inverse
        return normed, gain(k) * normed + shift(k), inverse

    projected = jnp.zeros((coarse_cells, c), f32)
    for k in range(4):
        y = gelu(branch_parts(k)[1]).astype(bf16)
        ref["branch_bf"][:, k * c : (k + 1) * c] = y
        projected = projected + dot(y, ref["proj"][k])
    pool_here = lax.broadcasted_iota(jnp.int32, (8, c), 0) < crops
    pool_pre = total_a[8:16]
    pool_average = row_of(pool_pre) * (1.0 / crops)
    pool_spread = jnp.where(pool_here, pool_pre - pool_average, 0.0)
    pool_inverse = lax.rsqrt(row_of(pool_spread * pool_spread) * (1.0 / crops) + epsilon)
    pool_normed = pool_spread * pool_inverse
    pool_before = gain(4) * pool_normed + shift(4)
    pool_bf = gelu(pool_before)
    pool_bf = jnp.concatenate([pool_bf, jnp.zeros((8, c), f32)], axis=0).astype(bf16)
    ref["pool_bf"][...] = pool_bf
    pool_term = dot(pool_bf, ref["proj"][4])
    my_row = lax.broadcasted_iota(jnp.int32, (16, c), 0) == my_crop
    projected = projected + row_of(jnp.where(my_row, pool_term, 0.0))
    merged_ext = ref["merged_ext"]
    merged_ext[pl.ds(FA, coarse_cells)] = projected
    put_pair(pair.at[0], core, row_of(projected), row_of(projected * projected))
    merged_copies = halo(
        1,
        merged_ext.at[pl.ds(FA, FA)],
        merged_ext.at[pl.ds(coarse_cells, FA)],
        merged_ext.at[pl.ds(FA + coarse_cells, FA)],
        merged_ext.at[pl.ds(0, FA)],
    )
    swaps[0].start()

    for copy in low_copies:
        copy.wait()
    low_average = total_a[16:17, 0:128] * (1.0 / fine_samples)
    low_variance = total_a[17:18, 0:128] * (1.0 / fine_samples) - low_average * low_average
    low_inverse_row = lax.rsqrt(low_variance + epsilon)
    low_average = spread_row(low_average)[0:low_width]
    low_inverse = spread_row(low_inverse_row)[0:low_width]
    lane = lax.broadcasted_iota(jnp.int32, (low_width, 128), 1)

    def low_parts(base):
        normed = (low_ext[:, pl.ds(base, 128)] - low_average) * low_inverse
        return normed, ref["low_gain"][...] * normed + ref["low_shift"][...]

    def low_row(i, base, kept):
        y = gelu(low_parts(base)[1]) * inside(i)
        lowx = ref["lowx"]
        lowx[0:low_width, pl.ds(base, 128)] = jnp.where(lane == 0, 0.0, pltpu.roll(y, 1, 1)).astype(bf16)
        lowx[low_width : 2 * low_width, pl.ds(base, 128)] = y.astype(bf16)
        lowx[2 * low_width : 3 * low_width, pl.ds(base, 128)] = jnp.where(
            lane == 127, 0.0, pltpu.roll(y, 127, 1)
        ).astype(bf16)
        return kept

    each_row(low_row, 0, rows + 2, 0)

    merged_sum, merged_square = get_pair(swaps[0].finish())
    for copy in merged_copies:
        copy.wait()
    merged_average, merged_inverse = moments(merged_sum, merged_square, coarse_samples)

    def merged_parts(first, count):
        normed = (merged_ext[pl.ds(first, count)] - merged_average) * merged_inverse
        return normed, gain(5) * normed + shift(5)

    coarse_wide = []
    for j in range(coarse_rows + 2):
        coarse_wide.append(dot_exact(ref["up"][...], gelu(merged_parts(j * FA, FA)[1])))
    for i in range(-1, rows + 1):
        lower, a, b = up_weights(i, me, n, rows, coarse_rows)
        put_three(ref["x1"], (i + 1) * 128, a * coarse_wide[lower] + b * coarse_wide[lower + 1])

    def conv_loop(source, weight, target, extra):
        def step(i, kept):
            base = pl.multiple_of(i * (chunk * 128), 128)
            total = None
            for a in range(3):
                term = dot(source[pl.ds(base + a * 128, chunk * 128)], weight[a])
                total = term if total is None else total + term
            if extra is not None:
                total = total + extra(base)
            target[pl.ds(base + 128, chunk * 128)] = total
            return kept[0] + fold(total), kept[1] + fold(total * total)

        return lax.fori_loop(0, rows // chunk, step, (zero, zero))

    def low_term(base):
        total = None
        for a in range(3):
            term = dot_tn(ref["lowx"][:, pl.ds(base + a * 128, chunk * 128)], ref["w1low"][a])
            total = term if total is None else total + term
        return total

    dec1, dec2, pushed, pushed1 = ref["dec1"], ref["dec2"], ref["pushed"], ref["pushed1"]
    total, square = conv_loop(ref["x1"], ref["w1"], dec1, low_term)
    put_pair(pair.at[1], core, row_of(total), row_of(square))
    dec1_copies = fine_halo(2, dec1)
    swaps[1].start()
    total, square = get_pair(swaps[1].finish())
    for copy in dec1_copies:
        copy.wait()
    first_average, first_inverse = moments(total, square, fine_samples)

    def first_parts(base):
        normed = (dec1[pl.ds(base, 128)] - first_average) * first_inverse
        return normed, gain(6) * normed + shift(6)

    def first_row(i, base, kept):
        put_three(ref["x2"], base, gelu(first_parts(base)[1]) * inside(i))
        return kept

    each_row(first_row, 0, rows + 2, 0)
    total, square = conv_loop(ref["x2"], ref["w2"], dec2, None)
    put_pair(pair.at[2], core, row_of(total), row_of(square))
    dec2_copies = fine_halo(3, dec2)
    swaps[2].start()
    total, square = get_pair(swaps[2].finish())
    for copy in dec2_copies:
        copy.wait()
    second_average, second_inverse = moments(total, square, fine_samples)

    def second_parts(base):
        normed = (dec2[pl.ds(base, 128)] - second_average) * second_inverse
        return normed, gain(7) * normed + shift(7)

    def second_row(i, base, kept):
        normed, before = second_parts(base)
        ref["second"][pl.ds(base, 128)] = gelu(before).astype(bf16)
        grad = dot_tn(ref["dlog"][:, pl.ds(base, 128)], ref["cls_t"][...])
        push = gelu_slope(before) * grad
        pushed[pl.ds(base, 128)] = push
        own_row = jnp.where(jnp.logical_and(i > 0, i < rows + 1), 1.0, 0.0)
        push = push * own_row
        return kept[0] + fold(push * normed), kept[1] + fold(push)

    along, summed = each_row(second_row, 0, rows + 2, (zero, zero))
    put_pair(pair.at[3], core, row_of(along), row_of(summed))
    swaps[3].start()
    second = ref["second"]

    def logit_row(i, base, kept):
        out = pl.multiple_of(base - 128, 128)
        value = dot_nt(ref["cls_t"][...], second[pl.ds(base, 128)]) + ref["bias"][...]
        ref["logits"][:, pl.ds(out, 128)] = value * ref["mask"][:, pl.ds(out, 128)]
        return kept

    each_row(logit_row, 1, rows + 1, 0)
    flip = ref["flip"]
    flip[pl.ds(9 * low_width, 32)] = dot(
        ref["dlog"][:, 128 : 128 + fine_cells], second[pl.ds(128, fine_cells)]
    )
    bias_grad = jnp.zeros((32, 128), f32)
    for i in range(1, rows + 1):
        bias_grad = bias_grad + ref["dlog"][:, i * 128 : (i + 1) * 128].astype(f32)
    wide_pair[1, core, 16:17, 0:32] = row_of(bias_grad.T)
    second_along, second_summed = get_pair(swaps[3].finish())

    def pull(push, normed, k, inverse, along, summed, count):
        return (gain(k) * inverse) * (push - summed * (1.0 / count) - normed * (along * (1.0 / count)))

    def dec2_row(i, base, kept):
        g = pull(
            pushed[pl.ds(base, 128)], second_parts(base)[0], 7, second_inverse,
            second_along, second_summed, fine_samples,
        )
        put_three(ref["g2"], base, g * inside(i))
        return kept

    each_row(dec2_row, 0, rows + 2, 0)

    def back_loop(source, weight, use, carry):
        def step(i, kept):
            base = pl.multiple_of(i * (chunk * 128), 128)
            total = None
            for t in range(9):
                a, e = t // 3, t % 3
                piece = source[pl.ds(base + (2 - a) * 128, chunk * 128), (2 - e) * c : (3 - e) * c]
                term = dot_nt(piece, weight[a, e * c : (e + 1) * c])
                total = term if total is None else total + term
            return use(base, total, kept)

        return lax.fori_loop(0, rows // chunk, step, carry)

    def first_use(base, grad, kept):
        at = pl.ds(pl.multiple_of(base + 128, 128), chunk * 128)
        normed = (dec1[at] - first_average) * first_inverse
        push = gelu_slope(gain(6) * normed + shift(6)) * grad
        pushed1[at] = push
        return kept[0] + fold(push * normed), kept[1] + fold(push)

    along, summed = back_loop(ref["g2"], ref["w2"], first_use, (zero, zero))
    put_pair(pair.at[4], core, row_of(along), row_of(summed))
    pushed_copies = fine_halo(4, pushed1)
    swaps[4].start()

    wgrads = ref["wgrads"]

    def weight_grads(first, source, gradient):
        for a in range(3):
            part = dot_tn(
                source[pl.ds(a * 128, fine_cells), c : 2 * c], gradient[pl.ds(128, fine_cells)]
            ).astype(bf16)
            for h in range(n):
                wgrads[h, first + a] = part[h * own : (h + 1) * own]

    weight_grads(0, ref["x2"], ref["g2"])
    first_along, first_summed = get_pair(swaps[4].finish())
    for copy in pushed_copies:
        copy.wait()

    def dec1_row(i, base, kept):
        g = pull(
            pushed1[pl.ds(base, 128)], first_parts(base)[0], 6, first_inverse,
            first_along, first_summed, fine_samples,
        ) * inside(i)
        put_three(ref["g1"], base, g)
        return kept

    each_row(dec1_row, 0, rows + 2, 0)

    def up_use(base, grad, kept):
        dec2[pl.ds(pl.multiple_of(base + 128, 128), chunk * 128)] = grad
        return kept

    back_loop(ref["g1"], ref["w1"], up_use, 0)
    yt = ref["yt"]

    def yt_row(i, base, kept):
        here = ref["g1"][pl.ds(base, 128), c : 2 * c]
        for a in range(3):
            band = slice(a * 3 * low_width, (a + 1) * 3 * low_width)
            yt[band, pl.ds(base, 128)] = dot_nt(ref["w1low"][a], here)
        return kept

    each_row(yt_row, 0, rows + 2, 0)

    def low_back_row(i, base, kept):
        total = None
        for t in range(9):
            a, e = t // 3, t % 3
            at = pl.ds(pl.multiple_of(base + (1 - a) * 128, 128), 128)
            piece = yt[t * low_width : (t + 1) * low_width, at]
            if e == 0:
                piece = jnp.where(lane == 127, 0.0, pltpu.roll(piece, 127, 1))
            if e == 2:
                piece = jnp.where(lane == 0, 0.0, pltpu.roll(piece, 1, 1))
            total = piece if total is None else total + piece
        normed, before = low_parts(base)
        push = gelu_slope(before) * total
        ref["low_push"][:, pl.ds(pl.multiple_of(base - 128, 128), 128)] = push
        return kept[0] + push * normed, kept[1] + push

    low_along, low_summed = each_row(low_back_row, 1, rows + 1, (low_zero, low_zero))

    part = ref["merged_part"]
    row_sums = [None] * (coarse_rows + 2)
    for i in range(rows):
        lower, a, b = up_weights(i, me, n, rows, coarse_rows)
        grad = dec2[pl.ds((i + 1) * 128, 128)]
        for j, weight in ((lower, a), (lower + 1, b)):
            row_sums[j] = weight * grad if row_sums[j] is None else row_sums[j] + weight * grad
    along, summed = zero, zero
    for j in range(coarse_rows + 2):
        grad = dot_exact(ref["up_t"][...], row_sums[j])
        part[pl.ds(j * FA, FA)] = grad
        normed, before = merged_parts(j * FA, FA)
        push = gelu_slope(before) * grad
        along, summed = along + fold(push * normed), summed + fold(push)
    put_pair(pair.at[5], core, row_of(along), row_of(summed))
    pair[5, core, 4:5, 0:low_width] = lanes_of(low_along)
    pair[5, core, 5:6, 0:low_width] = lanes_of(low_summed)
    part_copies = halo(
        5,
        part.at[pl.ds(0, FA)],
        part.at[pl.ds(FA + coarse_cells, FA)],
        part.at[pl.ds((coarse_rows + 3) * FA, FA)],
        part.at[pl.ds((coarse_rows + 2) * FA, FA)],
    )
    swaps[5].start()
    weight_grads(3, ref["x1"], ref["g1"])
    total_g = swaps[5].finish()
    for copy in part_copies:
        copy.wait()
    merged_along, merged_summed = get_pair(total_g)
    low_along, low_summed = spread_row(total_g[4:5])[0:low_width], spread_row(total_g[5:6])[0:low_width]
    ref["low_totals"][...] = total_g[4:6]

    up_here = jnp.where(me == 0, 0.0, 1.0)
    down_here = jnp.where(me == n - 1, 0.0, 1.0)
    proj_bf = ref["proj_bf"]
    for j in range(1, coarse_rows + 1):
        grad = part[pl.ds(j * FA, FA)]
        if j == 1:
            grad = grad + up_here * part[pl.ds((coarse_rows + 2) * FA, FA)]
        if j == coarse_rows:
            grad = grad + down_here * part[pl.ds((coarse_rows + 3) * FA, FA)]
        normed, before = merged_parts(j * FA, FA)
        push = gelu_slope(before) * grad
        g = pull(push, normed, 5, merged_inverse, merged_along, merged_summed, coarse_samples)
        proj_bf[pl.ds((j - 1) * FA, FA)] = g.astype(bf16)

    push_all = []
    for k in range(4):
        normed, before, _ = branch_parts(k)
        push = gelu_slope(before) * dot_nt(proj_bf[...], ref["proj"][k])
        push_all.append(push)
        wide_pair[1, core, k : k + 1] = row_of(push * normed)
        wide_pair[1, core, 4 + k : 5 + k] = row_of(push)
    proj_row = row_of(proj_bf[...].astype(f32))
    wide_pair[1, core, 8:16] = jnp.where(
        lax.broadcasted_iota(jnp.int32, (8, c), 0) == my_crop, proj_row, 0.0
    )
    total_h = wides[1].run()
    ref["proj_sums"][...] = total_h[8:16]
    for k in range(4):
        normed, _, inverse = branch_parts(k)
        g = pull(
            push_all[k], normed, k, inverse, total_h[k : k + 1], total_h[4 + k : 5 + k], coarse_samples
        )
        ref["branch_out"][:, k * c : (k + 1) * c] = g.astype(bf16)

    sums = total_h[8:16]
    sums_high = sums.astype(bf16).astype(f32)
    sums_low = sums - sums_high
    spare = jnp.concatenate([sums_high, sums_low], axis=0)
    spare_mid = spare.astype(bf16)
    spare_rest = (spare - spare_mid.astype(f32)).astype(bf16)
    pieces = dot_nt(spare_mid, ref["proj"][4]) + dot_nt(spare_rest, ref["proj"][4])
    pool_push = gelu_slope(pool_before) * (pieces[0:8] + pieces[8:16])
    pool_push = jnp.where(pool_here, pool_push, 0.0)
    pool_along, pool_summed = row_of(pool_push * pool_normed), row_of(pool_push)
    pool_grad = pull(pool_push, pool_normed, 4, pool_inverse, pool_along, pool_summed, crops)
    pool_grad = jnp.where(pool_here, pool_grad, 0.0)
    ref["pool_out"][...] = jnp.concatenate([pool_grad, jnp.zeros((8, c), f32)], axis=0).astype(bf16)

    totals = ref["totals"]
    totals[0:4] = total_h[0:4]
    totals[4:5] = pool_along
    totals[5:6] = merged_along
    totals[6:7] = first_along
    totals[7:8] = second_along
    totals[8:12] = total_h[4:8]
    totals[12:13] = pool_summed
    totals[13:14] = merged_summed
    totals[14:15] = first_summed
    totals[15:16] = second_summed
    totals[16:24] = total_h[16:24]

    def low_out_row(i, base, kept):
        at = pl.ds(pl.multiple_of(base - 128, 128), 128)
        normed = low_parts(base)[0]
        g = (ref["low_gain"][...] * low_inverse) * (
            ref["low_push"][:, at] - low_summed * (1.0 / fine_samples) - normed * (low_along * (1.0 / fine_samples))
        )
        ref["low_out"][:, at] = g.astype(bf16)
        return kept

    each_row(low_out_row, 1, rows + 1, 0)

    for a in range(3):
        flip[pl.ds(a * 3 * low_width, 3 * low_width)] = dot(
            ref["lowx"][:, a * 128 : a * 128 + fine_cells], ref["g1"][pl.ds(128, fine_cells), c : 2 * c]
        )
    flip[pl.ds(9 * low_width + 32, 48)] = jnp.zeros((48, c), f32)
    turned = flip[...].T.astype(bf16)
    for k in range(4):
        product = dot_tn(ref["branch_bf"][:, k * c : (k + 1) * c], proj_bf[...]).astype(bf16)
        for h in range(n):
            rows_h = product[h * own : (h + 1) * own]
            if k < 3:
                wgrads[h, 6, :, k * c : (k + 1) * c] = rows_h
            else:
                wgrads[h, 7, :, 0:c] = rows_h
                wgrads[h, 7, :, c : 3 * c] = turned[h * own : (h + 1) * own]


def decoder(crops, n, samples, *args):
    low, branch = args[1], args[0]
    low_width, cells = low.shape
    rows = cells // 128
    coarse = branch.shape[0]
    c = branch.shape[1] // 4
    chips = crops * n // 2
    outer = (rows + 2) * 128
    S = jax.ShapeDtypeStruct
    V = pltpu.VMEM
    vmem = pl.BlockSpec(memory_space=pltpu.VMEM)
    return pl.pallas_call(
        functools.partial(decoder_kernel, crops, n, samples),
        out_shape=[
            S((32, cells), f32),
            S((coarse, 4 * c), bf16),
            S((16, c), bf16),
            S((16, c), bf16),
            S((8, c), f32),
            S((low_width, cells), bf16),
            S((24, c), f32),
            S((2, 128), f32),
            S((n, 8, c // n, 3 * c), bf16),
        ],
        in_specs=[vmem] * len(args),
        out_specs=[vmem] * 9,
        scratch_shapes=[
            V((low_width, outer), f32),
            V((low_width, cells), f32),
            V((3 * low_width, outer), bf16),
            V((coarse + 2 * FA, c), f32),
            V((coarse + 4 * FA, c), f32),
            V((outer, c), f32),
            V((outer, c), f32),
            V((outer, c), f32),
            V((outer, c), f32),
            V((outer, 3 * c), bf16),
            V((outer, 3 * c), bf16),
            V((outer, 3 * c), bf16),
            V((outer, 3 * c), bf16),
            V((9 * low_width, outer), f32),
            V((coarse, 4 * c), bf16),
            V((coarse, c), bf16),
            V((outer, c), bf16),
            V((512, c), f32),
            V((2, 2, 24, c), f32),
            V((2, crops, 24, c), f32),
            V((2, n // 2, 24, c), f32),
            pltpu.SemaphoreType.DMA((2, 2)),
            pltpu.SemaphoreType.DMA((2, crops + n // 2)),
            pltpu.SemaphoreType.DMA((2, crops + n // 2)),
            V((6, 2, 8, 128), f32),
            V((6, chips, 8, 128), f32),
            pltpu.SemaphoreType.DMA((6, 2)),
            pltpu.SemaphoreType.DMA((6, chips)),
            pltpu.SemaphoreType.DMA((6, chips)),
            pltpu.SemaphoreType.DMA((6, 2)),
            pltpu.SemaphoreType.DMA((6, 2)),
        ],
        compiler_params=pltpu.CompilerParams(
            collective_id=0, has_side_effects=True, vmem_limit_bytes=60 * 1024 * 1024
        ),
    )(*args)


class Gather:
    def __init__(self, n, send, recv):
        my_crop, self.me = lax.axis_index("crop"), lax.axis_index("chan")
        self.n, self.chips = n, n // 2
        self.core = lax.rem(self.me, 2)
        self.other = (my_crop, self.me + 1 - 2 * self.core)
        self.send, self.recv = send, recv
        self.peer = lambda j: (my_crop, lax.rem(self.me + 2 * j, n))

    def block(self, j):
        return lax.rem(self.me - 2 * j + self.n, self.n)

    def other_block(self, j):
        return lax.rem(self.me + 1 - 2 * self.core - 2 * j + self.n, self.n)

    def start(self, at):
        self.at = at
        self.far, self.pairs = [], []
        for j in range(1, self.chips):
            here = at(self.me)
            self.far.append(remote(here, here, self.send.at[j], self.recv.at[j], self.peer(j)))
            self.far[-1].start()
        self.forward(0)

    def forward(self, j):
        here = self.at(self.block(j))
        k = self.chips + j
        self.pairs.append(remote(here, here, self.send.at[k], self.recv.at[k], self.other))
        self.pairs[-1].start()

    def arrive(self, j):
        self.far[j - 1].wait_recv()
        self.forward(j)

    def finish(self):
        for copy in self.pairs:
            copy.wait_recv()

    def drain(self):
        for copy in self.far + self.pairs:
            copy.wait_send()


BACK_IN = [
    "grad",
    "src",
    "point",
    "atrous",
    "pool",
    "pooled_grad",
    "low_grad",
    "low_in",
    "low_w",
    "wgrads",
]
BACK_OUT = [
    "features",
    "point_w",
    "atrous_w",
    "pool_w",
    "early",
    "low_w_out",
    "blocks",
]
BACK_SCRATCH = [
    "all_grad",
    "shifted",
    "turned",
    "total",
    "low_all",
    "first",
    "pairs",
    "crossed",
    "halves",
    "lined",
    "low_parts",
]
BACK_SEMS = [
    "g_send",
    "g_recv",
    "l_send",
    "l_recv",
    "c_send",
    "c_recv",
    "f_send",
    "f_recv",
    "w_send",
    "w_recv",
]


def back_kernel(crops, n, *refs):
    ref = dict(zip(BACK_IN + BACK_OUT + BACK_SCRATCH + BACK_SEMS, refs))
    my_crop, me = lax.axis_index("crop"), lax.axis_index("chan")
    chips = n // 2
    core, chip = lax.rem(me, 2), lax.div(me, 2)
    block, width = ref["grad"].shape
    c = width // 4
    c_in = ref["src"].shape[2]
    cells = FA * FA
    groups = 8 // crops
    other = (my_crop, me + 1 - 2 * core)
    over_crops = [(lax.rem(my_crop + i, crops), me) for i in range(1, crops)]
    over_chips = [(my_crop, lax.rem(me + 2 * j, n)) for j in range(1, chips)]
    wait_barrier = barrier_with([other] + over_crops + over_chips)
    crop_of = lambda i: lax.rem(my_crop - i + crops, crops)
    all_grad, src = ref["all_grad"], ref["src"]

    def grad_at(crop):
        def at(b):
            return all_grad.at[crop, pl.ds(pl.multiple_of(b * block, block), block)]

        return at

    all_grad[my_crop, pl.ds(pl.multiple_of(me * block, block), block)] = ref["grad"][...]
    ref["low_all"][me] = ref["low_grad"][...]
    wait_barrier()

    gather = Gather(n, ref["g_send"], ref["g_recv"])
    gather.start(grad_at(my_crop))
    crossing = {}

    def cross(j):
        here = grad_at(my_crop)(gather.block(j))
        for i in range(1, crops):
            k = (i - 1) * chips + j
            copy = remote(here, here, ref["c_send"].at[k], ref["c_recv"].at[k], over_crops[i - 1])
            copy.start()
            crossing[i, j] = copy

    cross(0)
    w_send, w_recv = ref["w_send"], ref["w_recv"]
    first_copies = []
    for z in range(chips):
        copy = remote(
            ref["wgrads"].at[2 * z + 1 - core], ref["first"].at[z], w_send.at[z], w_recv.at[z], other
        )
        copy.start()
        first_copies.append(copy)
    low_gather = Gather(n, ref["l_send"], ref["l_recv"])
    low_gather.start(lambda b: ref["low_all"].at[b])

    column = lax.rem(lax.broadcasted_iota(jnp.int32, (128, 1), 0), FA)

    def shift_three(source, target, rate, first, last):
        def step(i, kept):
            base = pl.multiple_of(i * 128, 128)
            here = source(base)
            w = here.shape[1]
            wide = here.astype(f32)
            for slot, by in ((0, first), (2, last)):
                ok = jnp.logical_and(column + by >= 0, column + by < FA)
                moved = jnp.where(ok, pltpu.roll(wide, (-by) % 128, 0), 0.0)
                target[pl.ds(base, 128), slot * w : (slot + 1) * w] = moved.astype(bf16)
            target[pl.ds(base, 128), w : 2 * w] = here
            return kept

        lax.fori_loop(0, cells // 128, step, 0)

    shifted = ref["shifted"]

    def shift_source(i):
        crop = crop_of(i)
        for k in range(3):
            rate = atrous_rates[k]
            shift_three(lambda base: src[crop, pl.ds(base, 128)], shifted.at[i % 3, k], rate, -rate, rate)

    shift_source(0)

    for copy in first_copies:
        copy.wait()
    pairs, first, wgrads = ref["pairs"], ref["first"], ref["wgrads"]
    for z in range(chips):
        for g in range(8):
            pairs[z, g] = (wgrads[2 * z + core, g].astype(f32) + first[z, g].astype(f32)).astype(bf16)
    at = chips
    cross_copies = []
    for i in range(1, crops):
        target = lax.rem(my_crop + i, crops)
        copy = remote(
            pairs.at[:, pl.ds(target * groups, groups)],
            ref["crossed"].at[my_crop],
            w_send.at[at],
            w_recv.at[at],
            over_crops[i - 1],
        )
        copy.start()
        cross_copies.append(copy)
        at += 1
    for z in range(chips):
        for g in range(groups):
            ref["crossed"][my_crop, z, g] = pairs[z, my_crop * groups + g]

    for j in range(1, chips):
        gather.arrive(j)
        cross(j)
    for i in range(1, min(3, crops)):
        shift_source(i)
    gather.finish()

    total, turned = ref["total"], ref["turned"]
    pool_row = dot_nt(ref["pooled_grad"][...], ref["pool"][...])
    my_row = lax.broadcasted_iota(jnp.int32, pool_row.shape, 0) == my_crop
    pool_row = row_of(jnp.where(my_row, pool_row, 0.0)) * (1.0 / cells)
    total[...] = dot_nt(all_grad[my_crop, :, 0:c], ref["point"][...]) + pool_row
    for k in range(3):
        rate = atrous_rates[k]
        shift_three(
            lambda base: all_grad[my_crop, pl.ds(base, 128), (k + 1) * c : (k + 2) * c],
            turned, rate, rate, -rate,
        )
        for a in range(3):
            move = (a - 1) * rate
            count = (FA - abs(move)) * FA
            to, off = max(move, 0) * FA, max(-move, 0) * FA
            term = None
            for e in range(3):
                piece = dot_nt(turned[pl.ds(off, count), e * c : (e + 1) * c], ref["atrous"][k, 3 * a + e])
                term = piece if term is None else term + piece
            total[pl.ds(to, count)] = total[pl.ds(to, count)] + term

    def weight_part(i):
        crop = crop_of(i)
        part = dot_tn(src[crop], all_grad[crop, :, 0:c])
        ref["point_w"][...] = part if i == 0 else ref["point_w"][...] + part
        for k in range(3):
            rate = atrous_rates[k]
            for a in range(3):
                move = (a - 1) * rate
                count = (FA - abs(move)) * FA
                from_src, off = max(move, 0) * FA, max(-move, 0) * FA
                part = dot_tn(
                    shifted[i % 3, k, pl.ds(from_src, count)],
                    all_grad[crop, pl.ds(off, count), (k + 1) * c : (k + 2) * c],
                )
                for e in range(3):
                    piece = part[e * c_in : (e + 1) * c_in]
                    if i > 0:
                        piece = ref["atrous_w"][k, 3 * a + e] + piece
                    ref["atrous_w"][k, 3 * a + e] = piece

    weight_part(0)
    ref["features"][...] = total[...].T

    for copy in cross_copies:
        copy.wait()
    line_copies = []
    halves, lined = ref["halves"], ref["lined"]
    for z in range(chips):
        for g in range(groups):
            value = ref["crossed"][0, z, g].astype(f32)
            for i in range(1, crops):
                value = value + ref["crossed"][i, z, g].astype(f32)
            halves[z, g] = value.astype(bf16)
    for j in range(1, chips):
        target = lax.rem(chip + j, chips)
        copy = remote(
            halves.at[target], lined.at[chip], w_send.at[at], w_recv.at[at], over_chips[j - 1]
        )
        copy.start()
        line_copies.append(copy)
        at += 1
    for g in range(groups):
        lined[chip, g] = halves[chip, g]

    for j in range(1, chips):
        low_gather.arrive(j)
    low_gather.finish()
    rows = ref["low_all"].shape[2] // 128
    low_in, low_all = ref["low_in"], ref["low_all"]
    low_total = None
    for b in range(n):
        here = low_all[b]
        span = slice(b * rows * 128, (b + 1) * rows * 128)
        ref["early"][:, span] = dot(ref["low_w"][...], here)
        part = dot_nt(low_in[:, span], here)
        low_total = part if low_total is None else low_total + part
    low_parts = ref["low_parts"]
    low_parts[my_crop] = jnp.zeros(low_parts.shape[1:], f32)
    low_parts[my_crop, :, 0 : low_total.shape[1]] = low_total
    low_copies = []
    for i in range(1, crops):
        here = low_parts.at[my_crop]
        low_copies.append(remote(here, here, w_send.at[at], w_recv.at[at], over_crops[i - 1]))
        low_copies[-1].start()
        at += 1

    for copy in line_copies:
        copy.wait()
    blocks = ref["blocks"]
    for g in range(groups):
        value = lined[0, g].astype(f32)
        for z in range(1, chips):
            value = value + lined[z, g].astype(f32)
        blocks[my_crop * groups + g] = value
    share_copies = []
    for i in range(1, crops):
        here = blocks.at[pl.ds(my_crop * groups, groups)]
        share_copies.append(remote(here, here, w_send.at[at], w_recv.at[at], over_crops[i - 1]))
        share_copies[-1].start()
        at += 1

    pair_copies = []
    for i in range(1, crops):
        if i + 2 < crops:
            shift_source(i + 2)
        crop = crop_of(i)
        here = []
        for j in range(chips):
            crossing[i, j].wait_recv()
            k = (i - 1) * chips + j
            place = grad_at(crop)(gather.block(j))
            copy = remote(place, place, ref["f_send"].at[k], ref["f_recv"].at[k], other)
            copy.start()
            here.append(copy)
        for copy in here:
            copy.wait_recv()
        pair_copies += here
        weight_part(i)

    pooled = []
    for i in range(crops):
        mean = row_of(src[i].astype(f32)) * (1.0 / cells)
        pooled.append(mean)
    pooled = jnp.concatenate(pooled + [jnp.zeros((16 - crops, c_in), f32)], axis=0).astype(bf16)
    ref["pool_w"][...] = dot_tn(pooled, ref["pooled_grad"][...])

    for copy in low_copies + share_copies:
        copy.wait()
    ref["low_w_out"][...] = jnp.sum(low_parts[...], axis=0)
    gather.drain()
    low_gather.drain()
    for copy in list(crossing.values()) + pair_copies:
        copy.wait_send()


def pyramid_back(crops, n, *args):
    grad, src, low_grad, low_in, wgrads = args[0], args[1], args[6], args[7], args[9]
    block, width = grad.shape
    c = width // 4
    c_in = src.shape[2]
    chips = n // 2
    cells = FA * FA
    low_rows, low_width = args[8].shape
    own, lanes = wgrads.shape[2:]
    groups = 8 // crops
    S = jax.ShapeDtypeStruct
    V = pltpu.VMEM
    D = pltpu.SemaphoreType.DMA
    vmem = pl.BlockSpec(memory_space=pltpu.VMEM)
    w_count = chips + 3 * (crops - 1) + chips
    return pl.pallas_call(
        functools.partial(back_kernel, crops, n),
        out_shape=[
            S((c_in, cells), f32),
            S((c_in, c), f32),
            S((3, 9, c_in, c), f32),
            S((c_in, c), f32),
            S((low_rows, low_in.shape[1]), f32),
            S((low_rows, 128), f32),
            S((8, own, lanes), f32),
        ],
        in_specs=[vmem] * len(args),
        out_specs=[vmem] * 7,
        scratch_shapes=[
            V((crops, cells, width), bf16),
            V((min(3, crops), 3, cells, 3 * c_in), bf16),
            V((cells, 3 * c), bf16),
            V((cells, c_in), f32),
            V((n,) + low_grad.shape, bf16),
            V((chips, 8, own, lanes), bf16),
            V((chips, 8, own, lanes), bf16),
            V((crops, chips, groups, own, lanes), bf16),
            V((chips, groups, own, lanes), bf16),
            V((chips, groups, own, lanes), bf16),
            V((crops, low_rows, 128), f32),
            D((n,)),
            D((n,)),
            D((n,)),
            D((n,)),
            D((crops * chips,)),
            D((crops * chips,)),
            D((crops * chips,)),
            D((crops * chips,)),
            D((w_count,)),
            D((w_count,)),
        ],
        compiler_params=pltpu.CompilerParams(
            collective_id=1, has_side_effects=True, vmem_limit_bytes=62 * 1024 * 1024
        ),
    )(*args)


def conv_forward(values, weight, rate, pad):
    kernel = weight.reshape(3, 3, weight.shape[1], weight.shape[2])
    return lax.conv_general_dilated(
        values[None],
        kernel,
        (1, 1),
        ((pad, pad), (rate, rate)),
        rhs_dilation=(rate, rate),
        dimension_numbers=("NHWC", "HWIO", "NHWC"),
        preferred_element_type=f32,
    )[0]


def up_rows(first, count, coarse_first, coarse_count, fine_side):
    fine = first + jnp.arange(count)
    pos = jnp.clip((fine.astype(f32) + 0.5) / 4.0 - 0.5, 0.0, FA - 1.0)
    coarse = (coarse_first + jnp.arange(coarse_count)).astype(f32)
    table = jnp.maximum(0.0, 1.0 - jnp.abs(pos[:, None] - coarse[None, :]))
    return jnp.where(((fine >= 0) & (fine < fine_side))[:, None], table, 0.0)


def own_rows(values, axis):
    size = values.shape[axis] // lax.axis_size("chan")
    return lax.dynamic_slice_in_dim(values, lax.axis_index("chan") * size, size, axis)


def per_device(
    features,
    low_in,
    offsets,
    d_logits,
    w_point,
    w_atrous,
    w_pool,
    w_proj,
    w_low,
    w_dec1,
    w_dec1_low,
    w_dec2,
    w_cls,
    b_cls,
    bn_gain,
    bn_shift,
    low_gain,
    low_shift,
):
    n = lax.axis_size("chan")
    crops = lax.axis_size("crop")
    me = lax.axis_index("chan")
    my_crop = lax.axis_index("crop")
    fine = low_in.shape[2]
    rows = fine // n
    coarse_rows = FA // n
    channels = w_dec2.shape[2]
    c_in = features.shape[1]
    low_width = w_low.shape[1]
    coarse_samples = FA * FA * crops
    fine_samples = fine * fine * crops

    own = w_dec2.shape[1]
    classes = w_cls.shape[1]
    side = w_dec1_low.transpose(2, 0, 1).reshape(own, 9 * low_width)
    tail = jnp.concatenate([side, w_cls], axis=1)
    tail = jnp.pad(tail, ((0, 0), (0, -tail.shape[1] % channels)))
    tail_rows = tail.shape[1] // channels
    tail = tail.reshape(own, tail_rows, channels).transpose(1, 0, 2)
    packed = lax.all_gather(jnp.concatenate([w_proj, w_dec1, tail, w_dec2]), "chan")
    packed = packed.transpose(1, 0, 2, 3).reshape(-1, channels, channels)
    proj_full, dec1_full = packed[:5], packed[5:14]
    tail_full = packed[14 : 14 + tail_rows].transpose(1, 0, 2).reshape(channels, -1)
    dec2_full = packed[14 + tail_rows :]
    dec1_low_full = tail_full[:, : 9 * low_width].reshape(channels, 9, low_width)
    dec1_low_full = dec1_low_full.transpose(1, 2, 0)
    cls_full = tail_full[:, 9 * low_width : 9 * low_width + classes]
    norms = lax.all_gather(jnp.concatenate([bn_gain, bn_shift]), "chan", axis=1, tiled=True)

    row_index = me * rows + jnp.arange(rows, dtype=jnp.int32)
    col_index = jnp.arange(fine, dtype=jnp.int32)
    rows_valid = offsets[0, 0] + 4 * row_index < SCENE_H
    cols_valid = offsets[0, 1] + 4 * col_index < SCENE_W
    mask = (rows_valid[:, None] & cols_valid[None, :]).astype(f32)

    source = features[0].T.reshape(FA, FA, c_in)
    parts = [jnp.einsum("hwc,co->hwo", source, w_point, preferred_element_type=f32)]
    for k in range(3):
        parts.append(conv_forward(source, w_atrous[k], atrous_rates[k], atrous_rates[k]))
    parts = jnp.concatenate([p.astype(bf16) for p in parts], axis=-1)
    low_terms = jnp.einsum("chw,co->how", low_in[0], w_low, preferred_element_type=f32).astype(bf16)
    low_pre = lax.psum_scatter(low_terms, "chan", scatter_dimension=0, tiled=True).astype(f32)
    low_pre = low_pre.transpose(1, 0, 2).reshape(low_width, rows * fine)
    branch_pre = lax.psum_scatter(parts, "chan", scatter_dimension=0, tiled=True).astype(f32)
    branch_pre = branch_pre.reshape(coarse_rows * FA, 4 * channels)

    pooled = jnp.mean(features[0].astype(f32), axis=1).astype(bf16)
    pool_part = jnp.dot(pooled[None], w_pool, preferred_element_type=f32)

    outer_rows = me * rows - 1 + jnp.arange(rows + 2, dtype=jnp.int32)
    outer_mask = (offsets[0, 0] + 4 * outer_rows < SCENE_H) & (outer_rows >= 0) & (outer_rows < fine)
    outer_mask = (outer_mask[:, None] & cols_valid[None, :]).astype(bf16)
    spare = 32 - classes
    outer_grad = jnp.pad(d_logits[0], ((0, spare), (1, 1), (0, 0)))
    outer_grad = lax.dynamic_slice_in_dim(outer_grad, me * rows, rows + 2, 1) * outer_mask
    wide_column = lambda v: jnp.broadcast_to(v[:, None], (v.shape[0], 128))
    table = up_rows(0, fine, 0, FA, fine)
    (
        logits, branch_grad, pool_grad, pool_bf, proj_sums, low_pre_bf, totals, low_totals, blocks,
    ) = decoder(
        crops,
        n,
        (coarse_samples, fine_samples),
        branch_pre,
        low_pre,
        pool_part,
        norms,
        wide_column(low_gain),
        wide_column(low_shift),
        proj_full,
        dec1_full.reshape(3, 3 * channels, channels),
        dec1_low_full.reshape(3, 3 * low_width, channels),
        dec2_full.reshape(3, 3 * channels, channels),
        jnp.pad(cls_full.T, ((0, spare), (0, 0))),
        wide_column(jnp.pad(b_cls, (0, spare))),
        outer_grad.reshape(32, (rows + 2) * fine),
        mask.reshape(1, rows * fine),
        table.astype(bf16),
        table.T.astype(bf16),
    )
    logits = logits[:classes].reshape(classes, rows, fine)
    pool_bf, proj_sums = pool_bf[:crops], proj_sums[:crops]
    proj_wgrad_pool = jnp.einsum("bc,bo->co", pool_bf.astype(f32), proj_sums, precision=highest)
    source_all = lax.all_gather(features[0].T, "crop", axis=0)
    feature_grad, point_wgrad, atrous_wgrad, pool_wgrad, early_grad, low_wgrad, blocks = pyramid_back(
        crops,
        n,
        branch_grad,
        source_all,
        w_point,
        w_atrous,
        w_pool,
        pool_grad,
        low_pre_bf,
        low_in[0].reshape(low_in.shape[1], fine * fine),
        w_low,
        blocks,
    )
    turn = lambda v: v.reshape(3, own, 3, channels)[:, :, ::-1].transpose(0, 2, 1, 3).reshape(9, own, channels)
    dec2_wgrad, dec1_wgrad = turn(blocks[0:3]), turn(blocks[3:6])
    proj_wgrad = blocks[6].reshape(own, 3, channels).transpose(1, 0, 2)
    last = blocks[7]
    proj_wgrad = jnp.concatenate(
        [proj_wgrad, last[None, :, :channels], own_rows(proj_wgrad_pool, 0)[None]], axis=0
    )
    last = last[:, channels:]
    side_wgrad = last[:, : 9 * low_width].reshape(own, 9, low_width).transpose(1, 2, 0)
    cls_weight_grad = last[:, 9 * low_width : 9 * low_width + classes]

    return (
        logits[None],
        feature_grad[None],
        early_grad.reshape(low_in.shape),
        point_wgrad,
        atrous_wgrad,
        pool_wgrad,
        proj_wgrad,
        low_wgrad[:, :low_width],
        dec1_wgrad,
        side_wgrad,
        dec2_wgrad,
        cls_weight_grad,
        totals[16, :classes],
        own_rows(totals[0:8], 1),
        own_rows(totals[8:16], 1),
        low_totals[0, :low_width],
        low_totals[1, :low_width],
    )


def solution(mesh):
    placed = (
        P("crop", "chan", None),
        P("crop", "chan", None, None),
        P("crop", None),
        P("crop", None, None, None),
        P("chan", None),
        P(None, None, "chan", None),
        P("chan", None),
        P(None, "chan", None),
        P("chan", None),
        P(None, "chan", None),
        P(None, None, "chan"),
        P(None, "chan", None),
        P("chan", None),
        P(),
        P(None, "chan"),
        P(None, "chan"),
        P(),
        P(),
    )
    return jax.shard_map(
        per_device,
        mesh=mesh,
        in_specs=placed,
        out_specs=(
            P("crop", None, "chan", None),
            P("crop", "chan", None),
            P("crop", "chan", None, None),
            P("chan", None),
            P(None, None, "chan", None),
            P("chan", None),
            P(None, "chan", None),
            P("chan", None),
            P(None, "chan", None),
            P(None, None, "chan"),
            P(None, "chan", None),
            P("chan", None),
            P(),
            P(None, "chan"),
            P(None, "chan"),
            P(),
            P(),
        ),
        check_vma=False,
    )
```

```python
import functools
import typing

import jax
import jax.numpy as jnp
from jax import lax
from jax.experimental import pallas as pl
from jax.experimental.pallas import tpu as pltpu
from jax.sharding import PartitionSpec as P

FA = 32
SCENE_H = 1024
SCENE_W = 2048

epsilon = 1e-05
highest = lax.Precision.HIGHEST
atrous_rates = (6, 12, 18)
f32 = jnp.float32
bf16 = jnp.bfloat16
BOTH = ("crop", "chan")


MESH = pl.DeviceIdType.MESH


def chip_peers(crops, n):
    my_crop, me = lax.axis_index("crop"), lax.axis_index("chan")
    core = lax.rem(me, 2)
    chips = n // 2
    other = (my_crop, me + 1 - 2 * core)
    far = []
    for i in range(crops):
        for j in range(chips):
            if i or j:
                far.append((lax.rem(my_crop + i, crops), lax.rem(me + 2 * j, n)))
    return other, far


GELU_A = 0.7978845608028654
GELU_B = 0.044715


def gelu(x):
    return 0.5 * x * (1.0 + jnp.tanh(GELU_A * (x + GELU_B * x * x * x)))


def gelu_slope(x):
    square = x * x
    t = jnp.tanh(GELU_A * x * (1.0 + GELU_B * square))
    return 0.5 * (1.0 + t) + (0.5 * GELU_A) * x * (1.0 - t * t) * (1.0 + (3.0 * GELU_B) * square)


def dot(a, b):
    return jnp.dot(a, b, preferred_element_type=f32)


def dot_nt(a, b):
    return lax.dot_general(a, b, (((1,), (1,)), ((), ())), preferred_element_type=f32)


def dot_tn(a, b):
    return lax.dot_general(a, b, (((0,), (0,)), ((), ())), preferred_element_type=f32)


def dot_exact(table, values):
    high = values.astype(bf16)
    rest = values - high.astype(f32)
    middle = rest.astype(bf16)
    low = (rest - middle.astype(f32)).astype(bf16)
    return dot(table, high) + (dot(table, middle) + dot(table, low))


def fold(values):
    return jnp.sum(values.reshape(values.shape[0] // 8, 8, values.shape[1]), axis=0)


def row_of(values):
    return jnp.sum(values, axis=0, keepdims=True)


def barrier_with(peers):
    barrier = pltpu.get_barrier_semaphore()
    for peer in peers:
        pl.semaphore_signal(barrier, inc=1, device_id=peer, device_id_type=MESH)
    return lambda: pl.semaphore_wait(barrier, len(peers))


def remote(src, dst, send, recv, peer):
    return pltpu.make_async_remote_copy(
        src_ref=src, dst_ref=dst, send_sem=send, recv_sem=recv, device_id=peer, device_id_type=MESH
    )


class Copies:
    def __init__(self, send, recv):
        self.send, self.recv, self.all = send, recv, []

    def start(self, src, dst, peer):
        k = len(self.all)
        copy = remote(src, dst, self.send.at[k], self.recv.at[k], peer)
        copy.start()
        self.all.append(copy)
        return copy

    def drain(self, kept):
        for copy in self.all:
            if not any(copy is other for other in kept):
                copy.wait_send()


def shift_three(source, target, rate, first, last):
    column = lax.rem(lax.broadcasted_iota(jnp.int32, (128, 1), 0), FA)

    def step(i, kept):
        base = pl.multiple_of(i * 128, 128)
        here = source(base)
        w = here.shape[1]
        wide = here.astype(f32)
        for slot, by in ((0, first), (2, last)):
            ok = jnp.logical_and(column + by >= 0, column + by < FA)
            moved = jnp.where(ok, pltpu.roll(wide, (-by) % 128, 0), 0.0)
            target[pl.ds(base, 128), slot * w : (slot + 1) * w] = moved.astype(bf16)
        target[pl.ds(base, 128), w : 2 * w] = here
        return kept

    lax.fori_loop(0, FA * FA // 128, step, 0)


class Swap:
    def __init__(self, crops, n, pair, slots, pair_sems, send, recv):
        self.other, self.far = chip_peers(crops, n)
        me = lax.axis_index("chan")
        self.core = lax.rem(me, 2)
        self.mine = lax.axis_index("crop") * (n // 2) + lax.div(me, 2)
        self.pair, self.slots, self.pair_sems = pair, slots, pair_sems
        self.send, self.recv = send, recv

    def start(self):
        here = self.pair.at[self.core]
        copy = remote(here, here, self.pair_sems.at[0], self.pair_sems.at[1], self.other)
        copy.start()
        copy.wait()
        self.slots[self.mine] = self.pair[0] + self.pair[1]
        self.copies = []
        for k, peer in enumerate(self.far):
            slot = self.slots.at[self.mine]
            copy = remote(slot, slot, self.send.at[k], self.recv.at[k], peer)
            copy.start()
            self.copies.append(copy)

    def finish(self):
        for copy in self.copies:
            copy.wait()
        return jnp.sum(self.slots[...], axis=0)


class WideSwap:
    def __init__(self, crops, n, pair, first, second, pair_sems, send, recv):
        my_crop, me = lax.axis_index("crop"), lax.axis_index("chan")
        self.core, self.crop, self.chip = lax.rem(me, 2), my_crop, lax.div(me, 2)
        self.other = (my_crop, me + 1 - 2 * self.core)
        self.over_crops = [(lax.rem(my_crop + i, crops), me) for i in range(1, crops)]
        self.over_chips = [(my_crop, lax.rem(me + 2 * j, n)) for j in range(1, n // 2)]
        self.pair, self.first, self.second = pair, first, second
        self.pair_sems, self.send, self.recv = pair_sems, send, recv

    def run(self):
        here = self.pair.at[self.core]
        copy = remote(here, here, self.pair_sems.at[0], self.pair_sems.at[1], self.other)
        copy.start()
        copy.wait()
        self.first[self.crop] = self.pair[0] + self.pair[1]
        k = 0
        copies = []
        for peer in self.over_crops:
            slot = self.first.at[self.crop]
            copies.append(remote(slot, slot, self.send.at[k], self.recv.at[k], peer))
            copies[-1].start()
            k += 1
        for copy in copies:
            copy.wait()
        self.second[self.chip] = jnp.sum(self.first[...], axis=0)
        copies = []
        for peer in self.over_chips:
            slot = self.second.at[self.chip]
            copies.append(remote(slot, slot, self.send.at[k], self.recv.at[k], peer))
            copies[-1].start()
            k += 1
        for copy in copies:
            copy.wait()
        return jnp.sum(self.second[...], axis=0)


def put_pair(ref, core, a, b):
    ref[core, 0:1] = a[:, :128]
    ref[core, 1:2] = a[:, 128:]
    ref[core, 2:3] = b[:, :128]
    ref[core, 3:4] = b[:, 128:]


def get_pair(total):
    return (
        jnp.concatenate([total[0:1], total[1:2]], axis=1),
        jnp.concatenate([total[2:3], total[3:4]], axis=1),
    )


def spread_row(row):
    return jnp.broadcast_to(row, (128, 128)).T


def up_weights(i, me, n, rows, coarse_rows):
    lower = (2 * i - 3) // 8
    upper_weight = (2 * i - 3 - 8 * lower) / 8.0
    a, b = 1.0 - upper_weight, upper_weight
    if lower < 0:
        top = me == 0
        a, b = jnp.where(top, 0.0, a), jnp.where(top, 1.0, b)
    if lower + 1 >= coarse_rows:
        bottom = me == n - 1
        a, b = jnp.where(bottom, 1.0, a), jnp.where(bottom, 0.0, b)
    if i < 0:
        a, b = jnp.where(me == 0, 0.0, a), jnp.where(me == 0, 0.0, b)
    if i >= rows:
        a, b = jnp.where(me == n - 1, 0.0, a), jnp.where(me == n - 1, 0.0, b)
    return lower + 1, a, b


class DecoderRefs(typing.NamedTuple):
    feat: object
    point: object
    atrous: object
    pool_w: object
    low_in: object
    low_wt: object
    packed: object
    norms_own: object
    low_gain: object
    low_shift: object
    bias: object
    dlog: object
    mask: object
    up: object
    up_t: object
    logits: object
    branch_out: object
    pool_out: object
    pool_bf: object
    proj_sums: object
    low_out: object
    totals: object
    low_totals: object
    wgrads: object
    src_all: object
    low_ext: object
    low_push: object
    lowx: object
    merged_ext: object
    merged_part: object
    dec1: object
    dec2: object
    pushed: object
    pushed1: object
    x1: object
    x2: object
    g2: object
    g1: object
    yt: object
    branch_bf: object
    proj_bf: object
    second: object
    flip: object
    branch: object
    staged: object
    arrived: object
    low_send: object
    low_pair: object
    low_sum: object
    low_recv: object
    gath: object
    norms_all: object
    norms: object
    proj: object
    w1: object
    tail: object
    w1low: object
    w2: object
    f_send: object
    f_recv: object


def decoder_kernel(crops, n, samples, *refs):
    ref = DecoderRefs(*refs[: len(DecoderRefs._fields)])
    rest = list(refs[len(DecoderRefs._fields) :])
    (wide_pair, wide_first, wide_second, wide_psem, wide_send, wide_recv) = rest[:6]
    (pair, slots, psem, send, recv, halo_send, halo_recv) = rest[6:13]

    coarse_samples, fine_samples = samples
    my_crop, me = lax.axis_index("crop"), lax.axis_index("chan")
    core = lax.rem(me, 2)
    above = (my_crop, lax.rem(me + n - 1, n))
    below = (my_crop, lax.rem(me + 1, n))
    low_width, low_chans = ref.low_wt.shape
    rows = ref.mask.shape[1] // 128
    fine_cells = rows * 128
    coarse_cells = ref.branch.shape[0]
    coarse_rows = coarse_cells // FA
    cells = FA * FA
    c_in, c = ref.point.shape
    own = c // n
    chips, chip = n // 2, lax.div(me, 2)
    pieces = ref.packed.shape[0]
    group = pieces // crops
    chunk = min(4, rows)

    other, far = chip_peers(crops, n)
    over_crops = [(lax.rem(my_crop + i, crops), me) for i in range(1, crops)]
    over_chips = [(my_crop, lax.rem(me + 2 * j, n)) for j in range(1, chips)]
    wait_barrier = barrier_with([other, above, below] + far)

    swaps = [
        Swap(crops, n, pair.at[i], slots.at[i], psem.at[i], send.at[i], recv.at[i])
        for i in range(pair.shape[0])
    ]
    wides = [
        WideSwap(
            crops, n, wide_pair.at[i], wide_first.at[i], wide_second.at[i],
            wide_psem.at[i], wide_send.at[i], wide_recv.at[i],
        )
        for i in range(2)
    ]
    front = Copies(ref.f_send, ref.f_recv)
    for i in range(pair.shape[0]):
        pair[i, core] = jnp.zeros((8, 128), f32)
    for i in range(2):
        wide_pair[i, core] = jnp.zeros(wide_pair.shape[2:], f32)

    def halo(i, first, last, to_above, to_below):
        copies = [
            remote(first, to_above, halo_send.at[i, 0], halo_recv.at[i, 0], above),
            remote(last, to_below, halo_send.at[i, 1], halo_recv.at[i, 1], below),
        ]
        for copy in copies:
            copy.start()
        return copies

    def fine_halo(i, values):
        return halo(
            i,
            values.at[pl.ds(128, 128)],
            values.at[pl.ds(rows * 128, 128)],
            values.at[pl.ds((rows + 1) * 128, 128)],
            values.at[pl.ds(0, 128)],
        )

    def gain(k):
        return ref.norms[k : k + 1]

    def shift(k):
        return ref.norms[8 + k : 9 + k]

    def moments(total, square, count):
        average = total * (1.0 / count)
        return average, lax.rsqrt(square * (1.0 / count) - average * average + epsilon)

    column = lax.broadcasted_iota(jnp.int32, (128, c), 0)

    def put_three(target, base, y):
        target[pl.ds(base, 128), 0:c] = jnp.where(column == 0, 0.0, pltpu.roll(y, 1, 0)).astype(bf16)
        target[pl.ds(base, 128), c : 2 * c] = y.astype(bf16)
        target[pl.ds(base, 128), 2 * c : 3 * c] = jnp.where(
            column == 127, 0.0, pltpu.roll(y, 127, 0)
        ).astype(bf16)

    def inside(i):
        at_top = jnp.logical_and(me == 0, i == 0)
        at_bottom = jnp.logical_and(me == n - 1, i == rows + 1)
        return jnp.where(jnp.logical_or(at_top, at_bottom), 0.0, 1.0)

    def each_row(body, first, last, carry):
        def step(i, kept):
            return body(i, pl.multiple_of(i * 128, 128), kept)

        return lax.fori_loop(first, last, step, carry)

    zero = jnp.zeros((8, c), f32)

    src_all, gath = ref.src_all, ref.gath
    for i in range(cells // 256):
        src_all[my_crop, pl.ds(i * 256, 256)] = ref.feat[:, i * 256 : (i + 1) * 256].T
    gath[me] = ref.packed[...]
    ref.norms_all[me] = ref.norms_own[...]
    wait_barrier()
    block_of = lambda j: lax.rem(me - 2 * j + n, n)
    crop_of = lambda i: lax.rem(my_crop - i + crops, crops)

    def piece_at(b, q):
        return gath.at[b, pl.ds(q * group, group)]

    norm_far, weight_far = [], []
    here = ref.norms_all.at[me]
    for peer in over_chips:
        norm_far.append(front.start(here, here, peer))
    norm_pairs = [front.start(here, here, other)]
    here = piece_at(me, my_crop)
    for peer in over_chips:
        weight_far.append(front.start(here, here, peer))
    weight_pairs = [front.start(gath.at[me], gath.at[me], other)]
    here = src_all.at[my_crop]
    feature_copies = [front.start(here, here, peer) for peer in over_crops]

    part, part_in, staged, arrived = ref.pushed, ref.pushed1, ref.staged, ref.arrived
    shifted = ref.g2

    def branch_partial(k):
        first = k * cells
        if k == 0:
            part[pl.ds(first, cells)] = dot(src_all[my_crop], ref.point[...])
        else:
            rate = atrous_rates[k - 1]
            shift_three(lambda base: src_all[my_crop, pl.ds(base, 128)], shifted, rate, -rate, rate)
            part[pl.ds(first, cells)] = dot(shifted[pl.ds(0, cells), 0 : 3 * c_in], ref.atrous[k - 1, 1])
            for a in (0, 2):
                move = (a - 1) * rate
                count = (FA - abs(move)) * FA
                to, off = first + max(-move, 0) * FA, max(move, 0) * FA
                part[pl.ds(to, count)] += dot(shifted[pl.ds(off, count), 0 : 3 * c_in], ref.atrous[k - 1, a])
        copies = []
        for z in range(chips):
            block = pl.multiple_of(first + (2 * z + 1 - core) * coarse_cells, coarse_cells)
            copies.append(
                front.start(
                    part.at[pl.ds(block, coarse_cells)],
                    part_in.at[pl.ds((k * chips + z) * coarse_cells, coarse_cells)],
                    other,
                )
            )
        return copies

    def pair_sum(k, z):
        block = pl.multiple_of(k * cells + (2 * z + core) * coarse_cells, coarse_cells)
        landed = pl.multiple_of((k * chips + z) * coarse_cells, coarse_cells)
        return part[pl.ds(block, coarse_cells)] + part_in[pl.ds(landed, coarse_cells)]

    branch_far, waited = [], []

    def branch_out(k, copies):
        for copy in copies:
            copy.wait()
            waited.append(copy)
        for z in range(chips):
            staged[k, z] = pair_sum(k, z).astype(bf16)
        ref.branch[:, k * c : (k + 1) * c] = pair_sum(k, chip)
        for j in range(1, chips):
            target = lax.rem(chip + j, chips)
            branch_far.append((k, j, front.start(staged.at[k, target], arrived.at[k, chip], over_chips[j - 1])))

    order = (0, 3, 2, 1)
    before = branch_partial(order[0])
    for at in range(1, 4):
        after = branch_partial(order[at])
        branch_out(order[at - 1], before)
        before = after

    low_send, low_pair = ref.low_send, ref.low_pair

    def low_block(b):
        span = pl.ds(pl.multiple_of(b * fine_cells, fine_cells), fine_cells)
        return dot(ref.low_wt[...], ref.low_in[:, span])

    low_copies = []
    for z in range(chips):
        low_send[z] = low_block(2 * z + 1 - core)
        low_copies.append(front.start(low_send.at[z], low_pair.at[z], other))
    branch_out(order[3], before)
    weight_crossed = []
    for j in range(1, chips):
        weight_far[j - 1].wait_recv()
        here = piece_at(block_of(j), my_crop)
        for i in range(1, crops):
            weight_crossed.append((i, j, front.start(here, here, over_crops[i - 1])))
        weight_pairs.append(front.start(here, here, other))
    for j in range(1, chips):
        norm_far[j - 1].wait_recv()
        here = ref.norms_all.at[block_of(j)]
        norm_pairs.append(front.start(here, here, other))
    for z in range(chips):
        low_copies[z].wait_recv()
        ref.low_sum[z] = (low_block(2 * z + core) + low_pair[z]).astype(bf16)
    low_far = []
    for j in range(1, chips):
        target = lax.rem(chip + j, chips)
        low_far.append(front.start(ref.low_sum.at[target], ref.low_recv.at[chip], over_chips[j - 1]))

    pooled = row_of(src_all[my_crop].astype(f32)) * (1.0 / cells)
    pooled = jnp.concatenate([pooled, jnp.zeros((15, c_in), f32)], axis=0).astype(bf16)
    pool_part = dot(pooled, ref.pool_w[...])[0:1]

    for copy in norm_pairs:
        copy.wait_recv()
    for b in range(n):
        ref.norms[:, b * own : (b + 1) * own] = ref.norms_all[b, :, 0:own]

    for k, j, copy in branch_far:
        copy.wait_recv()
        here = lax.rem(chip - j + chips, chips)
        ref.branch[:, k * c : (k + 1) * c] += arrived[k, here].astype(f32)

    wide = wide_pair.at[0]
    for k in range(4):
        v = ref.branch[:, k * c : (k + 1) * c]
        wide[core, k : k + 1] = row_of(v)
        wide[core, 4 + k : 5 + k] = row_of(v * v)
    wide[core, 8:16] = jnp.where(
        lax.broadcasted_iota(jnp.int32, (8, c), 0) == my_crop, pool_part, 0.0
    )
    for i, j, copy in weight_crossed:
        copy.wait_recv()
        here = piece_at(block_of(j), crop_of(i))
        weight_pairs.append(front.start(here, here, other))
    total_a = wides[0].run()
    for copy in weight_pairs:
        copy.wait_recv()
    proj, w1, w2, tail = ref.proj, ref.w1, ref.w2, ref.tail
    for b in range(n):
        mine = pl.ds(b * own, own)
        for k in range(5):
            proj[k, mine] = gath[b, k]

    def branch_parts(k):
        average, inverse = moments(total_a[k : k + 1], total_a[4 + k : 5 + k], coarse_samples)
        normed = (ref.branch[:, k * c : (k + 1) * c] - average) * inverse
        return normed, gain(k) * normed + shift(k), inverse

    projected = jnp.zeros((coarse_cells, c), f32)
    for k in range(4):
        y = gelu(branch_parts(k)[1]).astype(bf16)
        ref.branch_bf[:, k * c : (k + 1) * c] = y
        projected = projected + dot(y, ref.proj[k])
    pool_here = lax.broadcasted_iota(jnp.int32, (8, c), 0) < crops
    pool_pre = total_a[8:16]
    pool_average = row_of(pool_pre) * (1.0 / crops)
    pool_spread = jnp.where(pool_here, pool_pre - pool_average, 0.0)
    pool_inverse = lax.rsqrt(row_of(pool_spread * pool_spread) * (1.0 / crops) + epsilon)
    pool_normed = pool_spread * pool_inverse
    pool_before = gain(4) * pool_normed + shift(4)
    pool_bf = gelu(pool_before)
    pool_bf = jnp.concatenate([pool_bf, jnp.zeros((8, c), f32)], axis=0).astype(bf16)
    ref.pool_bf[...] = pool_bf
    pool_term = dot(pool_bf, ref.proj[4])
    my_row = lax.broadcasted_iota(jnp.int32, (16, c), 0) == my_crop
    projected = projected + row_of(jnp.where(my_row, pool_term, 0.0))
    merged_ext = ref.merged_ext
    merged_ext[pl.ds(FA, coarse_cells)] = projected
    put_pair(pair.at[0], core, row_of(projected), row_of(projected * projected))
    merged_copies = halo(
        1,
        merged_ext.at[pl.ds(FA, FA)],
        merged_ext.at[pl.ds(coarse_cells, FA)],
        merged_ext.at[pl.ds(FA + coarse_cells, FA)],
        merged_ext.at[pl.ds(0, FA)],
    )
    swaps[0].start()

    for b in range(n):
        mine = pl.ds(b * own, own)
        for t in range(9):
            a, e = t // 3, t % 3
            w1[a, pl.ds(e * c + b * own, own)] = gath[b, 5 + t]
            w2[a, pl.ds(e * c + b * own, own)] = gath[b, 16 + t]
        tail[mine, 0:c] = gath[b, 14]
        tail[mine, c : 2 * c] = gath[b, 15]
    turned = tail[...].T
    for a in range(3):
        ref.w1low[a] = turned[a * 3 * low_width : (a + 1) * 3 * low_width]
    cls_t = turned[9 * low_width : 9 * low_width + 32]

    for copy in low_far:
        copy.wait_recv()
    low_ext = ref.low_ext
    low_total = low_block(me) + low_pair[chip]
    for j in range(1, chips):
        low_total = low_total + ref.low_recv[lax.rem(chip - j + chips, chips)].astype(f32)
    low_ext[:, 128 : 128 + fine_cells] = low_total
    low_edges = halo(
        0,
        low_ext.at[:, pl.ds(128, 128)],
        low_ext.at[:, pl.ds(rows * 128, 128)],
        low_ext.at[:, pl.ds((rows + 1) * 128, 128)],
        low_ext.at[:, pl.ds(0, 128)],
    )

    def add_low(i, base, kept):
        v = low_ext[:, pl.ds(base, 128)]
        return kept[0] + v, kept[1] + v * v

    low_zero = jnp.zeros((low_width, 128), f32)
    low_sum, low_square = each_row(add_low, 1, rows + 1, (low_zero, low_zero))

    def lanes_of(values):
        return row_of(values.T)

    pair[6, core, 0:1, 0:low_width] = lanes_of(low_sum)
    pair[6, core, 1:2, 0:low_width] = lanes_of(low_square)
    swaps[6].start()
    merged_sum, merged_square = get_pair(swaps[0].finish())
    for copy in merged_copies:
        copy.wait()
    merged_average, merged_inverse = moments(merged_sum, merged_square, coarse_samples)

    def merged_parts(first, count):
        normed = (merged_ext[pl.ds(first, count)] - merged_average) * merged_inverse
        return normed, gain(5) * normed + shift(5)

    coarse_wide = []
    for j in range(coarse_rows + 2):
        coarse_wide.append(dot_exact(ref.up[...], gelu(merged_parts(j * FA, FA)[1])))
    for i in range(-1, rows + 1):
        lower, a, b = up_weights(i, me, n, rows, coarse_rows)
        put_three(ref.x1, (i + 1) * 128, a * coarse_wide[lower] + b * coarse_wide[lower + 1])

    total_l = swaps[6].finish()
    for copy in low_edges:
        copy.wait()
    low_average = total_l[0:1] * (1.0 / fine_samples)
    low_variance = total_l[1:2] * (1.0 / fine_samples) - low_average * low_average
    low_inverse_row = lax.rsqrt(low_variance + epsilon)
    low_average = spread_row(low_average)[0:low_width]
    low_inverse = spread_row(low_inverse_row)[0:low_width]
    lane = lax.broadcasted_iota(jnp.int32, (low_width, 128), 1)

    def low_parts(base):
        normed = (low_ext[:, pl.ds(base, 128)] - low_average) * low_inverse
        return normed, ref.low_gain[...] * normed + ref.low_shift[...]

    def low_row(i, base, kept):
        y = gelu(low_parts(base)[1]) * inside(i)
        lowx = ref.lowx
        lowx[0:low_width, pl.ds(base, 128)] = jnp.where(lane == 0, 0.0, pltpu.roll(y, 1, 1)).astype(bf16)
        lowx[low_width : 2 * low_width, pl.ds(base, 128)] = y.astype(bf16)
        lowx[2 * low_width : 3 * low_width, pl.ds(base, 128)] = jnp.where(
            lane == 127, 0.0, pltpu.roll(y, 127, 1)
        ).astype(bf16)
        return kept

    each_row(low_row, 0, rows + 2, 0)

    def conv_loop(source, weight, target, extra):
        def step(i, kept):
            base = pl.multiple_of(i * (chunk * 128), 128)
            total = None
            for a in range(3):
                term = dot(source[pl.ds(base + a * 128, chunk * 128)], weight[a])
                total = term if total is None else total + term
            if extra is not None:
                total = total + extra(base)
            target[pl.ds(base + 128, chunk * 128)] = total
            return kept[0] + fold(total), kept[1] + fold(total * total)

        return lax.fori_loop(0, rows // chunk, step, (zero, zero))

    def low_term(base):
        total = None
        for a in range(3):
            term = dot_tn(ref.lowx[:, pl.ds(base + a * 128, chunk * 128)], ref.w1low[a])
            total = term if total is None else total + term
        return total

    dec1, dec2, pushed, pushed1 = ref.dec1, ref.dec2, ref.pushed, ref.pushed1
    total, square = conv_loop(ref.x1, ref.w1, dec1, low_term)
    put_pair(pair.at[1], core, row_of(total), row_of(square))
    dec1_copies = fine_halo(2, dec1)
    swaps[1].start()
    total, square = get_pair(swaps[1].finish())
    for copy in dec1_copies:
        copy.wait()
    first_average, first_inverse = moments(total, square, fine_samples)

    def first_parts(base):
        normed = (dec1[pl.ds(base, 128)] - first_average) * first_inverse
        return normed, gain(6) * normed + shift(6)

    def first_row(i, base, kept):
        put_three(ref.x2, base, gelu(first_parts(base)[1]) * inside(i))
        return kept

    each_row(first_row, 0, rows + 2, 0)
    total, square = conv_loop(ref.x2, ref.w2, dec2, None)
    put_pair(pair.at[2], core, row_of(total), row_of(square))
    dec2_copies = fine_halo(3, dec2)
    swaps[2].start()
    total, square = get_pair(swaps[2].finish())
    for copy in dec2_copies:
        copy.wait()
    second_average, second_inverse = moments(total, square, fine_samples)

    def second_parts(base):
        normed = (dec2[pl.ds(base, 128)] - second_average) * second_inverse
        return normed, gain(7) * normed + shift(7)

    def second_row(i, base, kept):
        normed, before = second_parts(base)
        ref.second[pl.ds(base, 128)] = gelu(before).astype(bf16)
        grad = dot_tn(ref.dlog[:, pl.ds(base, 128)], cls_t)
        push = gelu_slope(before) * grad
        pushed[pl.ds(base, 128)] = push
        own_row = jnp.where(jnp.logical_and(i > 0, i < rows + 1), 1.0, 0.0)
        push = push * own_row
        return kept[0] + fold(push * normed), kept[1] + fold(push)

    along, summed = each_row(second_row, 0, rows + 2, (zero, zero))
    put_pair(pair.at[3], core, row_of(along), row_of(summed))
    swaps[3].start()
    second = ref.second

    def logit_row(i, base, kept):
        out = pl.multiple_of(base - 128, 128)
        value = dot_nt(cls_t, second[pl.ds(base, 128)]) + ref.bias[...]
        ref.logits[:, pl.ds(out, 128)] = value * ref.mask[:, pl.ds(out, 128)]
        return kept

    each_row(logit_row, 1, rows + 1, 0)
    flip = ref.flip
    flip[pl.ds(9 * low_width, 32)] = dot(
        ref.dlog[:, 128 : 128 + fine_cells], second[pl.ds(128, fine_cells)]
    )
    bias_grad = jnp.zeros((32, 128), f32)
    for i in range(1, rows + 1):
        bias_grad = bias_grad + ref.dlog[:, i * 128 : (i + 1) * 128].astype(f32)
    wide_pair[1, core, 16:17, 0:32] = row_of(bias_grad.T)
    second_along, second_summed = get_pair(swaps[3].finish())

    def pull(push, normed, k, inverse, along, summed, count):
        return (gain(k) * inverse) * (push - summed * (1.0 / count) - normed * (along * (1.0 / count)))

    def dec2_row(i, base, kept):
        g = pull(
            pushed[pl.ds(base, 128)], second_parts(base)[0], 7, second_inverse,
            second_along, second_summed, fine_samples,
        )
        put_three(ref.g2, base, g * inside(i))
        return kept

    each_row(dec2_row, 0, rows + 2, 0)

    def back_loop(source, weight, use, carry):
        def step(i, kept):
            base = pl.multiple_of(i * (chunk * 128), 128)
            total = None
            for t in range(9):
                a, e = t // 3, t % 3
                piece = source[pl.ds(base + (2 - a) * 128, chunk * 128), (2 - e) * c : (3 - e) * c]
                term = dot_nt(piece, weight[a, e * c : (e + 1) * c])
                total = term if total is None else total + term
            return use(base, total, kept)

        return lax.fori_loop(0, rows // chunk, step, carry)

    def first_use(base, grad, kept):
        at = pl.ds(pl.multiple_of(base + 128, 128), chunk * 128)
        normed = (dec1[at] - first_average) * first_inverse
        push = gelu_slope(gain(6) * normed + shift(6)) * grad
        pushed1[at] = push
        return kept[0] + fold(push * normed), kept[1] + fold(push)

    along, summed = back_loop(ref.g2, ref.w2, first_use, (zero, zero))
    put_pair(pair.at[4], core, row_of(along), row_of(summed))
    pushed_copies = fine_halo(4, pushed1)
    swaps[4].start()

    wgrads = ref.wgrads

    def weight_grads(first, source, gradient):
        for a in range(3):
            part = dot_tn(
                source[pl.ds(a * 128, fine_cells), c : 2 * c], gradient[pl.ds(128, fine_cells)]
            ).astype(bf16)
            for h in range(n):
                wgrads[h, first + a] = part[h * own : (h + 1) * own]

    weight_grads(0, ref.x2, ref.g2)
    first_along, first_summed = get_pair(swaps[4].finish())
    for copy in pushed_copies:
        copy.wait()

    def dec1_row(i, base, kept):
        g = pull(
            pushed1[pl.ds(base, 128)], first_parts(base)[0], 6, first_inverse,
            first_along, first_summed, fine_samples,
        ) * inside(i)
        put_three(ref.g1, base, g)
        return kept

    each_row(dec1_row, 0, rows + 2, 0)

    def up_use(base, grad, kept):
        dec2[pl.ds(pl.multiple_of(base + 128, 128), chunk * 128)] = grad
        return kept

    back_loop(ref.g1, ref.w1, up_use, 0)
    yt = ref.yt

    def low_back_row(i, local, base, kept):
        total = None
        for t in range(9):
            a, e = t // 3, t % 3
            at = pl.ds((local + 2 - a) * 128, 128)
            piece = yt[t * low_width : (t + 1) * low_width, at]
            if e == 0:
                piece = jnp.where(lane == 127, 0.0, pltpu.roll(piece, 127, 1))
            if e == 2:
                piece = jnp.where(lane == 0, 0.0, pltpu.roll(piece, 1, 1))
            total = piece if total is None else total + piece
        normed, before = low_parts(base)
        push = gelu_slope(before) * total
        ref.low_push[:, pl.ds(pl.multiple_of(base - 128, 128), 128)] = push
        return kept[0] + push * normed, kept[1] + push

    def low_back_chunk(i, kept):
        base = pl.multiple_of(i * (chunk * 128), 128)
        here = ref.g1[pl.ds(base, (chunk + 2) * 128), c : 2 * c]
        for a in range(3):
            yt[a * 3 * low_width : (a + 1) * 3 * low_width] = dot_nt(ref.w1low[a], here)
        for local in range(chunk):
            kept = low_back_row(i, local, pl.multiple_of(base + (local + 1) * 128, 128), kept)
        return kept

    low_along, low_summed = lax.fori_loop(0, rows // chunk, low_back_chunk, (low_zero, low_zero))

    part = ref.merged_part
    row_sums = [None] * (coarse_rows + 2)
    for i in range(rows):
        lower, a, b = up_weights(i, me, n, rows, coarse_rows)
        grad = dec2[pl.ds((i + 1) * 128, 128)]
        for j, weight in ((lower, a), (lower + 1, b)):
            row_sums[j] = weight * grad if row_sums[j] is None else row_sums[j] + weight * grad
    along, summed = zero, zero
    for j in range(coarse_rows + 2):
        grad = dot_exact(ref.up_t[...], row_sums[j])
        part[pl.ds(j * FA, FA)] = grad
        normed, before = merged_parts(j * FA, FA)
        push = gelu_slope(before) * grad
        along, summed = along + fold(push * normed), summed + fold(push)
    put_pair(pair.at[5], core, row_of(along), row_of(summed))
    pair[5, core, 4:5, 0:low_width] = lanes_of(low_along)
    pair[5, core, 5:6, 0:low_width] = lanes_of(low_summed)
    part_copies = halo(
        5,
        part.at[pl.ds(0, FA)],
        part.at[pl.ds(FA + coarse_cells, FA)],
        part.at[pl.ds((coarse_rows + 3) * FA, FA)],
        part.at[pl.ds((coarse_rows + 2) * FA, FA)],
    )
    swaps[5].start()
    weight_grads(3, ref.x1, ref.g1)
    total_g = swaps[5].finish()
    for copy in part_copies:
        copy.wait()
    merged_along, merged_summed = get_pair(total_g)
    low_along, low_summed = spread_row(total_g[4:5])[0:low_width], spread_row(total_g[5:6])[0:low_width]
    ref.low_totals[...] = total_g[4:6]

    up_here = jnp.where(me == 0, 0.0, 1.0)
    down_here = jnp.where(me == n - 1, 0.0, 1.0)
    proj_bf = ref.proj_bf
    for j in range(1, coarse_rows + 1):
        grad = part[pl.ds(j * FA, FA)]
        if j == 1:
            grad = grad + up_here * part[pl.ds((coarse_rows + 2) * FA, FA)]
        if j == coarse_rows:
            grad = grad + down_here * part[pl.ds((coarse_rows + 3) * FA, FA)]
        normed, before = merged_parts(j * FA, FA)
        push = gelu_slope(before) * grad
        g = pull(push, normed, 5, merged_inverse, merged_along, merged_summed, coarse_samples)
        proj_bf[pl.ds((j - 1) * FA, FA)] = g.astype(bf16)

    push_all = []
    for k in range(4):
        normed, before, _ = branch_parts(k)
        push = gelu_slope(before) * dot_nt(proj_bf[...], ref.proj[k])
        push_all.append(push)
        wide_pair[1, core, k : k + 1] = row_of(push * normed)
        wide_pair[1, core, 4 + k : 5 + k] = row_of(push)
    proj_row = row_of(proj_bf[...].astype(f32))
    wide_pair[1, core, 8:16] = jnp.where(
        lax.broadcasted_iota(jnp.int32, (8, c), 0) == my_crop, proj_row, 0.0
    )
    total_h = wides[1].run()
    ref.proj_sums[...] = total_h[8:16]
    for k in range(4):
        normed, _, inverse = branch_parts(k)
        g = pull(
            push_all[k], normed, k, inverse, total_h[k : k + 1], total_h[4 + k : 5 + k], coarse_samples
        )
        ref.branch_out[:, k * c : (k + 1) * c] = g.astype(bf16)

    sums = total_h[8:16]
    sums_high = sums.astype(bf16).astype(f32)
    sums_low = sums - sums_high
    spare = jnp.concatenate([sums_high, sums_low], axis=0)
    spare_mid = spare.astype(bf16)
    spare_rest = (spare - spare_mid.astype(f32)).astype(bf16)
    pieces = dot_nt(spare_mid, ref.proj[4]) + dot_nt(spare_rest, ref.proj[4])
    pool_push = gelu_slope(pool_before) * (pieces[0:8] + pieces[8:16])
    pool_push = jnp.where(pool_here, pool_push, 0.0)
    pool_along, pool_summed = row_of(pool_push * pool_normed), row_of(pool_push)
    pool_grad = pull(pool_push, pool_normed, 4, pool_inverse, pool_along, pool_summed, crops)
    pool_grad = jnp.where(pool_here, pool_grad, 0.0)
    ref.pool_out[...] = jnp.concatenate([pool_grad, jnp.zeros((8, c), f32)], axis=0).astype(bf16)

    totals = ref.totals
    totals[0:4] = total_h[0:4]
    totals[4:5] = pool_along
    totals[5:6] = merged_along
    totals[6:7] = first_along
    totals[7:8] = second_along
    totals[8:12] = total_h[4:8]
    totals[12:13] = pool_summed
    totals[13:14] = merged_summed
    totals[14:15] = first_summed
    totals[15:16] = second_summed
    totals[16:24] = total_h[16:24]

    def low_out_row(i, base, kept):
        at = pl.ds(pl.multiple_of(base - 128, 128), 128)
        normed = low_parts(base)[0]
        g = (ref.low_gain[...] * low_inverse) * (
            ref.low_push[:, at] - low_summed * (1.0 / fine_samples) - normed * (low_along * (1.0 / fine_samples))
        )
        ref.low_out[:, at] = g.astype(bf16)
        return kept

    each_row(low_out_row, 1, rows + 1, 0)

    for a in range(3):
        flip[pl.ds(a * 3 * low_width, 3 * low_width)] = dot(
            ref.lowx[:, a * 128 : a * 128 + fine_cells], ref.g1[pl.ds(128, fine_cells), c : 2 * c]
        )
    flip[pl.ds(9 * low_width + 32, 48)] = jnp.zeros((48, c), f32)
    turned = flip[...].T.astype(bf16)
    for k in range(4):
        product = dot_tn(ref.branch_bf[:, k * c : (k + 1) * c], proj_bf[...]).astype(bf16)
        for h in range(n):
            rows_h = product[h * own : (h + 1) * own]
            if k < 3:
                wgrads[h, 6, :, k * c : (k + 1) * c] = rows_h
            else:
                wgrads[h, 7, :, 0:c] = rows_h
                wgrads[h, 7, :, c : 3 * c] = turned[h * own : (h + 1) * own]
    for copy in feature_copies:
        copy.wait_recv()
    front.drain(waited)


def decoder(crops, n, samples, *args):
    ref = DecoderRefs(*args, *([None] * (len(DecoderRefs._fields) - len(args))))
    c_in, c = ref.point.shape
    low_width = ref.low_wt.shape[0]
    cells = ref.mask.shape[1]
    rows = cells // 128
    coarse = FA * FA // n
    own = c // n
    pieces = ref.packed.shape[0]
    chips = n // 2
    all_chips = crops * chips
    outer = (rows + 2) * 128
    chunk = min(4, rows)
    count = (crops - 1) + 4 * (2 * chips - 1) + 2 * chips - 1
    count += (crops + 2) * (chips - 1) + 1 + (crops - 1) * (chips - 1) + 2 * chips
    S = jax.ShapeDtypeStruct
    V = pltpu.VMEM
    D = pltpu.SemaphoreType.DMA
    vmem = pl.BlockSpec(memory_space=pltpu.VMEM)
    return pl.pallas_call(
        functools.partial(decoder_kernel, crops, n, samples),
        out_shape=[
            S((32, cells), f32),
            S((coarse, 4 * c), bf16),
            S((16, c), bf16),
            S((16, c), bf16),
            S((8, c), f32),
            S((low_width, cells), bf16),
            S((24, c), f32),
            S((2, 128), f32),
            S((n, 8, own, 3 * c), bf16),
            S((crops, FA * FA, c_in), bf16),
        ],
        in_specs=[vmem] * len(args),
        out_specs=[vmem] * 10,
        scratch_shapes=[
            V((low_width, outer), f32),
            V((low_width, cells), f32),
            V((3 * low_width, outer), bf16),
            V((coarse + 2 * FA, c), f32),
            V((coarse + 4 * FA, c), f32),
            V((outer, c), f32),
            V((outer, c), f32),
            V((max(outer, 4 * FA * FA), c), f32),
            V((max(outer, 2 * FA * FA), c), f32),
            V((outer, 3 * c), bf16),
            V((outer, 3 * c), bf16),
            V((max(outer, FA * FA), 3 * c), bf16),
            V((outer, 3 * c), bf16),
            V((9 * low_width, (chunk + 2) * 128), f32),
            V((coarse, 4 * c), bf16),
            V((coarse, c), bf16),
            V((outer, c), bf16),
            V((512, c), f32),
            V((coarse, 4 * c), f32),
            V((4, chips, coarse, c), bf16),
            V((4, chips, coarse, c), bf16),
            V((chips, low_width, cells), f32),
            V((chips, low_width, cells), f32),
            V((chips, low_width, cells), bf16),
            V((chips, low_width, cells), bf16),
            V((n, pieces, own, c), bf16),
            V((n, 16, 128), f32),
            V((16, c), f32),
            V((5, c, c), bf16),
            V((3, 3 * c, c), bf16),
            V((c, 2 * c), bf16),
            V((3, 3 * low_width, c), bf16),
            V((3, 3 * c, c), bf16),
            D((count,)),
            D((count,)),
            V((2, 2, 24, c), f32),
            V((2, crops, 24, c), f32),
            V((2, chips, 24, c), f32),
            D((2, 2)),
            D((2, crops + chips)),
            D((2, crops + chips)),
            V((7, 2, 8, 128), f32),
            V((7, all_chips, 8, 128), f32),
            D((7, 2)),
            D((7, all_chips)),
            D((7, all_chips)),
            D((6, 2)),
            D((6, 2)),
        ],
        compiler_params=pltpu.CompilerParams(
            collective_id=0, has_side_effects=True, vmem_limit_bytes=62 * 1024 * 1024
        ),
    )(*args)


class Gather:
    def __init__(self, n, send, recv):
        my_crop, self.me = lax.axis_index("crop"), lax.axis_index("chan")
        self.n, self.chips = n, n // 2
        self.core = lax.rem(self.me, 2)
        self.other = (my_crop, self.me + 1 - 2 * self.core)
        self.send, self.recv = send, recv
        self.peer = lambda j: (my_crop, lax.rem(self.me + 2 * j, n))

    def block(self, j):
        return lax.rem(self.me - 2 * j + self.n, self.n)

    def other_block(self, j):
        return lax.rem(self.me + 1 - 2 * self.core - 2 * j + self.n, self.n)

    def start(self, at):
        self.at = at
        self.far, self.pairs = [], []
        for j in range(1, self.chips):
            here = at(self.me)
            self.far.append(remote(here, here, self.send.at[j], self.recv.at[j], self.peer(j)))
            self.far[-1].start()
        self.forward(0)

    def forward(self, j):
        here = self.at(self.block(j))
        k = self.chips + j
        self.pairs.append(remote(here, here, self.send.at[k], self.recv.at[k], self.other))
        self.pairs[-1].start()

    def arrive(self, j):
        self.far[j - 1].wait_recv()
        self.forward(j)

    def finish(self):
        for copy in self.pairs:
            copy.wait_recv()

    def drain(self):
        for copy in self.far + self.pairs:
            copy.wait_send()


class BackRefs(typing.NamedTuple):
    grad: object
    src: object
    point: object
    atrous: object
    pool: object
    pooled_grad: object
    low_grad: object
    low_in: object
    low_w: object
    wgrads: object
    features: object
    point_w: object
    atrous_w: object
    pool_w: object
    early: object
    low_w_out: object
    blocks: object
    all_grad: object
    shifted: object
    turned: object
    total: object
    low_all: object
    first: object
    pairs: object
    crossed: object
    halves: object
    lined: object
    low_parts: object
    g_send: object
    g_recv: object
    l_send: object
    l_recv: object
    c_send: object
    c_recv: object
    f_send: object
    f_recv: object
    w_send: object
    w_recv: object


def back_kernel(crops, n, *refs):
    ref = BackRefs(*refs)
    my_crop, me = lax.axis_index("crop"), lax.axis_index("chan")
    chips = n // 2
    core, chip = lax.rem(me, 2), lax.div(me, 2)
    block, width = ref.grad.shape
    c = width // 4
    c_in = ref.src.shape[2]
    cells = FA * FA
    groups = 8 // crops
    other = (my_crop, me + 1 - 2 * core)
    over_crops = [(lax.rem(my_crop + i, crops), me) for i in range(1, crops)]
    over_chips = [(my_crop, lax.rem(me + 2 * j, n)) for j in range(1, chips)]
    wait_barrier = barrier_with([other] + over_crops + over_chips)
    crop_of = lambda i: lax.rem(my_crop - i + crops, crops)
    all_grad, src = ref.all_grad, ref.src

    def grad_at(crop):
        def at(b):
            return all_grad.at[crop, pl.ds(pl.multiple_of(b * block, block), block)]

        return at

    all_grad[my_crop, pl.ds(pl.multiple_of(me * block, block), block)] = ref.grad[...]
    ref.low_all[me] = ref.low_grad[...]
    wait_barrier()

    gather = Gather(n, ref.g_send, ref.g_recv)
    gather.start(grad_at(my_crop))
    crossing = {}

    def cross(j):
        here = grad_at(my_crop)(gather.block(j))
        for i in range(1, crops):
            k = (i - 1) * chips + j
            copy = remote(here, here, ref.c_send.at[k], ref.c_recv.at[k], over_crops[i - 1])
            copy.start()
            crossing[i, j] = copy

    cross(0)
    w_send, w_recv = ref.w_send, ref.w_recv
    first_copies = []
    for z in range(chips):
        copy = remote(
            ref.wgrads.at[2 * z + 1 - core], ref.first.at[z], w_send.at[z], w_recv.at[z], other
        )
        copy.start()
        first_copies.append(copy)
    low_gather = Gather(n, ref.l_send, ref.l_recv)
    low_gather.start(lambda b: ref.low_all.at[b])

    shifted = ref.shifted

    def shift_source(i):
        crop = crop_of(i)
        for k in range(3):
            rate = atrous_rates[k]
            shift_three(lambda base: src[crop, pl.ds(base, 128)], shifted.at[i % 3, k], rate, -rate, rate)

    shift_source(0)

    for copy in first_copies:
        copy.wait()
    pairs, first, wgrads = ref.pairs, ref.first, ref.wgrads
    for z in range(chips):
        for g in range(8):
            pairs[z, g] = (wgrads[2 * z + core, g].astype(f32) + first[z, g].astype(f32)).astype(bf16)
    at = chips
    cross_copies = []
    for i in range(1, crops):
        target = lax.rem(my_crop + i, crops)
        copy = remote(
            pairs.at[:, pl.ds(target * groups, groups)],
            ref.crossed.at[my_crop],
            w_send.at[at],
            w_recv.at[at],
            over_crops[i - 1],
        )
        copy.start()
        cross_copies.append(copy)
        at += 1
    for z in range(chips):
        for g in range(groups):
            ref.crossed[my_crop, z, g] = pairs[z, my_crop * groups + g]

    for j in range(1, chips):
        gather.arrive(j)
        cross(j)
    for i in range(1, min(3, crops)):
        shift_source(i)
    gather.finish()

    total, turned = ref.total, ref.turned
    pool_row = dot_nt(ref.pooled_grad[...], ref.pool[...])
    my_row = lax.broadcasted_iota(jnp.int32, pool_row.shape, 0) == my_crop
    pool_row = row_of(jnp.where(my_row, pool_row, 0.0)) * (1.0 / cells)
    total[...] = dot_nt(all_grad[my_crop, :, 0:c], ref.point[...]) + pool_row
    for k in range(3):
        rate = atrous_rates[k]
        shift_three(
            lambda base: all_grad[my_crop, pl.ds(base, 128), (k + 1) * c : (k + 2) * c],
            turned, rate, rate, -rate,
        )
        for a in range(3):
            move = (a - 1) * rate
            count = (FA - abs(move)) * FA
            to, off = max(move, 0) * FA, max(-move, 0) * FA
            term = None
            for e in range(3):
                piece = dot_nt(turned[pl.ds(off, count), e * c : (e + 1) * c], ref.atrous[k, 3 * a + e])
                term = piece if term is None else term + piece
            total[pl.ds(to, count)] = total[pl.ds(to, count)] + term

    def weight_part(i):
        crop = crop_of(i)
        part = dot_tn(src[crop], all_grad[crop, :, 0:c])
        ref.point_w[...] = part if i == 0 else ref.point_w[...] + part
        for k in range(3):
            rate = atrous_rates[k]
            for a in range(3):
                move = (a - 1) * rate
                count = (FA - abs(move)) * FA
                from_src, off = max(move, 0) * FA, max(-move, 0) * FA
                part = dot_tn(
                    shifted[i % 3, k, pl.ds(from_src, count)],
                    all_grad[crop, pl.ds(off, count), (k + 1) * c : (k + 2) * c],
                )
                for e in range(3):
                    piece = part[e * c_in : (e + 1) * c_in]
                    if i > 0:
                        piece = ref.atrous_w[k, 3 * a + e] + piece
                    ref.atrous_w[k, 3 * a + e] = piece

    weight_part(0)
    ref.features[...] = total[...].T

    for copy in cross_copies:
        copy.wait()
    line_copies = []
    halves, lined = ref.halves, ref.lined
    for z in range(chips):
        for g in range(groups):
            value = ref.crossed[0, z, g].astype(f32)
            for i in range(1, crops):
                value = value + ref.crossed[i, z, g].astype(f32)
            halves[z, g] = value.astype(bf16)
    for j in range(1, chips):
        target = lax.rem(chip + j, chips)
        copy = remote(
            halves.at[target], lined.at[chip], w_send.at[at], w_recv.at[at], over_chips[j - 1]
        )
        copy.start()
        line_copies.append(copy)
        at += 1
    for g in range(groups):
        lined[chip, g] = halves[chip, g]

    for j in range(1, chips):
        low_gather.arrive(j)
    low_gather.finish()
    rows = ref.low_all.shape[2] // 128
    low_in, low_all = ref.low_in, ref.low_all
    low_total = None
    for b in range(n):
        here = low_all[b]
        span = slice(b * rows * 128, (b + 1) * rows * 128)
        ref.early[:, span] = dot(ref.low_w[...], here)
        part = dot_nt(low_in[:, span], here)
        low_total = part if low_total is None else low_total + part
    low_parts = ref.low_parts
    low_parts[my_crop] = jnp.zeros(low_parts.shape[1:], f32)
    low_parts[my_crop, :, 0 : low_total.shape[1]] = low_total
    low_copies = []
    for i in range(1, crops):
        here = low_parts.at[my_crop]
        low_copies.append(remote(here, here, w_send.at[at], w_recv.at[at], over_crops[i - 1]))
        low_copies[-1].start()
        at += 1

    for copy in line_copies:
        copy.wait()
    blocks = ref.blocks
    for g in range(groups):
        value = lined[0, g].astype(f32)
        for z in range(1, chips):
            value = value + lined[z, g].astype(f32)
        blocks[my_crop * groups + g] = value
    share_copies = []
    for i in range(1, crops):
        here = blocks.at[pl.ds(my_crop * groups, groups)]
        share_copies.append(remote(here, here, w_send.at[at], w_recv.at[at], over_crops[i - 1]))
        share_copies[-1].start()
        at += 1

    pair_copies = []
    for i in range(1, crops):
        if i + 2 < crops:
            shift_source(i + 2)
        crop = crop_of(i)
        here = []
        for j in range(chips):
            crossing[i, j].wait_recv()
            k = (i - 1) * chips + j
            place = grad_at(crop)(gather.block(j))
            copy = remote(place, place, ref.f_send.at[k], ref.f_recv.at[k], other)
            copy.start()
            here.append(copy)
        for copy in here:
            copy.wait_recv()
        pair_copies += here
        weight_part(i)

    pooled = []
    for i in range(crops):
        mean = row_of(src[i].astype(f32)) * (1.0 / cells)
        pooled.append(mean)
    pooled = jnp.concatenate(pooled + [jnp.zeros((16 - crops, c_in), f32)], axis=0).astype(bf16)
    ref.pool_w[...] = dot_tn(pooled, ref.pooled_grad[...])

    for copy in low_copies + share_copies:
        copy.wait()
    ref.low_w_out[...] = jnp.sum(low_parts[...], axis=0)
    gather.drain()
    low_gather.drain()
    for copy in list(crossing.values()) + pair_copies:
        copy.wait_send()


def pyramid_back(crops, n, *args):
    grad, src, low_grad, low_in, wgrads = args[0], args[1], args[6], args[7], args[9]
    block, width = grad.shape
    c = width // 4
    c_in = src.shape[2]
    chips = n // 2
    cells = FA * FA
    low_rows, low_width = args[8].shape
    own, lanes = wgrads.shape[2:]
    groups = 8 // crops
    S = jax.ShapeDtypeStruct
    V = pltpu.VMEM
    D = pltpu.SemaphoreType.DMA
    vmem = pl.BlockSpec(memory_space=pltpu.VMEM)
    w_count = chips + 3 * (crops - 1) + chips
    return pl.pallas_call(
        functools.partial(back_kernel, crops, n),
        out_shape=[
            S((c_in, cells), f32),
            S((c_in, c), f32),
            S((3, 9, c_in, c), f32),
            S((c_in, c), f32),
            S((low_rows, low_in.shape[1]), f32),
            S((low_rows, 128), f32),
            S((8, own, lanes), f32),
        ],
        in_specs=[vmem] * len(args),
        out_specs=[vmem] * 7,
        scratch_shapes=[
            V((crops, cells, width), bf16),
            V((min(3, crops), 3, cells, 3 * c_in), bf16),
            V((cells, 3 * c), bf16),
            V((cells, c_in), f32),
            V((n,) + low_grad.shape, bf16),
            V((chips, 8, own, lanes), bf16),
            V((chips, 8, own, lanes), bf16),
            V((crops, chips, groups, own, lanes), bf16),
            V((chips, groups, own, lanes), bf16),
            V((chips, groups, own, lanes), bf16),
            V((crops, low_rows, 128), f32),
            D((n,)),
            D((n,)),
            D((n,)),
            D((n,)),
            D((crops * chips,)),
            D((crops * chips,)),
            D((crops * chips,)),
            D((crops * chips,)),
            D((w_count,)),
            D((w_count,)),
        ],
        compiler_params=pltpu.CompilerParams(
            collective_id=1, has_side_effects=True, vmem_limit_bytes=62 * 1024 * 1024
        ),
    )(*args)


def up_rows(first, count, coarse_first, coarse_count, fine_side):
    fine = first + jnp.arange(count)
    pos = jnp.clip((fine.astype(f32) + 0.5) / 4.0 - 0.5, 0.0, FA - 1.0)
    coarse = (coarse_first + jnp.arange(coarse_count)).astype(f32)
    table = jnp.maximum(0.0, 1.0 - jnp.abs(pos[:, None] - coarse[None, :]))
    return jnp.where(((fine >= 0) & (fine < fine_side))[:, None], table, 0.0)


def own_rows(values, axis):
    size = values.shape[axis] // lax.axis_size("chan")
    return lax.dynamic_slice_in_dim(values, lax.axis_index("chan") * size, size, axis)


def per_device(
    features,
    low_in,
    offsets,
    d_logits,
    w_point,
    w_atrous,
    w_pool,
    w_proj,
    w_low,
    w_dec1,
    w_dec1_low,
    w_dec2,
    w_cls,
    b_cls,
    bn_gain,
    bn_shift,
    low_gain,
    low_shift,
):
    n = lax.axis_size("chan")
    crops = lax.axis_size("crop")
    me = lax.axis_index("chan")
    my_crop = lax.axis_index("crop")
    fine = low_in.shape[2]
    rows = fine // n
    coarse_rows = FA // n
    channels = w_dec2.shape[2]
    c_in = features.shape[1]
    low_width = w_low.shape[1]
    coarse_samples = FA * FA * crops
    fine_samples = fine * fine * crops

    own = w_dec2.shape[1]
    classes = w_cls.shape[1]
    side = w_dec1_low.transpose(2, 0, 1).reshape(own, 9 * low_width)
    tail = jnp.concatenate([side, w_cls], axis=1)
    tail = jnp.pad(tail, ((0, 0), (0, 2 * channels - tail.shape[1])))
    tail = tail.reshape(own, 2, channels).transpose(1, 0, 2)
    packed = jnp.concatenate([w_proj, w_dec1, tail, w_dec2])
    packed = jnp.pad(packed, ((0, -packed.shape[0] % crops), (0, 0), (0, 0)))
    norms_own = jnp.pad(jnp.concatenate([bn_gain, bn_shift]), ((0, 0), (0, 128 - own)))

    row_index = me * rows + jnp.arange(rows, dtype=jnp.int32)
    col_index = jnp.arange(fine, dtype=jnp.int32)
    rows_valid = offsets[0, 0] + 4 * row_index < SCENE_H
    cols_valid = offsets[0, 1] + 4 * col_index < SCENE_W
    mask = (rows_valid[:, None] & cols_valid[None, :]).astype(f32)

    outer_rows = me * rows - 1 + jnp.arange(rows + 2, dtype=jnp.int32)
    outer_mask = (offsets[0, 0] + 4 * outer_rows < SCENE_H) & (outer_rows >= 0) & (outer_rows < fine)
    outer_mask = (outer_mask[:, None] & cols_valid[None, :]).astype(bf16)
    spare = 32 - classes
    outer_grad = jnp.pad(d_logits[0], ((0, spare), (1, 1), (0, 0)))
    outer_grad = lax.dynamic_slice_in_dim(outer_grad, me * rows, rows + 2, 1) * outer_mask
    wide_column = lambda v: jnp.broadcast_to(v[:, None], (v.shape[0], 128))
    table = up_rows(0, fine, 0, FA, fine)
    low_flat = low_in[0].reshape(low_in.shape[1], fine * fine)
    (
        logits, branch_grad, pool_grad, pool_bf, proj_sums, low_pre_bf, totals, low_totals, blocks,
        source_all,
    ) = decoder(
        crops,
        n,
        (coarse_samples, fine_samples),
        features[0],
        w_point,
        w_atrous.reshape(3, 3, 3 * c_in, channels),
        w_pool,
        low_flat,
        w_low.T,
        packed,
        norms_own,
        wide_column(low_gain),
        wide_column(low_shift),
        wide_column(jnp.pad(b_cls, (0, spare))),
        outer_grad.reshape(32, (rows + 2) * fine),
        mask.reshape(1, rows * fine),
        table.astype(bf16),
        table.T.astype(bf16),
    )
    logits = logits[:classes].reshape(classes, rows, fine)
    pool_bf, proj_sums = pool_bf[:crops], proj_sums[:crops]
    proj_wgrad_pool = jnp.einsum("bc,bo->co", pool_bf.astype(f32), proj_sums, precision=highest)
    feature_grad, point_wgrad, atrous_wgrad, pool_wgrad, early_grad, low_wgrad, blocks = pyramid_back(
        crops,
        n,
        branch_grad,
        source_all,
        w_point,
        w_atrous,
        w_pool,
        pool_grad,
        low_pre_bf,
        low_flat,
        w_low,
        blocks,
    )
    turn = lambda v: v.reshape(3, own, 3, channels)[:, :, ::-1].transpose(0, 2, 1, 3).reshape(9, own, channels)
    dec2_wgrad, dec1_wgrad = turn(blocks[0:3]), turn(blocks[3:6])
    proj_wgrad = blocks[6].reshape(own, 3, channels).transpose(1, 0, 2)
    last = blocks[7]
    proj_wgrad = jnp.concatenate(
        [proj_wgrad, last[None, :, :channels], own_rows(proj_wgrad_pool, 0)[None]], axis=0
    )
    last = last[:, channels:]
    side_wgrad = last[:, : 9 * low_width].reshape(own, 9, low_width).transpose(1, 2, 0)
    cls_weight_grad = last[:, 9 * low_width : 9 * low_width + classes]

    return (
        logits[None],
        feature_grad[None],
        early_grad.reshape(low_in.shape),
        point_wgrad,
        atrous_wgrad,
        pool_wgrad,
        proj_wgrad,
        low_wgrad[:, :low_width],
        dec1_wgrad,
        side_wgrad,
        dec2_wgrad,
        cls_weight_grad,
        totals[16, :classes],
        own_rows(totals[0:8], 1),
        own_rows(totals[8:16], 1),
        low_totals[0, :low_width],
        low_totals[1, :low_width],
    )


def solution(mesh):
    placed = (
        P("crop", "chan", None),
        P("crop", "chan", None, None),
        P("crop", None),
        P("crop", None, None, None),
        P("chan", None),
        P(None, None, "chan", None),
        P("chan", None),
        P(None, "chan", None),
        P("chan", None),
        P(None, "chan", None),
        P(None, None, "chan"),
        P(None, "chan", None),
        P("chan", None),
        P(),
        P(None, "chan"),
        P(None, "chan"),
        P(),
        P(),
    )
    return jax.shard_map(
        per_device,
        mesh=mesh,
        in_specs=placed,
        out_specs=(
            P("crop", None, "chan", None),
            P("crop", "chan", None),
            P("crop", "chan", None, None),
            P("chan", None),
            P(None, None, "chan", None),
            P("chan", None),
            P(None, "chan", None),
            P("chan", None),
            P(None, "chan", None),
            P(None, None, "chan"),
            P(None, "chan", None),
            P("chan", None),
            P(),
            P(None, "chan"),
            P(None, "chan"),
            P(),
            P(),
        ),
        check_vma=False,
    )
```

```python
import functools
import typing

import jax
import jax.numpy as jnp
from jax import lax
from jax.experimental import pallas as pl
from jax.experimental.pallas import tpu as pltpu
from jax.sharding import PartitionSpec as P

FA = 32
SCENE_H = 1024
SCENE_W = 2048

epsilon = 1e-05
highest = lax.Precision.HIGHEST
atrous_rates = (6, 12, 18)
f32 = jnp.float32
bf16 = jnp.bfloat16
BOTH = ("crop", "chan")


MESH = pl.DeviceIdType.MESH


def chip_peers(crops, n):
    my_crop, me = lax.axis_index("crop"), lax.axis_index("chan")
    core = lax.rem(me, 2)
    chips = n // 2
    other = (my_crop, me + 1 - 2 * core)
    far = []
    for i in range(crops):
        for j in range(chips):
            if i or j:
                far.append((lax.rem(my_crop + i, crops), lax.rem(me + 2 * j, n)))
    return other, far


GELU_A = 0.7978845608028654
GELU_B = 0.044715


def gelu(x):
    return 0.5 * x * (1.0 + jnp.tanh(GELU_A * (x + GELU_B * x * x * x)))


def gelu_slope(x):
    square = x * x
    t = jnp.tanh(GELU_A * x * (1.0 + GELU_B * square))
    return 0.5 * (1.0 + t) + (0.5 * GELU_A) * x * (1.0 - t * t) * (1.0 + (3.0 * GELU_B) * square)


def dot(a, b):
    return jnp.dot(a, b, preferred_element_type=f32)


def dot_nt(a, b):
    return lax.dot_general(a, b, (((1,), (1,)), ((), ())), preferred_element_type=f32)


def dot_tn(a, b):
    return lax.dot_general(a, b, (((0,), (0,)), ((), ())), preferred_element_type=f32)


def dot_exact(table, values):
    high = values.astype(bf16)
    rest = values - high.astype(f32)
    middle = rest.astype(bf16)
    low = (rest - middle.astype(f32)).astype(bf16)
    return dot(table, high) + (dot(table, middle) + dot(table, low))


def fold(values):
    return jnp.sum(values.reshape(values.shape[0] // 8, 8, values.shape[1]), axis=0)


def row_of(values):
    return jnp.sum(values, axis=0, keepdims=True)


def barrier_with(peers):
    barrier = pltpu.get_barrier_semaphore()
    for peer in peers:
        pl.semaphore_signal(barrier, inc=1, device_id=peer, device_id_type=MESH)
    return lambda: pl.semaphore_wait(barrier, len(peers))


def remote(src, dst, send, recv, peer):
    return pltpu.make_async_remote_copy(
        src_ref=src, dst_ref=dst, send_sem=send, recv_sem=recv, device_id=peer, device_id_type=MESH
    )


class Copies:
    def __init__(self, send, recv):
        self.send, self.recv, self.all = send, recv, []

    def start(self, src, dst, peer):
        k = len(self.all)
        copy = remote(src, dst, self.send.at[k], self.recv.at[k], peer)
        copy.start()
        self.all.append(copy)
        return copy

    def drain(self, kept):
        for copy in self.all:
            if not any(copy is other for other in kept):
                copy.wait_send()


def shift_three(source, target, rate, first, last):
    column = lax.rem(lax.broadcasted_iota(jnp.int32, (128, 1), 0), FA)

    def step(i, kept):
        base = pl.multiple_of(i * 128, 128)
        here = source(base)
        w = here.shape[1]
        wide = here.astype(f32)
        for slot, by in ((0, first), (2, last)):
            ok = jnp.logical_and(column + by >= 0, column + by < FA)
            moved = jnp.where(ok, pltpu.roll(wide, (-by) % 128, 0), 0.0)
            target[pl.ds(base, 128), slot * w : (slot + 1) * w] = moved.astype(bf16)
        target[pl.ds(base, 128), w : 2 * w] = here
        return kept

    lax.fori_loop(0, FA * FA // 128, step, 0)


class Swap:
    def __init__(self, crops, n, pair, slots, pair_sems, send, recv):
        self.other, self.far = chip_peers(crops, n)
        me = lax.axis_index("chan")
        self.core = lax.rem(me, 2)
        self.mine = lax.axis_index("crop") * (n // 2) + lax.div(me, 2)
        self.pair, self.slots, self.pair_sems = pair, slots, pair_sems
        self.send, self.recv = send, recv

    def start(self):
        here = self.pair.at[self.core]
        copy = remote(here, here, self.pair_sems.at[0], self.pair_sems.at[1], self.other)
        copy.start()
        copy.wait()
        self.slots[self.mine] = self.pair[0] + self.pair[1]
        self.copies = []
        for k, peer in enumerate(self.far):
            slot = self.slots.at[self.mine]
            copy = remote(slot, slot, self.send.at[k], self.recv.at[k], peer)
            copy.start()
            self.copies.append(copy)

    def finish(self):
        for copy in self.copies:
            copy.wait()
        return jnp.sum(self.slots[...], axis=0)


class WideSwap:
    def __init__(self, crops, n, pair, first, second, pair_sems, send, recv):
        my_crop, me = lax.axis_index("crop"), lax.axis_index("chan")
        self.core, self.crop, self.chip = lax.rem(me, 2), my_crop, lax.div(me, 2)
        self.other = (my_crop, me + 1 - 2 * self.core)
        self.over_crops = [(lax.rem(my_crop + i, crops), me) for i in range(1, crops)]
        self.over_chips = [(my_crop, lax.rem(me + 2 * j, n)) for j in range(1, n // 2)]
        self.pair, self.first, self.second = pair, first, second
        self.pair_sems, self.send, self.recv = pair_sems, send, recv

    def run(self, then=None):
        here = self.pair.at[self.core]
        copy = remote(here, here, self.pair_sems.at[0], self.pair_sems.at[1], self.other)
        copy.start()
        copy.wait()
        self.first[self.crop] = self.pair[0] + self.pair[1]
        k = 0
        copies = []
        for peer in self.over_crops:
            slot = self.first.at[self.crop]
            copies.append(remote(slot, slot, self.send.at[k], self.recv.at[k], peer))
            copies[-1].start()
            k += 1
        for copy in copies:
            copy.wait()
        self.second[self.chip] = jnp.sum(self.first[...], axis=0)
        copies = []
        for peer in self.over_chips:
            slot = self.second.at[self.chip]
            copies.append(remote(slot, slot, self.send.at[k], self.recv.at[k], peer))
            copies[-1].start()
            k += 1
        if then is not None:
            then()
        for copy in copies:
            copy.wait()
        return jnp.sum(self.second[...], axis=0)


def put_pair(ref, core, a, b):
    ref[core, 0:1] = a[:, :128]
    ref[core, 1:2] = a[:, 128:]
    ref[core, 2:3] = b[:, :128]
    ref[core, 3:4] = b[:, 128:]


def get_pair(total):
    return (
        jnp.concatenate([total[0:1], total[1:2]], axis=1),
        jnp.concatenate([total[2:3], total[3:4]], axis=1),
    )


def spread_row(row):
    return jnp.broadcast_to(row, (128, 128)).T


def up_weights(i, me, n, rows, coarse_rows):
    lower = (2 * i - 3) // 8
    upper_weight = (2 * i - 3 - 8 * lower) / 8.0
    a, b = 1.0 - upper_weight, upper_weight
    if lower < 0:
        top = me == 0
        a, b = jnp.where(top, 0.0, a), jnp.where(top, 1.0, b)
    if lower + 1 >= coarse_rows:
        bottom = me == n - 1
        a, b = jnp.where(bottom, 1.0, a), jnp.where(bottom, 0.0, b)
    if i < 0:
        a, b = jnp.where(me == 0, 0.0, a), jnp.where(me == 0, 0.0, b)
    if i >= rows:
        a, b = jnp.where(me == n - 1, 0.0, a), jnp.where(me == n - 1, 0.0, b)
    return lower + 1, a, b


class DecoderRefs(typing.NamedTuple):
    offsets: object
    feat: object
    point: object
    atrous: object
    pool_w: object
    low_in: object
    low_w: object
    w_proj: object
    w_dec1: object
    w_side: object
    w_dec2: object
    w_cls: object
    own_gain: object
    own_shift: object
    low_gain: object
    low_shift: object
    bias: object
    dlog: object
    logits: object
    branch_out: object
    pool_out: object
    low_out: object
    gain_grad: object
    shift_grad: object
    bias_grad: object
    low_gain_grad: object
    low_shift_grad: object
    pool_proj: object
    dec2_w: object
    wgrads: object
    src_all: object
    low_ext: object
    low_push: object
    lowx: object
    merged_ext: object
    merged_part: object
    dec1: object
    dec2: object
    pushed: object
    pushed1: object
    x1: object
    x2: object
    g2: object
    g1: object
    yt: object
    branch_bf: object
    proj_bf: object
    second: object
    flip: object
    branch: object
    staged: object
    arrived: object
    low_send: object
    low_pair: object
    low_sum: object
    low_recv: object
    gath: object
    norms_all: object
    norms: object
    proj: object
    w1: object
    tail: object
    w1low: object
    w2: object
    cls_all: object
    cls_t: object
    dmask: object
    columns: object
    own_w: object
    r_first: object
    r_pairs: object
    r_crossed: object
    r_halves: object
    r_lined: object
    r_out: object
    f_send: object
    f_recv: object


def rest_groups(crops):
    return -(-15 // crops) * crops


def weight_groups(crops):
    return -(-8 // crops) * crops, -(-9 // crops) * crops


def decoder_kernel(crops, n, samples, *refs):
    ref = DecoderRefs(*refs[: len(DecoderRefs._fields)])
    rest = list(refs[len(DecoderRefs._fields) :])
    (wide_pair, wide_first, wide_second, wide_psem, wide_send, wide_recv) = rest[:6]
    (pair, slots, psem, send, recv, halo_send, halo_recv) = rest[6:13]

    coarse_samples, fine_samples = samples
    my_crop, me = lax.axis_index("crop"), lax.axis_index("chan")
    core = lax.rem(me, 2)
    above = (my_crop, lax.rem(me + n - 1, n))
    below = (my_crop, lax.rem(me + 1, n))
    low_chans, low_width = ref.low_w.shape
    classes = ref.w_cls.shape[1]
    rows = ref.dlog.shape[1] // 128 - 2
    fine_cells = rows * 128
    coarse_cells = ref.branch.shape[0]
    coarse_rows = coarse_cells // FA
    cells = FA * FA
    c_in, c = ref.point.shape
    own = c // n
    chips, chip = n // 2, lax.div(me, 2)
    small, large = weight_groups(crops)
    chunk = min(4, rows)

    other, far = chip_peers(crops, n)
    over_crops = [(lax.rem(my_crop + i, crops), me) for i in range(1, crops)]
    over_chips = [(my_crop, lax.rem(me + 2 * j, n)) for j in range(1, chips)]
    wait_barrier = barrier_with([other, above, below] + far)

    swaps = [
        Swap(crops, n, pair.at[i], slots.at[i], psem.at[i], send.at[0 if i == 6 else (i + 1) % 2], recv.at[i])
        for i in range(pair.shape[0])
    ]
    wides = [
        WideSwap(
            crops, n, wide_pair.at[i], wide_first.at[i], wide_second.at[i],
            wide_psem.at[i], wide_send.at[i], wide_recv.at[i],
        )
        for i in range(2)
    ]
    front = Copies(ref.f_send, ref.f_recv)
    for i in range(pair.shape[0]):
        pair[i, core] = jnp.zeros((8, 128), f32)
    for i in range(2):
        wide_pair[i, core] = jnp.zeros(wide_pair.shape[2:], f32)

    def halo(i, first, last, to_above, to_below):
        copies = [
            remote(first, to_above, halo_send.at[i, 0], halo_recv.at[i, 0], above),
            remote(last, to_below, halo_send.at[i, 1], halo_recv.at[i, 1], below),
        ]
        for copy in copies:
            copy.start()
        return copies

    def fine_halo(i, values):
        return halo(
            i,
            values.at[pl.ds(128, 128)],
            values.at[pl.ds(rows * 128, 128)],
            values.at[pl.ds((rows + 1) * 128, 128)],
            values.at[pl.ds(0, 128)],
        )

    def gain(k):
        return ref.norms[k : k + 1]

    def shift(k):
        return ref.norms[8 + k : 9 + k]

    def moments(total, square, count):
        average = total * (1.0 / count)
        return average, lax.rsqrt(square * (1.0 / count) - average * average + epsilon)

    column = lax.broadcasted_iota(jnp.int32, (128, c), 0)

    def put_three(target, base, y):
        target[pl.ds(base, 128), 0:c] = jnp.where(column == 0, 0.0, pltpu.roll(y, 1, 0)).astype(bf16)
        target[pl.ds(base, 128), c : 2 * c] = y.astype(bf16)
        target[pl.ds(base, 128), 2 * c : 3 * c] = jnp.where(
            column == 127, 0.0, pltpu.roll(y, 127, 0)
        ).astype(bf16)

    def inside(i):
        at_top = jnp.logical_and(me == 0, i == 0)
        at_bottom = jnp.logical_and(me == n - 1, i == rows + 1)
        return jnp.where(jnp.logical_or(at_top, at_bottom), 0.0, 1.0)

    def each_row(body, first, last, carry):
        def step(i, kept):
            return body(i, pl.multiple_of(i * 128, 128), kept)

        return lax.fori_loop(first, last, step, carry)

    zero = jnp.zeros((8, c), f32)

    src_all, gath = ref.src_all, ref.gath
    for i in range(cells // 256):
        src_all[my_crop, pl.ds(i * 256, 256)] = ref.feat[:, i * 256 : (i + 1) * 256].T
    flip = ref.flip
    flip[...] = jnp.zeros(flip.shape, f32)
    flip[0 : 9 * low_width, 0:own] = ref.w_side[...].astype(f32)
    for k in range(5):
        gath[me, k] = ref.w_proj[k]
    turned = flip[:, 0:128].T[0:own].astype(bf16)
    gath[me, 5] = turned[:, 0:c]
    gath[me, 6] = turned[:, c : 2 * c]
    gath[me, 7] = jnp.zeros((own, c), bf16)
    gath[me, 7, :, 0:classes] = ref.w_cls[...]
    for k in range(8, small):
        gath[me, k] = jnp.zeros((own, c), bf16)
    for t in range(9, large):
        gath[me, small + t] = jnp.zeros((own, c), bf16)
        gath[me, small + large + t] = jnp.zeros((own, c), bf16)
    for t in range(9):
        gath[me, small + t] = ref.w_dec1[t]
        gath[me, small + large + t] = ref.w_dec2[t]
    columns = ref.columns
    columns[...] = jnp.zeros(columns.shape, f32)
    columns[0:1, 0:low_width] = ref.low_gain[...]
    columns[1:2, 0:low_width] = ref.low_shift[...]
    columns[2:3, 0:classes] = ref.bias[...]
    ref.norms_all[me] = jnp.zeros((16, 128), f32)
    ref.norms_all[me, 0:8, 0:own] = ref.own_gain[...]
    ref.norms_all[me, 8:16, 0:own] = ref.own_shift[...]
    wait_barrier()
    block_of = lambda j: lax.rem(me - 2 * j + n, n)
    crop_of = lambda i: lax.rem(my_crop - i + crops, crops)

    class Spread:
        def __init__(self, first, size):
            per = size // crops
            self.at = lambda b, q: gath.at[b, pl.ds(first + q * per, per)]
            self.first, self.size = first, size

        def start(self):
            here = self.at(me, my_crop)
            self.far = [front.start(here, here, peer) for peer in over_chips]
            here = gath.at[me, pl.ds(self.first, self.size)]
            self.pairs = [front.start(here, here, other)]

        def cross(self):
            self.crossed = []
            for j in range(1, chips):
                self.far[j - 1].wait_recv()
                here = self.at(block_of(j), my_crop)
                for i in range(1, crops):
                    self.crossed.append((i, j, front.start(here, here, over_crops[i - 1])))
                self.pairs.append(front.start(here, here, other))

        def cores(self):
            for i, j, copy in self.crossed:
                copy.wait_recv()
                here = self.at(block_of(j), crop_of(i))
                self.pairs.append(front.start(here, here, other))

        def finish(self):
            for copy in self.pairs:
                copy.wait_recv()

    norm_far = []
    here = ref.norms_all.at[me]
    for peer in over_chips:
        norm_far.append(front.start(here, here, peer))
    norm_pairs = [front.start(here, here, other)]
    spread = [Spread(0, small), Spread(small, large), Spread(small + large, large)]
    spread[0].start()
    spread[1].start()
    low_send, low_pair = ref.low_send, ref.low_pair

    def low_block(b):
        span = pl.ds(pl.multiple_of(b * fine_cells, fine_cells), fine_cells)
        return dot_tn(ref.low_w[...], ref.low_in[:, span])

    low_copies = []
    for z in range(chips):
        low_send[z] = low_block(2 * z + 1 - core)
        low_copies.append(front.start(low_send.at[z], low_pair.at[z], other))
    part, part_in, staged, arrived = ref.pushed, ref.pushed1, ref.staged, ref.arrived
    shifted = ref.g2

    def branch_partial(k):
        first = k * cells
        if k == 0:
            part[pl.ds(first, cells)] = dot(src_all[my_crop], ref.point[...])
        else:
            rate = atrous_rates[k - 1]
            shift_three(lambda base: src_all[my_crop, pl.ds(base, 128)], shifted, rate, -rate, rate)
            part[pl.ds(first, cells)] = dot(shifted[pl.ds(0, cells), 0 : 3 * c_in], ref.atrous[k - 1, 1])
            for a in (0, 2):
                move = (a - 1) * rate
                count = (FA - abs(move)) * FA
                to, off = first + max(-move, 0) * FA, max(move, 0) * FA
                part[pl.ds(to, count)] += dot(shifted[pl.ds(off, count), 0 : 3 * c_in], ref.atrous[k - 1, a])
        copies = []
        for z in range(chips):
            block = pl.multiple_of(first + (2 * z + 1 - core) * coarse_cells, coarse_cells)
            copies.append(
                front.start(
                    part.at[pl.ds(block, coarse_cells)],
                    part_in.at[pl.ds((k * chips + z) * coarse_cells, coarse_cells)],
                    other,
                )
            )
        return copies

    def pair_sum(k, z):
        block = pl.multiple_of(k * cells + (2 * z + core) * coarse_cells, coarse_cells)
        landed = pl.multiple_of((k * chips + z) * coarse_cells, coarse_cells)
        return part[pl.ds(block, coarse_cells)] + part_in[pl.ds(landed, coarse_cells)]

    branch_far, waited = [], []

    def branch_out(k, copies):
        for copy in copies:
            copy.wait()
            waited.append(copy)
        for z in range(chips):
            staged[k, z] = pair_sum(k, z).astype(bf16)
        ref.branch[:, k * c : (k + 1) * c] = pair_sum(k, chip)
        for j in range(1, chips):
            target = lax.rem(chip + j, chips)
            branch_far.append((k, j, front.start(staged.at[k, target], arrived.at[k, chip], over_chips[j - 1])))

    order = (0, 3, 2, 1)
    before = branch_partial(order[0])
    for at in range(1, 4):
        after = branch_partial(order[at])
        branch_out(order[at - 1], before)
        before = after
        if at == 2:
            spread[0].cross()
        if at == 1:
            for z in range(chips):
                low_copies[z].wait_recv()
                ref.low_sum[z] = (low_block(2 * z + core) + low_pair[z]).astype(bf16)
            low_far = []
            for j in range(1, chips):
                target = lax.rem(chip + j, chips)
                low_far.append(front.start(ref.low_sum.at[target], ref.low_recv.at[chip], over_chips[j - 1]))

    branch_out(order[3], before)
    spread[1].cross()
    here = src_all.at[my_crop]
    feature_copies = [front.start(here, here, peer) for peer in over_crops]
    for j in range(1, chips):
        norm_far[j - 1].wait_recv()
        here = ref.norms_all.at[block_of(j)]
        norm_pairs.append(front.start(here, here, other))
    pooled = row_of(src_all[my_crop].astype(f32)) * (1.0 / cells)
    pooled = jnp.concatenate([pooled, jnp.zeros((15, c_in), f32)], axis=0).astype(bf16)
    pool_part = dot(pooled, ref.pool_w[...])[0:1]

    spread[0].cores()
    spread[1].cores()
    for copy in norm_pairs:
        copy.wait_recv()
    for b in range(n):
        ref.norms[:, b * own : (b + 1) * own] = ref.norms_all[b, :, 0:own]

    for copy in low_far:
        copy.wait_recv()
    low_ext = ref.low_ext
    low_total = low_block(me) + low_pair[chip]
    for j in range(1, chips):
        low_total = low_total + ref.low_recv[lax.rem(chip - j + chips, chips)].astype(f32)
    low_ext[:, 128 : 128 + fine_cells] = low_total
    low_edges = halo(
        0,
        low_ext.at[:, pl.ds(128, 128)],
        low_ext.at[:, pl.ds(rows * 128, 128)],
        low_ext.at[:, pl.ds((rows + 1) * 128, 128)],
        low_ext.at[:, pl.ds(0, 128)],
    )

    def add_low(i, base, kept):
        v = low_ext[:, pl.ds(base, 128)]
        return kept[0] + v, kept[1] + v * v

    low_zero = jnp.zeros((low_width, 128), f32)
    low_sum, low_square = each_row(add_low, 1, rows + 1, (low_zero, low_zero))

    def lanes_of(values):
        return row_of(values.T)

    pair[6, core, 0:1, 0:low_width] = lanes_of(low_sum)
    pair[6, core, 1:2, 0:low_width] = lanes_of(low_square)
    swaps[6].start()

    for k, j, copy in branch_far:
        copy.wait_recv()
        here = lax.rem(chip - j + chips, chips)
        ref.branch[:, k * c : (k + 1) * c] += arrived[k, here].astype(f32)
    wide = wide_pair.at[0]
    for k in range(4):
        v = ref.branch[:, k * c : (k + 1) * c]
        wide[core, k : k + 1] = row_of(v)
        wide[core, 4 + k : 5 + k] = row_of(v * v)
    wide[core, 8:16] = jnp.where(
        lax.broadcasted_iota(jnp.int32, (8, c), 0) == my_crop, pool_part, 0.0
    )
    total_a = wides[0].run(spread[2].start)
    spread[0].finish()
    proj, w1, w2, tail = ref.proj, ref.w1, ref.w2, ref.tail
    for b in range(n):
        mine = pl.ds(b * own, own)
        for k in range(5):
            proj[k, mine] = gath[b, k]

    def place_conv(target, first):
        for b in range(n):
            for t in range(9):
                a, e = t // 3, t % 3
                target[a, pl.ds(e * c + b * own, own)] = gath[b, first + t]

    def branch_parts(k):
        average, inverse = moments(total_a[k : k + 1], total_a[4 + k : 5 + k], coarse_samples)
        normed = (ref.branch[:, k * c : (k + 1) * c] - average) * inverse
        return normed, gain(k) * normed + shift(k), inverse

    projected = jnp.zeros((coarse_cells, c), f32)
    for k in range(4):
        y = gelu(branch_parts(k)[1]).astype(bf16)
        ref.branch_bf[:, k * c : (k + 1) * c] = y
        projected = projected + dot(y, ref.proj[k])
    pool_here = lax.broadcasted_iota(jnp.int32, (8, c), 0) < crops
    pool_pre = total_a[8:16]
    pool_average = row_of(pool_pre) * (1.0 / crops)
    pool_spread = jnp.where(pool_here, pool_pre - pool_average, 0.0)
    pool_inverse = lax.rsqrt(row_of(pool_spread * pool_spread) * (1.0 / crops) + epsilon)
    pool_normed = pool_spread * pool_inverse
    pool_before = gain(4) * pool_normed + shift(4)
    pool_bf = gelu(pool_before)
    pool_bf = jnp.concatenate([pool_bf, jnp.zeros((8, c), f32)], axis=0).astype(bf16)
    pool_term = dot(pool_bf, ref.proj[4])
    my_row = lax.broadcasted_iota(jnp.int32, (16, c), 0) == my_crop
    projected = projected + row_of(jnp.where(my_row, pool_term, 0.0))
    merged_ext = ref.merged_ext
    merged_ext[pl.ds(FA, coarse_cells)] = projected
    put_pair(pair.at[0], core, row_of(projected), row_of(projected * projected))
    merged_copies = halo(
        1,
        merged_ext.at[pl.ds(FA, FA)],
        merged_ext.at[pl.ds(coarse_cells, FA)],
        merged_ext.at[pl.ds(FA + coarse_cells, FA)],
        merged_ext.at[pl.ds(0, FA)],
    )
    swaps[0].start()

    total_l = swaps[6].finish()
    for copy in low_edges:
        copy.wait()
    low_average = total_l[0:1] * (1.0 / fine_samples)
    low_variance = total_l[1:2] * (1.0 / fine_samples) - low_average * low_average
    low_inverse_row = lax.rsqrt(low_variance + epsilon)
    low_average = spread_row(low_average)[0:low_width]
    low_inverse = spread_row(low_inverse_row)[0:low_width]
    lane = lax.broadcasted_iota(jnp.int32, (low_width, 128), 1)
    low_gain = spread_row(columns[0:1])[0:low_width]
    low_shift = spread_row(columns[1:2])[0:low_width]

    def low_parts(base):
        normed = (low_ext[:, pl.ds(base, 128)] - low_average) * low_inverse
        return normed, low_gain * normed + low_shift

    def low_row(i, base, kept):
        y = gelu(low_parts(base)[1]) * inside(i)
        lowx = ref.lowx
        lowx[0:low_width, pl.ds(base, 128)] = jnp.where(lane == 0, 0.0, pltpu.roll(y, 1, 1)).astype(bf16)
        lowx[low_width : 2 * low_width, pl.ds(base, 128)] = y.astype(bf16)
        lowx[2 * low_width : 3 * low_width, pl.ds(base, 128)] = jnp.where(
            lane == 127, 0.0, pltpu.roll(y, 127, 1)
        ).astype(bf16)
        return kept

    each_row(low_row, 0, rows + 2, 0)

    for b in range(n):
        mine = pl.ds(b * own, own)
        tail[mine, 0:c] = gath[b, 5]
        tail[mine, c : 2 * c] = gath[b, 6]
        ref.cls_all[mine] = gath[b, 7, :, 0:128]
    turned = tail[...].T
    for a in range(3):
        ref.w1low[a] = turned[a * 3 * low_width : (a + 1) * 3 * low_width]
    cls_lane = lax.broadcasted_iota(jnp.int32, (c, 128), 1)
    cls_clean = jnp.where(cls_lane < classes, ref.cls_all[...].astype(f32), 0.0)
    ref.cls_t[...] = cls_clean.T[0:32].astype(bf16)
    spread[2].cross()
    merged_sum, merged_square = get_pair(swaps[0].finish())
    for copy in merged_copies:
        copy.wait()
    merged_average, merged_inverse = moments(merged_sum, merged_square, coarse_samples)

    def merged_parts(first, count):
        normed = (merged_ext[pl.ds(first, count)] - merged_average) * merged_inverse
        return normed, gain(5) * normed + shift(5)

    fine_at = lax.broadcasted_iota(jnp.int32, (128, FA), 0).astype(f32)
    coarse_at = lax.broadcasted_iota(jnp.int32, (128, FA), 1).astype(f32)
    place = jnp.clip((fine_at + 0.5) / 4.0 - 0.5, 0.0, FA - 1.0)
    up = jnp.maximum(0.0, 1.0 - jnp.abs(place - coarse_at)).astype(bf16)
    coarse_wide = []
    for j in range(coarse_rows + 2):
        coarse_wide.append(dot_exact(up, gelu(merged_parts(j * FA, FA)[1])))
    for i in range(-1, rows + 1):
        lower, a, b = up_weights(i, me, n, rows, coarse_rows)
        put_three(ref.x1, (i + 1) * 128, a * coarse_wide[lower] + b * coarse_wide[lower + 1])
    spread[2].cores()
    spread[1].finish()
    place_conv(w1, small)
    dec1, dec2, pushed, pushed1 = ref.dec1, ref.dec2, ref.pushed, ref.pushed1

    def conv_piece(source, weight, base):
        total = None
        for a in range(3):
            term = dot(source[pl.ds(base + a * 128, chunk * 128)], weight[a])
            total = term if total is None else total + term
        return total

    def conv_loop(piece, target):
        def step(i, kept):
            base = pl.multiple_of(i * (chunk * 128), 128)
            total = piece(base)
            target[pl.ds(base + 128, chunk * 128)] = total
            return kept[0] + fold(total), kept[1] + fold(total * total)

        return lax.fori_loop(0, rows // chunk, step, (zero, zero))


    def first_piece(base):
        total = conv_piece(ref.x1, w1, base)
        for a in range(3):
            total = total + dot_tn(ref.lowx[:, pl.ds(base + a * 128, chunk * 128)], ref.w1low[a])
        return total

    total, square = conv_loop(first_piece, dec1)
    put_pair(pair.at[1], core, row_of(total), row_of(square))
    dec1_copies = fine_halo(2, dec1)
    swaps[1].start()
    total, square = get_pair(swaps[1].finish())
    for copy in dec1_copies:
        copy.wait()
    first_average, first_inverse = moments(total, square, fine_samples)

    def first_parts(base):
        normed = (dec1[pl.ds(base, 128)] - first_average) * first_inverse
        return normed, gain(6) * normed + shift(6)

    def first_row(i, base, kept):
        put_three(ref.x2, base, gelu(first_parts(base)[1]) * inside(i))
        return kept

    each_row(first_row, 0, rows + 2, 0)
    spread[2].finish()
    place_conv(w2, small + large)
    total, square = conv_loop(lambda base: conv_piece(ref.x2, w2, base), dec2)
    put_pair(pair.at[2], core, row_of(total), row_of(square))
    dec2_copies = fine_halo(3, dec2)
    swaps[2].start()
    total, square = get_pair(swaps[2].finish())
    for copy in dec2_copies:
        copy.wait()
    second_average, second_inverse = moments(total, square, fine_samples)

    cls_t = ref.cls_t[...]
    bias = spread_row(columns[2:3])[0:32]
    col_here = ref.offsets[0, 1] + 4 * lax.broadcasted_iota(jnp.int32, (1, 128), 1) < SCENE_W
    col_mask = jnp.where(col_here, 1.0, 0.0)

    def scene_mask(i):
        row_here = ref.offsets[0, 0] + 4 * (me * rows + i - 1) < SCENE_H
        return col_mask * jnp.where(row_here, 1.0, 0.0)

    def masked_row(i, base):
        return ref.dlog[:, pl.ds(base, 128)] * scene_mask(i).astype(bf16)

    def second_parts(base):
        normed = (dec2[pl.ds(base, 128)] - second_average) * second_inverse
        return normed, gain(7) * normed + shift(7)

    def second_row(i, base, kept):
        normed, before = second_parts(base)
        ref.second[pl.ds(base, 128)] = gelu(before).astype(bf16)
        masked = masked_row(i, base)
        ref.dmask[:, pl.ds(base, 128)] = masked
        grad = dot_tn(masked, cls_t)
        push = gelu_slope(before) * grad
        pushed[pl.ds(base, 128)] = push
        own_row = jnp.where(jnp.logical_and(i > 0, i < rows + 1), 1.0, 0.0)
        push = push * own_row
        return kept[0] + fold(push * normed), kept[1] + fold(push)

    along, summed = each_row(second_row, 0, rows + 2, (zero, zero))
    put_pair(pair.at[3], core, row_of(along), row_of(summed))
    swaps[3].start()
    second = ref.second

    def logit_row(i, base, kept):
        out = pl.multiple_of(base - 128, 128)
        value = dot_nt(cls_t, second[pl.ds(base, 128)]) + bias
        ref.logits[:, pl.ds(out, 128)] = value * scene_mask(i)
        return kept

    each_row(logit_row, 1, rows + 1, 0)
    flip[pl.ds(9 * low_width, 32)] = dot(
        ref.dmask[:, 128 : 128 + fine_cells], second[pl.ds(128, fine_cells)]
    )
    bias_grad = jnp.zeros((32, 128), f32)
    for i in range(1, rows + 1):
        bias_grad = bias_grad + ref.dmask[:, i * 128 : (i + 1) * 128].astype(f32)
    wide_pair[1, core, 16:17, 0:32] = row_of(bias_grad.T)
    second_along, second_summed = get_pair(swaps[3].finish())

    def pull(push, normed, k, inverse, along, summed, count):
        return (gain(k) * inverse) * (push - summed * (1.0 / count) - normed * (along * (1.0 / count)))

    def dec2_row(i, base, kept):
        g = pull(
            pushed[pl.ds(base, 128)], second_parts(base)[0], 7, second_inverse,
            second_along, second_summed, fine_samples,
        )
        put_three(ref.g2, base, g * inside(i))
        return kept

    each_row(dec2_row, 0, rows + 2, 0)

    def back_loop(source, weight, use, carry):
        def step(i, kept):
            base = pl.multiple_of(i * (chunk * 128), 128)
            total = None
            for t in range(9):
                a, e = t // 3, t % 3
                piece = source[pl.ds(base + (2 - a) * 128, chunk * 128), (2 - e) * c : (3 - e) * c]
                term = dot_nt(piece, weight[a, e * c : (e + 1) * c])
                total = term if total is None else total + term
            return use(base, total, kept)

        return lax.fori_loop(0, rows // chunk, step, carry)

    def first_use(base, grad, kept):
        at = pl.ds(pl.multiple_of(base + 128, 128), chunk * 128)
        normed = (dec1[at] - first_average) * first_inverse
        push = gelu_slope(gain(6) * normed + shift(6)) * grad
        pushed1[at] = push
        return kept[0] + fold(push * normed), kept[1] + fold(push)

    along, summed = back_loop(ref.g2, ref.w2, first_use, (zero, zero))
    put_pair(pair.at[4], core, row_of(along), row_of(summed))
    pushed_copies = fine_halo(4, pushed1)
    swaps[4].start()

    wgrads = ref.wgrads

    reduce_two = Reduce(
        crops, n, front, ref.own_w, ref.r_first, ref.r_pairs, ref.r_crossed, ref.r_halves, ref.r_lined, ref.r_out
    )

    def weight_grads(target, source, gradient):
        for a in range(3):
            part = dot_tn(
                source[pl.ds(a * 128, fine_cells), c : 2 * c], gradient[pl.ds(128, fine_cells)]
            ).astype(bf16)
            for e in range(3):
                tap = part[:, (2 - e) * c : (3 - e) * c]
                for h in range(n):
                    target[h, 3 * a + e] = tap[h * own : (h + 1) * own]

    weight_grads(ref.own_w, ref.x2, ref.g2)
    for t in range(9, large):
        for h in range(n):
            ref.own_w[h, t] = jnp.zeros((own, c), bf16)
    reduce_two.cores()
    first_along, first_summed = get_pair(swaps[4].finish())
    reduce_two.over_the_crops()
    for copy in pushed_copies:
        copy.wait()

    def dec1_row(i, base, kept):
        g = pull(
            pushed1[pl.ds(base, 128)], first_parts(base)[0], 6, first_inverse,
            first_along, first_summed, fine_samples,
        ) * inside(i)
        put_three(ref.g1, base, g)
        return kept

    each_row(dec1_row, 0, rows + 2, 0)

    def up_use(base, grad, kept):
        dec2[pl.ds(pl.multiple_of(base + 128, 128), chunk * 128)] = grad
        return kept

    back_loop(ref.g1, ref.w1, up_use, 0)
    yt = ref.yt

    def low_back_row(i, local, base, kept):
        total = None
        for t in range(9):
            a, e = t // 3, t % 3
            at = pl.ds((local + 2 - a) * 128, 128)
            piece = yt[t * low_width : (t + 1) * low_width, at]
            if e == 0:
                piece = jnp.where(lane == 127, 0.0, pltpu.roll(piece, 127, 1))
            if e == 2:
                piece = jnp.where(lane == 0, 0.0, pltpu.roll(piece, 1, 1))
            total = piece if total is None else total + piece
        normed, before = low_parts(base)
        push = gelu_slope(before) * total
        ref.low_push[:, pl.ds(pl.multiple_of(base - 128, 128), 128)] = push
        return kept[0] + push * normed, kept[1] + push

    def low_back_chunk(i, kept):
        base = pl.multiple_of(i * (chunk * 128), 128)
        here = ref.g1[pl.ds(base, (chunk + 2) * 128), c : 2 * c]
        for a in range(3):
            yt[a * 3 * low_width : (a + 1) * 3 * low_width] = dot_nt(ref.w1low[a], here)
        for local in range(chunk):
            kept = low_back_row(i, local, pl.multiple_of(base + (local + 1) * 128, 128), kept)
        return kept

    low_along, low_summed = lax.fori_loop(0, rows // chunk, low_back_chunk, (low_zero, low_zero))

    part = ref.merged_part
    fine_at = lax.broadcasted_iota(jnp.int32, (FA, 128), 1).astype(f32)
    coarse_at = lax.broadcasted_iota(jnp.int32, (FA, 128), 0).astype(f32)
    place = jnp.clip((fine_at + 0.5) / 4.0 - 0.5, 0.0, FA - 1.0)
    up_t = jnp.maximum(0.0, 1.0 - jnp.abs(place - coarse_at)).astype(bf16)
    row_sums = [None] * (coarse_rows + 2)
    for i in range(rows):
        lower, a, b = up_weights(i, me, n, rows, coarse_rows)
        grad = dec2[pl.ds((i + 1) * 128, 128)]
        for j, weight in ((lower, a), (lower + 1, b)):
            row_sums[j] = weight * grad if row_sums[j] is None else row_sums[j] + weight * grad
    along, summed = zero, zero
    for j in range(coarse_rows + 2):
        grad = dot_exact(up_t, row_sums[j])
        part[pl.ds(j * FA, FA)] = grad
        normed, before = merged_parts(j * FA, FA)
        push = gelu_slope(before) * grad
        along, summed = along + fold(push * normed), summed + fold(push)
    put_pair(pair.at[5], core, row_of(along), row_of(summed))
    pair[5, core, 4:5, 0:low_width] = lanes_of(low_along)
    pair[5, core, 5:6, 0:low_width] = lanes_of(low_summed)
    part_copies = halo(
        5,
        part.at[pl.ds(0, FA)],
        part.at[pl.ds(FA + coarse_cells, FA)],
        part.at[pl.ds((coarse_rows + 3) * FA, FA)],
        part.at[pl.ds((coarse_rows + 2) * FA, FA)],
    )
    swaps[5].start()
    reduce_two.over_the_chips()
    weight_grads(wgrads, ref.x1, ref.g1)
    total_g = swaps[5].finish()
    for copy in part_copies:
        copy.wait()
    merged_along, merged_summed = get_pair(total_g)
    low_along, low_summed = spread_row(total_g[4:5])[0:low_width], spread_row(total_g[5:6])[0:low_width]
    ref.low_gain_grad[...] = total_g[4:5, 0:low_width]
    ref.low_shift_grad[...] = total_g[5:6, 0:low_width]

    up_here = jnp.where(me == 0, 0.0, 1.0)
    down_here = jnp.where(me == n - 1, 0.0, 1.0)
    proj_bf = ref.proj_bf
    for j in range(1, coarse_rows + 1):
        grad = part[pl.ds(j * FA, FA)]
        if j == 1:
            grad = grad + up_here * part[pl.ds((coarse_rows + 2) * FA, FA)]
        if j == coarse_rows:
            grad = grad + down_here * part[pl.ds((coarse_rows + 3) * FA, FA)]
        normed, before = merged_parts(j * FA, FA)
        push = gelu_slope(before) * grad
        g = pull(push, normed, 5, merged_inverse, merged_along, merged_summed, coarse_samples)
        proj_bf[pl.ds((j - 1) * FA, FA)] = g.astype(bf16)

    push_all = []
    for k in range(4):
        normed, before, _ = branch_parts(k)
        push = gelu_slope(before) * dot_nt(proj_bf[...], ref.proj[k])
        push_all.append(push)
        wide_pair[1, core, k : k + 1] = row_of(push * normed)
        wide_pair[1, core, 4 + k : 5 + k] = row_of(push)
    proj_row = row_of(proj_bf[...].astype(f32))
    wide_pair[1, core, 8:16] = jnp.where(
        lax.broadcasted_iota(jnp.int32, (8, c), 0) == my_crop, proj_row, 0.0
    )
    total_h = wides[1].run(reduce_two.to_all_crops)
    for k in range(4):
        normed, _, inverse = branch_parts(k)
        g = pull(
            push_all[k], normed, k, inverse, total_h[k : k + 1], total_h[4 + k : 5 + k], coarse_samples
        )
        ref.branch_out[:, k * c : (k + 1) * c] = g.astype(bf16)

    sums = total_h[8:16]
    sums_high = sums.astype(bf16).astype(f32)
    sums_low = sums - sums_high
    spare = jnp.concatenate([sums_high, sums_low], axis=0)
    spare_mid = spare.astype(bf16)
    spare_rest = (spare - spare_mid.astype(f32)).astype(bf16)
    pieces = dot_nt(spare_mid, ref.proj[4]) + dot_nt(spare_rest, ref.proj[4])
    pool_push = gelu_slope(pool_before) * (pieces[0:8] + pieces[8:16])
    pool_push = jnp.where(pool_here, pool_push, 0.0)
    pool_along, pool_summed = row_of(pool_push * pool_normed), row_of(pool_push)
    pool_grad = pull(pool_push, pool_normed, 4, pool_inverse, pool_along, pool_summed, crops)
    pool_grad = jnp.where(pool_here, pool_grad, 0.0)
    ref.pool_out[...] = jnp.concatenate([pool_grad, jnp.zeros((8, c), f32)], axis=0).astype(bf16)

    gain_rows = [total_h[0:4], pool_along, merged_along, first_along, second_along]
    shift_rows = [total_h[4:8], pool_summed, merged_summed, first_summed, second_summed]
    turn = c - me * own
    ref.gain_grad[...] = pltpu.roll(jnp.concatenate(gain_rows, axis=0), turn, 1)[:, 0:own]
    ref.shift_grad[...] = pltpu.roll(jnp.concatenate(shift_rows, axis=0), turn, 1)[:, 0:own]
    ref.bias_grad[...] = total_h[16:17, 0:classes]
    pool_rows = jnp.zeros((c, c), f32)
    rest = jnp.concatenate([sums, jnp.zeros((8, c), f32)], axis=0)
    for _ in range(3):
        high = rest.astype(bf16)
        pool_rows = pool_rows + dot_tn(pool_bf, high)
        rest = rest - high.astype(f32)
    dec1[pl.ds(0, c)] = pool_rows
    ref.pool_proj[...] = dec1[pl.ds(pl.multiple_of(me * own, own), own)]

    def low_out_row(i, base, kept):
        at = pl.ds(pl.multiple_of(base - 128, 128), 128)
        normed = low_parts(base)[0]
        g = (low_gain * low_inverse) * (
            ref.low_push[:, at] - low_summed * (1.0 / fine_samples) - normed * (low_along * (1.0 / fine_samples))
        )
        ref.low_out[:, at] = g.astype(bf16)
        return kept

    each_row(low_out_row, 1, rows + 1, 0)

    for a in range(3):
        flip[pl.ds(a * 3 * low_width, 3 * low_width)] = dot(
            ref.lowx[:, a * 128 : a * 128 + fine_cells], ref.g1[pl.ds(128, fine_cells), c : 2 * c]
        )
    flip[pl.ds(9 * low_width + 32, 48)] = jnp.zeros((48, c), f32)
    turned = flip[...].T.astype(bf16)
    for k in range(4):
        product = dot_tn(ref.branch_bf[:, k * c : (k + 1) * c], proj_bf[...]).astype(bf16)
        for h in range(n):
            rows_h = product[h * own : (h + 1) * own]
            wgrads[h, 9 + k] = rows_h
    for h in range(n):
        wgrads[h, 13] = turned[h * own : (h + 1) * own, 0:c]
        wgrads[h, 14] = turned[h * own : (h + 1) * own, c : 2 * c]
        for k in range(15, wgrads.shape[1]):
            wgrads[h, k] = jnp.zeros((own, c), bf16)
    reduce_two.finish()
    for t in range(9):
        ref.dec2_w[t] = ref.r_out[t].astype(f32)
    for copy in feature_copies:
        copy.wait_recv()
    front.drain(waited)


def decoder(crops, n, samples, *args):
    ref = DecoderRefs(*args, *([None] * (len(DecoderRefs._fields) - len(args))))
    c_in, c = ref.point.shape
    low_width = ref.low_w.shape[1]
    classes = ref.w_cls.shape[1]
    rows = ref.dlog.shape[1] // 128 - 2
    cells = rows * 128
    coarse = FA * FA // n
    own = c // n
    small, large = weight_groups(crops)
    chips = n // 2
    all_chips = crops * chips
    outer = (rows + 2) * 128
    chunk = min(4, rows)
    count = (crops - 1) + 4 * (2 * chips - 1) + 2 * chips - 1
    count += 2 * chips - 1 + 3 * (1 + 2 * crops * (chips - 1)) + reduce_copies(crops, n)
    S = jax.ShapeDtypeStruct
    V = pltpu.VMEM
    D = pltpu.SemaphoreType.DMA
    vmem = pl.BlockSpec(memory_space=pltpu.VMEM)
    return pl.pallas_call(
        functools.partial(decoder_kernel, crops, n, samples),
        out_shape=[
            S((32, cells), f32),
            S((coarse, 4 * c), bf16),
            S((16, c), bf16),
            S((low_width, cells), bf16),
            S((8, own), f32),
            S((8, own), f32),
            S((1, classes), f32),
            S((1, low_width), f32),
            S((1, low_width), f32),
            S((own, c), f32),
            S((9, own, c), f32),
            S((n, rest_groups(crops), own, c), bf16),
            S((crops, FA * FA, c_in), bf16),
        ],
        in_specs=[pl.BlockSpec(memory_space=pltpu.SMEM)] + [vmem] * (len(args) - 1),
        out_specs=[vmem] * 13,
        scratch_shapes=[
            V((low_width, outer), f32),
            V((low_width, cells), f32),
            V((3 * low_width, outer), bf16),
            V((coarse + 2 * FA, c), f32),
            V((coarse + 4 * FA, c), f32),
            V((outer, c), f32),
            V((outer, c), f32),
            V((max(outer, 4 * FA * FA), c), f32),
            V((max(outer, 2 * FA * FA), c), f32),
            V((outer, 3 * c), bf16),
            V((outer, 3 * c), bf16),
            V((max(outer, FA * FA), 3 * c), bf16),
            V((outer, 3 * c), bf16),
            V((9 * low_width, (chunk + 2) * 128), f32),
            V((coarse, 4 * c), bf16),
            V((coarse, c), bf16),
            V((outer, c), bf16),
            V((512, c), f32),
            V((coarse, 4 * c), f32),
            V((4, chips, coarse, c), bf16),
            V((4, chips, coarse, c), bf16),
            V((chips, low_width, cells), f32),
            V((chips, low_width, cells), f32),
            V((chips, low_width, cells), bf16),
            V((chips, low_width, cells), bf16),
            V((n, small + 2 * large, own, c), bf16),
            V((n, 16, 128), f32),
            V((16, c), f32),
            V((5, c, c), bf16),
            V((3, 3 * c, c), bf16),
            V((c, 2 * c), bf16),
            V((3, 3 * low_width, c), bf16),
            V((3, 3 * c, c), bf16),
            V((c, 128), bf16),
            V((32, c), bf16),
            V((32, outer), bf16),
            V((8, 128), f32),
            V((n, large, own, c), bf16),
            *reduce_scratch(crops, n, large, own, c),
            D((count,)),
            D((count,)),
            V((2, 2, 24, c), f32),
            V((2, crops, 24, c), f32),
            V((2, chips, 24, c), f32),
            D((2, 2)),
            D((2, crops + chips)),
            D((2, crops + chips)),
            V((7, 2, 8, 128), f32),
            V((7, all_chips, 8, 128), f32),
            D((7, 2)),
            D((2, all_chips)),
            D((7, all_chips)),
            D((6, 2)),
            D((6, 2)),
        ],
        compiler_params=pltpu.CompilerParams(
            collective_id=0, has_side_effects=True, vmem_limit_bytes=62 * 1024 * 1024
        ),
    )(*args)


class Reduce:
    def __init__(self, crops, n, copies, source, first, pairs, crossed, halves, lined, out):
        my_crop, me = lax.axis_index("crop"), lax.axis_index("chan")
        self.crops, self.chips, self.copies = crops, n // 2, copies
        self.crop, self.core, self.chip = my_crop, lax.rem(me, 2), lax.div(me, 2)
        self.other = (my_crop, me + 1 - 2 * self.core)
        self.over_crops = [(lax.rem(my_crop + i, crops), me) for i in range(1, crops)]
        self.over_chips = [(my_crop, lax.rem(me + 2 * j, n)) for j in range(1, n // 2)]
        self.source, self.first, self.pairs, self.crossed = source, first, pairs, crossed
        self.halves, self.lined, self.out = halves, lined, out
        self.size = source.shape[1]
        self.share = self.size // crops

    def wait(self):
        for copy in self.moving:
            copy.wait_recv()

    def cores(self):
        self.moving = []
        for z in range(self.chips):
            block = self.source.at[2 * z + 1 - self.core]
            self.moving.append(self.copies.start(block, self.first.at[z], self.other))

    def over_the_crops(self):
        self.wait()
        for z in range(self.chips):
            for g in range(self.size):
                both = self.source[2 * z + self.core, g].astype(f32) + self.first[z, g].astype(f32)
                self.pairs[z, g] = both.astype(bf16)
        self.moving = []
        for i in range(1, self.crops):
            target = lax.rem(self.crop + i, self.crops)
            block = self.pairs.at[:, pl.ds(target * self.share, self.share)]
            self.moving.append(
                self.copies.start(block, self.crossed.at[self.crop], self.over_crops[i - 1])
            )
        for z in range(self.chips):
            for g in range(self.share):
                self.crossed[self.crop, z, g] = self.pairs[z, self.crop * self.share + g]

    def over_the_chips(self):
        self.wait()
        for z in range(self.chips):
            for g in range(self.share):
                value = self.crossed[0, z, g].astype(f32)
                for i in range(1, self.crops):
                    value = value + self.crossed[i, z, g].astype(f32)
                self.halves[z, g] = value.astype(bf16)
        self.moving = []
        for j in range(1, self.chips):
            target = lax.rem(self.chip + j, self.chips)
            self.moving.append(
                self.copies.start(
                    self.halves.at[target], self.lined.at[self.chip], self.over_chips[j - 1]
                )
            )
        for g in range(self.share):
            self.lined[self.chip, g] = self.halves[self.chip, g]

    def to_all_crops(self):
        self.wait()
        for g in range(self.share):
            value = self.lined[0, g].astype(f32)
            for z in range(1, self.chips):
                value = value + self.lined[z, g].astype(f32)
            self.out[self.crop * self.share + g] = value.astype(bf16)
        here = self.out.at[pl.ds(self.crop * self.share, self.share)]
        self.moving = [self.copies.start(here, here, peer) for peer in self.over_crops]

    def finish(self):
        self.wait()


def reduce_scratch(crops, n, size, own, c):
    chips, share = n // 2, size // crops
    V = pltpu.VMEM
    return [
        V((chips, size, own, c), bf16),
        V((chips, size, own, c), bf16),
        V((crops, chips, share, own, c), bf16),
        V((chips, share, own, c), bf16),
        V((chips, share, own, c), bf16),
        V((size, own, c), bf16),
    ]


def reduce_copies(crops, n):
    return 2 * (n // 2) - 1 + 2 * (crops - 1)


class Gather:
    def __init__(self, n, send, recv):
        my_crop, self.me = lax.axis_index("crop"), lax.axis_index("chan")
        self.n, self.chips = n, n // 2
        self.core = lax.rem(self.me, 2)
        self.other = (my_crop, self.me + 1 - 2 * self.core)
        self.send, self.recv = send, recv
        self.peer = lambda j: (my_crop, lax.rem(self.me + 2 * j, n))

    def block(self, j):
        return lax.rem(self.me - 2 * j + self.n, self.n)

    def other_block(self, j):
        return lax.rem(self.me + 1 - 2 * self.core - 2 * j + self.n, self.n)

    def start(self, at):
        self.at = at
        self.far, self.pairs = [], []
        for j in range(1, self.chips):
            here = at(self.me)
            self.far.append(remote(here, here, self.send.at[j], self.recv.at[j], self.peer(j)))
            self.far[-1].start()
        self.forward(0)

    def forward(self, j):
        here = self.at(self.block(j))
        k = self.chips + j
        self.pairs.append(remote(here, here, self.send.at[k], self.recv.at[k], self.other))
        self.pairs[-1].start()

    def arrive(self, j):
        self.far[j - 1].wait_recv()
        self.forward(j)

    def finish(self):
        for copy in self.pairs:
            copy.wait_recv()

    def drain(self):
        for copy in self.far + self.pairs:
            copy.wait_send()


class BackRefs(typing.NamedTuple):
    grad: object
    src: object
    point: object
    atrous: object
    pool: object
    pooled_grad: object
    low_grad: object
    low_in: object
    wgrads: object
    features: object
    point_w: object
    atrous_w: object
    pool_w: object
    low_w_out: object
    blocks: object
    low_full: object
    last_grad: object
    last_src: object
    all_grad: object
    shifted: object
    turned: object
    total: object
    r_first: object
    r_pairs: object
    r_crossed: object
    r_halves: object
    r_lined: object
    r_out: object
    low_parts: object
    g_send: object
    g_recv: object
    l_send: object
    l_recv: object
    c_send: object
    c_recv: object


def back_kernel(crops, n, *refs):
    ref = BackRefs(*refs)
    my_crop, me = lax.axis_index("crop"), lax.axis_index("chan")
    chips = n // 2
    core, chip = lax.rem(me, 2), lax.div(me, 2)
    block, width = ref.grad.shape
    c = width // 4
    half = width // 2
    c_in = ref.src.shape[2]
    cells = FA * FA
    relay = crops == 4
    other = (my_crop, me + 1 - 2 * core)
    over_crops = [(lax.rem(my_crop + i, crops), me) for i in range(1, crops)]
    over_chips = [(my_crop, lax.rem(me + 2 * j, n)) for j in range(1, chips)]
    wait_barrier = barrier_with([other] + over_crops + over_chips)
    all_grad, src = ref.all_grad, ref.src
    if relay:
        along_x = my_crop + 1 - 2 * lax.rem(my_crop, 2)
        along_y = my_crop + 2 - 4 * lax.div(my_crop, 2)
        crop_list = [my_crop, along_x, along_y, 3 - my_crop]
    else:
        crop_list = [my_crop] + [lax.rem(my_crop - i + crops, crops) for i in range(1, crops)]

    def grad_at(crop):
        def at(b):
            return all_grad.at[crop, pl.ds(pl.multiple_of(b * block, block), block)]

        return at

    def lanes_at(crop, b, first):
        return all_grad.at[crop, pl.ds(pl.multiple_of(b * block, block), block), pl.ds(first, half)]

    all_grad[my_crop, pl.ds(pl.multiple_of(me * block, block), block)] = ref.grad[...]
    ref.low_full[me] = ref.low_grad[...]
    wait_barrier()

    gather = Gather(n, ref.g_send, ref.g_recv)
    gather.start(grad_at(my_crop))
    moves = Copies(ref.c_send, ref.c_recv)
    crossing = {}

    def cross(j):
        here = grad_at(my_crop)(gather.block(j))
        if relay:
            for i, crop in ((1, along_x), (2, along_y)):
                crossing[i, j] = moves.start(here, here, (crop, me))
        else:
            for i in range(1, crops):
                crossing[i, j] = moves.start(here, here, over_crops[i - 1])

    core_copies = {}

    def pass_on(i, j):
        crossing[i, j].wait_recv()
        b = gather.block(j)
        crop = crop_list[i]
        if relay and i == 1:
            here = lanes_at(crop, b, 0)
            crossing[3, j, 0] = moves.start(here, here, (along_y, me))
        if relay and i == 2:
            here = lanes_at(crop, b, half)
            crossing[3, j, 1] = moves.start(here, here, (along_x, me))
        place = grad_at(crop)(b)
        core_copies[i, j] = moves.start(place, place, other)

    def pass_across(j):
        crossing[3, j, 0].wait_recv()
        crossing[3, j, 1].wait_recv()
        place = grad_at(crop_list[3])(gather.block(j))
        core_copies[3, j] = moves.start(place, place, other)

    cross(0)
    reduce = Reduce(
        crops, n, moves, ref.wgrads, ref.r_first, ref.r_pairs, ref.r_crossed, ref.r_halves, ref.r_lined, ref.r_out
    )
    reduce.cores()
    shifted = ref.shifted

    def shift_source(i):
        crop = crop_list[i]
        for k in range(3):
            rate = atrous_rates[k]
            shift_three(lambda base: src[crop, pl.ds(base, 128)], shifted.at[i % 3, k], rate, -rate, rate)

    shift_source(0)
    reduce.over_the_crops()
    for i in range(1, min(3, crops)):
        shift_source(i)
    for j in range(1, chips):
        gather.arrive(j)
        cross(j)
    reduce.over_the_chips()
    low_gather = Gather(n, ref.l_send, ref.l_recv)
    low_gather.start(lambda b: ref.low_full.at[b])
    if relay:
        pass_on(1, 0)
        pass_on(2, 0)
    gather.finish()

    total, turned = ref.total, ref.turned
    pool_row = dot_nt(ref.pooled_grad[...], ref.pool[...])
    my_row = lax.broadcasted_iota(jnp.int32, pool_row.shape, 0) == my_crop
    pool_row = row_of(jnp.where(my_row, pool_row, 0.0)) * (1.0 / cells)
    total[...] = dot_nt(all_grad[my_crop, :, 0:c], ref.point[...]) + pool_row
    for k in range(3):
        rate = atrous_rates[k]
        shift_three(
            lambda base: all_grad[my_crop, pl.ds(base, 128), (k + 1) * c : (k + 2) * c],
            turned, rate, rate, -rate,
        )
        for a in range(3):
            move = (a - 1) * rate
            count = (FA - abs(move)) * FA
            to, off = max(move, 0) * FA, max(-move, 0) * FA
            term = None
            for e in range(3):
                piece = dot_nt(turned[pl.ds(off, count), e * c : (e + 1) * c], ref.atrous[k, 3 * a + e])
                term = piece if term is None else term + piece
            total[pl.ds(to, count)] = total[pl.ds(to, count)] + term

    def weight_part(i):
        crop = crop_list[i]
        part = dot_tn(src[crop], all_grad[crop, :, 0:c])
        ref.point_w[...] = part if i == 0 else ref.point_w[...] + part
        for k in range(3):
            rate = atrous_rates[k]
            for a in range(3):
                move = (a - 1) * rate
                count = (FA - abs(move)) * FA
                from_src, off = max(move, 0) * FA, max(-move, 0) * FA
                part = dot_tn(
                    shifted[i % 3, k, pl.ds(from_src, count)],
                    all_grad[crop, pl.ds(off, count), (k + 1) * c : (k + 2) * c],
                )
                for e in range(3):
                    piece = part[e * c_in : (e + 1) * c_in]
                    if i > 0:
                        piece = ref.atrous_w[k, 3 * a + e] + piece
                    ref.atrous_w[k, 3 * a + e] = piece

    weight_part(0)
    ref.features[...] = total[...].T
    if relay:
        for j in range(1, chips):
            pass_on(1, j)
            pass_on(2, j)

    def low_part():
        for j in range(1, chips):
            low_gather.arrive(j)
        low_gather.finish()
        rows = ref.low_full.shape[2] // 128
        low_in, low_all = ref.low_in, ref.low_full
        low_total = None
        for b in range(n):
            here = low_all[b]
            span = slice(b * rows * 128, (b + 1) * rows * 128)
            part = dot_nt(low_in[:, span], here)
            low_total = part if low_total is None else low_total + part
        low_parts = ref.low_parts
        low_parts[my_crop] = jnp.zeros(low_parts.shape[1:], f32)
        low_parts[my_crop, :, 0 : low_total.shape[1]] = low_total
        here = low_parts.at[my_crop]
        low_copies = [moves.start(here, here, peer) for peer in over_crops]
        return low_copies

    for i in range(1, crops):
        if i + 2 < crops - 1:
            shift_source(i + 2)
        for j in range(chips):
            if not relay:
                pass_on(i, j)
            elif i == 3:
                pass_across(j)
        for j in range(chips):
            core_copies[i, j].wait_recv()
        if i < crops - 1:
            weight_part(i)
        if i == min(2, crops - 1):
            reduce.to_all_crops()
            low_copies = low_part()

    ref.last_grad[...] = all_grad[crop_list[-1]]
    ref.last_src[...] = src[crop_list[-1]]
    pooled = []
    for i in range(crops):
        mean = row_of(src[i].astype(f32)) * (1.0 / cells)
        pooled.append(mean)
    pooled = jnp.concatenate(pooled + [jnp.zeros((16 - crops, c_in), f32)], axis=0).astype(bf16)
    ref.pool_w[...] = dot_tn(pooled, ref.pooled_grad[...])

    reduce.finish()
    for g in range(ref.blocks.shape[0]):
        ref.blocks[g] = ref.r_out[g].astype(f32)
    for copy in low_copies:
        copy.wait_recv()
    ref.low_w_out[...] = jnp.sum(ref.low_parts[...], axis=0)
    gather.drain()
    low_gather.drain()
    moves.drain([])


def pyramid_back(crops, n, *args):
    grad, src, low_grad, low_in, wgrads = args[0], args[1], args[6], args[7], args[8]
    block, width = grad.shape
    c = width // 4
    c_in = src.shape[2]
    chips = n // 2
    cells = FA * FA
    low_rows = low_in.shape[0]
    own, lanes = wgrads.shape[2:]
    S = jax.ShapeDtypeStruct
    V = pltpu.VMEM
    D = pltpu.SemaphoreType.DMA
    vmem = pl.BlockSpec(memory_space=pltpu.VMEM)
    count = 3 * crops * chips + crops - 1 + reduce_copies(crops, n)
    return pl.pallas_call(
        functools.partial(back_kernel, crops, n),
        out_shape=[
            S((c_in, cells), f32),
            S((c_in, c), f32),
            S((3, 9, c_in, c), f32),
            S((c_in, c), f32),
            S((low_rows, 128), f32),
            S((15, own, lanes), f32),
            S((n,) + low_grad.shape, bf16),
            S((cells, width), bf16),
            S((cells, c_in), bf16),
        ],
        in_specs=[vmem] * len(args),
        out_specs=[vmem] * 9,
        scratch_shapes=[
            V((crops, cells, width), bf16),
            V((min(3, crops), 3, cells, 3 * c_in), bf16),
            V((cells, 3 * c), bf16),
            V((cells, c_in), f32),
            *reduce_scratch(crops, n, wgrads.shape[1], own, lanes),
            V((crops, low_rows, 128), f32),
            D((n,)),
            D((n,)),
            D((n,)),
            D((n,)),
            D((count,)),
            D((count,)),
        ],
        compiler_params=pltpu.CompilerParams(
            collective_id=1, has_side_effects=True, vmem_limit_bytes=62 * 1024 * 1024
        ),
    )(*args)


class FinishRefs(typing.NamedTuple):
    atrous_part: object
    point_part: object
    last_grad: object
    last_src: object
    features_in: object
    pool_in: object
    low_full: object
    low_w: object
    low_w_part: object
    logits_in: object
    dec2_in: object
    blocks: object
    pool_proj: object
    bias_in: object
    gain_in: object
    shift_in: object
    low_gain_in: object
    low_shift_in: object
    logits: object
    features: object
    early: object
    point: object
    atrous: object
    pool: object
    proj: object
    low_w_out: object
    dec1: object
    side: object
    dec2: object
    cls: object
    bias: object
    gain: object
    shift: object
    low_gain: object
    low_shift: object
    turned: object


def finish_kernel(*refs):
    ref = FinishRefs(*refs)
    step = pl.program_id(0)
    c_in, c = ref.point_part.shape
    cells = FA * FA
    classes, rows = ref.logits.shape[0], ref.logits.shape[1]
    low_width = ref.low_gain.shape[1]
    own = ref.cls.shape[0]

    def branch(k):
        rate = atrous_rates[k]
        shift_three(lambda base: ref.last_src[pl.ds(base, 128)], ref.turned, rate, -rate, rate)
        for a in range(3):
            move = (a - 1) * rate
            count = (FA - abs(move)) * FA
            from_src, off = max(move, 0) * FA, max(-move, 0) * FA
            part = dot_tn(
                ref.turned[pl.ds(from_src, count)],
                ref.last_grad[pl.ds(off, count), (k + 1) * c : (k + 2) * c],
            )
            for e in range(3):
                t = 3 * a + e
                ref.atrous[0, t] = ref.atrous_part[0, t] + part[e * c_in : (e + 1) * c_in]

    def low_features():
        for b in range(ref.low_full.shape[0]):
            value = dot(ref.low_w[...], ref.low_full[b])
            ref.early[:, b * rows : (b + 1) * rows] = value.reshape(value.shape[0], rows, 128)
        ref.low_w_out[...] = ref.low_w_part[:, 0:low_width]

    def small():
        ref.point[...] = ref.point_part[...] + dot_tn(ref.last_src[...], ref.last_grad[:, 0:c])
        ref.pool[...] = ref.pool_in[...]
        ref.logits[...] = ref.logits_in[0:classes].reshape(classes, rows, 128)
        ref.dec2[...] = ref.dec2_in[...]
        for t in range(9):
            ref.dec1[t] = ref.blocks[t]
        for k in range(4):
            ref.proj[k] = ref.blocks[9 + k]
        ref.proj[4] = ref.pool_proj[...]
        tail = jnp.concatenate([ref.blocks[13], ref.blocks[14]], axis=1)
        wide = jnp.concatenate([tail, jnp.zeros((128 - own, 2 * c), f32)], axis=0).T
        for t in range(9):
            ref.side[t] = wide[t * low_width : (t + 1) * low_width, 0:own]
        first = 9 * low_width // 128 * 128
        ref.cls[...] = pltpu.roll(tail[:, first : first + 128], first + 128 - 9 * low_width, 1)[:, 0:classes]
        ref.bias[...] = ref.bias_in[...]
        ref.gain[...] = ref.gain_in[...]
        ref.shift[...] = ref.shift_in[...]
        ref.low_gain[...] = ref.low_gain_in[...]
        ref.low_shift[...] = ref.low_shift_in[...]

    def first():
        branch(0)
        ref.features[...] = ref.features_in[...]

    def second():
        branch(1)
        low_features()

    def third():
        branch(2)
        small()

    for k, body in enumerate((first, second, third)):
        pl.when(step == k)(body)


def finish(shapes, *args):
    parts = FinishRefs(*args, *([None] * (len(FinishRefs._fields) - len(args))))
    c_in, c = parts.point_part.shape
    whole = lambda v: pl.BlockSpec(v.shape, lambda k, r=len(v.shape): (0,) * r)
    piece = pl.BlockSpec((1, 9, c_in, c), lambda k: (k, 0, 0, 0))
    outs = [jax.ShapeDtypeStruct(shape, f32) for shape in shapes]
    return pl.pallas_call(
        finish_kernel,
        grid=(3,),
        out_shape=outs,
        in_specs=[piece] + [whole(v) for v in args[1:]],
        out_specs=[piece if v.shape == args[0].shape else whole(v) for v in outs],
        scratch_shapes=[pltpu.VMEM((FA * FA, 3 * c_in), bf16)],
        compiler_params=pltpu.CompilerParams(vmem_limit_bytes=60 * 1024 * 1024),
    )(*args)


def per_device(
    features,
    low_in,
    offsets,
    d_logits,
    w_point,
    w_atrous,
    w_pool,
    w_proj,
    w_low,
    w_dec1,
    w_dec1_low,
    w_dec2,
    w_cls,
    b_cls,
    bn_gain,
    bn_shift,
    low_gain,
    low_shift,
):
    n = lax.axis_size("chan")
    crops = lax.axis_size("crop")
    me = lax.axis_index("chan")
    fine = low_in.shape[2]
    rows = fine // n
    coarse_rows = FA // n
    channels = w_dec2.shape[2]
    c_in = features.shape[1]
    low_width = w_low.shape[1]
    coarse_samples = FA * FA * crops
    fine_samples = fine * fine * crops

    classes = w_cls.shape[1]
    spare = 32 - classes
    outer_grad = jnp.pad(d_logits[0], ((0, spare), (1, 1), (0, 0)))
    outer_grad = lax.dynamic_slice_in_dim(outer_grad, me * rows, rows + 2, 1)
    low_flat = low_in[0].reshape(low_in.shape[1], fine * fine)
    (
        logits, branch_grad, pool_grad, low_pre_bf, gain_grad, shift_grad, bias_grad,
        low_gain_grad, low_shift_grad, pool_proj, dec2_wgrad, blocks, source_all,
    ) = decoder(
        crops,
        n,
        (coarse_samples, fine_samples),
        offsets,
        features[0],
        w_point,
        w_atrous.reshape(3, 3, 3 * c_in, channels),
        w_pool,
        low_flat,
        w_low,
        w_proj,
        w_dec1,
        w_dec1_low.reshape(9 * low_width, -1),
        w_dec2,
        w_cls,
        bn_gain,
        bn_shift,
        low_gain[None],
        low_shift[None],
        b_cls[None],
        outer_grad.reshape(32, (rows + 2) * fine),
    )
    feature_grad, point_wgrad, atrous_wgrad, pool_wgrad, low_wgrad, blocks, low_full, last_grad, last_src = (
        pyramid_back(
            crops,
            n,
            branch_grad,
            source_all,
            w_point,
            w_atrous,
            w_pool,
            pool_grad,
            low_pre_bf,
            low_flat,
            blocks,
        )
    )
    own = w_dec2.shape[1]
    shapes = [
        (classes, rows, fine),
        (c_in, FA * FA),
        low_in.shape[1:],
        (c_in, channels),
        (3, 9, c_in, channels),
        (c_in, channels),
        (5, own, channels),
        (low_in.shape[1], low_width),
        (9, own, channels),
        (9, low_width, own),
        (9, own, channels),
        (own, classes),
        (1, classes),
        (8, own),
        (8, own),
        (1, low_width),
        (1, low_width),
    ]
    outs = finish(
        shapes,
        atrous_wgrad,
        point_wgrad,
        last_grad,
        last_src,
        feature_grad,
        pool_wgrad,
        low_full,
        w_low,
        low_wgrad,
        logits,
        dec2_wgrad,
        blocks,
        pool_proj,
        bias_grad,
        gain_grad,
        shift_grad,
        low_gain_grad,
        low_shift_grad,
    )
    outs = list(outs)
    for k in (0, 1, 2):
        outs[k] = outs[k][None]
    for k in (12, 15, 16):
        outs[k] = outs[k][0]
    return tuple(outs)


def solution(mesh):
    placed = (
        P("crop", "chan", None),
        P("crop", "chan", None, None),
        P("crop", None),
        P("crop", None, None, None),
        P("chan", None),
        P(None, None, "chan", None),
        P("chan", None),
        P(None, "chan", None),
        P("chan", None),
        P(None, "chan", None),
        P(None, None, "chan"),
        P(None, "chan", None),
        P("chan", None),
        P(),
        P(None, "chan"),
        P(None, "chan"),
        P(),
        P(),
    )
    return jax.shard_map(
        per_device,
        mesh=mesh,
        in_specs=placed,
        out_specs=(
            P("crop", None, "chan", None),
            P("crop", "chan", None),
            P("crop", "chan", None, None),
            P("chan", None),
            P(None, None, "chan", None),
            P("chan", None),
            P(None, "chan", None),
            P("chan", None),
            P(None, "chan", None),
            P(None, None, "chan"),
            P(None, "chan", None),
            P("chan", None),
            P(),
            P(None, "chan"),
            P(None, "chan"),
            P(),
            P(),
        ),
        check_vma=False,
    )
```

```python
import functools
import typing

import jax
import jax.numpy as jnp
from jax import lax
from jax.experimental import pallas as pl
from jax.experimental.pallas import tpu as pltpu
from jax.sharding import PartitionSpec as P

FA = 32
SCENE_H = 1024
SCENE_W = 2048

epsilon = 1e-05
highest = lax.Precision.HIGHEST
atrous_rates = (6, 12, 18)
f32 = jnp.float32
bf16 = jnp.bfloat16
BOTH = ("crop", "chan")


MESH = pl.DeviceIdType.MESH


def chip_peers(crops, n):
    my_crop, me = lax.axis_index("crop"), lax.axis_index("chan")
    core = lax.rem(me, 2)
    chips = n // 2
    other = (my_crop, me + 1 - 2 * core)
    far = []
    for i in range(crops):
        for j in range(chips):
            if i or j:
                far.append((lax.rem(my_crop + i, crops), lax.rem(me + 2 * j, n)))
    return other, far


GELU_A = 0.7978845608028654
GELU_B = 0.044715


def gelu(x):
    return 0.5 * x * (1.0 + jnp.tanh(GELU_A * (x + GELU_B * x * x * x)))


def gelu_both(x):
    square = x * x
    t = jnp.tanh(GELU_A * x * (1.0 + GELU_B * square))
    upper = 0.5 * (1.0 + t)
    return x * upper, upper + (0.5 * GELU_A) * x * (1.0 - t * t) * (1.0 + (3.0 * GELU_B) * square)


def gelu_slope(x):
    square = x * x
    t = jnp.tanh(GELU_A * x * (1.0 + GELU_B * square))
    return 0.5 * (1.0 + t) + (0.5 * GELU_A) * x * (1.0 - t * t) * (1.0 + (3.0 * GELU_B) * square)


def dot(a, b):
    return jnp.dot(a, b, preferred_element_type=f32)


def dot_nt(a, b):
    return lax.dot_general(a, b, (((1,), (1,)), ((), ())), preferred_element_type=f32)


def dot_tn(a, b):
    return lax.dot_general(a, b, (((0,), (0,)), ((), ())), preferred_element_type=f32)


def dot_exact(table, values):
    high = values.astype(bf16)
    rest = values - high.astype(f32)
    middle = rest.astype(bf16)
    low = (rest - middle.astype(f32)).astype(bf16)
    return dot(table, high) + (dot(table, middle) + dot(table, low))


def fold(values):
    return jnp.sum(values.reshape(values.shape[0] // 8, 8, values.shape[1]), axis=0)


def row_of(values):
    return jnp.sum(values, axis=0, keepdims=True)


def barrier_with(peers):
    barrier = pltpu.get_barrier_semaphore()
    for peer in peers:
        pl.semaphore_signal(barrier, inc=1, device_id=peer, device_id_type=MESH)
    return lambda: pl.semaphore_wait(barrier, len(peers))


def remote(src, dst, send, recv, peer):
    return pltpu.make_async_remote_copy(
        src_ref=src, dst_ref=dst, send_sem=send, recv_sem=recv, device_id=peer, device_id_type=MESH
    )


class Copies:
    def __init__(self, send, recv):
        self.send, self.recv, self.all = send, recv, []

    def start(self, src, dst, peer):
        k = len(self.all)
        copy = remote(src, dst, self.send.at[k], self.recv.at[k], peer)
        copy.start()
        self.all.append(copy)
        return copy

    def drain(self, kept):
        for copy in self.all:
            if not any(copy is other for other in kept):
                copy.wait_send()


def shift_three(source, target, rate, first, last):
    column = lax.rem(lax.broadcasted_iota(jnp.int32, (128, 1), 0), FA)

    def step(i, kept):
        base = pl.multiple_of(i * 128, 128)
        here = source(base)
        w = here.shape[1]
        wide = here.astype(f32)
        for slot, by in ((0, first), (2, last)):
            ok = jnp.logical_and(column + by >= 0, column + by < FA)
            moved = jnp.where(ok, pltpu.roll(wide, (-by) % 128, 0), 0.0)
            target[pl.ds(base, 128), slot * w : (slot + 1) * w] = moved.astype(bf16)
        target[pl.ds(base, 128), w : 2 * w] = here
        return kept

    lax.fori_loop(0, FA * FA // 128, step, 0)


class Swap:
    def __init__(self, crops, n, pair, slots, pair_sems, send, recv):
        self.other, self.far = chip_peers(crops, n)
        me = lax.axis_index("chan")
        self.core = lax.rem(me, 2)
        self.mine = lax.axis_index("crop") * (n // 2) + lax.div(me, 2)
        self.pair, self.slots, self.pair_sems = pair, slots, pair_sems
        self.send, self.recv = send, recv

    def start(self):
        here = self.pair.at[self.core]
        copy = remote(here, here, self.pair_sems.at[0], self.pair_sems.at[1], self.other)
        copy.start()
        copy.wait()
        self.slots[self.mine] = self.pair[0] + self.pair[1]
        self.copies = []
        for k, peer in enumerate(self.far):
            slot = self.slots.at[self.mine]
            copy = remote(slot, slot, self.send.at[k], self.recv.at[k], peer)
            copy.start()
            self.copies.append(copy)

    def finish(self):
        for copy in self.copies:
            copy.wait_recv()
        return jnp.sum(self.slots[...], axis=0)

    def drain(self):
        for copy in self.copies:
            copy.wait_send()


class WideSwap:
    def __init__(self, crops, n, pair, first, second, pair_sems, send, recv):
        my_crop, me = lax.axis_index("crop"), lax.axis_index("chan")
        self.core, self.crop, self.chip = lax.rem(me, 2), my_crop, lax.div(me, 2)
        self.other = (my_crop, me + 1 - 2 * self.core)
        self.over_crops = [(lax.rem(my_crop + i, crops), me) for i in range(1, crops)]
        self.over_chips = [(my_crop, lax.rem(me + 2 * j, n)) for j in range(1, n // 2)]
        self.pair, self.first, self.second = pair, first, second
        self.pair_sems, self.send, self.recv = pair_sems, send, recv

    def run(self, then=None):
        here = self.pair.at[self.core]
        copy = remote(here, here, self.pair_sems.at[0], self.pair_sems.at[1], self.other)
        copy.start()
        copy.wait()
        self.first[self.crop] = self.pair[0] + self.pair[1]
        k = 0
        copies = []
        for peer in self.over_crops:
            slot = self.first.at[self.crop]
            copies.append(remote(slot, slot, self.send.at[k], self.recv.at[k], peer))
            copies[-1].start()
            k += 1
        for copy in copies:
            copy.wait()
        self.second[self.chip] = jnp.sum(self.first[...], axis=0)
        copies = []
        for peer in self.over_chips:
            slot = self.second.at[self.chip]
            copies.append(remote(slot, slot, self.send.at[k], self.recv.at[k], peer))
            copies[-1].start()
            k += 1
        if then is not None:
            then()
        for copy in copies:
            copy.wait()
        return jnp.sum(self.second[...], axis=0)


def put_pair(ref, core, a, b):
    ref[core, 0:1] = a[:, :128]
    ref[core, 1:2] = a[:, 128:]
    ref[core, 2:3] = b[:, :128]
    ref[core, 3:4] = b[:, 128:]


def get_pair(total):
    return (
        jnp.concatenate([total[0:1], total[1:2]], axis=1),
        jnp.concatenate([total[2:3], total[3:4]], axis=1),
    )


def spread_row(row):
    return jnp.broadcast_to(row, (128, 128)).T


def up_weights(i, me, n, rows, coarse_rows):
    lower = (2 * i - 3) // 8
    upper_weight = (2 * i - 3 - 8 * lower) / 8.0
    a, b = 1.0 - upper_weight, upper_weight
    if lower < 0:
        top = me == 0
        a, b = jnp.where(top, 0.0, a), jnp.where(top, 1.0, b)
    if lower + 1 >= coarse_rows:
        bottom = me == n - 1
        a, b = jnp.where(bottom, 1.0, a), jnp.where(bottom, 0.0, b)
    if i < 0:
        a, b = jnp.where(me == 0, 0.0, a), jnp.where(me == 0, 0.0, b)
    if i >= rows:
        a, b = jnp.where(me == n - 1, 0.0, a), jnp.where(me == n - 1, 0.0, b)
    return lower + 1, a, b


class DecoderRefs(typing.NamedTuple):
    offsets: object
    feat: object
    point: object
    atrous_hbm: object
    pool_w: object
    low_in: object
    low_w: object
    w_proj: object
    w_dec1: object
    w_side: object
    w_dec2: object
    w_cls: object
    own_gain: object
    own_shift: object
    low_gain: object
    low_shift: object
    bias: object
    dlog: object
    logits_hbm: object
    branch_hbm: object
    low_hbm: object
    pack_hbm: object
    dec2_hbm: object
    wgrads_hbm: object
    src_all: object
    atrous: object
    src_own: object
    logits: object
    branch_out: object
    low_out: object
    pack: object
    dec2_w: object
    wgrads: object
    low_ext: object
    low_push: object
    lowx: object
    merged_ext: object
    merged_part: object
    dec1: object
    dec2: object
    pushed: object
    pushed1: object
    x1: object
    x2: object
    g2: object
    g1: object
    yt: object
    branch_bf: object
    proj_bf: object
    second: object
    flip: object
    branch: object
    staged: object
    arrived: object
    low_send: object
    low_pair: object
    low_sum: object
    low_recv: object
    gath: object
    norms_all: object
    norms: object
    proj: object
    w1: object
    tail: object
    w1low: object
    w2: object
    cls_all: object
    cls_t: object
    dmask: object
    columns: object
    own_w: object
    r_first: object
    r_pairs: object
    r_crossed: object
    r_halves: object
    r_lined: object
    r_out: object
    local: object
    f_send: object
    f_recv: object


def rest_groups(crops):
    return -(-15 // crops) * crops


def weight_groups(crops):
    return -(-8 // crops) * crops, -(-9 // crops) * crops


def decoder_kernel(crops, n, samples, *refs):
    ref = DecoderRefs(*refs[: len(DecoderRefs._fields)])
    rest = list(refs[len(DecoderRefs._fields) :])
    (wide_pair, wide_first, wide_second, wide_psem, wide_send, wide_recv) = rest[:6]
    (pair, slots, psem, send, recv, halo_send, halo_recv) = rest[6:13]

    coarse_samples, fine_samples = samples
    my_crop, me = lax.axis_index("crop"), lax.axis_index("chan")
    core = lax.rem(me, 2)
    above = (my_crop, lax.rem(me + n - 1, n))
    below = (my_crop, lax.rem(me + 1, n))
    low_chans, low_width = ref.low_w.shape
    classes = ref.w_cls.shape[0]
    rows = ref.dlog.shape[1] // 128 - 2
    fine_cells = rows * 128
    coarse_cells = ref.branch.shape[0]
    coarse_rows = coarse_cells // FA
    cells = FA * FA
    c_in, c = ref.point.shape
    own = c // n
    chips, chip = n // 2, lax.div(me, 2)
    small, large = weight_groups(crops)
    chunk = min(4, rows)

    other, far = chip_peers(crops, n)
    over_crops = [(lax.rem(my_crop + i, crops), me) for i in range(1, crops)]
    over_chips = [(my_crop, lax.rem(me + 2 * j, n)) for j in range(1, chips)]
    wait_barrier = barrier_with([other, above, below] + far)

    swaps = [
        Swap(crops, n, pair.at[i], slots.at[i], psem.at[i], send.at[0 if i == 6 else (i + 1) % 2], recv.at[i])
        for i in range(pair.shape[0])
    ]
    wides = [
        WideSwap(
            crops, n, wide_pair.at[i], wide_first.at[i], wide_second.at[i],
            wide_psem.at[i], wide_send.at[i], wide_recv.at[i],
        )
        for i in range(2)
    ]
    front = Copies(ref.f_send, ref.f_recv)
    for i in range(pair.shape[0]):
        pair[i, core] = jnp.zeros((8, 128), f32)
    for i in range(2):
        wide_pair[i, core] = jnp.zeros(wide_pair.shape[2:], f32)

    def halo(i, first, last, to_above, to_below):
        copies = [
            remote(first, to_above, halo_send.at[i, 0], halo_recv.at[i, 0], above),
            remote(last, to_below, halo_send.at[i, 1], halo_recv.at[i, 1], below),
        ]
        for copy in copies:
            copy.start()
        return copies

    def fine_halo(i, values):
        return halo(
            i,
            values.at[pl.ds(128, 128)],
            values.at[pl.ds(rows * 128, 128)],
            values.at[pl.ds((rows + 1) * 128, 128)],
            values.at[pl.ds(0, 128)],
        )

    def gain(k):
        return ref.norms[k : k + 1]

    def shift(k):
        return ref.norms[8 + k : 9 + k]

    def moments(total, square, count):
        average = total * (1.0 / count)
        return average, lax.rsqrt(square * (1.0 / count) - average * average + epsilon)

    column = lax.broadcasted_iota(jnp.int32, (128, c), 0)

    def put_three(target, base, y):
        target[pl.ds(base, 128), 0:c] = jnp.where(column == 0, 0.0, pltpu.roll(y, 1, 0)).astype(bf16)
        target[pl.ds(base, 128), c : 2 * c] = y.astype(bf16)
        target[pl.ds(base, 128), 2 * c : 3 * c] = jnp.where(
            column == 127, 0.0, pltpu.roll(y, 127, 0)
        ).astype(bf16)

    def inside(i):
        at_top = jnp.logical_and(me == 0, i == 0)
        at_bottom = jnp.logical_and(me == n - 1, i == rows + 1)
        return jnp.where(jnp.logical_or(at_top, at_bottom), 0.0, 1.0)

    def each_row(body, first, last, carry):
        def step(i, kept):
            return body(i, pl.multiple_of(i * 128, 128), kept)

        return lax.fori_loop(first, last, step, carry)

    zero = jnp.zeros((8, c), f32)

    src_all, src_own, gath = ref.src_all, ref.src_own, ref.gath
    local_copies = []

    def local(src, dst):
        copy = pltpu.make_async_copy(src, dst, ref.local.at[len(local_copies)])
        copy.start()
        local_copies.append(copy)

    local(ref.atrous_hbm, ref.atrous)
    for i in range(cells // 256):
        src_own[pl.ds(i * 256, 256)] = ref.feat[:, i * 256 : (i + 1) * 256].T
    local(src_own, src_all.at[my_crop])
    flip = ref.flip
    flip[...] = jnp.zeros(flip.shape, f32)
    flip[0:classes, 0:own] = ref.w_cls[...].astype(f32)
    own_cls = flip[0:128, 0:128].T[0:own, 0:classes].astype(bf16)
    flip[0:classes, 0:own] = jnp.zeros((classes, own), f32)
    for t in range(9):
        flip[0:own, 128:256] = jnp.zeros((own, 128), f32)
        flip[0:own, 128 : 128 + low_width] = ref.w_side[t].astype(f32)
        flip[t * low_width : (t + 1) * low_width, 0:128] = flip[0:128, 128:256].T[0:low_width]
    for k in range(5):
        gath[me, k] = ref.w_proj[k]
    turned = flip[:, 0:128].T[0:own].astype(bf16)
    gath[me, 5] = turned[:, 0:c]
    gath[me, 6] = turned[:, c : 2 * c]
    gath[me, 7] = jnp.zeros((own, c), bf16)
    gath[me, 7, :, 0:classes] = own_cls
    for k in range(8, small):
        gath[me, k] = jnp.zeros((own, c), bf16)
    for t in range(9, large):
        gath[me, small + t] = jnp.zeros((own, c), bf16)
        gath[me, small + large + t] = jnp.zeros((own, c), bf16)
    for t in range(9):
        gath[me, small + t] = ref.w_dec1[t]
        gath[me, small + large + t] = ref.w_dec2[t]
    columns = ref.columns
    columns[...] = jnp.zeros(columns.shape, f32)
    columns[0:1, 0:low_width] = ref.low_gain[...]
    columns[1:2, 0:low_width] = ref.low_shift[...]
    columns[2:3, 0:classes] = ref.bias[...]
    ref.norms_all[me] = jnp.zeros((16, 128), f32)
    ref.norms_all[me, 0:8, 0:own] = ref.own_gain[...]
    ref.norms_all[me, 8:16, 0:own] = ref.own_shift[...]
    wait_barrier()
    block_of = lambda j: lax.rem(me - 2 * j + n, n)
    crop_of = lambda i: lax.rem(my_crop - i + crops, crops)

    class Spread:
        def __init__(self, first, size):
            per = size // crops
            self.at = lambda b, q: gath.at[b, pl.ds(first + q * per, per)]
            self.first, self.size = first, size

        def start(self):
            here = self.at(me, my_crop)
            self.far = [front.start(here, here, peer) for peer in over_chips]
            here = gath.at[me, pl.ds(self.first, self.size)]
            self.pairs = [front.start(here, here, other)]

        def cross(self):
            self.crossed = []
            for j in range(1, chips):
                self.far[j - 1].wait_recv()
                here = self.at(block_of(j), my_crop)
                for i in range(1, crops):
                    self.crossed.append((i, j, front.start(here, here, over_crops[i - 1])))
                self.pairs.append(front.start(here, here, other))

        def cores(self):
            for i, j, copy in self.crossed:
                copy.wait_recv()
                here = self.at(block_of(j), crop_of(i))
                self.pairs.append(front.start(here, here, other))

        def finish(self):
            for copy in self.pairs:
                copy.wait_recv()

    norm_far = []
    here = ref.norms_all.at[me]
    for peer in over_chips:
        norm_far.append(front.start(here, here, peer))
    norm_pairs = [front.start(here, here, other)]
    spread = [Spread(0, small), Spread(small, large), Spread(small + large, large)]
    spread[0].start()
    spread[1].start()
    low_send, low_pair = ref.low_send, ref.low_pair

    def low_block(b):
        span = pl.ds(pl.multiple_of(b * fine_cells, fine_cells), fine_cells)
        return dot_tn(ref.low_w[...], ref.low_in[:, span])

    low_copies = []
    for z in range(chips):
        low_send[z] = low_block(2 * z + 1 - core)
        low_copies.append(front.start(low_send.at[z], low_pair.at[z], other))
    part, part_in, staged, arrived = ref.pushed, ref.pushed1, ref.staged, ref.arrived
    shifted = ref.g2

    order = (0, 3, 2, 1)

    def branch_partial(k):
        first = k * cells
        if k == 0:
            part[pl.ds(first, cells)] = dot(src_own[...], ref.point[...])
        else:
            rate = atrous_rates[k - 1]
            if k == order[1]:
                local_copies[0].wait()
            shift_three(lambda base: src_own[pl.ds(base, 128)], shifted, rate, -rate, rate)
            part[pl.ds(first, cells)] = dot(shifted[pl.ds(0, cells), 0 : 3 * c_in], ref.atrous[k - 1, 1])
            for a in (0, 2):
                move = (a - 1) * rate
                count = (FA - abs(move)) * FA
                to, off = first + max(-move, 0) * FA, max(move, 0) * FA
                part[pl.ds(to, count)] += dot(shifted[pl.ds(off, count), 0 : 3 * c_in], ref.atrous[k - 1, a])
        copies = []
        for z in range(chips):
            block = pl.multiple_of(first + (2 * z + 1 - core) * coarse_cells, coarse_cells)
            copies.append(
                front.start(
                    part.at[pl.ds(block, coarse_cells)],
                    part_in.at[pl.ds((k * chips + z) * coarse_cells, coarse_cells)],
                    other,
                )
            )
        return copies

    def pair_sum(k, z):
        block = pl.multiple_of(k * cells + (2 * z + core) * coarse_cells, coarse_cells)
        landed = pl.multiple_of((k * chips + z) * coarse_cells, coarse_cells)
        return part[pl.ds(block, coarse_cells)] + part_in[pl.ds(landed, coarse_cells)]

    branch_far, waited = [], []

    def branch_out(k, copies):
        for copy in copies:
            copy.wait()
            waited.append(copy)
        for z in range(chips):
            staged[k, z] = pair_sum(k, z).astype(bf16)
        ref.branch[:, k * c : (k + 1) * c] = pair_sum(k, chip)
        for j in range(1, chips):
            target = lax.rem(chip + j, chips)
            branch_far.append((k, j, front.start(staged.at[k, target], arrived.at[k, chip], over_chips[j - 1])))

    before = branch_partial(order[0])
    for at in range(1, 4):
        after = branch_partial(order[at])
        branch_out(order[at - 1], before)
        before = after
        if at == 2:
            spread[0].cross()
        if at == 1:
            for z in range(chips):
                low_copies[z].wait_recv()
                ref.low_sum[z] = (low_block(2 * z + core) + low_pair[z]).astype(bf16)
            low_far = []
            for j in range(1, chips):
                target = lax.rem(chip + j, chips)
                low_far.append(front.start(ref.low_sum.at[target], ref.low_recv.at[chip], over_chips[j - 1]))

    branch_out(order[3], before)
    spread[1].cross()
    feature_copies = [front.start(src_own, src_all.at[my_crop], peer) for peer in over_crops]
    for j in range(1, chips):
        norm_far[j - 1].wait_recv()
        here = ref.norms_all.at[block_of(j)]
        norm_pairs.append(front.start(here, here, other))
    pooled = row_of(src_own[...].astype(f32)) * (1.0 / cells)
    pooled = jnp.concatenate([pooled, jnp.zeros((15, c_in), f32)], axis=0).astype(bf16)
    pool_part = dot(pooled, ref.pool_w[...])[0:1]

    spread[0].cores()
    spread[1].cores()
    for copy in norm_pairs:
        copy.wait_recv()
    for b in range(n):
        ref.norms[:, b * own : (b + 1) * own] = ref.norms_all[b, :, 0:own]

    for copy in low_far:
        copy.wait_recv()
    low_ext = ref.low_ext
    low_total = low_block(me) + low_pair[chip]
    for j in range(1, chips):
        low_total = low_total + ref.low_recv[lax.rem(chip - j + chips, chips)].astype(f32)
    low_ext[:, 128 : 128 + fine_cells] = low_total
    low_edges = halo(
        0,
        low_ext.at[:, pl.ds(128, 128)],
        low_ext.at[:, pl.ds(rows * 128, 128)],
        low_ext.at[:, pl.ds((rows + 1) * 128, 128)],
        low_ext.at[:, pl.ds(0, 128)],
    )

    def add_low(i, base, kept):
        v = low_ext[:, pl.ds(base, 128)]
        return kept[0] + v, kept[1] + v * v

    low_zero = jnp.zeros((low_width, 128), f32)
    low_sum, low_square = each_row(add_low, 1, rows + 1, (low_zero, low_zero))

    def lanes_of(values):
        return row_of(values.T)

    pair[6, core, 0:1, 0:low_width] = lanes_of(low_sum)
    pair[6, core, 1:2, 0:low_width] = lanes_of(low_square)
    swaps[6].start()

    for k, j, copy in branch_far:
        copy.wait_recv()
        here = lax.rem(chip - j + chips, chips)
        ref.branch[:, k * c : (k + 1) * c] += arrived[k, here].astype(f32)
    wide = wide_pair.at[0]
    for k in range(4):
        v = ref.branch[:, k * c : (k + 1) * c]
        wide[core, k : k + 1] = row_of(v)
        wide[core, 4 + k : 5 + k] = row_of(v * v)
    wide[core, 8:16] = jnp.where(
        lax.broadcasted_iota(jnp.int32, (8, c), 0) == my_crop, pool_part, 0.0
    )
    total_a = wides[0].run(spread[2].start)
    spread[0].finish()
    proj, w1, w2, tail = ref.proj, ref.w1, ref.w2, ref.tail
    for b in range(n):
        mine = pl.ds(b * own, own)
        for k in range(5):
            proj[k, mine] = gath[b, k]

    def place_conv(target, first):
        for b in range(n):
            for t in range(9):
                a, e = t // 3, t % 3
                target[a, pl.ds(e * c + b * own, own)] = gath[b, first + t]

    def branch_parts(k):
        average, inverse = moments(total_a[k : k + 1], total_a[4 + k : 5 + k], coarse_samples)
        normed = (ref.branch[:, k * c : (k + 1) * c] - average) * inverse
        return normed, gain(k) * normed + shift(k), inverse

    projected = jnp.zeros((coarse_cells, c), f32)
    for k in range(4):
        y = gelu(branch_parts(k)[1]).astype(bf16)
        ref.branch_bf[:, k * c : (k + 1) * c] = y
        projected = projected + dot(y, ref.proj[k])
    pool_here = lax.broadcasted_iota(jnp.int32, (8, c), 0) < crops
    pool_pre = total_a[8:16]
    pool_average = row_of(pool_pre) * (1.0 / crops)
    pool_spread = jnp.where(pool_here, pool_pre - pool_average, 0.0)
    pool_inverse = lax.rsqrt(row_of(pool_spread * pool_spread) * (1.0 / crops) + epsilon)
    pool_normed = pool_spread * pool_inverse
    pool_before = gain(4) * pool_normed + shift(4)
    pool_bf = gelu(pool_before)
    pool_bf = jnp.concatenate([pool_bf, jnp.zeros((8, c), f32)], axis=0).astype(bf16)
    pool_term = dot(pool_bf, ref.proj[4])
    my_row = lax.broadcasted_iota(jnp.int32, (16, c), 0) == my_crop
    projected = projected + row_of(jnp.where(my_row, pool_term, 0.0))
    merged_ext = ref.merged_ext
    merged_ext[pl.ds(FA, coarse_cells)] = projected
    put_pair(pair.at[0], core, row_of(projected), row_of(projected * projected))
    merged_copies = halo(
        1,
        merged_ext.at[pl.ds(FA, FA)],
        merged_ext.at[pl.ds(coarse_cells, FA)],
        merged_ext.at[pl.ds(FA + coarse_cells, FA)],
        merged_ext.at[pl.ds(0, FA)],
    )
    swaps[0].start()

    total_l = swaps[6].finish()
    for copy in low_edges:
        copy.wait()
    low_average = total_l[0:1] * (1.0 / fine_samples)
    low_variance = total_l[1:2] * (1.0 / fine_samples) - low_average * low_average
    low_inverse_row = lax.rsqrt(low_variance + epsilon)
    low_average = spread_row(low_average)[0:low_width]
    low_inverse = spread_row(low_inverse_row)[0:low_width]
    lane = lax.broadcasted_iota(jnp.int32, (low_width, 128), 1)
    low_gain = spread_row(columns[0:1])[0:low_width]
    low_shift = spread_row(columns[1:2])[0:low_width]

    def low_parts(base):
        normed = (low_ext[:, pl.ds(base, 128)] - low_average) * low_inverse
        return normed, low_gain * normed + low_shift

    def low_row(i, base, kept):
        y = gelu(low_parts(base)[1]) * inside(i)
        lowx = ref.lowx
        lowx[0:low_width, pl.ds(base, 128)] = jnp.where(lane == 0, 0.0, pltpu.roll(y, 1, 1)).astype(bf16)
        lowx[low_width : 2 * low_width, pl.ds(base, 128)] = y.astype(bf16)
        lowx[2 * low_width : 3 * low_width, pl.ds(base, 128)] = jnp.where(
            lane == 127, 0.0, pltpu.roll(y, 127, 1)
        ).astype(bf16)
        return kept

    each_row(low_row, 0, rows + 2, 0)

    for b in range(n):
        mine = pl.ds(b * own, own)
        tail[mine, 0:c] = gath[b, 5]
        tail[mine, c : 2 * c] = gath[b, 6]
        ref.cls_all[mine] = gath[b, 7, :, 0:128]
    turned = tail[...].T
    for a in range(3):
        ref.w1low[a] = turned[a * 3 * low_width : (a + 1) * 3 * low_width]
    cls_lane = lax.broadcasted_iota(jnp.int32, (c, 128), 1)
    cls_clean = jnp.where(cls_lane < classes, ref.cls_all[...].astype(f32), 0.0)
    ref.cls_t[...] = cls_clean.T[0:32].astype(bf16)
    spread[2].cross()
    merged_sum, merged_square = get_pair(swaps[0].finish())
    for copy in merged_copies:
        copy.wait()
    merged_average, merged_inverse = moments(merged_sum, merged_square, coarse_samples)

    def merged_parts(first, count):
        normed = (merged_ext[pl.ds(first, count)] - merged_average) * merged_inverse
        return normed, gain(5) * normed + shift(5)

    fine_at = lax.broadcasted_iota(jnp.int32, (128, FA), 0).astype(f32)
    coarse_at = lax.broadcasted_iota(jnp.int32, (128, FA), 1).astype(f32)
    place = jnp.clip((fine_at + 0.5) / 4.0 - 0.5, 0.0, FA - 1.0)
    up = jnp.maximum(0.0, 1.0 - jnp.abs(place - coarse_at)).astype(bf16)
    coarse_wide = []
    for j in range(coarse_rows + 2):
        coarse_wide.append(dot_exact(up, gelu(merged_parts(j * FA, FA)[1])))
    for i in range(-1, rows + 1):
        lower, a, b = up_weights(i, me, n, rows, coarse_rows)
        put_three(ref.x1, (i + 1) * 128, a * coarse_wide[lower] + b * coarse_wide[lower + 1])
    spread[2].cores()
    spread[1].finish()
    place_conv(w1, small)
    dec1, dec2, pushed, pushed1 = ref.dec1, ref.dec2, ref.pushed, ref.pushed1

    def conv_piece(source, weight, base):
        total = None
        for a in range(3):
            term = dot(source[pl.ds(base + a * 128, chunk * 128)], weight[a])
            total = term if total is None else total + term
        return total

    def conv_loop(piece, target):
        def step(i, kept):
            base = pl.multiple_of(i * (chunk * 128), 128)
            total = piece(base)
            target[pl.ds(base + 128, chunk * 128)] = total
            return kept[0] + fold(total), kept[1] + fold(total * total)

        return lax.fori_loop(0, rows // chunk, step, (zero, zero))


    def first_piece(base):
        total = conv_piece(ref.x1, w1, base)
        for a in range(3):
            total = total + dot_tn(ref.lowx[:, pl.ds(base + a * 128, chunk * 128)], ref.w1low[a])
        return total

    total, square = conv_loop(first_piece, dec1)
    put_pair(pair.at[1], core, row_of(total), row_of(square))
    swaps[6].drain()
    swaps[1].start()
    dec1_copies = fine_halo(2, dec1)
    total, square = get_pair(swaps[1].finish())
    for copy in dec1_copies:
        copy.wait()
    first_average, first_inverse = moments(total, square, fine_samples)

    def first_parts(base):
        normed = (dec1[pl.ds(base, 128)] - first_average) * first_inverse
        return normed, gain(6) * normed + shift(6)

    def first_row(i, base, kept):
        put_three(ref.x2, base, gelu(first_parts(base)[1]) * inside(i))
        return kept

    each_row(first_row, 0, rows + 2, 0)
    spread[2].finish()
    place_conv(w2, small + large)
    total, square = conv_loop(lambda base: conv_piece(ref.x2, w2, base), dec2)
    put_pair(pair.at[2], core, row_of(total), row_of(square))
    swaps[0].drain()
    swaps[2].start()
    dec2_copies = fine_halo(3, dec2)
    total, square = get_pair(swaps[2].finish())
    for copy in dec2_copies:
        copy.wait()
    second_average, second_inverse = moments(total, square, fine_samples)

    cls_t = ref.cls_t[...]
    bias = spread_row(columns[2:3])[0:32]
    col_here = ref.offsets[0, 1] + 4 * lax.broadcasted_iota(jnp.int32, (1, 128), 1) < SCENE_W
    col_mask = jnp.where(col_here, 1.0, 0.0)

    def scene_mask(i):
        row_here = ref.offsets[0, 0] + 4 * (me * rows + i - 1) < SCENE_H
        return col_mask * jnp.where(row_here, 1.0, 0.0)

    def masked_row(i, base):
        return ref.dlog[:, pl.ds(base, 128)] * scene_mask(i).astype(bf16)

    def second_parts(base):
        normed = (dec2[pl.ds(base, 128)] - second_average) * second_inverse
        return normed, gain(7) * normed + shift(7)

    def second_row(i, base, kept):
        normed, before = second_parts(base)
        value, slope = gelu_both(before)
        ref.second[pl.ds(base, 128)] = value.astype(bf16)
        masked = masked_row(i, base)
        ref.dmask[:, pl.ds(base, 128)] = masked
        grad = dot_tn(masked, cls_t)
        push = slope * grad
        pushed[pl.ds(base, 128)] = push
        own_row = jnp.where(jnp.logical_and(i > 0, i < rows + 1), 1.0, 0.0)
        push = push * own_row
        return kept[0] + fold(push * normed), kept[1] + fold(push)

    along, summed = each_row(second_row, 0, rows + 2, (zero, zero))
    put_pair(pair.at[3], core, row_of(along), row_of(summed))
    swaps[1].drain()
    swaps[3].start()
    second = ref.second

    def logit_row(i, base, kept):
        out = pl.multiple_of(base - 128, 128)
        value = dot_nt(cls_t, second[pl.ds(base, 128)]) + bias
        ref.logits[:, pl.ds(out, 128)] = value * scene_mask(i)
        return kept

    each_row(logit_row, 1, rows + 1, 0)
    local(ref.logits, ref.logits_hbm)
    flip[pl.ds(9 * low_width, 32)] = dot(
        ref.dmask[:, 128 : 128 + fine_cells], second[pl.ds(128, fine_cells)]
    )
    bias_grad = jnp.zeros((32, 128), f32)
    for i in range(1, rows + 1):
        bias_grad = bias_grad + ref.dmask[:, i * 128 : (i + 1) * 128].astype(f32)
    wide_pair[1, core, 16:17, 0:32] = row_of(bias_grad.T)
    second_along, second_summed = get_pair(swaps[3].finish())

    def pull(push, normed, k, inverse, along, summed, count):
        return (gain(k) * inverse) * (push - summed * (1.0 / count) - normed * (along * (1.0 / count)))

    def dec2_row(i, base, kept):
        g = pull(
            pushed[pl.ds(base, 128)], second_parts(base)[0], 7, second_inverse,
            second_along, second_summed, fine_samples,
        )
        put_three(ref.g2, base, g * inside(i))
        return kept

    each_row(dec2_row, 0, rows + 2, 0)

    def back_loop(source, weight, use, carry):
        def step(i, kept):
            base = pl.multiple_of(i * (chunk * 128), 128)
            total = None
            for t in range(9):
                a, e = t // 3, t % 3
                piece = source[pl.ds(base + (2 - a) * 128, chunk * 128), (2 - e) * c : (3 - e) * c]
                term = dot_nt(piece, weight[a, e * c : (e + 1) * c])
                total = term if total is None else total + term
            return use(base, total, kept)

        return lax.fori_loop(0, rows // chunk, step, carry)

    def first_use(base, grad, kept):
        at = pl.ds(pl.multiple_of(base + 128, 128), chunk * 128)
        normed = (dec1[at] - first_average) * first_inverse
        push = gelu_slope(gain(6) * normed + shift(6)) * grad
        pushed1[at] = push
        return kept[0] + fold(push * normed), kept[1] + fold(push)

    along, summed = back_loop(ref.g2, ref.w2, first_use, (zero, zero))
    put_pair(pair.at[4], core, row_of(along), row_of(summed))
    swaps[2].drain()
    swaps[4].start()
    pushed_copies = fine_halo(4, pushed1)

    wgrads = ref.wgrads

    reduce_two = Reduce(
        crops, n, front, ref.own_w, ref.r_first, ref.r_pairs, ref.r_crossed, ref.r_halves, ref.r_lined, ref.r_out
    )

    def weight_grads(target, source, gradient):
        for a in range(3):
            part = dot_tn(
                source[pl.ds(a * 128, fine_cells), c : 2 * c], gradient[pl.ds(128, fine_cells)]
            ).astype(bf16)
            for e in range(3):
                tap = part[:, (2 - e) * c : (3 - e) * c]
                for h in range(n):
                    target[h, 3 * a + e] = tap[h * own : (h + 1) * own]

    weight_grads(ref.own_w, ref.x2, ref.g2)
    for t in range(9, large):
        for h in range(n):
            ref.own_w[h, t] = jnp.zeros((own, c), bf16)
    reduce_two.cores()
    first_along, first_summed = get_pair(swaps[4].finish())
    reduce_two.over_the_crops()
    for copy in pushed_copies:
        copy.wait()

    def dec1_row(i, base, kept):
        g = pull(
            pushed1[pl.ds(base, 128)], first_parts(base)[0], 6, first_inverse,
            first_along, first_summed, fine_samples,
        ) * inside(i)
        put_three(ref.g1, base, g)
        return kept

    each_row(dec1_row, 0, rows + 2, 0)

    def up_use(base, grad, kept):
        dec2[pl.ds(pl.multiple_of(base + 128, 128), chunk * 128)] = grad
        return kept

    back_loop(ref.g1, ref.w1, up_use, 0)
    yt = ref.yt

    def low_back_row(i, local, base, kept):
        total = None
        for t in range(9):
            a, e = t // 3, t % 3
            at = pl.ds((local + 2 - a) * 128, 128)
            piece = yt[t * low_width : (t + 1) * low_width, at]
            if e == 0:
                piece = jnp.where(lane == 127, 0.0, pltpu.roll(piece, 127, 1))
            if e == 2:
                piece = jnp.where(lane == 0, 0.0, pltpu.roll(piece, 1, 1))
            total = piece if total is None else total + piece
        normed, before = low_parts(base)
        push = gelu_slope(before) * total
        ref.low_push[:, pl.ds(pl.multiple_of(base - 128, 128), 128)] = push
        return kept[0] + push * normed, kept[1] + push

    def low_back_chunk(i, kept):
        base = pl.multiple_of(i * (chunk * 128), 128)
        here = ref.g1[pl.ds(base, (chunk + 2) * 128), c : 2 * c]
        for a in range(3):
            yt[a * 3 * low_width : (a + 1) * 3 * low_width] = dot_nt(ref.w1low[a], here)
        for local in range(chunk):
            kept = low_back_row(i, local, pl.multiple_of(base + (local + 1) * 128, 128), kept)
        return kept

    low_along, low_summed = lax.fori_loop(0, rows // chunk, low_back_chunk, (low_zero, low_zero))

    part = ref.merged_part
    fine_at = lax.broadcasted_iota(jnp.int32, (FA, 128), 1).astype(f32)
    coarse_at = lax.broadcasted_iota(jnp.int32, (FA, 128), 0).astype(f32)
    place = jnp.clip((fine_at + 0.5) / 4.0 - 0.5, 0.0, FA - 1.0)
    up_t = jnp.maximum(0.0, 1.0 - jnp.abs(place - coarse_at)).astype(bf16)
    row_sums = [None] * (coarse_rows + 2)
    for i in range(rows):
        lower, a, b = up_weights(i, me, n, rows, coarse_rows)
        grad = dec2[pl.ds((i + 1) * 128, 128)]
        for j, weight in ((lower, a), (lower + 1, b)):
            row_sums[j] = weight * grad if row_sums[j] is None else row_sums[j] + weight * grad
    along, summed = zero, zero
    for j in range(coarse_rows + 2):
        grad = dot_exact(up_t, row_sums[j])
        part[pl.ds(j * FA, FA)] = grad
        normed, before = merged_parts(j * FA, FA)
        push = gelu_slope(before) * grad
        along, summed = along + fold(push * normed), summed + fold(push)
    put_pair(pair.at[5], core, row_of(along), row_of(summed))
    pair[5, core, 4:5, 0:low_width] = lanes_of(low_along)
    pair[5, core, 5:6, 0:low_width] = lanes_of(low_summed)
    part_copies = halo(
        5,
        part.at[pl.ds(0, FA)],
        part.at[pl.ds(FA + coarse_cells, FA)],
        part.at[pl.ds((coarse_rows + 3) * FA, FA)],
        part.at[pl.ds((coarse_rows + 2) * FA, FA)],
    )
    swaps[3].drain()
    swaps[5].start()
    reduce_two.over_the_chips()
    weight_grads(wgrads, ref.x1, ref.g1)
    local(wgrads.at[:, pl.ds(0, 9)], ref.wgrads_hbm.at[:, pl.ds(0, 9)])
    total_g = swaps[5].finish()
    for copy in part_copies:
        copy.wait()
    merged_along, merged_summed = get_pair(total_g)
    low_along, low_summed = spread_row(total_g[4:5])[0:low_width], spread_row(total_g[5:6])[0:low_width]
    pack = ref.pack
    pack[17:18, 0:128] = total_g[4:5]
    pack[18:19, 0:128] = total_g[5:6]
    up_here = jnp.where(me == 0, 0.0, 1.0)
    down_here = jnp.where(me == n - 1, 0.0, 1.0)
    proj_bf = ref.proj_bf
    for j in range(1, coarse_rows + 1):
        grad = part[pl.ds(j * FA, FA)]
        if j == 1:
            grad = grad + up_here * part[pl.ds((coarse_rows + 2) * FA, FA)]
        if j == coarse_rows:
            grad = grad + down_here * part[pl.ds((coarse_rows + 3) * FA, FA)]
        normed, before = merged_parts(j * FA, FA)
        push = gelu_slope(before) * grad
        g = pull(push, normed, 5, merged_inverse, merged_along, merged_summed, coarse_samples)
        proj_bf[pl.ds((j - 1) * FA, FA)] = g.astype(bf16)

    push_all = []
    for k in range(4):
        normed, before, _ = branch_parts(k)
        push = gelu_slope(before) * dot_nt(proj_bf[...], ref.proj[k])
        push_all.append(push)
        wide_pair[1, core, k : k + 1] = row_of(push * normed)
        wide_pair[1, core, 4 + k : 5 + k] = row_of(push)
    proj_row = row_of(proj_bf[...].astype(f32))
    wide_pair[1, core, 8:16] = jnp.where(
        lax.broadcasted_iota(jnp.int32, (8, c), 0) == my_crop, proj_row, 0.0
    )
    total_h = wides[1].run(reduce_two.to_all_crops)
    for k in range(4):
        normed, _, inverse = branch_parts(k)
        g = pull(
            push_all[k], normed, k, inverse, total_h[k : k + 1], total_h[4 + k : 5 + k], coarse_samples
        )
        ref.branch_out[:, k * c : (k + 1) * c] = g.astype(bf16)

    sums = total_h[8:16]
    sums_high = sums.astype(bf16).astype(f32)
    sums_low = sums - sums_high
    spare = jnp.concatenate([sums_high, sums_low], axis=0)
    spare_mid = spare.astype(bf16)
    spare_rest = (spare - spare_mid.astype(f32)).astype(bf16)
    pieces = dot_nt(spare_mid, ref.proj[4]) + dot_nt(spare_rest, ref.proj[4])
    pool_push = gelu_slope(pool_before) * (pieces[0:8] + pieces[8:16])
    pool_push = jnp.where(pool_here, pool_push, 0.0)
    pool_along, pool_summed = row_of(pool_push * pool_normed), row_of(pool_push)
    pool_grad = pull(pool_push, pool_normed, 4, pool_inverse, pool_along, pool_summed, crops)
    pool_grad = jnp.where(pool_here, pool_grad, 0.0)
    pack[24:32] = pool_grad
    pack[32:40] = jnp.zeros((8, c), f32)

    gain_rows = [total_h[0:4], pool_along, merged_along, first_along, second_along]
    shift_rows = [total_h[4:8], pool_summed, merged_summed, first_summed, second_summed]
    turn = c - me * own
    pack[0:8] = pltpu.roll(jnp.concatenate(gain_rows, axis=0), turn, 1)
    pack[8:16] = pltpu.roll(jnp.concatenate(shift_rows, axis=0), turn, 1)
    pack[16:17] = total_h[16:17]
    pool_rows = jnp.zeros((c, c), f32)
    rest = jnp.concatenate([sums, jnp.zeros((8, c), f32)], axis=0)
    for _ in range(3):
        high = rest.astype(bf16)
        pool_rows = pool_rows + dot_tn(pool_bf, high)
        rest = rest - high.astype(f32)
    dec1[pl.ds(0, c)] = pool_rows
    pack[40 : 40 + own] = dec1[pl.ds(pl.multiple_of(me * own, own), own)]
    local(pack, ref.pack_hbm)

    def low_out_row(i, base, kept):
        at = pl.ds(pl.multiple_of(base - 128, 128), 128)
        normed = low_parts(base)[0]
        g = (low_gain * low_inverse) * (
            ref.low_push[:, at] - low_summed * (1.0 / fine_samples) - normed * (low_along * (1.0 / fine_samples))
        )
        ref.low_out[:, at] = g.astype(bf16)
        return kept

    each_row(low_out_row, 1, rows + 1, 0)
    local(ref.low_out, ref.low_hbm)
    local(ref.branch_out, ref.branch_hbm)

    for a in range(3):
        flip[pl.ds(a * 3 * low_width, 3 * low_width)] = dot(
            ref.lowx[:, a * 128 : a * 128 + fine_cells], ref.g1[pl.ds(128, fine_cells), c : 2 * c]
        )
    flip[pl.ds(9 * low_width + 32, 48)] = jnp.zeros((48, c), f32)
    turned = flip[...].T.astype(bf16)
    for k in range(4):
        product = dot_tn(ref.branch_bf[:, k * c : (k + 1) * c], proj_bf[...]).astype(bf16)
        for h in range(n):
            rows_h = product[h * own : (h + 1) * own]
            wgrads[h, 9 + k] = rows_h
    for h in range(n):
        wgrads[h, 13] = turned[h * own : (h + 1) * own, 0:c]
        wgrads[h, 14] = turned[h * own : (h + 1) * own, c : 2 * c]
        for k in range(15, wgrads.shape[1]):
            wgrads[h, k] = jnp.zeros((own, c), bf16)
    local(wgrads.at[:, pl.ds(9, wgrads.shape[1] - 9)], ref.wgrads_hbm.at[:, pl.ds(9, wgrads.shape[1] - 9)])
    reduce_two.finish()
    for t in range(9):
        ref.dec2_w[t] = ref.r_out[t].astype(f32)
    local(ref.dec2_w, ref.dec2_hbm)
    for copy in feature_copies:
        copy.wait_recv()
    front.drain(waited)
    swaps[4].drain()
    swaps[5].drain()
    for copy in local_copies[1:]:
        copy.wait()


def decoder(crops, n, samples, *args):
    ref = DecoderRefs(*args, *([None] * (len(DecoderRefs._fields) - len(args))))
    c_in, c = ref.point.shape
    low_width = ref.low_w.shape[1]
    rows = ref.dlog.shape[1] // 128 - 2
    cells = rows * 128
    coarse = FA * FA // n
    own = c // n
    small, large = weight_groups(crops)
    chips = n // 2
    all_chips = crops * chips
    outer = (rows + 2) * 128
    chunk = min(4, rows)
    count = (crops - 1) + 4 * (2 * chips - 1) + 2 * chips - 1
    count += 2 * chips - 1 + 3 * (1 + 2 * crops * (chips - 1)) + reduce_copies(crops, n)
    S = jax.ShapeDtypeStruct
    V = pltpu.VMEM
    D = pltpu.SemaphoreType.DMA
    vmem = pl.BlockSpec(memory_space=pltpu.VMEM)
    hbm = pl.BlockSpec(memory_space=pl.ANY)
    return pl.pallas_call(
        functools.partial(decoder_kernel, crops, n, samples),
        out_shape=[
            S((32, cells), f32),
            S((coarse, 4 * c), bf16),
            S((low_width, cells), bf16),
            S((40 + own, c), f32),
            S((9, own, c), f32),
            S((n, rest_groups(crops), own, c), bf16),
            S((crops, FA * FA, c_in), bf16),
        ],
        in_specs=[pl.BlockSpec(memory_space=pltpu.SMEM), vmem, vmem, hbm] + [vmem] * (len(args) - 4),
        out_specs=[hbm] * 7,
        scratch_shapes=[
            V(ref.atrous_hbm.shape, bf16),
            V((FA * FA, c_in), bf16),
            V((32, cells), f32),
            V((coarse, 4 * c), bf16),
            V((low_width, cells), bf16),
            V((40 + own, c), f32),
            V((9, own, c), f32),
            V((n, rest_groups(crops), own, c), bf16),
            V((low_width, outer), f32),
            V((low_width, cells), f32),
            V((3 * low_width, outer), bf16),
            V((coarse + 2 * FA, c), f32),
            V((coarse + 4 * FA, c), f32),
            V((outer, c), f32),
            V((outer, c), f32),
            V((max(outer, 4 * FA * FA), c), f32),
            V((max(outer, 2 * FA * FA), c), f32),
            V((outer, 3 * c), bf16),
            V((outer, 3 * c), bf16),
            V((max(outer, FA * FA), 3 * c), bf16),
            V((outer, 3 * c), bf16),
            V((9 * low_width, (chunk + 2) * 128), f32),
            V((coarse, 4 * c), bf16),
            V((coarse, c), bf16),
            V((outer, c), bf16),
            V((512, c), f32),
            V((coarse, 4 * c), f32),
            V((4, chips, coarse, c), bf16),
            V((4, chips, coarse, c), bf16),
            V((chips, low_width, cells), f32),
            V((chips, low_width, cells), f32),
            V((chips, low_width, cells), bf16),
            V((chips, low_width, cells), bf16),
            V((n, small + 2 * large, own, c), bf16),
            V((n, 16, 128), f32),
            V((16, c), f32),
            V((5, c, c), bf16),
            V((3, 3 * c, c), bf16),
            V((c, 2 * c), bf16),
            V((3, 3 * low_width, c), bf16),
            V((3, 3 * c, c), bf16),
            V((c, 128), bf16),
            V((32, c), bf16),
            V((32, outer), bf16),
            V((8, 128), f32),
            V((n, large, own, c), bf16),
            *reduce_scratch(crops, n, large, own, c),
            D((16,)),
            D((count,)),
            D((count,)),
            V((2, 2, 24, c), f32),
            V((2, crops, 24, c), f32),
            V((2, chips, 24, c), f32),
            D((2, 2)),
            D((2, crops + chips)),
            D((2, crops + chips)),
            V((7, 2, 8, 128), f32),
            V((7, all_chips, 8, 128), f32),
            D((7, 2)),
            D((2, all_chips)),
            D((7, all_chips)),
            D((6, 2)),
            D((6, 2)),
        ],
        compiler_params=pltpu.CompilerParams(
            collective_id=0, has_side_effects=True, vmem_limit_bytes=62 * 1024 * 1024
        ),
    )(*args)


class Reduce:
    def __init__(self, crops, n, copies, source, first, pairs, crossed, halves, lined, out, mine=None, mine_sems=None):
        my_crop, me = lax.axis_index("crop"), lax.axis_index("chan")
        self.crops, self.chips, self.copies = crops, n // 2, copies
        self.crop, self.core, self.chip = my_crop, lax.rem(me, 2), lax.div(me, 2)
        self.other = (my_crop, me + 1 - 2 * self.core)
        self.over_crops = [(lax.rem(my_crop + i, crops), me) for i in range(1, crops)]
        self.over_chips = [(my_crop, lax.rem(me + 2 * j, n)) for j in range(1, n // 2)]
        self.source, self.first, self.pairs, self.crossed = source, first, pairs, crossed
        self.halves, self.lined, self.out = halves, lined, out
        self.mine, self.mine_sems = mine, mine_sems
        self.size = source.shape[1]
        self.share = self.size // crops

    def wait(self):
        for copy in self.moving:
            copy.wait_recv()

    def cores(self):
        self.moving = []
        for z in range(self.chips):
            block = self.source.at[2 * z + 1 - self.core]
            self.moving.append(self.copies.start(block, self.first.at[z], self.other))
        self.loads = []
        if self.mine is not None:
            for z in range(self.chips):
                block = self.source.at[2 * z + self.core]
                self.loads.append(pltpu.make_async_copy(block, self.mine.at[z], self.mine_sems.at[z]))
                self.loads[-1].start()

    def over_the_crops(self):
        self.wait()
        for copy in self.loads:
            copy.wait()
        for z in range(self.chips):
            for g in range(self.size):
                here = self.source[2 * z + self.core, g] if self.mine is None else self.mine[z, g]
                both = here.astype(f32) + self.first[z, g].astype(f32)
                self.pairs[z, g] = both.astype(bf16)
        self.moving = []
        for i in range(1, self.crops):
            target = lax.rem(self.crop + i, self.crops)
            block = self.pairs.at[:, pl.ds(target * self.share, self.share)]
            self.moving.append(
                self.copies.start(block, self.crossed.at[self.crop], self.over_crops[i - 1])
            )
        for z in range(self.chips):
            for g in range(self.share):
                self.crossed[self.crop, z, g] = self.pairs[z, self.crop * self.share + g]

    def over_the_chips(self):
        self.wait()
        for z in range(self.chips):
            for g in range(self.share):
                value = self.crossed[0, z, g].astype(f32)
                for i in range(1, self.crops):
                    value = value + self.crossed[i, z, g].astype(f32)
                self.halves[z, g] = value.astype(bf16)
        self.moving = []
        for j in range(1, self.chips):
            target = lax.rem(self.chip + j, self.chips)
            self.moving.append(
                self.copies.start(
                    self.halves.at[target], self.lined.at[self.chip], self.over_chips[j - 1]
                )
            )
        for g in range(self.share):
            self.lined[self.chip, g] = self.halves[self.chip, g]

    def to_all_crops(self):
        self.wait()
        for g in range(self.share):
            value = self.lined[0, g].astype(f32)
            for z in range(1, self.chips):
                value = value + self.lined[z, g].astype(f32)
            self.out[self.crop * self.share + g] = value.astype(bf16)
        here = self.out.at[pl.ds(self.crop * self.share, self.share)]
        self.moving = [self.copies.start(here, here, peer) for peer in self.over_crops]

    def finish(self):
        self.wait()


def reduce_scratch(crops, n, size, own, c):
    chips, share = n // 2, size // crops
    V = pltpu.VMEM
    return [
        V((chips, size, own, c), bf16),
        V((chips, size, own, c), bf16),
        V((crops, chips, share, own, c), bf16),
        V((chips, share, own, c), bf16),
        V((chips, share, own, c), bf16),
        V((size, own, c), bf16),
    ]


def reduce_copies(crops, n):
    return 2 * (n // 2) - 1 + 2 * (crops - 1)


class Gather:
    def __init__(self, n, send, recv):
        my_crop, self.me = lax.axis_index("crop"), lax.axis_index("chan")
        self.n, self.chips = n, n // 2
        self.core = lax.rem(self.me, 2)
        self.other = (my_crop, self.me + 1 - 2 * self.core)
        self.send, self.recv = send, recv
        self.peer = lambda j: (my_crop, lax.rem(self.me + 2 * j, n))

    def block(self, j):
        return lax.rem(self.me - 2 * j + self.n, self.n)

    def other_block(self, j):
        return lax.rem(self.me + 1 - 2 * self.core - 2 * j + self.n, self.n)

    def start(self, at):
        self.at = at
        self.far, self.pairs = [], []
        for j in range(1, self.chips):
            here = at(self.me)
            self.far.append(remote(here, here, self.send.at[j], self.recv.at[j], self.peer(j)))
            self.far[-1].start()
        self.forward(0)

    def forward(self, j):
        here = self.at(self.block(j))
        k = self.chips + j
        self.pairs.append(remote(here, here, self.send.at[k], self.recv.at[k], self.other))
        self.pairs[-1].start()

    def arrive(self, j):
        self.far[j - 1].wait_recv()
        self.forward(j)

    def finish(self):
        for copy in self.pairs:
            copy.wait_recv()

    def drain(self):
        for copy in self.far + self.pairs:
            copy.wait_send()


class BackRefs(typing.NamedTuple):
    grad: object
    src_hbm: object
    point: object
    atrous_hbm: object
    pool: object
    pack: object
    low_grad: object
    low_in_hbm: object
    wgrads: object
    features_hbm: object
    point_w: object
    atrous_w_hbm: object
    pool_w: object
    low_w_out: object
    blocks: object
    low_full_hbm: object
    last_grad: object
    last_src: object
    src: object
    atrous: object
    low_in: object
    features: object
    atrous_w: object
    low_full: object
    mine: object
    local: object
    m_sems: object
    all_grad: object
    shifted: object
    turned: object
    total: object
    r_first: object
    r_pairs: object
    r_crossed: object
    r_halves: object
    r_lined: object
    r_out: object
    low_parts: object
    g_send: object
    g_recv: object
    l_send: object
    l_recv: object
    c_send: object
    c_recv: object


def back_kernel(crops, n, *refs):
    ref = BackRefs(*refs)
    my_crop, me = lax.axis_index("crop"), lax.axis_index("chan")
    chips = n // 2
    core, chip = lax.rem(me, 2), lax.div(me, 2)
    block, width = ref.grad.shape
    c = width // 4
    half = width // 2
    c_in = ref.src.shape[2]
    cells = FA * FA
    relay = crops == 4
    other = (my_crop, me + 1 - 2 * core)
    over_crops = [(lax.rem(my_crop + i, crops), me) for i in range(1, crops)]
    over_chips = [(my_crop, lax.rem(me + 2 * j, n)) for j in range(1, chips)]
    wait_barrier = barrier_with([other] + over_crops + over_chips)
    all_grad, src = ref.all_grad, ref.src
    if relay:
        along_x = my_crop + 1 - 2 * lax.rem(my_crop, 2)
        along_y = my_crop + 2 - 4 * lax.div(my_crop, 2)
        crop_list = [my_crop, along_x, along_y, 3 - my_crop]
    else:
        crop_list = [my_crop] + [lax.rem(my_crop - i + crops, crops) for i in range(1, crops)]

    def grad_at(crop):
        def at(b):
            return all_grad.at[crop, pl.ds(pl.multiple_of(b * block, block), block)]

        return at

    def lanes_at(crop, b, first):
        return all_grad.at[crop, pl.ds(pl.multiple_of(b * block, block), block), pl.ds(first, half)]

    local_copies = []

    def local(src, dst):
        copy = pltpu.make_async_copy(src, dst, ref.local.at[len(local_copies)])
        copy.start()
        local_copies.append(copy)

    local(ref.src_hbm, src)
    local(ref.src_hbm.at[crop_list[-1]], ref.last_src)
    local(ref.atrous_hbm, ref.atrous)
    local(ref.low_in_hbm, ref.low_in)
    pooled_grad = ref.pack[24:40].astype(bf16)
    all_grad[my_crop, pl.ds(pl.multiple_of(me * block, block), block)] = ref.grad[...]
    ref.low_full[me] = ref.low_grad[...]
    wait_barrier()

    gather = Gather(n, ref.g_send, ref.g_recv)
    gather.start(grad_at(my_crop))
    moves = Copies(ref.c_send, ref.c_recv)
    crossing = {}

    def cross(j):
        here = grad_at(my_crop)(gather.block(j))
        if relay:
            for i, crop in ((1, along_x), (2, along_y)):
                crossing[i, j] = moves.start(here, here, (crop, me))
        else:
            for i in range(1, crops):
                crossing[i, j] = moves.start(here, here, over_crops[i - 1])

    core_copies = {}

    def pass_on(i, j):
        crossing[i, j].wait_recv()
        b = gather.block(j)
        crop = crop_list[i]
        if relay and i == 1:
            here = lanes_at(crop, b, 0)
            crossing[3, j, 0] = moves.start(here, here, (along_y, me))
        if relay and i == 2:
            here = lanes_at(crop, b, half)
            crossing[3, j, 1] = moves.start(here, here, (along_x, me))
        place = grad_at(crop)(b)
        core_copies[i, j] = moves.start(place, place, other)

    def pass_across(j):
        crossing[3, j, 0].wait_recv()
        crossing[3, j, 1].wait_recv()
        place = grad_at(crop_list[3])(gather.block(j))
        core_copies[3, j] = moves.start(place, place, other)

    cross(0)
    reduce = Reduce(
        crops, n, moves, ref.wgrads, ref.r_first, ref.r_pairs, ref.r_crossed, ref.r_halves, ref.r_lined, ref.r_out,
        ref.mine, ref.m_sems,
    )
    reduce.cores()
    shifted = ref.shifted

    def shift_source(i):
        crop = crop_list[i]
        for k in range(3):
            rate = atrous_rates[k]
            shift_three(lambda base: src[crop, pl.ds(base, 128)], shifted.at[i % 3, k], rate, -rate, rate)

    local_copies[0].wait()
    shift_source(0)
    reduce.over_the_crops()
    for i in range(1, min(3, crops)):
        shift_source(i)
    for j in range(1, chips):
        gather.arrive(j)
        cross(j)
    reduce.over_the_chips()
    low_gather = Gather(n, ref.l_send, ref.l_recv)
    low_gather.start(lambda b: ref.low_full.at[b])
    if relay:
        pass_on(1, 0)
        pass_on(2, 0)
    gather.finish()

    total, turned = ref.total, ref.turned
    pool_row = dot_nt(pooled_grad, ref.pool[...])
    my_row = lax.broadcasted_iota(jnp.int32, pool_row.shape, 0) == my_crop
    pool_row = row_of(jnp.where(my_row, pool_row, 0.0)) * (1.0 / cells)
    local_copies[2].wait()
    total[...] = dot_nt(all_grad[my_crop, :, 0:c], ref.point[...]) + pool_row
    for k in range(3):
        rate = atrous_rates[k]
        shift_three(
            lambda base: all_grad[my_crop, pl.ds(base, 128), (k + 1) * c : (k + 2) * c],
            turned, rate, rate, -rate,
        )
        for a in range(3):
            move = (a - 1) * rate
            count = (FA - abs(move)) * FA
            to, off = max(move, 0) * FA, max(-move, 0) * FA
            term = None
            for e in range(3):
                piece = dot_nt(turned[pl.ds(off, count), e * c : (e + 1) * c], ref.atrous[k, 3 * a + e])
                term = piece if term is None else term + piece
            total[pl.ds(to, count)] = total[pl.ds(to, count)] + term

    def weight_part(i):
        crop = crop_list[i]
        part = dot_tn(src[crop], all_grad[crop, :, 0:c])
        ref.point_w[...] = part if i == 0 else ref.point_w[...] + part
        for k in range(3):
            rate = atrous_rates[k]
            for a in range(3):
                move = (a - 1) * rate
                count = (FA - abs(move)) * FA
                from_src, off = max(move, 0) * FA, max(-move, 0) * FA
                part = dot_tn(
                    shifted[i % 3, k, pl.ds(from_src, count)],
                    all_grad[crop, pl.ds(off, count), (k + 1) * c : (k + 2) * c],
                )
                for e in range(3):
                    piece = part[e * c_in : (e + 1) * c_in]
                    if i > 0:
                        piece = ref.atrous_w[k, 3 * a + e] + piece
                    ref.atrous_w[k, 3 * a + e] = piece
            if i == crops - 2:
                local(ref.atrous_w.at[k], ref.atrous_w_hbm.at[k])

    weight_part(0)
    ref.features[...] = total[...].T
    local(ref.features, ref.features_hbm)
    if relay:
        for j in range(1, chips):
            pass_on(1, j)
            pass_on(2, j)

    def low_part():
        for j in range(1, chips):
            low_gather.arrive(j)
        low_gather.finish()
        local(ref.low_full, ref.low_full_hbm)
        local_copies[3].wait()
        rows = ref.low_full.shape[2] // 128
        low_in, low_all = ref.low_in, ref.low_full
        low_total = None
        for b in range(n):
            here = low_all[b]
            span = slice(b * rows * 128, (b + 1) * rows * 128)
            part = dot_nt(low_in[:, span], here)
            low_total = part if low_total is None else low_total + part
        low_parts = ref.low_parts
        low_parts[my_crop] = jnp.zeros(low_parts.shape[1:], f32)
        low_parts[my_crop, :, 0 : low_total.shape[1]] = low_total
        here = low_parts.at[my_crop]
        low_copies = [moves.start(here, here, peer) for peer in over_crops]
        return low_copies

    for i in range(1, crops):
        if i + 2 < crops - 1:
            shift_source(i + 2)
        for j in range(chips):
            if not relay:
                pass_on(i, j)
            elif i == 3:
                pass_across(j)
        for j in range(chips):
            core_copies[i, j].wait_recv()
        if i < crops - 1:
            weight_part(i)
        if i == min(2, crops - 1):
            reduce.to_all_crops()
            low_copies = low_part()

    local(all_grad.at[crop_list[-1]], ref.last_grad)
    pooled = []
    for i in range(crops):
        mean = row_of(src[i].astype(f32)) * (1.0 / cells)
        pooled.append(mean)
    pooled = jnp.concatenate(pooled + [jnp.zeros((16 - crops, c_in), f32)], axis=0).astype(bf16)
    ref.pool_w[...] = dot_tn(pooled, pooled_grad)

    reduce.finish()
    for g in range(ref.blocks.shape[0]):
        ref.blocks[g] = ref.r_out[g].astype(f32)
    for copy in low_copies:
        copy.wait_recv()
    ref.low_w_out[...] = jnp.sum(ref.low_parts[...], axis=0)
    gather.drain()
    low_gather.drain()
    moves.drain([])
    for k, copy in enumerate(local_copies):
        if k not in (0, 2, 3):
            copy.wait()


def pyramid_back(crops, n, *args):
    grad, src, low_grad, low_in, wgrads = args[0], args[1], args[6], args[7], args[8]
    block, width = grad.shape
    c = width // 4
    c_in = src.shape[2]
    chips = n // 2
    cells = FA * FA
    low_rows = low_in.shape[0]
    own, lanes = wgrads.shape[2:]
    S = jax.ShapeDtypeStruct
    V = pltpu.VMEM
    D = pltpu.SemaphoreType.DMA
    vmem = pl.BlockSpec(memory_space=pltpu.VMEM)
    hbm = pl.BlockSpec(memory_space=pl.ANY)
    count = 3 * crops * chips + crops - 1 + reduce_copies(crops, n)
    return pl.pallas_call(
        functools.partial(back_kernel, crops, n),
        out_shape=[
            S((c_in, cells), f32),
            S((c_in, c), f32),
            S((3, 9, c_in, c), f32),
            S((c_in, c), f32),
            S((low_rows, 128), f32),
            S((15, own, lanes), f32),
            S((n,) + low_grad.shape, bf16),
            S((cells, width), bf16),
            S((cells, c_in), bf16),
        ],
        in_specs=[vmem, hbm, vmem, hbm, vmem, vmem, vmem, hbm, hbm],
        out_specs=[hbm, vmem, hbm, vmem, vmem, vmem, hbm, hbm, hbm],
        scratch_shapes=[
            V(src.shape, bf16),
            V(args[3].shape, bf16),
            V(low_in.shape, bf16),
            V((c_in, cells), f32),
            V((3, 9, c_in, c), f32),
            V((n,) + low_grad.shape, bf16),
            V((chips,) + wgrads.shape[1:], bf16),
            D((12,)),
            D((chips,)),
            V((crops, cells, width), bf16),
            V((min(3, crops), 3, cells, 3 * c_in), bf16),
            V((cells, 3 * c), bf16),
            V((cells, c_in), f32),
            *reduce_scratch(crops, n, wgrads.shape[1], own, lanes),
            V((crops, low_rows, 128), f32),
            D((n,)),
            D((n,)),
            D((n,)),
            D((n,)),
            D((count,)),
            D((count,)),
        ],
        compiler_params=pltpu.CompilerParams(
            collective_id=1, has_side_effects=True, vmem_limit_bytes=62 * 1024 * 1024
        ),
    )(*args)


class FinishRefs(typing.NamedTuple):
    atrous_part: object
    point_part: object
    last_grad: object
    last_src: object
    features_in: object
    pool_in: object
    low_full: object
    low_w: object
    low_w_part: object
    logits_in: object
    dec2_in: object
    blocks: object
    pack: object
    logits: object
    features: object
    early: object
    point: object
    atrous: object
    pool: object
    proj: object
    low_w_out: object
    dec1: object
    side: object
    dec2: object
    cls: object
    bias: object
    gain: object
    shift: object
    low_gain: object
    low_shift: object
    turned: object


def finish_kernel(*refs):
    ref = FinishRefs(*refs)
    step = pl.program_id(0)
    c_in, c = ref.point_part.shape
    cells = FA * FA
    classes, rows = ref.logits.shape[0], ref.logits.shape[1]
    low_width = ref.low_gain.shape[1]
    own = ref.cls.shape[1]

    def branch(k):
        rate = atrous_rates[k]
        shift_three(lambda base: ref.last_src[pl.ds(base, 128)], ref.turned, rate, -rate, rate)
        for a in range(3):
            move = (a - 1) * rate
            count = (FA - abs(move)) * FA
            from_src, off = max(move, 0) * FA, max(-move, 0) * FA
            part = dot_tn(
                ref.turned[pl.ds(from_src, count)],
                ref.last_grad[pl.ds(off, count), (k + 1) * c : (k + 2) * c],
            )
            for e in range(3):
                t = 3 * a + e
                ref.atrous[0, t] = ref.atrous_part[0, t] + part[e * c_in : (e + 1) * c_in]

    def low_features():
        for b in range(ref.low_full.shape[0]):
            value = dot(ref.low_w[...], ref.low_full[b])
            ref.early[:, b * rows : (b + 1) * rows] = value.reshape(value.shape[0], rows, 128)
        ref.low_w_out[...] = ref.low_w_part[:, 0:low_width]

    def small():
        ref.point[...] = ref.point_part[...] + dot_tn(ref.last_src[...], ref.last_grad[:, 0:c])
        ref.pool[...] = ref.pool_in[...]
        ref.logits[...] = ref.logits_in[0:classes].reshape(classes, rows, 128)
        ref.dec2[...] = ref.dec2_in[...]
        for t in range(9):
            ref.dec1[t] = ref.blocks[t]
        for k in range(4):
            ref.proj[k] = ref.blocks[9 + k]
        pack = ref.pack
        ref.proj[4] = pack[40 : 40 + own]
        tail = jnp.concatenate([ref.blocks[13], ref.blocks[14]], axis=1)
        width = 2 * c
        for t in range(9):
            ref.side[t] = pltpu.roll(tail, (width - t * low_width) % width, 1)[:, 0:low_width]
        cls = pltpu.roll(tail, width - 9 * low_width, 1)[:, 0:128]
        cls = jnp.concatenate([cls, jnp.zeros((128 - own, 128), f32)], axis=0)
        ref.cls[...] = cls.T[0:classes, 0:own]
        ref.gain[...] = pack[0:8, 0:own]
        ref.shift[...] = pack[8:16, 0:own]
        ref.bias[...] = pack[16:17, 0:classes]
        ref.low_gain[...] = pack[17:18, 0:low_width]
        ref.low_shift[...] = pack[18:19, 0:low_width]

    def first():
        branch(0)
        ref.features[...] = ref.features_in[...]

    def second():
        branch(1)
        low_features()

    def third():
        branch(2)
        small()

    for k, body in enumerate((first, second, third)):
        pl.when(step == k)(body)


def finish(shapes, *args):
    parts = FinishRefs(*args, *([None] * (len(FinishRefs._fields) - len(args))))
    c_in, c = parts.point_part.shape
    whole = lambda v: pl.BlockSpec(v.shape, lambda k, r=len(v.shape): (0,) * r)
    piece = pl.BlockSpec((1, 9, c_in, c), lambda k: (k, 0, 0, 0))
    outs = [jax.ShapeDtypeStruct(shape, f32) for shape in shapes]
    return pl.pallas_call(
        finish_kernel,
        grid=(3,),
        out_shape=outs,
        in_specs=[piece] + [whole(v) for v in args[1:]],
        out_specs=[piece if v.shape == args[0].shape else whole(v) for v in outs],
        scratch_shapes=[pltpu.VMEM((FA * FA, 3 * c_in), bf16)],
        compiler_params=pltpu.CompilerParams(vmem_limit_bytes=60 * 1024 * 1024),
    )(*args)


def per_device(
    features,
    low_in,
    offsets,
    d_logits,
    w_point,
    w_atrous,
    w_pool,
    w_proj,
    w_low,
    w_dec1,
    w_dec1_low,
    w_dec2,
    w_cls,
    b_cls,
    bn_gain,
    bn_shift,
    low_gain,
    low_shift,
):
    n = lax.axis_size("chan")
    crops = lax.axis_size("crop")
    me = lax.axis_index("chan")
    fine = low_in.shape[2]
    rows = fine // n
    coarse_rows = FA // n
    channels = w_dec2.shape[2]
    c_in = features.shape[1]
    low_width = w_low.shape[1]
    coarse_samples = FA * FA * crops
    fine_samples = fine * fine * crops

    classes = w_cls.shape[1]
    spare = 32 - classes
    outer_grad = jnp.pad(d_logits[0], ((0, spare), (1, 1), (0, 0)))
    outer_grad = lax.dynamic_slice_in_dim(outer_grad, me * rows, rows + 2, 1)
    low_flat = low_in[0].reshape(low_in.shape[1], fine * fine)
    logits, branch_grad, low_pre_bf, pack, dec2_wgrad, blocks, source_all = decoder(
        crops,
        n,
        (coarse_samples, fine_samples),
        offsets,
        features[0],
        w_point,
        w_atrous.reshape(3, 3, 3 * c_in, channels),
        w_pool,
        low_flat,
        w_low,
        w_proj,
        w_dec1,
        w_dec1_low.transpose(0, 2, 1),
        w_dec2,
        w_cls.T,
        bn_gain,
        bn_shift,
        low_gain[None],
        low_shift[None],
        b_cls[None],
        outer_grad.reshape(32, (rows + 2) * fine),
    )
    feature_grad, point_wgrad, atrous_wgrad, pool_wgrad, low_wgrad, blocks, low_full, last_grad, last_src = (
        pyramid_back(
            crops,
            n,
            branch_grad,
            source_all,
            w_point,
            w_atrous,
            w_pool,
            pack,
            low_pre_bf,
            low_flat,
            blocks,
        )
    )
    own = w_dec2.shape[1]
    shapes = [
        (classes, rows, fine),
        (c_in, FA * FA),
        low_in.shape[1:],
        (c_in, channels),
        (3, 9, c_in, channels),
        (c_in, channels),
        (5, own, channels),
        (low_in.shape[1], low_width),
        (9, own, channels),
        (9, own, low_width),
        (9, own, channels),
        (classes, own),
        (1, classes),
        (8, own),
        (8, own),
        (1, low_width),
        (1, low_width),
    ]
    outs = finish(
        shapes,
        atrous_wgrad,
        point_wgrad,
        last_grad,
        last_src,
        feature_grad,
        pool_wgrad,
        low_full,
        w_low,
        low_wgrad,
        logits,
        dec2_wgrad,
        blocks,
        pack,
    )
    outs = list(outs)
    for k in (0, 1, 2):
        outs[k] = outs[k][None]
    for k in (12, 15, 16):
        outs[k] = outs[k][0]
    outs[9] = outs[9].transpose(0, 2, 1)
    outs[11] = outs[11].T
    return tuple(outs)


def solution(mesh):
    placed = (
        P("crop", "chan", None),
        P("crop", "chan", None, None),
        P("crop", None),
        P("crop", None, None, None),
        P("chan", None),
        P(None, None, "chan", None),
        P("chan", None),
        P(None, "chan", None),
        P("chan", None),
        P(None, "chan", None),
        P(None, None, "chan"),
        P(None, "chan", None),
        P("chan", None),
        P(),
        P(None, "chan"),
        P(None, "chan"),
        P(),
        P(),
    )
    return jax.shard_map(
        per_device,
        mesh=mesh,
        in_specs=placed,
        out_specs=(
            P("crop", None, "chan", None),
            P("crop", "chan", None),
            P("crop", "chan", None, None),
            P("chan", None),
            P(None, None, "chan", None),
            P("chan", None),
            P(None, "chan", None),
            P("chan", None),
            P(None, "chan", None),
            P(None, None, "chan"),
            P(None, "chan", None),
            P("chan", None),
            P(),
            P(None, "chan"),
            P(None, "chan"),
            P(),
            P(),
        ),
        check_vma=False,
    )
```

```python
import functools
import typing

import jax
import jax.numpy as jnp
from jax import lax
from jax.experimental import pallas as pl
from jax.experimental.pallas import tpu as pltpu
from jax.sharding import PartitionSpec as P

FA = 32
SCENE_H = 1024
SCENE_W = 2048

epsilon = 1e-05
highest = lax.Precision.HIGHEST
atrous_rates = (6, 12, 18)
f32 = jnp.float32
bf16 = jnp.bfloat16
BOTH = ("crop", "chan")


MESH = pl.DeviceIdType.MESH


def chip_peers(crops, n):
    my_crop, me = lax.axis_index("crop"), lax.axis_index("chan")
    core = lax.rem(me, 2)
    chips = n // 2
    other = (my_crop, me + 1 - 2 * core)
    far = []
    for i in range(crops):
        for j in range(chips):
            if i or j:
                far.append((lax.rem(my_crop + i, crops), lax.rem(me + 2 * j, n)))
    return other, far


GELU_A = 0.7978845608028654
GELU_B = 0.044715


def gelu(x):
    return 0.5 * x * (1.0 + jnp.tanh(GELU_A * (x + GELU_B * x * x * x)))


def gelu_both(x):
    square = x * x
    t = jnp.tanh(GELU_A * x * (1.0 + GELU_B * square))
    upper = 0.5 * (1.0 + t)
    return x * upper, upper + (0.5 * GELU_A) * x * (1.0 - t * t) * (1.0 + (3.0 * GELU_B) * square)


def gelu_slope(x):
    square = x * x
    t = jnp.tanh(GELU_A * x * (1.0 + GELU_B * square))
    return 0.5 * (1.0 + t) + (0.5 * GELU_A) * x * (1.0 - t * t) * (1.0 + (3.0 * GELU_B) * square)


def dot(a, b):
    return jnp.dot(a, b, preferred_element_type=f32)


def dot_nt(a, b):
    return lax.dot_general(a, b, (((1,), (1,)), ((), ())), preferred_element_type=f32)


def dot_tn(a, b):
    return lax.dot_general(a, b, (((0,), (0,)), ((), ())), preferred_element_type=f32)


def dot_exact(table, values):
    high = values.astype(bf16)
    rest = values - high.astype(f32)
    middle = rest.astype(bf16)
    low = (rest - middle.astype(f32)).astype(bf16)
    return dot(table, high) + (dot(table, middle) + dot(table, low))


def fold(values):
    return jnp.sum(values.reshape(values.shape[0] // 8, 8, values.shape[1]), axis=0)


def row_of(values):
    return jnp.sum(values, axis=0, keepdims=True)


def barrier_with(peers):
    barrier = pltpu.get_barrier_semaphore()
    for peer in peers:
        pl.semaphore_signal(barrier, inc=1, device_id=peer, device_id_type=MESH)
    return lambda: pl.semaphore_wait(barrier, len(peers))


def remote(src, dst, send, recv, peer):
    return pltpu.make_async_remote_copy(
        src_ref=src, dst_ref=dst, send_sem=send, recv_sem=recv, device_id=peer, device_id_type=MESH
    )


class Copies:
    def __init__(self, send, recv):
        self.send, self.recv, self.all, self.next = send, recv, [], 0

    def make(self, src, dst, peer, send=None):
        k = self.next
        self.next += 1
        return remote(src, dst, self.send.at[k if send is None else send], self.recv.at[k], peer)

    def start(self, src, dst, peer):
        copy = self.make(src, dst, peer)
        copy.start()
        self.all.append(copy)
        return copy

    def drain(self, kept):
        for copy in self.all:
            if not any(copy is other for other in kept):
                copy.wait_send()


class LineSum:
    def __init__(self, n, copies, staged, arrived, spare, refill):
        my_crop, me = lax.axis_index("crop"), lax.axis_index("chan")
        core, self.chip = lax.rem(me, 2), lax.div(me, 2)
        self.chips, self.copies, self.staged, self.arrived = n // 2, copies, staged, arrived
        self.spare, self.refill = spare, refill
        self.peer = lambda z: (my_crop, 2 * z + core)
        self.line = self.chips == 4
        if self.line:
            self.beside = self.chip + 1 - 2 * lax.rem(self.chip, 2)
            self.over = lax.rem(self.chip + 2, 4)
            self.mirror = 3 - self.chip
            self.end = jnp.logical_or(self.chip == 0, self.chip == 3)
            self.inner = jnp.logical_not(self.end)

    def send(self, z):
        return self.copies.start(self.staged.at[z], self.arrived.at[self.chip], self.peer(z))

    def start(self):
        if not self.line:
            targets = [lax.rem(self.chip + j, self.chips) for j in range(1, self.chips)]
            self.direct = [self.send(z) for z in targets]
            return
        here = self.staged.at[self.mirror]
        k = self.copies.next
        self.passed = self.copies.make(here, self.spare, self.peer(self.beside))
        self.middle = self.copies.make(here, self.arrived.at[self.chip], self.peer(self.mirror), k)
        self.copies.all.append(self.passed)
        pl.when(self.end)(self.passed.start)
        pl.when(self.inner)(self.middle.start)
        self.first = self.send(self.beside)

    def second(self):
        if not self.line:
            return

        def merge():
            self.passed.wait_recv()
            both = self.refill(self.over) + self.spare[...].astype(f32)
            self.staged[self.over] = both.astype(bf16)

        pl.when(self.inner)(merge)
        self.crossed = self.send(self.over)

    def finish(self, add):
        if not self.line:
            for j in range(1, self.chips):
                self.direct[j - 1].wait_recv()
                add(self.arrived[lax.rem(self.chip - j + self.chips, self.chips)].astype(f32))
            return
        self.first.wait_recv()
        add(self.arrived[self.beside].astype(f32))

        def third():
            self.middle.wait_recv()
            add(self.arrived[self.mirror].astype(f32))

        pl.when(self.inner)(third)
        self.crossed.wait_recv()
        add(self.arrived[self.over].astype(f32))


def shift_three(source, target, rate, first, last):
    column = lax.rem(lax.broadcasted_iota(jnp.int32, (128, 1), 0), FA)

    def step(i, kept):
        base = pl.multiple_of(i * 128, 128)
        here = source(base)
        w = here.shape[1]
        wide = here.astype(f32)
        for slot, by in ((0, first), (2, last)):
            ok = jnp.logical_and(column + by >= 0, column + by < FA)
            moved = jnp.where(ok, pltpu.roll(wide, (-by) % 128, 0), 0.0)
            target[pl.ds(base, 128), slot * w : (slot + 1) * w] = moved.astype(bf16)
        target[pl.ds(base, 128), w : 2 * w] = here
        return kept

    lax.fori_loop(0, FA * FA // 128, step, 0)


class Swap:
    def __init__(self, crops, n, pair, slots, pair_sems, send, recv):
        self.other, self.far = chip_peers(crops, n)
        me = lax.axis_index("chan")
        self.core = lax.rem(me, 2)
        self.mine = lax.axis_index("crop") * (n // 2) + lax.div(me, 2)
        self.pair, self.slots, self.pair_sems = pair, slots, pair_sems
        self.send, self.recv = send, recv

    def start(self):
        here = self.pair.at[self.core]
        copy = remote(here, here, self.pair_sems.at[0], self.pair_sems.at[1], self.other)
        copy.start()
        copy.wait()
        self.slots[self.mine] = self.pair[0] + self.pair[1]
        self.copies = []
        for k, peer in enumerate(self.far):
            slot = self.slots.at[self.mine]
            copy = remote(slot, slot, self.send.at[k], self.recv.at[k], peer)
            copy.start()
            self.copies.append(copy)

    def finish(self):
        for copy in self.copies:
            copy.wait_recv()
        return jnp.sum(self.slots[...], axis=0)

    def drain(self):
        for copy in self.copies:
            copy.wait_send()


class WideSwap:
    def __init__(self, crops, n, pair, first, second, pair_sems, send, recv):
        my_crop, me = lax.axis_index("crop"), lax.axis_index("chan")
        self.core, self.crop, self.chip = lax.rem(me, 2), my_crop, lax.div(me, 2)
        self.other = (my_crop, me + 1 - 2 * self.core)
        self.over_crops = [(lax.rem(my_crop + i, crops), me) for i in range(1, crops)]
        self.over_chips = [(my_crop, lax.rem(me + 2 * j, n)) for j in range(1, n // 2)]
        self.pair, self.first, self.second = pair, first, second
        self.pair_sems, self.send, self.recv = pair_sems, send, recv

    def run(self, then=None):
        here = self.pair.at[self.core]
        copy = remote(here, here, self.pair_sems.at[0], self.pair_sems.at[1], self.other)
        copy.start()
        copy.wait()
        self.first[self.crop] = self.pair[0] + self.pair[1]
        k = 0
        copies = []
        for peer in self.over_crops:
            slot = self.first.at[self.crop]
            copies.append(remote(slot, slot, self.send.at[k], self.recv.at[k], peer))
            copies[-1].start()
            k += 1
        for copy in copies:
            copy.wait()
        self.second[self.chip] = jnp.sum(self.first[...], axis=0)
        copies = []
        for peer in self.over_chips:
            slot = self.second.at[self.chip]
            copies.append(remote(slot, slot, self.send.at[k], self.recv.at[k], peer))
            copies[-1].start()
            k += 1
        if then is not None:
            then()
        for copy in copies:
            copy.wait()
        return jnp.sum(self.second[...], axis=0)


def put_pair(ref, core, a, b):
    ref[core, 0:1] = a[:, :128]
    ref[core, 1:2] = a[:, 128:]
    ref[core, 2:3] = b[:, :128]
    ref[core, 3:4] = b[:, 128:]


def get_pair(total):
    return (
        jnp.concatenate([total[0:1], total[1:2]], axis=1),
        jnp.concatenate([total[2:3], total[3:4]], axis=1),
    )


def spread_row(row):
    return jnp.broadcast_to(row, (128, 128)).T


def up_weights(i, me, n, rows, coarse_rows):
    lower = (2 * i - 3) // 8
    upper_weight = (2 * i - 3 - 8 * lower) / 8.0
    a, b = 1.0 - upper_weight, upper_weight
    if lower < 0:
        top = me == 0
        a, b = jnp.where(top, 0.0, a), jnp.where(top, 1.0, b)
    if lower + 1 >= coarse_rows:
        bottom = me == n - 1
        a, b = jnp.where(bottom, 1.0, a), jnp.where(bottom, 0.0, b)
    if i < 0:
        a, b = jnp.where(me == 0, 0.0, a), jnp.where(me == 0, 0.0, b)
    if i >= rows:
        a, b = jnp.where(me == n - 1, 0.0, a), jnp.where(me == n - 1, 0.0, b)
    return lower + 1, a, b


class DecoderRefs(typing.NamedTuple):
    offsets: object
    feat: object
    point: object
    atrous_hbm: object
    pool_w: object
    low_rows: object
    low_w: object
    w_proj: object
    w_dec1: object
    w_side: object
    w_dec2: object
    w_cls: object
    own_gain: object
    own_shift: object
    low_gain: object
    low_shift: object
    bias: object
    dlog: object
    logits_hbm: object
    branch_hbm: object
    low_hbm: object
    pack_hbm: object
    dec2_hbm: object
    wgrads_hbm: object
    src_all: object
    low_flat: object
    low_in: object
    atrous: object
    src_own: object
    logits: object
    branch_out: object
    low_out: object
    pack: object
    dec2_w: object
    wgrads: object
    low_ext: object
    low_push: object
    lowx: object
    merged_ext: object
    merged_part: object
    dec1: object
    dec2: object
    pushed: object
    pushed1: object
    x1: object
    x2: object
    g2: object
    g1: object
    yt: object
    branch_bf: object
    proj_bf: object
    second: object
    flip: object
    branch: object
    staged: object
    arrived: object
    low_send: object
    low_pair: object
    low_sum: object
    low_recv: object
    spare: object
    low_spare: object
    gath: object
    norms_all: object
    norms: object
    proj: object
    w1: object
    tail: object
    w1low: object
    w2: object
    cls_all: object
    cls_t: object
    dmask: object
    columns: object
    own_w: object
    r_first: object
    r_pairs: object
    r_crossed: object
    r_halves: object
    r_lined: object
    r_out: object
    local: object
    f_send: object
    f_recv: object


def rest_groups(crops):
    return -(-15 // crops) * crops


def weight_groups(crops):
    return -(-8 // crops) * crops, -(-9 // crops) * crops


def decoder_kernel(crops, n, samples, *refs):
    ref = DecoderRefs(*refs[: len(DecoderRefs._fields)])
    rest = list(refs[len(DecoderRefs._fields) :])
    (wide_pair, wide_first, wide_second, wide_psem, wide_send, wide_recv) = rest[:6]
    (pair, slots, psem, send, recv, halo_send, halo_recv) = rest[6:13]

    coarse_samples, fine_samples = samples
    my_crop, me = lax.axis_index("crop"), lax.axis_index("chan")
    core = lax.rem(me, 2)
    above = (my_crop, lax.rem(me + n - 1, n))
    below = (my_crop, lax.rem(me + 1, n))
    low_chans, low_width = ref.low_w.shape
    classes = ref.w_cls.shape[0]
    rows = ref.dlog.shape[1] // 128 - 2
    fine_cells = rows * 128
    coarse_cells = ref.branch.shape[0]
    coarse_rows = coarse_cells // FA
    cells = FA * FA
    c_in, c = ref.point.shape
    own = c // n
    chips, chip = n // 2, lax.div(me, 2)
    small, large = weight_groups(crops)
    chunk = min(4, rows)

    other, far = chip_peers(crops, n)
    over_crops = [(lax.rem(my_crop + i, crops), me) for i in range(1, crops)]
    over_chips = [(my_crop, lax.rem(me + 2 * j, n)) for j in range(1, chips)]
    wait_barrier = barrier_with([other, above, below] + far)

    swaps = [
        Swap(crops, n, pair.at[i], slots.at[i], psem.at[i], send.at[0 if i == 6 else (i + 1) % 2], recv.at[i])
        for i in range(pair.shape[0])
    ]
    wides = [
        WideSwap(
            crops, n, wide_pair.at[i], wide_first.at[i], wide_second.at[i],
            wide_psem.at[i], wide_send.at[i], wide_recv.at[i],
        )
        for i in range(2)
    ]
    front = Copies(ref.f_send, ref.f_recv)
    for i in range(pair.shape[0]):
        pair[i, core] = jnp.zeros((8, 128), f32)
    for i in range(2):
        wide_pair[i, core] = jnp.zeros(wide_pair.shape[2:], f32)

    def halo(i, first, last, to_above, to_below):
        copies = [
            remote(first, to_above, halo_send.at[i, 0], halo_recv.at[i, 0], above),
            remote(last, to_below, halo_send.at[i, 1], halo_recv.at[i, 1], below),
        ]
        for copy in copies:
            copy.start()
        return copies

    def fine_halo(i, values):
        return halo(
            i,
            values.at[pl.ds(128, 128)],
            values.at[pl.ds(rows * 128, 128)],
            values.at[pl.ds((rows + 1) * 128, 128)],
            values.at[pl.ds(0, 128)],
        )

    def gain(k):
        return ref.norms[k : k + 1]

    def shift(k):
        return ref.norms[8 + k : 9 + k]

    def moments(total, square, count):
        average = total * (1.0 / count)
        return average, lax.rsqrt(square * (1.0 / count) - average * average + epsilon)

    column = lax.broadcasted_iota(jnp.int32, (128, c), 0)

    def put_three(target, base, y):
        target[pl.ds(base, 128), 0:c] = jnp.where(column == 0, 0.0, pltpu.roll(y, 1, 0)).astype(bf16)
        target[pl.ds(base, 128), c : 2 * c] = y.astype(bf16)
        target[pl.ds(base, 128), 2 * c : 3 * c] = jnp.where(
            column == 127, 0.0, pltpu.roll(y, 127, 0)
        ).astype(bf16)

    def inside(i):
        at_top = jnp.logical_and(me == 0, i == 0)
        at_bottom = jnp.logical_and(me == n - 1, i == rows + 1)
        return jnp.where(jnp.logical_or(at_top, at_bottom), 0.0, 1.0)

    def each_row(body, first, last, carry):
        def step(i, kept):
            return body(i, pl.multiple_of(i * 128, 128), kept)

        return lax.fori_loop(first, last, step, carry)

    zero = jnp.zeros((8, c), f32)

    src_all, src_own, gath = ref.src_all, ref.src_own, ref.gath
    local_copies = []

    def local(src, dst):
        copy = pltpu.make_async_copy(src, dst, ref.local.at[len(local_copies)])
        copy.start()
        local_copies.append(copy)

    local(ref.atrous_hbm, ref.atrous)
    for i in range(cells // 256):
        src_own[pl.ds(i * 256, 256)] = ref.feat[:, i * 256 : (i + 1) * 256].T
    local(src_own, src_all.at[my_crop])
    for i in range(0, ref.low_rows.shape[1], 16):
        here = ref.low_rows[:, i : i + 16].astype(f32)
        ref.low_in[:, i * 128 : (i + 16) * 128] = here.reshape(low_chans, 16 * 128).astype(bf16)
    local(ref.low_in, ref.low_flat)
    flip = ref.flip
    flip[...] = jnp.zeros(flip.shape, f32)
    flip[0:classes, 0:own] = ref.w_cls[...].astype(f32)
    own_cls = flip[0:128, 0:128].T[0:own, 0:classes].astype(bf16)
    flip[0:classes, 0:own] = jnp.zeros((classes, own), f32)
    for t in range(9):
        flip[0:own, 128:256] = jnp.zeros((own, 128), f32)
        flip[0:own, 128 : 128 + low_width] = ref.w_side[t].astype(f32)
        flip[t * low_width : (t + 1) * low_width, 0:128] = flip[0:128, 128:256].T[0:low_width]
    for k in range(5):
        gath[me, k] = ref.w_proj[k]
    turned = flip[:, 0:128].T[0:own].astype(bf16)
    gath[me, 5] = turned[:, 0:c]
    gath[me, 6] = turned[:, c : 2 * c]
    gath[me, 7] = jnp.zeros((own, c), bf16)
    gath[me, 7, :, 0:classes] = own_cls
    for k in range(8, small):
        gath[me, k] = jnp.zeros((own, c), bf16)
    for t in range(9, large):
        gath[me, small + t] = jnp.zeros((own, c), bf16)
        gath[me, small + large + t] = jnp.zeros((own, c), bf16)
    for t in range(9):
        gath[me, small + t] = ref.w_dec1[t]
        gath[me, small + large + t] = ref.w_dec2[t]
    columns = ref.columns
    columns[...] = jnp.zeros(columns.shape, f32)
    columns[0:1, 0:low_width] = ref.low_gain[...]
    columns[1:2, 0:low_width] = ref.low_shift[...]
    columns[2:3, 0:classes] = ref.bias[...]
    ref.norms_all[me] = jnp.zeros((16, 128), f32)
    ref.norms_all[me, 0:8, 0:own] = ref.own_gain[...]
    ref.norms_all[me, 8:16, 0:own] = ref.own_shift[...]
    wait_barrier()
    block_of = lambda j: lax.rem(me - 2 * j + n, n)
    crop_of = lambda i: lax.rem(my_crop - i + crops, crops)

    class Spread:
        def __init__(self, first, size):
            per = size // crops
            self.at = lambda b, q: gath.at[b, pl.ds(first + q * per, per)]
            self.first, self.size = first, size

        def start(self):
            here = self.at(me, my_crop)
            self.far = [front.start(here, here, peer) for peer in over_chips]
            here = gath.at[me, pl.ds(self.first, self.size)]
            self.pairs = [front.start(here, here, other)]

        def cross(self):
            self.crossed = []
            for j in range(1, chips):
                self.far[j - 1].wait_recv()
                here = self.at(block_of(j), my_crop)
                for i in range(1, crops):
                    self.crossed.append((i, j, front.start(here, here, over_crops[i - 1])))
                self.pairs.append(front.start(here, here, other))

        def cores(self):
            for i, j, copy in self.crossed:
                copy.wait_recv()
                here = self.at(block_of(j), crop_of(i))
                self.pairs.append(front.start(here, here, other))

        def finish(self):
            for copy in self.pairs:
                copy.wait_recv()

    norm_far = []
    here = ref.norms_all.at[me]
    for peer in over_chips:
        norm_far.append(front.start(here, here, peer))
    norm_pairs = [front.start(here, here, other)]
    spread = [Spread(0, small), Spread(small, large), Spread(small + large, large)]
    spread[0].start()
    spread[1].start()
    feature_copies = [front.start(src_own, src_all.at[my_crop], peer) for peer in over_crops]
    low_send, low_pair = ref.low_send, ref.low_pair

    def low_block(b):
        span = pl.ds(pl.multiple_of(b * fine_cells, fine_cells), fine_cells)
        return dot_tn(ref.low_w[...], ref.low_in[:, span])

    low_copies = []
    for z in range(chips):
        low_send[z] = low_block(2 * z + 1 - core)
        low_copies.append(front.start(low_send.at[z], low_pair.at[z], other))
    part, part_in, staged, arrived = ref.pushed, ref.pushed1, ref.staged, ref.arrived
    shifted = ref.g2

    order = (0, 3, 2, 1)

    def branch_partial(k):
        first = k * cells
        if k == 0:
            part[pl.ds(first, cells)] = dot(src_own[...], ref.point[...])
        else:
            rate = atrous_rates[k - 1]
            if k == order[1]:
                local_copies[0].wait()
            shift_three(lambda base: src_own[pl.ds(base, 128)], shifted, rate, -rate, rate)
            part[pl.ds(first, cells)] = dot(shifted[pl.ds(0, cells), 0 : 3 * c_in], ref.atrous[k - 1, 1])
            for a in (0, 2):
                move = (a - 1) * rate
                count = (FA - abs(move)) * FA
                to, off = first + max(-move, 0) * FA, max(move, 0) * FA
                part[pl.ds(to, count)] += dot(shifted[pl.ds(off, count), 0 : 3 * c_in], ref.atrous[k - 1, a])
        copies = []
        for z in range(chips):
            block = pl.multiple_of(first + (2 * z + 1 - core) * coarse_cells, coarse_cells)
            copies.append(
                front.start(
                    part.at[pl.ds(block, coarse_cells)],
                    part_in.at[pl.ds((k * chips + z) * coarse_cells, coarse_cells)],
                    other,
                )
            )
        return copies

    def pair_sum(k, z):
        block = pl.multiple_of(k * cells + (2 * z + core) * coarse_cells, coarse_cells)
        landed = pl.multiple_of((k * chips + z) * coarse_cells, coarse_cells)
        return part[pl.ds(block, coarse_cells)] + part_in[pl.ds(landed, coarse_cells)]

    waited = []
    branch_lines = [
        LineSum(n, front, staged.at[k], arrived.at[k], ref.spare.at[k], functools.partial(pair_sum, k))
        for k in range(4)
    ]

    def branch_out(k, copies):
        for copy in copies:
            copy.wait()
            waited.append(copy)
        for z in range(chips):
            staged[k, z] = pair_sum(k, z).astype(bf16)
        ref.branch[:, k * c : (k + 1) * c] = pair_sum(k, chip)
        branch_lines[k].start()

    before = branch_partial(order[0])
    for at in range(1, 4):
        after = branch_partial(order[at])
        branch_out(order[at - 1], before)
        before = after
        if at == 2:
            spread[0].cross()
        if at == 1:
            for z in range(chips):
                low_copies[z].wait_recv()
                ref.low_sum[z] = (low_block(2 * z + core) + low_pair[z]).astype(bf16)
            low_line = LineSum(
                n, front, ref.low_sum, ref.low_recv, ref.low_spare, lambda z: low_block(2 * z + core) + low_pair[z]
            )
            low_line.start()
        if at == 2:
            branch_lines[order[0]].second()
        if at == 3:
            spread[1].cross()
            low_line.second()
            branch_lines[order[1]].second()
    branch_out(order[3], before)
    branch_lines[order[2]].second()
    for j in range(1, chips):
        norm_far[j - 1].wait_recv()
        here = ref.norms_all.at[block_of(j)]
        norm_pairs.append(front.start(here, here, other))
    pooled = row_of(src_own[...].astype(f32)) * (1.0 / cells)
    pooled = jnp.concatenate([pooled, jnp.zeros((15, c_in), f32)], axis=0).astype(bf16)
    pool_part = dot(pooled, ref.pool_w[...])[0:1]

    branch_lines[order[3]].second()
    for copy in norm_pairs:
        copy.wait_recv()
    for b in range(n):
        ref.norms[:, b * own : (b + 1) * own] = ref.norms_all[b, :, 0:own]

    low_ext = ref.low_ext
    own_low = pl.ds(128, fine_cells)
    low_ext[:, own_low] = low_block(me) + low_pair[chip]

    def add_to_low(value):
        low_ext[:, own_low] += value

    low_line.finish(add_to_low)
    low_edges = halo(
        0,
        low_ext.at[:, pl.ds(128, 128)],
        low_ext.at[:, pl.ds(rows * 128, 128)],
        low_ext.at[:, pl.ds((rows + 1) * 128, 128)],
        low_ext.at[:, pl.ds(0, 128)],
    )

    def add_low(i, base, kept):
        v = low_ext[:, pl.ds(base, 128)]
        return kept[0] + v, kept[1] + v * v

    low_zero = jnp.zeros((low_width, 128), f32)
    low_sum, low_square = each_row(add_low, 1, rows + 1, (low_zero, low_zero))

    def lanes_of(values):
        return row_of(values.T)

    pair[6, core, 0:1, 0:low_width] = lanes_of(low_sum)
    pair[6, core, 1:2, 0:low_width] = lanes_of(low_square)
    swaps[6].start()

    for k in order:

        def add_to_branch(value, k=k):
            ref.branch[:, k * c : (k + 1) * c] += value

        branch_lines[k].finish(add_to_branch)

    spread[0].cores()
    spread[1].cores()
    wide = wide_pair.at[0]
    for k in range(4):
        v = ref.branch[:, k * c : (k + 1) * c]
        wide[core, k : k + 1] = row_of(v)
        wide[core, 4 + k : 5 + k] = row_of(v * v)
    wide[core, 8:16] = jnp.where(
        lax.broadcasted_iota(jnp.int32, (8, c), 0) == my_crop, pool_part, 0.0
    )
    total_a = wides[0].run(spread[2].start)
    spread[0].finish()
    proj, w1, w2, tail = ref.proj, ref.w1, ref.w2, ref.tail
    for b in range(n):
        mine = pl.ds(b * own, own)
        for k in range(5):
            proj[k, mine] = gath[b, k]

    def place_conv(target, first):
        for b in range(n):
            for t in range(9):
                a, e = t // 3, t % 3
                target[a, pl.ds(e * c + b * own, own)] = gath[b, first + t]

    def branch_parts(k):
        average, inverse = moments(total_a[k : k + 1], total_a[4 + k : 5 + k], coarse_samples)
        normed = (ref.branch[:, k * c : (k + 1) * c] - average) * inverse
        return normed, gain(k) * normed + shift(k), inverse

    projected = jnp.zeros((coarse_cells, c), f32)
    for k in range(4):
        y = gelu(branch_parts(k)[1]).astype(bf16)
        ref.branch_bf[:, k * c : (k + 1) * c] = y
        projected = projected + dot(y, ref.proj[k])
    pool_here = lax.broadcasted_iota(jnp.int32, (8, c), 0) < crops
    pool_pre = total_a[8:16]
    pool_average = row_of(pool_pre) * (1.0 / crops)
    pool_spread = jnp.where(pool_here, pool_pre - pool_average, 0.0)
    pool_inverse = lax.rsqrt(row_of(pool_spread * pool_spread) * (1.0 / crops) + epsilon)
    pool_normed = pool_spread * pool_inverse
    pool_before = gain(4) * pool_normed + shift(4)
    pool_bf = gelu(pool_before)
    pool_bf = jnp.concatenate([pool_bf, jnp.zeros((8, c), f32)], axis=0).astype(bf16)
    pool_term = dot(pool_bf, ref.proj[4])
    my_row = lax.broadcasted_iota(jnp.int32, (16, c), 0) == my_crop
    projected = projected + row_of(jnp.where(my_row, pool_term, 0.0))
    merged_ext = ref.merged_ext
    merged_ext[pl.ds(FA, coarse_cells)] = projected
    put_pair(pair.at[0], core, row_of(projected), row_of(projected * projected))
    merged_copies = halo(
        1,
        merged_ext.at[pl.ds(FA, FA)],
        merged_ext.at[pl.ds(coarse_cells, FA)],
        merged_ext.at[pl.ds(FA + coarse_cells, FA)],
        merged_ext.at[pl.ds(0, FA)],
    )
    swaps[0].start()

    total_l = swaps[6].finish()
    for copy in low_edges:
        copy.wait()
    low_average = total_l[0:1] * (1.0 / fine_samples)
    low_variance = total_l[1:2] * (1.0 / fine_samples) - low_average * low_average
    low_inverse_row = lax.rsqrt(low_variance + epsilon)
    low_average = spread_row(low_average)[0:low_width]
    low_inverse = spread_row(low_inverse_row)[0:low_width]
    lane = lax.broadcasted_iota(jnp.int32, (low_width, 128), 1)
    low_gain = spread_row(columns[0:1])[0:low_width]
    low_shift = spread_row(columns[1:2])[0:low_width]

    def low_parts(base):
        normed = (low_ext[:, pl.ds(base, 128)] - low_average) * low_inverse
        return normed, low_gain * normed + low_shift

    def low_row(i, base, kept):
        y = gelu(low_parts(base)[1]) * inside(i)
        lowx = ref.lowx
        lowx[0:low_width, pl.ds(base, 128)] = jnp.where(lane == 0, 0.0, pltpu.roll(y, 1, 1)).astype(bf16)
        lowx[low_width : 2 * low_width, pl.ds(base, 128)] = y.astype(bf16)
        lowx[2 * low_width : 3 * low_width, pl.ds(base, 128)] = jnp.where(
            lane == 127, 0.0, pltpu.roll(y, 127, 1)
        ).astype(bf16)
        return kept

    each_row(low_row, 0, rows + 2, 0)

    for b in range(n):
        mine = pl.ds(b * own, own)
        tail[mine, 0:c] = gath[b, 5]
        tail[mine, c : 2 * c] = gath[b, 6]
        ref.cls_all[mine] = gath[b, 7, :, 0:128]
    turned = tail[...].T
    for a in range(3):
        ref.w1low[a] = turned[a * 3 * low_width : (a + 1) * 3 * low_width]
    cls_lane = lax.broadcasted_iota(jnp.int32, (c, 128), 1)
    cls_clean = jnp.where(cls_lane < classes, ref.cls_all[...].astype(f32), 0.0)
    ref.cls_t[...] = cls_clean.T[0:32].astype(bf16)
    spread[2].cross()
    merged_sum, merged_square = get_pair(swaps[0].finish())
    for copy in merged_copies:
        copy.wait()
    merged_average, merged_inverse = moments(merged_sum, merged_square, coarse_samples)

    def merged_parts(first, count):
        normed = (merged_ext[pl.ds(first, count)] - merged_average) * merged_inverse
        return normed, gain(5) * normed + shift(5)

    fine_at = lax.broadcasted_iota(jnp.int32, (128, FA), 0).astype(f32)
    coarse_at = lax.broadcasted_iota(jnp.int32, (128, FA), 1).astype(f32)
    place = jnp.clip((fine_at + 0.5) / 4.0 - 0.5, 0.0, FA - 1.0)
    up = jnp.maximum(0.0, 1.0 - jnp.abs(place - coarse_at)).astype(bf16)
    coarse_wide = []
    for j in range(coarse_rows + 2):
        coarse_wide.append(dot_exact(up, gelu(merged_parts(j * FA, FA)[1])))
    for i in range(-1, rows + 1):
        lower, a, b = up_weights(i, me, n, rows, coarse_rows)
        put_three(ref.x1, (i + 1) * 128, a * coarse_wide[lower] + b * coarse_wide[lower + 1])
    spread[1].finish()
    place_conv(w1, small)
    dec1, dec2, pushed, pushed1 = ref.dec1, ref.dec2, ref.pushed, ref.pushed1

    def conv_piece(source, weight, base):
        total = None
        for a in range(3):
            term = dot(source[pl.ds(base + a * 128, chunk * 128)], weight[a])
            total = term if total is None else total + term
        return total

    def conv_loop(piece, target):
        def step(i, kept):
            base = pl.multiple_of(i * (chunk * 128), 128)
            total = piece(base)
            target[pl.ds(base + 128, chunk * 128)] = total
            return kept[0] + fold(total), kept[1] + fold(total * total)

        return lax.fori_loop(0, rows // chunk, step, (zero, zero))


    def first_piece(base):
        total = conv_piece(ref.x1, w1, base)
        for a in range(3):
            total = total + dot_tn(ref.lowx[:, pl.ds(base + a * 128, chunk * 128)], ref.w1low[a])
        return total

    total, square = conv_loop(first_piece, dec1)
    spread[2].cores()
    put_pair(pair.at[1], core, row_of(total), row_of(square))
    swaps[6].drain()
    swaps[1].start()
    dec1_copies = fine_halo(2, dec1)
    total, square = get_pair(swaps[1].finish())
    for copy in dec1_copies:
        copy.wait()
    first_average, first_inverse = moments(total, square, fine_samples)

    def first_parts(base):
        normed = (dec1[pl.ds(base, 128)] - first_average) * first_inverse
        return normed, gain(6) * normed + shift(6)

    def first_row(i, base, kept):
        put_three(ref.x2, base, gelu(first_parts(base)[1]) * inside(i))
        return kept

    each_row(first_row, 0, rows + 2, 0)
    spread[2].finish()
    place_conv(w2, small + large)
    total, square = conv_loop(lambda base: conv_piece(ref.x2, w2, base), dec2)
    put_pair(pair.at[2], core, row_of(total), row_of(square))
    swaps[0].drain()
    swaps[2].start()
    dec2_copies = fine_halo(3, dec2)
    total, square = get_pair(swaps[2].finish())
    for copy in dec2_copies:
        copy.wait()
    second_average, second_inverse = moments(total, square, fine_samples)

    cls_t = ref.cls_t[...]
    bias = spread_row(columns[2:3])[0:32]
    col_here = ref.offsets[0, 1] + 4 * lax.broadcasted_iota(jnp.int32, (1, 128), 1) < SCENE_W
    col_mask = jnp.where(col_here, 1.0, 0.0)

    def scene_mask(i):
        row_here = ref.offsets[0, 0] + 4 * (me * rows + i - 1) < SCENE_H
        return col_mask * jnp.where(row_here, 1.0, 0.0)

    def masked_row(i, base):
        return ref.dlog[:, pl.ds(base, 128)] * scene_mask(i).astype(bf16)

    def second_parts(base):
        normed = (dec2[pl.ds(base, 128)] - second_average) * second_inverse
        return normed, gain(7) * normed + shift(7)

    def second_row(i, base, kept):
        normed, before = second_parts(base)
        value, slope = gelu_both(before)
        ref.second[pl.ds(base, 128)] = value.astype(bf16)
        masked = masked_row(i, base)
        ref.dmask[:, pl.ds(base, 128)] = masked
        grad = dot_tn(masked, cls_t)
        push = slope * grad
        pushed[pl.ds(base, 128)] = push
        own_row = jnp.where(jnp.logical_and(i > 0, i < rows + 1), 1.0, 0.0)
        push = push * own_row
        return kept[0] + fold(push * normed), kept[1] + fold(push)

    along, summed = each_row(second_row, 0, rows + 2, (zero, zero))
    put_pair(pair.at[3], core, row_of(along), row_of(summed))
    swaps[1].drain()
    swaps[3].start()
    second = ref.second

    def logit_row(i, base, kept):
        out = pl.multiple_of(base - 128, 128)
        value = dot_nt(cls_t, second[pl.ds(base, 128)]) + bias
        ref.logits[:, pl.ds(out, 128)] = value * scene_mask(i)
        return kept

    each_row(logit_row, 1, rows + 1, 0)
    local(ref.logits, ref.logits_hbm)
    flip[pl.ds(9 * low_width, 32)] = dot(
        ref.dmask[:, 128 : 128 + fine_cells], second[pl.ds(128, fine_cells)]
    )
    bias_grad = jnp.zeros((32, 128), f32)
    for i in range(1, rows + 1):
        bias_grad = bias_grad + ref.dmask[:, i * 128 : (i + 1) * 128].astype(f32)
    wide_pair[1, core, 16:17, 0:32] = row_of(bias_grad.T)
    second_along, second_summed = get_pair(swaps[3].finish())

    def pull(push, normed, k, inverse, along, summed, count):
        return (gain(k) * inverse) * (push - summed * (1.0 / count) - normed * (along * (1.0 / count)))

    def dec2_row(i, base, kept):
        g = pull(
            pushed[pl.ds(base, 128)], second_parts(base)[0], 7, second_inverse,
            second_along, second_summed, fine_samples,
        )
        put_three(ref.g2, base, g * inside(i))
        return kept

    each_row(dec2_row, 0, rows + 2, 0)

    def back_loop(source, weight, use, carry):
        def step(i, kept):
            base = pl.multiple_of(i * (chunk * 128), 128)
            total = None
            for t in range(9):
                a, e = t // 3, t % 3
                piece = source[pl.ds(base + (2 - a) * 128, chunk * 128), (2 - e) * c : (3 - e) * c]
                term = dot_nt(piece, weight[a, e * c : (e + 1) * c])
                total = term if total is None else total + term
            return use(base, total, kept)

        return lax.fori_loop(0, rows // chunk, step, carry)

    def first_use(base, grad, kept):
        at = pl.ds(pl.multiple_of(base + 128, 128), chunk * 128)
        normed = (dec1[at] - first_average) * first_inverse
        push = gelu_slope(gain(6) * normed + shift(6)) * grad
        pushed1[at] = push
        return kept[0] + fold(push * normed), kept[1] + fold(push)

    along, summed = back_loop(ref.g2, ref.w2, first_use, (zero, zero))
    put_pair(pair.at[4], core, row_of(along), row_of(summed))
    swaps[2].drain()
    swaps[4].start()
    pushed_copies = fine_halo(4, pushed1)

    wgrads = ref.wgrads

    reduce_two = Reduce(
        crops, n, front, ref.own_w, ref.r_first, ref.r_pairs, ref.r_crossed, ref.r_halves, ref.r_lined, ref.r_out
    )

    def weight_grads(target, source, gradient):
        for a in range(3):
            part = dot_tn(
                source[pl.ds(a * 128, fine_cells), c : 2 * c], gradient[pl.ds(128, fine_cells)]
            ).astype(bf16)
            for e in range(3):
                tap = part[:, (2 - e) * c : (3 - e) * c]
                for h in range(n):
                    target[h, 3 * a + e] = tap[h * own : (h + 1) * own]

    weight_grads(ref.own_w, ref.x2, ref.g2)
    for t in range(9, large):
        for h in range(n):
            ref.own_w[h, t] = jnp.zeros((own, c), bf16)
    reduce_two.cores()
    first_along, first_summed = get_pair(swaps[4].finish())
    reduce_two.over_the_crops()
    for copy in pushed_copies:
        copy.wait()

    def dec1_row(i, base, kept):
        g = pull(
            pushed1[pl.ds(base, 128)], first_parts(base)[0], 6, first_inverse,
            first_along, first_summed, fine_samples,
        ) * inside(i)
        put_three(ref.g1, base, g)
        return kept

    each_row(dec1_row, 0, rows + 2, 0)

    def up_use(base, grad, kept):
        dec2[pl.ds(pl.multiple_of(base + 128, 128), chunk * 128)] = grad
        return kept

    back_loop(ref.g1, ref.w1, up_use, 0)
    yt = ref.yt

    def low_back_row(i, local, base, kept):
        total = None
        for t in range(9):
            a, e = t // 3, t % 3
            at = pl.ds((local + 2 - a) * 128, 128)
            piece = yt[t * low_width : (t + 1) * low_width, at]
            if e == 0:
                piece = jnp.where(lane == 127, 0.0, pltpu.roll(piece, 127, 1))
            if e == 2:
                piece = jnp.where(lane == 0, 0.0, pltpu.roll(piece, 1, 1))
            total = piece if total is None else total + piece
        normed, before = low_parts(base)
        push = gelu_slope(before) * total
        ref.low_push[:, pl.ds(pl.multiple_of(base - 128, 128), 128)] = push
        return kept[0] + push * normed, kept[1] + push

    def low_back_chunk(i, kept):
        base = pl.multiple_of(i * (chunk * 128), 128)
        here = ref.g1[pl.ds(base, (chunk + 2) * 128), c : 2 * c]
        for a in range(3):
            yt[a * 3 * low_width : (a + 1) * 3 * low_width] = dot_nt(ref.w1low[a], here)
        for local in range(chunk):
            kept = low_back_row(i, local, pl.multiple_of(base + (local + 1) * 128, 128), kept)
        return kept

    low_along, low_summed = lax.fori_loop(0, rows // chunk, low_back_chunk, (low_zero, low_zero))

    part = ref.merged_part
    fine_at = lax.broadcasted_iota(jnp.int32, (FA, 128), 1).astype(f32)
    coarse_at = lax.broadcasted_iota(jnp.int32, (FA, 128), 0).astype(f32)
    place = jnp.clip((fine_at + 0.5) / 4.0 - 0.5, 0.0, FA - 1.0)
    up_t = jnp.maximum(0.0, 1.0 - jnp.abs(place - coarse_at)).astype(bf16)
    row_sums = [None] * (coarse_rows + 2)
    for i in range(rows):
        lower, a, b = up_weights(i, me, n, rows, coarse_rows)
        grad = dec2[pl.ds((i + 1) * 128, 128)]
        for j, weight in ((lower, a), (lower + 1, b)):
            row_sums[j] = weight * grad if row_sums[j] is None else row_sums[j] + weight * grad
    along, summed = zero, zero
    for j in range(coarse_rows + 2):
        grad = dot_exact(up_t, row_sums[j])
        part[pl.ds(j * FA, FA)] = grad
        normed, before = merged_parts(j * FA, FA)
        push = gelu_slope(before) * grad
        along, summed = along + fold(push * normed), summed + fold(push)
    put_pair(pair.at[5], core, row_of(along), row_of(summed))
    pair[5, core, 4:5, 0:low_width] = lanes_of(low_along)
    pair[5, core, 5:6, 0:low_width] = lanes_of(low_summed)
    part_copies = halo(
        5,
        part.at[pl.ds(0, FA)],
        part.at[pl.ds(FA + coarse_cells, FA)],
        part.at[pl.ds((coarse_rows + 3) * FA, FA)],
        part.at[pl.ds((coarse_rows + 2) * FA, FA)],
    )
    swaps[3].drain()
    swaps[5].start()
    reduce_two.over_the_chips()
    weight_grads(wgrads, ref.x1, ref.g1)
    local(wgrads.at[:, pl.ds(0, 9)], ref.wgrads_hbm.at[:, pl.ds(0, 9)])
    total_g = swaps[5].finish()
    for copy in part_copies:
        copy.wait()
    merged_along, merged_summed = get_pair(total_g)
    low_along, low_summed = spread_row(total_g[4:5])[0:low_width], spread_row(total_g[5:6])[0:low_width]
    pack = ref.pack
    pack[17:18, 0:128] = total_g[4:5]
    pack[18:19, 0:128] = total_g[5:6]
    up_here = jnp.where(me == 0, 0.0, 1.0)
    down_here = jnp.where(me == n - 1, 0.0, 1.0)
    proj_bf = ref.proj_bf
    for j in range(1, coarse_rows + 1):
        grad = part[pl.ds(j * FA, FA)]
        if j == 1:
            grad = grad + up_here * part[pl.ds((coarse_rows + 2) * FA, FA)]
        if j == coarse_rows:
            grad = grad + down_here * part[pl.ds((coarse_rows + 3) * FA, FA)]
        normed, before = merged_parts(j * FA, FA)
        push = gelu_slope(before) * grad
        g = pull(push, normed, 5, merged_inverse, merged_along, merged_summed, coarse_samples)
        proj_bf[pl.ds((j - 1) * FA, FA)] = g.astype(bf16)

    push_all = []
    for k in range(4):
        normed, before, _ = branch_parts(k)
        push = gelu_slope(before) * dot_nt(proj_bf[...], ref.proj[k])
        push_all.append(push)
        wide_pair[1, core, k : k + 1] = row_of(push * normed)
        wide_pair[1, core, 4 + k : 5 + k] = row_of(push)
    proj_row = row_of(proj_bf[...].astype(f32))
    wide_pair[1, core, 8:16] = jnp.where(
        lax.broadcasted_iota(jnp.int32, (8, c), 0) == my_crop, proj_row, 0.0
    )
    total_h = wides[1].run()
    reduce_two.to_all_crops()
    for k in range(4):
        normed, _, inverse = branch_parts(k)
        g = pull(
            push_all[k], normed, k, inverse, total_h[k : k + 1], total_h[4 + k : 5 + k], coarse_samples
        )
        ref.branch_out[:, k * c : (k + 1) * c] = g.astype(bf16)

    sums = total_h[8:16]
    sums_high = sums.astype(bf16).astype(f32)
    sums_low = sums - sums_high
    spare = jnp.concatenate([sums_high, sums_low], axis=0)
    spare_mid = spare.astype(bf16)
    spare_rest = (spare - spare_mid.astype(f32)).astype(bf16)
    pieces = dot_nt(spare_mid, ref.proj[4]) + dot_nt(spare_rest, ref.proj[4])
    pool_push = gelu_slope(pool_before) * (pieces[0:8] + pieces[8:16])
    pool_push = jnp.where(pool_here, pool_push, 0.0)
    pool_along, pool_summed = row_of(pool_push * pool_normed), row_of(pool_push)
    pool_grad = pull(pool_push, pool_normed, 4, pool_inverse, pool_along, pool_summed, crops)
    pool_grad = jnp.where(pool_here, pool_grad, 0.0)
    pack[24:32] = pool_grad
    pack[32:40] = jnp.zeros((8, c), f32)

    gain_rows = [total_h[0:4], pool_along, merged_along, first_along, second_along]
    shift_rows = [total_h[4:8], pool_summed, merged_summed, first_summed, second_summed]
    turn = c - me * own
    pack[0:8] = pltpu.roll(jnp.concatenate(gain_rows, axis=0), turn, 1)
    pack[8:16] = pltpu.roll(jnp.concatenate(shift_rows, axis=0), turn, 1)
    pack[16:17] = total_h[16:17]
    pool_rows = jnp.zeros((c, c), f32)
    rest = jnp.concatenate([sums, jnp.zeros((8, c), f32)], axis=0)
    for _ in range(3):
        high = rest.astype(bf16)
        pool_rows = pool_rows + dot_tn(pool_bf, high)
        rest = rest - high.astype(f32)
    dec1[pl.ds(0, c)] = pool_rows
    pack[40 : 40 + own] = dec1[pl.ds(pl.multiple_of(me * own, own), own)]
    local(pack, ref.pack_hbm)

    def low_out_row(i, base, kept):
        at = pl.ds(pl.multiple_of(base - 128, 128), 128)
        normed = low_parts(base)[0]
        g = (low_gain * low_inverse) * (
            ref.low_push[:, at] - low_summed * (1.0 / fine_samples) - normed * (low_along * (1.0 / fine_samples))
        )
        ref.low_out[:, at] = g.astype(bf16)
        return kept

    each_row(low_out_row, 1, rows + 1, 0)
    local(ref.low_out, ref.low_hbm)
    local(ref.branch_out, ref.branch_hbm)

    for a in range(3):
        flip[pl.ds(a * 3 * low_width, 3 * low_width)] = dot(
            ref.lowx[:, a * 128 : a * 128 + fine_cells], ref.g1[pl.ds(128, fine_cells), c : 2 * c]
        )
    flip[pl.ds(9 * low_width + 32, 48)] = jnp.zeros((48, c), f32)
    turned = flip[...].T.astype(bf16)
    for k in range(4):
        product = dot_tn(ref.branch_bf[:, k * c : (k + 1) * c], proj_bf[...]).astype(bf16)
        for h in range(n):
            rows_h = product[h * own : (h + 1) * own]
            wgrads[h, 9 + k] = rows_h
    for h in range(n):
        wgrads[h, 13] = turned[h * own : (h + 1) * own, 0:c]
        wgrads[h, 14] = turned[h * own : (h + 1) * own, c : 2 * c]
        for k in range(15, wgrads.shape[1]):
            wgrads[h, k] = jnp.zeros((own, c), bf16)
    local(wgrads.at[:, pl.ds(9, wgrads.shape[1] - 9)], ref.wgrads_hbm.at[:, pl.ds(9, wgrads.shape[1] - 9)])
    reduce_two.finish()
    for t in range(9):
        ref.dec2_w[t] = ref.r_out[t].astype(f32)
    local(ref.dec2_w, ref.dec2_hbm)
    for copy in feature_copies:
        copy.wait_recv()
    front.drain(waited)
    swaps[4].drain()
    swaps[5].drain()
    for copy in local_copies[1:]:
        copy.wait()


def decoder(crops, n, samples, *args):
    ref = DecoderRefs(*args, *([None] * (len(DecoderRefs._fields) - len(args))))
    c_in, c = ref.point.shape
    low_width = ref.low_w.shape[1]
    rows = ref.dlog.shape[1] // 128 - 2
    cells = rows * 128
    coarse = FA * FA // n
    own = c // n
    small, large = weight_groups(crops)
    chips = n // 2
    all_chips = crops * chips
    outer = (rows + 2) * 128
    chunk = min(4, rows)
    count = (crops - 1) + 4 * (2 * chips - 1) + 2 * chips - 1
    count += 2 * chips - 1 + 3 * (1 + 2 * crops * (chips - 1)) + reduce_copies(crops, n) + 5
    S = jax.ShapeDtypeStruct
    V = pltpu.VMEM
    D = pltpu.SemaphoreType.DMA
    vmem = pl.BlockSpec(memory_space=pltpu.VMEM)
    hbm = pl.BlockSpec(memory_space=pl.ANY)
    return pl.pallas_call(
        functools.partial(decoder_kernel, crops, n, samples),
        out_shape=[
            S((32, cells), f32),
            S((coarse, 4 * c), bf16),
            S((low_width, cells), bf16),
            S((40 + own, c), f32),
            S((9, own, c), f32),
            S((n, rest_groups(crops), own, c), bf16),
            S((crops, FA * FA, c_in), bf16),
            S((ref.low_rows.shape[0], ref.low_rows.shape[1] * 128), bf16),
        ],
        in_specs=[pl.BlockSpec(memory_space=pltpu.SMEM), vmem, vmem, hbm] + [vmem] * (len(args) - 4),
        out_specs=[hbm] * 8,
        scratch_shapes=[
            V((ref.low_rows.shape[0], ref.low_rows.shape[1] * 128), bf16),
            V(ref.atrous_hbm.shape, bf16),
            V((FA * FA, c_in), bf16),
            V((32, cells), f32),
            V((coarse, 4 * c), bf16),
            V((low_width, cells), bf16),
            V((40 + own, c), f32),
            V((9, own, c), f32),
            V((n, rest_groups(crops), own, c), bf16),
            V((low_width, outer), f32),
            V((low_width, cells), f32),
            V((3 * low_width, outer), bf16),
            V((coarse + 2 * FA, c), f32),
            V((coarse + 4 * FA, c), f32),
            V((outer, c), f32),
            V((outer, c), f32),
            V((max(outer, 4 * FA * FA), c), f32),
            V((max(outer, 2 * FA * FA), c), f32),
            V((outer, 3 * c), bf16),
            V((outer, 3 * c), bf16),
            V((max(outer, FA * FA), 3 * c), bf16),
            V((outer, 3 * c), bf16),
            V((9 * low_width, (chunk + 2) * 128), f32),
            V((coarse, 4 * c), bf16),
            V((coarse, c), bf16),
            V((outer, c), bf16),
            V((512, c), f32),
            V((coarse, 4 * c), f32),
            V((4, chips, coarse, c), bf16),
            V((4, chips, coarse, c), bf16),
            V((chips, low_width, cells), f32),
            V((chips, low_width, cells), f32),
            V((chips, low_width, cells), bf16),
            V((chips, low_width, cells), bf16),
            V((4, coarse, c), bf16),
            V((low_width, cells), bf16),
            V((n, small + 2 * large, own, c), bf16),
            V((n, 16, 128), f32),
            V((16, c), f32),
            V((5, c, c), bf16),
            V((3, 3 * c, c), bf16),
            V((c, 2 * c), bf16),
            V((3, 3 * low_width, c), bf16),
            V((3, 3 * c, c), bf16),
            V((c, 128), bf16),
            V((32, c), bf16),
            V((32, outer), bf16),
            V((8, 128), f32),
            V((n, large, own, c), bf16),
            *reduce_scratch(crops, n, large, own, c),
            D((16,)),
            D((count,)),
            D((count,)),
            V((2, 2, 24, c), f32),
            V((2, crops, 24, c), f32),
            V((2, chips, 24, c), f32),
            D((2, 2)),
            D((2, crops + chips)),
            D((2, crops + chips)),
            V((7, 2, 8, 128), f32),
            V((7, all_chips, 8, 128), f32),
            D((7, 2)),
            D((2, all_chips)),
            D((7, all_chips)),
            D((6, 2)),
            D((6, 2)),
        ],
        compiler_params=pltpu.CompilerParams(
            collective_id=0, has_side_effects=True, vmem_limit_bytes=62 * 1024 * 1024
        ),
    )(*args)


class Reduce:
    def __init__(self, crops, n, copies, source, first, pairs, crossed, halves, lined, out, mine=None, mine_sems=None):
        my_crop, me = lax.axis_index("crop"), lax.axis_index("chan")
        self.crops, self.chips, self.copies = crops, n // 2, copies
        self.crop, self.core, self.chip = my_crop, lax.rem(me, 2), lax.div(me, 2)
        self.other = (my_crop, me + 1 - 2 * self.core)
        self.over_crops = [(lax.rem(my_crop + i, crops), me) for i in range(1, crops)]
        self.over_chips = [(my_crop, lax.rem(me + 2 * j, n)) for j in range(1, n // 2)]
        self.source, self.first, self.pairs, self.crossed = source, first, pairs, crossed
        self.halves, self.lined, self.out = halves, lined, out
        self.mine, self.mine_sems = mine, mine_sems
        self.size = source.shape[1]
        self.share = self.size // crops

    def wait(self):
        for copy in self.moving:
            copy.wait_recv()

    def cores(self):
        self.moving = []
        for z in range(self.chips):
            block = self.source.at[2 * z + 1 - self.core]
            self.moving.append(self.copies.start(block, self.first.at[z], self.other))
        self.loads = []
        if self.mine is not None:
            for z in range(self.chips):
                block = self.source.at[2 * z + self.core]
                self.loads.append(pltpu.make_async_copy(block, self.mine.at[z], self.mine_sems.at[z]))
                self.loads[-1].start()

    def over_the_crops(self):
        self.wait()
        for copy in self.loads:
            copy.wait()
        for z in range(self.chips):
            for g in range(self.size):
                here = self.source[2 * z + self.core, g] if self.mine is None else self.mine[z, g]
                both = here.astype(f32) + self.first[z, g].astype(f32)
                self.pairs[z, g] = both.astype(bf16)
        self.moving = []
        for i in range(1, self.crops):
            target = lax.rem(self.crop + i, self.crops)
            block = self.pairs.at[:, pl.ds(target * self.share, self.share)]
            self.moving.append(
                self.copies.start(block, self.crossed.at[self.crop], self.over_crops[i - 1])
            )
        for z in range(self.chips):
            for g in range(self.share):
                self.crossed[self.crop, z, g] = self.pairs[z, self.crop * self.share + g]

    def over_the_chips(self):
        self.wait()
        for z in range(self.chips):
            for g in range(self.share):
                value = self.crossed[0, z, g].astype(f32)
                for i in range(1, self.crops):
                    value = value + self.crossed[i, z, g].astype(f32)
                self.halves[z, g] = value.astype(bf16)
        self.moving = []
        for j in range(1, self.chips):
            target = lax.rem(self.chip + j, self.chips)
            self.moving.append(
                self.copies.start(
                    self.halves.at[target], self.lined.at[self.chip], self.over_chips[j - 1]
                )
            )
        for g in range(self.share):
            self.lined[self.chip, g] = self.halves[self.chip, g]

    def to_all_crops(self):
        self.wait()
        for g in range(self.share):
            value = self.lined[0, g].astype(f32)
            for z in range(1, self.chips):
                value = value + self.lined[z, g].astype(f32)
            self.out[self.crop * self.share + g] = value.astype(bf16)
        here = self.out.at[pl.ds(self.crop * self.share, self.share)]
        self.moving = [self.copies.start(here, here, peer) for peer in self.over_crops]

    def finish(self):
        self.wait()


def reduce_scratch(crops, n, size, own, c):
    chips, share = n // 2, size // crops
    V = pltpu.VMEM
    return [
        V((chips, size, own, c), bf16),
        V((chips, size, own, c), bf16),
        V((crops, chips, share, own, c), bf16),
        V((chips, share, own, c), bf16),
        V((chips, share, own, c), bf16),
        V((size, own, c), bf16),
    ]


def reduce_copies(crops, n):
    return 2 * (n // 2) - 1 + 2 * (crops - 1)


class Gather:
    def __init__(self, n, send, recv):
        my_crop, self.me = lax.axis_index("crop"), lax.axis_index("chan")
        self.n, self.chips = n, n // 2
        self.core = lax.rem(self.me, 2)
        self.other = (my_crop, self.me + 1 - 2 * self.core)
        self.send, self.recv = send, recv
        self.peer = lambda j: (my_crop, lax.rem(self.me + 2 * j, n))

    def block(self, j):
        return lax.rem(self.me - 2 * j + self.n, self.n)

    def other_block(self, j):
        return lax.rem(self.me + 1 - 2 * self.core - 2 * j + self.n, self.n)

    def start(self, at):
        self.at = at
        self.far, self.pairs = [], []
        for j in range(1, self.chips):
            here = at(self.me)
            self.far.append(remote(here, here, self.send.at[j], self.recv.at[j], self.peer(j)))
            self.far[-1].start()
        self.forward(0)

    def forward(self, j):
        here = self.at(self.block(j))
        k = self.chips + j
        self.pairs.append(remote(here, here, self.send.at[k], self.recv.at[k], self.other))
        self.pairs[-1].start()

    def arrive(self, j):
        self.far[j - 1].wait_recv()
        self.forward(j)

    def finish(self):
        for copy in self.pairs:
            copy.wait_recv()

    def drain(self):
        for copy in self.far + self.pairs:
            copy.wait_send()


class LineGather(Gather):
    def __init__(self, n, send, recv):
        super().__init__(n, send, recv)
        my_crop, self.chip = lax.axis_index("crop"), lax.div(self.me, 2)
        self.end = jnp.logical_or(self.chip == 0, self.chip == 3)
        self.inner = jnp.logical_not(self.end)
        beside = self.chip + 1 - 2 * lax.rem(self.chip, 2)
        over, mirror = lax.rem(self.chip + 2, 4), 3 - self.chip
        second = jnp.where(self.end, over, mirror)
        third = jnp.where(self.end, mirror, over)
        self.order = [2 * z + self.core for z in (self.chip, beside, second, third)]
        self.to = lambda z: (my_crop, 2 * z + self.core)
        self.beside, self.over, self.mirror = beside, over, mirror

    def block(self, j):
        return self.order[j]

    def start(self, at):
        self.at = at
        self.pairs = []
        here = at(self.me)
        make = lambda k, block, z, s=None: remote(
            block, block, self.send.at[k if s is None else s], self.recv.at[k], self.to(z)
        )
        self.first = make(0, here, self.beside)
        self.first.start()
        self.middle = make(1, here, self.mirror)
        self.long = make(2, here, self.over, 1)
        pl.when(self.inner)(self.middle.start)
        pl.when(self.end)(self.long.start)
        self.passed = [make(3, at(self.order[2]), self.beside), make(8, at(self.order[3]), self.beside)]
        self.forward(0)

    def arrive(self, j):
        if j == 1:
            self.first.wait_recv()
        else:
            come, on = (self.middle, self.long)[j - 2], self.passed[j - 2]

            def pass_it():
                come.wait_recv()
                on.start()

            pl.when(self.inner)(pass_it)
            pl.when(self.end)(on.wait_recv)
        self.forward(j)

    def drain(self):
        self.first.wait_send()
        self.middle.wait_send()
        for copy in self.pairs:
            copy.wait_send()

        def passed():
            for copy in self.passed:
                copy.wait_send()

        pl.when(self.inner)(passed)


def gather_over(n, send, recv):
    return LineGather(n, send, recv) if n // 2 == 4 else Gather(n, send, recv)


class BackRefs(typing.NamedTuple):
    grad: object
    src_hbm: object
    point: object
    atrous_hbm: object
    pool: object
    pack: object
    low_grad: object
    low_in_hbm: object
    wgrads: object
    features_hbm: object
    point_w: object
    atrous_w_hbm: object
    pool_w: object
    low_w_out: object
    blocks: object
    low_full_hbm: object
    last_grad: object
    last_src: object
    src: object
    atrous: object
    low_in: object
    features: object
    atrous_w: object
    low_full: object
    mine: object
    local: object
    m_sems: object
    all_grad: object
    shifted: object
    turned: object
    total: object
    r_first: object
    r_pairs: object
    r_crossed: object
    r_halves: object
    r_lined: object
    r_out: object
    low_parts: object
    g_send: object
    g_recv: object
    l_send: object
    l_recv: object
    c_send: object
    c_recv: object


def back_kernel(crops, n, *refs):
    ref = BackRefs(*refs)
    my_crop, me = lax.axis_index("crop"), lax.axis_index("chan")
    chips = n // 2
    core, chip = lax.rem(me, 2), lax.div(me, 2)
    block, width = ref.grad.shape
    c = width // 4
    half = width // 2
    c_in = ref.src.shape[2]
    cells = FA * FA
    relay = crops == 4
    other = (my_crop, me + 1 - 2 * core)
    over_crops = [(lax.rem(my_crop + i, crops), me) for i in range(1, crops)]
    over_chips = [(my_crop, lax.rem(me + 2 * j, n)) for j in range(1, chips)]
    wait_barrier = barrier_with([other] + over_crops + over_chips)
    all_grad, src = ref.all_grad, ref.src
    if relay:
        along_x = my_crop + 1 - 2 * lax.rem(my_crop, 2)
        along_y = my_crop + 2 - 4 * lax.div(my_crop, 2)
        crop_list = [my_crop, along_x, along_y, 3 - my_crop]
    else:
        crop_list = [my_crop] + [lax.rem(my_crop - i + crops, crops) for i in range(1, crops)]

    def grad_at(crop):
        def at(b):
            return all_grad.at[crop, pl.ds(pl.multiple_of(b * block, block), block)]

        return at

    def lanes_at(crop, b, first):
        return all_grad.at[crop, pl.ds(pl.multiple_of(b * block, block), block), pl.ds(first, half)]

    local_copies = []

    def local(src, dst):
        copy = pltpu.make_async_copy(src, dst, ref.local.at[len(local_copies)])
        copy.start()
        local_copies.append(copy)

    local(ref.src_hbm, src)
    local(ref.src_hbm.at[crop_list[-1]], ref.last_src)
    local(ref.atrous_hbm, ref.atrous)
    local(ref.low_in_hbm, ref.low_in)
    pooled_grad = ref.pack[24:40].astype(bf16)
    all_grad[my_crop, pl.ds(pl.multiple_of(me * block, block), block)] = ref.grad[...]
    ref.low_full[me] = ref.low_grad[...]
    wait_barrier()

    gather = gather_over(n, ref.g_send, ref.g_recv)
    gather.start(grad_at(my_crop))
    moves = Copies(ref.c_send, ref.c_recv)
    crossing = {}

    def cross(j):
        here = grad_at(my_crop)(gather.block(j))
        if relay:
            for i, crop in ((1, along_x), (2, along_y)):
                crossing[i, j] = moves.start(here, here, (crop, me))
        else:
            for i in range(1, crops):
                crossing[i, j] = moves.start(here, here, over_crops[i - 1])

    core_copies = {}

    def pass_on(i, j):
        crossing[i, j].wait_recv()
        b = gather.block(j)
        crop = crop_list[i]
        if relay and i == 1:
            here = lanes_at(crop, b, 0)
            crossing[3, j, 0] = moves.start(here, here, (along_y, me))
        if relay and i == 2:
            here = lanes_at(crop, b, half)
            crossing[3, j, 1] = moves.start(here, here, (along_x, me))
        place = grad_at(crop)(b)
        core_copies[i, j] = moves.start(place, place, other)

    def pass_across(j):
        crossing[3, j, 0].wait_recv()
        crossing[3, j, 1].wait_recv()
        place = grad_at(crop_list[3])(gather.block(j))
        core_copies[3, j] = moves.start(place, place, other)

    cross(0)
    reduce = Reduce(
        crops, n, moves, ref.wgrads, ref.r_first, ref.r_pairs, ref.r_crossed, ref.r_halves, ref.r_lined, ref.r_out,
        ref.mine, ref.m_sems,
    )
    reduce.cores()
    shifted = ref.shifted

    def shift_source(i):
        crop = crop_list[i]
        for k in range(3):
            rate = atrous_rates[k]
            shift_three(lambda base: src[crop, pl.ds(base, 128)], shifted.at[i % 3, k], rate, -rate, rate)

    local_copies[0].wait()
    shift_source(0)
    reduce.over_the_crops()
    for i in range(1, min(3, crops)):
        shift_source(i)
    for j in range(1, chips):
        gather.arrive(j)
        cross(j)
    reduce.over_the_chips()
    low_gather = Gather(n, ref.l_send, ref.l_recv)
    low_gather.start(lambda b: ref.low_full.at[b])
    if relay:
        pass_on(1, 0)
        pass_on(2, 0)
    gather.finish()

    total, turned = ref.total, ref.turned
    pool_row = dot_nt(pooled_grad, ref.pool[...])
    my_row = lax.broadcasted_iota(jnp.int32, pool_row.shape, 0) == my_crop
    pool_row = row_of(jnp.where(my_row, pool_row, 0.0)) * (1.0 / cells)
    local_copies[2].wait()
    total[...] = dot_nt(all_grad[my_crop, :, 0:c], ref.point[...]) + pool_row
    for k in range(3):
        rate = atrous_rates[k]
        shift_three(
            lambda base: all_grad[my_crop, pl.ds(base, 128), (k + 1) * c : (k + 2) * c],
            turned, rate, rate, -rate,
        )
        for a in range(3):
            move = (a - 1) * rate
            count = (FA - abs(move)) * FA
            to, off = max(move, 0) * FA, max(-move, 0) * FA
            term = None
            for e in range(3):
                piece = dot_nt(turned[pl.ds(off, count), e * c : (e + 1) * c], ref.atrous[k, 3 * a + e])
                term = piece if term is None else term + piece
            total[pl.ds(to, count)] = total[pl.ds(to, count)] + term

    def weight_part(i):
        crop = crop_list[i]
        part = dot_tn(src[crop], all_grad[crop, :, 0:c])
        ref.point_w[...] = part if i == 0 else ref.point_w[...] + part
        for k in range(3):
            rate = atrous_rates[k]
            for a in range(3):
                move = (a - 1) * rate
                count = (FA - abs(move)) * FA
                from_src, off = max(move, 0) * FA, max(-move, 0) * FA
                part = dot_tn(
                    shifted[i % 3, k, pl.ds(from_src, count)],
                    all_grad[crop, pl.ds(off, count), (k + 1) * c : (k + 2) * c],
                )
                for e in range(3):
                    piece = part[e * c_in : (e + 1) * c_in]
                    if i > 0:
                        piece = ref.atrous_w[k, 3 * a + e] + piece
                    ref.atrous_w[k, 3 * a + e] = piece
            if i == crops - 2:
                local(ref.atrous_w.at[k], ref.atrous_w_hbm.at[k])

    weight_part(0)
    ref.features[...] = total[...].T
    local(ref.features, ref.features_hbm)
    if relay:
        for j in range(1, chips):
            pass_on(1, j)
            pass_on(2, j)

    def low_part():
        for j in range(1, chips):
            low_gather.arrive(j)
        low_gather.finish()
        local(ref.low_full, ref.low_full_hbm)
        local_copies[3].wait()
        rows = ref.low_full.shape[2] // 128
        low_in, low_all = ref.low_in, ref.low_full
        low_total = None
        for b in range(n):
            here = low_all[b]
            span = slice(b * rows * 128, (b + 1) * rows * 128)
            part = dot_nt(low_in[:, span], here)
            low_total = part if low_total is None else low_total + part
        low_parts = ref.low_parts
        low_parts[my_crop] = jnp.zeros(low_parts.shape[1:], f32)
        low_parts[my_crop, :, 0 : low_total.shape[1]] = low_total
        here = low_parts.at[my_crop]
        low_copies = [moves.start(here, here, peer) for peer in over_crops]
        return low_copies

    for i in range(1, crops):
        if i + 2 < crops - 1:
            shift_source(i + 2)
        for j in range(chips):
            if not relay:
                pass_on(i, j)
            elif i == 3:
                pass_across(j)
        for j in range(chips):
            core_copies[i, j].wait_recv()
        if i < crops - 1:
            weight_part(i)
        if i == min(2, crops - 1):
            reduce.to_all_crops()
            low_copies = low_part()

    local(all_grad.at[crop_list[-1]], ref.last_grad)
    pooled = []
    for i in range(crops):
        mean = row_of(src[i].astype(f32)) * (1.0 / cells)
        pooled.append(mean)
    pooled = jnp.concatenate(pooled + [jnp.zeros((16 - crops, c_in), f32)], axis=0).astype(bf16)
    ref.pool_w[...] = dot_tn(pooled, pooled_grad)

    reduce.finish()
    for g in range(ref.blocks.shape[0]):
        ref.blocks[g] = ref.r_out[g].astype(f32)
    for copy in low_copies:
        copy.wait_recv()
    ref.low_w_out[...] = jnp.sum(ref.low_parts[...], axis=0)
    gather.drain()
    low_gather.drain()
    moves.drain([])
    for k, copy in enumerate(local_copies):
        if k not in (0, 2, 3):
            copy.wait()


def pyramid_back(crops, n, *args):
    grad, src, low_grad, low_in, wgrads = args[0], args[1], args[6], args[7], args[8]
    block, width = grad.shape
    c = width // 4
    c_in = src.shape[2]
    chips = n // 2
    cells = FA * FA
    low_rows = low_in.shape[0]
    own, lanes = wgrads.shape[2:]
    S = jax.ShapeDtypeStruct
    V = pltpu.VMEM
    D = pltpu.SemaphoreType.DMA
    vmem = pl.BlockSpec(memory_space=pltpu.VMEM)
    hbm = pl.BlockSpec(memory_space=pl.ANY)
    count = 3 * crops * chips + crops - 1 + reduce_copies(crops, n)
    return pl.pallas_call(
        functools.partial(back_kernel, crops, n),
        out_shape=[
            S((c_in, cells), f32),
            S((c_in, c), f32),
            S((3, 9, c_in, c), f32),
            S((c_in, c), f32),
            S((low_rows, 128), f32),
            S((15, own, lanes), f32),
            S((n,) + low_grad.shape, bf16),
            S((cells, width), bf16),
            S((cells, c_in), bf16),
        ],
        in_specs=[vmem, hbm, vmem, hbm, vmem, vmem, vmem, hbm, hbm],
        out_specs=[hbm, vmem, hbm, vmem, vmem, vmem, hbm, hbm, hbm],
        scratch_shapes=[
            V(src.shape, bf16),
            V(args[3].shape, bf16),
            V(low_in.shape, bf16),
            V((c_in, cells), f32),
            V((3, 9, c_in, c), f32),
            V((n,) + low_grad.shape, bf16),
            V((chips,) + wgrads.shape[1:], bf16),
            D((12,)),
            D((chips,)),
            V((crops, cells, width), bf16),
            V((min(3, crops), 3, cells, 3 * c_in), bf16),
            V((cells, 3 * c), bf16),
            V((cells, c_in), f32),
            *reduce_scratch(crops, n, wgrads.shape[1], own, lanes),
            V((crops, low_rows, 128), f32),
            D((n + 1,)),
            D((n + 1,)),
            D((n + 1,)),
            D((n + 1,)),
            D((count,)),
            D((count,)),
        ],
        compiler_params=pltpu.CompilerParams(
            collective_id=1, has_side_effects=True, vmem_limit_bytes=62 * 1024 * 1024
        ),
    )(*args)


class FinishRefs(typing.NamedTuple):
    atrous_part: object
    point_part: object
    last_grad: object
    last_src: object
    features_in: object
    pool_in: object
    low_full: object
    low_w: object
    low_w_part: object
    logits_in: object
    dec2_in: object
    blocks: object
    pack: object
    logits: object
    features: object
    early: object
    point: object
    atrous: object
    pool: object
    proj: object
    low_w_out: object
    dec1: object
    side: object
    dec2: object
    cls: object
    bias: object
    gain: object
    shift: object
    low_gain: object
    low_shift: object
    v_atrous: object
    v_grad: object
    v_src: object
    v_low: object
    v_logits: object
    v_early: object
    v_point: object
    v_proj: object
    v_low_w: object
    v_side: object
    v_cls: object
    v_bias: object
    v_gain: object
    v_shift: object
    v_low_gain: object
    v_low_shift: object
    turned: object
    sems: object


def finish_kernel(*refs):
    ref = FinishRefs(*refs)
    copies = []

    def move(src, dst):
        copy = pltpu.make_async_copy(src, dst, ref.sems.at[len(copies)])
        copy.start()
        copies.append(copy)
        return copy

    c_in, c = ref.v_point.shape
    classes, rows = ref.v_logits.shape[0], ref.v_logits.shape[1]
    low_width = ref.v_low_w.shape[1]
    own = ref.v_cls.shape[1]
    loaded = [move(ref.last_grad, ref.v_grad), move(ref.last_src, ref.v_src)]
    parts = [move(ref.atrous_part.at[k], ref.v_atrous.at[k]) for k in range(3)]
    low = move(ref.low_full, ref.v_low)
    straight = [
        move(ref.features_in, ref.features),
        move(ref.pool_in, ref.pool),
        move(ref.dec2_in, ref.dec2),
        move(ref.blocks.at[pl.ds(0, 9)], ref.dec1),
        move(ref.blocks.at[pl.ds(9, 4)], ref.proj.at[pl.ds(0, 4)]),
        move(ref.pack.at[pl.ds(40, own)], ref.proj.at[4]),
    ]

    ref.v_logits[...] = ref.logits_in[0:classes].reshape(classes, rows, 128)
    straight.append(move(ref.v_logits, ref.logits))
    pack = ref.pack
    tail = jnp.concatenate([ref.blocks[13], ref.blocks[14]], axis=1)
    width = 2 * c
    for t in range(9):
        ref.v_side[t] = pltpu.roll(tail, (width - t * low_width) % width, 1)[:, 0:low_width]
    cls = pltpu.roll(tail, width - 9 * low_width, 1)[:, 0:128]
    cls = jnp.concatenate([cls, jnp.zeros((128 - own, 128), f32)], axis=0)
    ref.v_cls[...] = cls.T[0:classes, 0:own]
    ref.v_low_w[...] = ref.low_w_part[:, 0:low_width]
    ref.v_gain[...] = pack[0:8, 0:own]
    ref.v_shift[...] = pack[8:16, 0:own]
    ref.v_bias[...] = pack[16:17, 0:classes]
    ref.v_low_gain[...] = pack[17:18, 0:low_width]
    ref.v_low_shift[...] = pack[18:19, 0:low_width]
    for src, dst in (
        (ref.v_side, ref.side),
        (ref.v_cls, ref.cls),
        (ref.v_low_w, ref.low_w_out),
        (ref.v_gain, ref.gain),
        (ref.v_shift, ref.shift),
        (ref.v_bias, ref.bias),
        (ref.v_low_gain, ref.low_gain),
        (ref.v_low_shift, ref.low_shift),
    ):
        straight.append(move(src, dst))

    for copy in loaded:
        copy.wait()
    for k in range(3):
        rate = atrous_rates[k]
        shift_three(lambda base: ref.v_src[pl.ds(base, 128)], ref.turned, rate, -rate, rate)
        parts[k].wait()
        for a in range(3):
            by = (a - 1) * rate
            count = (FA - abs(by)) * FA
            from_src, off = max(by, 0) * FA, max(-by, 0) * FA
            part = dot_tn(
                ref.turned[pl.ds(from_src, count)],
                ref.v_grad[pl.ds(off, count), (k + 1) * c : (k + 2) * c],
            )
            for e in range(3):
                ref.v_atrous[k, 3 * a + e] += part[e * c_in : (e + 1) * c_in]
        straight.append(move(ref.v_atrous.at[k], ref.atrous.at[k]))
        if k == 0:
            low.wait()
            for b in range(ref.low_full.shape[0]):
                value = dot(ref.low_w[...], ref.v_low[b])
                ref.v_early[:, b * rows : (b + 1) * rows] = value.reshape(value.shape[0], rows, 128)
            straight.append(move(ref.v_early, ref.early))
            ref.v_point[...] = ref.point_part[...] + dot_tn(ref.v_src[...], ref.v_grad[:, 0:c])
            straight.append(move(ref.v_point, ref.point))
    for copy in straight:
        copy.wait()


def finish(shapes, *args):
    parts = FinishRefs(*args, *([None] * (len(FinishRefs._fields) - len(args))))
    c_in = parts.point_part.shape[0]
    vmem = pl.BlockSpec(memory_space=pltpu.VMEM)
    hbm = pl.BlockSpec(memory_space=pl.ANY)
    V = pltpu.VMEM
    held = [V(shapes[k], f32) for k in (0, 2, 3)]
    held += [V(shapes[k], f32) for k in (6, 7, 9, 11, 12, 13, 14, 15, 16)]
    return pl.pallas_call(
        finish_kernel,
        out_shape=[jax.ShapeDtypeStruct(shape, f32) for shape in shapes],
        in_specs=[hbm, vmem, hbm, hbm, vmem, vmem, hbm, vmem, vmem, vmem, vmem, vmem, vmem],
        out_specs=[hbm] * len(shapes),
        scratch_shapes=[
            V(parts.atrous_part.shape, f32),
            V(parts.last_grad.shape, bf16),
            V(parts.last_src.shape, bf16),
            V(parts.low_full.shape, bf16),
            *held,
            V((FA * FA, 3 * c_in), bf16),
            pltpu.SemaphoreType.DMA((32,)),
        ],
        compiler_params=pltpu.CompilerParams(vmem_limit_bytes=60 * 1024 * 1024),
    )(*args)


def per_device(
    features,
    low_in,
    offsets,
    d_logits,
    w_point,
    w_atrous,
    w_pool,
    w_proj,
    w_low,
    w_dec1,
    w_dec1_low,
    w_dec2,
    w_cls,
    b_cls,
    bn_gain,
    bn_shift,
    low_gain,
    low_shift,
):
    n = lax.axis_size("chan")
    crops = lax.axis_size("crop")
    me = lax.axis_index("chan")
    fine = low_in.shape[2]
    rows = fine // n
    coarse_rows = FA // n
    channels = w_dec2.shape[2]
    c_in = features.shape[1]
    low_width = w_low.shape[1]
    coarse_samples = FA * FA * crops
    fine_samples = fine * fine * crops

    classes = w_cls.shape[1]
    spare = 32 - classes
    outer_grad = jnp.pad(d_logits[0], ((0, spare), (1, 1), (0, 0)))
    outer_grad = lax.dynamic_slice_in_dim(outer_grad, me * rows, rows + 2, 1)
    logits, branch_grad, low_pre_bf, pack, dec2_wgrad, blocks, source_all, low_flat = decoder(
        crops,
        n,
        (coarse_samples, fine_samples),
        offsets,
        features[0],
        w_point,
        w_atrous.reshape(3, 3, 3 * c_in, channels),
        w_pool,
        low_in[0],
        w_low,
        w_proj,
        w_dec1,
        w_dec1_low.transpose(0, 2, 1),
        w_dec2,
        w_cls.T,
        bn_gain,
        bn_shift,
        low_gain[None],
        low_shift[None],
        b_cls[None],
        outer_grad.reshape(32, (rows + 2) * fine),
    )
    feature_grad, point_wgrad, atrous_wgrad, pool_wgrad, low_wgrad, blocks, low_full, last_grad, last_src = (
        pyramid_back(
            crops,
            n,
            branch_grad,
            source_all,
            w_point,
            w_atrous,
            w_pool,
            pack,
            low_pre_bf,
            low_flat,
            blocks,
        )
    )
    own = w_dec2.shape[1]
    shapes = [
        (classes, rows, fine),
        (c_in, FA * FA),
        low_in.shape[1:],
        (c_in, channels),
        (3, 9, c_in, channels),
        (c_in, channels),
        (5, own, channels),
        (low_in.shape[1], low_width),
        (9, own, channels),
        (9, own, low_width),
        (9, own, channels),
        (classes, own),
        (1, classes),
        (8, own),
        (8, own),
        (1, low_width),
        (1, low_width),
    ]
    outs = finish(
        shapes,
        atrous_wgrad,
        point_wgrad,
        last_grad,
        last_src,
        feature_grad,
        pool_wgrad,
        low_full,
        w_low,
        low_wgrad,
        logits,
        dec2_wgrad,
        blocks,
        pack,
    )
    outs = list(outs)
    for k in (0, 1, 2):
        outs[k] = outs[k][None]
    for k in (12, 15, 16):
        outs[k] = outs[k][0]
    outs[9] = outs[9].transpose(0, 2, 1)
    outs[11] = outs[11].T
    return tuple(outs)


def solution(mesh):
    placed = (
        P("crop", "chan", None),
        P("crop", "chan", None, None),
        P("crop", None),
        P("crop", None, None, None),
        P("chan", None),
        P(None, None, "chan", None),
        P("chan", None),
        P(None, "chan", None),
        P("chan", None),
        P(None, "chan", None),
        P(None, None, "chan"),
        P(None, "chan", None),
        P("chan", None),
        P(),
        P(None, "chan"),
        P(None, "chan"),
        P(),
        P(),
    )
    return jax.shard_map(
        per_device,
        mesh=mesh,
        in_specs=placed,
        out_specs=(
            P("crop", None, "chan", None),
            P("crop", "chan", None),
            P("crop", "chan", None, None),
            P("chan", None),
            P(None, None, "chan", None),
            P("chan", None),
            P(None, "chan", None),
            P("chan", None),
            P(None, "chan", None),
            P(None, None, "chan"),
            P(None, "chan", None),
            P("chan", None),
            P(),
            P(None, "chan"),
            P(None, "chan"),
            P(),
            P(),
        ),
        check_vma=False,
    )
```

```python
import functools
import typing

import jax
import jax.numpy as jnp
from jax import lax
from jax.experimental import pallas as pl
from jax.experimental.pallas import tpu as pltpu
from jax.sharding import PartitionSpec as P

FA = 32
SCENE_H = 1024
SCENE_W = 2048

epsilon = 1e-05
highest = lax.Precision.HIGHEST
atrous_rates = (6, 12, 18)
f32 = jnp.float32
bf16 = jnp.bfloat16
BOTH = ("crop", "chan")


MESH = pl.DeviceIdType.MESH


def chip_peers(crops, n):
    my_crop, me = lax.axis_index("crop"), lax.axis_index("chan")
    core = lax.rem(me, 2)
    chips = n // 2
    other = (my_crop, me + 1 - 2 * core)
    far = []
    for i in range(crops):
        for j in range(chips):
            if i or j:
                far.append((lax.rem(my_crop + i, crops), lax.rem(me + 2 * j, n)))
    return other, far


GELU_A = 0.7978845608028654
GELU_B = 0.044715


def gelu(x):
    return 0.5 * x * (1.0 + jnp.tanh(GELU_A * (x + GELU_B * x * x * x)))


def gelu_both(x):
    square = x * x
    t = jnp.tanh(GELU_A * x * (1.0 + GELU_B * square))
    upper = 0.5 * (1.0 + t)
    return x * upper, upper + (0.5 * GELU_A) * x * (1.0 - t * t) * (1.0 + (3.0 * GELU_B) * square)


def gelu_slope(x):
    square = x * x
    t = jnp.tanh(GELU_A * x * (1.0 + GELU_B * square))
    return 0.5 * (1.0 + t) + (0.5 * GELU_A) * x * (1.0 - t * t) * (1.0 + (3.0 * GELU_B) * square)


def dot(a, b):
    return jnp.dot(a, b, preferred_element_type=f32)


def dot_nt(a, b):
    return lax.dot_general(a, b, (((1,), (1,)), ((), ())), preferred_element_type=f32)


def dot_tn(a, b):
    return lax.dot_general(a, b, (((0,), (0,)), ((), ())), preferred_element_type=f32)


def dot_exact(table, values):
    high = values.astype(bf16)
    rest = values - high.astype(f32)
    middle = rest.astype(bf16)
    low = (rest - middle.astype(f32)).astype(bf16)
    return dot(table, high) + (dot(table, middle) + dot(table, low))


def fold(values):
    return jnp.sum(values.reshape(values.shape[0] // 8, 8, values.shape[1]), axis=0)


def row_of(values):
    return jnp.sum(values, axis=0, keepdims=True)


def barrier_with(peers):
    barrier = pltpu.get_barrier_semaphore()
    for peer in peers:
        pl.semaphore_signal(barrier, inc=1, device_id=peer, device_id_type=MESH)
    return lambda: pl.semaphore_wait(barrier, len(peers))


def remote(src, dst, send, recv, peer):
    return pltpu.make_async_remote_copy(
        src_ref=src, dst_ref=dst, send_sem=send, recv_sem=recv, device_id=peer, device_id_type=MESH
    )


class Copies:
    def __init__(self, send, recv):
        self.send, self.recv, self.all, self.next = send, recv, [], 0

    def make(self, src, dst, peer, send=None):
        k = self.next
        self.next += 1
        return remote(src, dst, self.send.at[k if send is None else send], self.recv.at[k], peer)

    def start(self, src, dst, peer):
        copy = self.make(src, dst, peer)
        copy.start()
        self.all.append(copy)
        return copy

    def drain(self, kept):
        for copy in self.all:
            if not any(copy is other for other in kept):
                copy.wait_send()


class LineSum:
    def __init__(self, n, copies, staged, arrived, spare, refill):
        my_crop, me = lax.axis_index("crop"), lax.axis_index("chan")
        core, self.chip = lax.rem(me, 2), lax.div(me, 2)
        self.chips, self.copies, self.staged, self.arrived = n // 2, copies, staged, arrived
        self.spare, self.refill = spare, refill
        self.peer = lambda z: (my_crop, 2 * z + core)
        self.line = self.chips == 4
        if self.line:
            self.beside = self.chip + 1 - 2 * lax.rem(self.chip, 2)
            self.over = lax.rem(self.chip + 2, 4)
            self.mirror = 3 - self.chip
            self.end = jnp.logical_or(self.chip == 0, self.chip == 3)
            self.inner = jnp.logical_not(self.end)

    def send(self, z):
        return self.copies.start(self.staged.at[z], self.arrived.at[self.chip], self.peer(z))

    def start(self):
        if not self.line:
            targets = [lax.rem(self.chip + j, self.chips) for j in range(1, self.chips)]
            self.direct = [self.send(z) for z in targets]
            return
        here = self.staged.at[self.mirror]
        k = self.copies.next
        self.passed = self.copies.make(here, self.spare, self.peer(self.beside))
        self.middle = self.copies.make(here, self.arrived.at[self.chip], self.peer(self.mirror), k)
        self.copies.all.append(self.passed)
        pl.when(self.end)(self.passed.start)
        pl.when(self.inner)(self.middle.start)
        self.first = self.send(self.beside)

    def second(self):
        if not self.line:
            return

        def merge():
            self.passed.wait_recv()
            both = self.refill(self.over) + self.spare[...].astype(f32)
            self.staged[self.over] = both.astype(bf16)

        pl.when(self.inner)(merge)
        self.crossed = self.send(self.over)

    def finish(self, add):
        if not self.line:
            for j in range(1, self.chips):
                self.direct[j - 1].wait_recv()
                add(self.arrived[lax.rem(self.chip - j + self.chips, self.chips)].astype(f32))
            return
        self.first.wait_recv()
        add(self.arrived[self.beside].astype(f32))

        def third():
            self.middle.wait_recv()
            add(self.arrived[self.mirror].astype(f32))

        pl.when(self.inner)(third)
        self.crossed.wait_recv()
        add(self.arrived[self.over].astype(f32))


def shift_three(source, target, rate, first, last):
    column = lax.rem(lax.broadcasted_iota(jnp.int32, (128, 1), 0), FA)

    def step(i, kept):
        base = pl.multiple_of(i * 128, 128)
        here = source(base)
        w = here.shape[1]
        wide = here.astype(f32)
        for slot, by in ((0, first), (2, last)):
            ok = jnp.logical_and(column + by >= 0, column + by < FA)
            moved = jnp.where(ok, pltpu.roll(wide, (-by) % 128, 0), 0.0)
            target[pl.ds(base, 128), slot * w : (slot + 1) * w] = moved.astype(bf16)
        target[pl.ds(base, 128), w : 2 * w] = here
        return kept

    lax.fori_loop(0, FA * FA // 128, step, 0)


class Swap:
    def __init__(self, crops, n, pair, slots, pair_sems, send, recv):
        self.other, self.far = chip_peers(crops, n)
        me = lax.axis_index("chan")
        self.core = lax.rem(me, 2)
        self.mine = lax.axis_index("crop") * (n // 2) + lax.div(me, 2)
        self.pair, self.slots, self.pair_sems = pair, slots, pair_sems
        self.send, self.recv = send, recv

    def start(self):
        here = self.pair.at[self.core]
        copy = remote(here, here, self.pair_sems.at[0], self.pair_sems.at[1], self.other)
        copy.start()
        copy.wait()
        self.slots[self.mine] = self.pair[0] + self.pair[1]
        self.copies = []
        for k, peer in enumerate(self.far):
            slot = self.slots.at[self.mine]
            copy = remote(slot, slot, self.send.at[k], self.recv.at[k], peer)
            copy.start()
            self.copies.append(copy)

    def finish(self):
        for copy in self.copies:
            copy.wait_recv()
        return jnp.sum(self.slots[...], axis=0)

    def drain(self):
        for copy in self.copies:
            copy.wait_send()


class WideSwap:
    def __init__(self, crops, n, pair, first, second, pair_sems, send, recv):
        my_crop, me = lax.axis_index("crop"), lax.axis_index("chan")
        self.core, self.crop, self.chip = lax.rem(me, 2), my_crop, lax.div(me, 2)
        self.other = (my_crop, me + 1 - 2 * self.core)
        self.over_crops = [(lax.rem(my_crop + i, crops), me) for i in range(1, crops)]
        self.over_chips = [(my_crop, lax.rem(me + 2 * j, n)) for j in range(1, n // 2)]
        self.pair, self.first, self.second = pair, first, second
        self.pair_sems, self.send, self.recv = pair_sems, send, recv

    def run(self, then=None):
        here = self.pair.at[self.core]
        copy = remote(here, here, self.pair_sems.at[0], self.pair_sems.at[1], self.other)
        copy.start()
        copy.wait()
        self.first[self.crop] = self.pair[0] + self.pair[1]
        k = 0
        copies = []
        for peer in self.over_crops:
            slot = self.first.at[self.crop]
            copies.append(remote(slot, slot, self.send.at[k], self.recv.at[k], peer))
            copies[-1].start()
            k += 1
        for copy in copies:
            copy.wait()
        self.second[self.chip] = jnp.sum(self.first[...], axis=0)
        copies = []
        for peer in self.over_chips:
            slot = self.second.at[self.chip]
            copies.append(remote(slot, slot, self.send.at[k], self.recv.at[k], peer))
            copies[-1].start()
            k += 1
        if then is not None:
            then()
        for copy in copies:
            copy.wait()
        return jnp.sum(self.second[...], axis=0)


def put_pair(ref, core, a, b):
    ref[core, 0:1] = a[:, :128]
    ref[core, 1:2] = a[:, 128:]
    ref[core, 2:3] = b[:, :128]
    ref[core, 3:4] = b[:, 128:]


def get_pair(total):
    return (
        jnp.concatenate([total[0:1], total[1:2]], axis=1),
        jnp.concatenate([total[2:3], total[3:4]], axis=1),
    )


def spread_row(row):
    return jnp.broadcast_to(row, (128, 128)).T


def up_weights(i, me, n, rows, coarse_rows):
    lower = (2 * i - 3) // 8
    upper_weight = (2 * i - 3 - 8 * lower) / 8.0
    a, b = 1.0 - upper_weight, upper_weight
    if lower < 0:
        top = me == 0
        a, b = jnp.where(top, 0.0, a), jnp.where(top, 1.0, b)
    if lower + 1 >= coarse_rows:
        bottom = me == n - 1
        a, b = jnp.where(bottom, 1.0, a), jnp.where(bottom, 0.0, b)
    if i < 0:
        a, b = jnp.where(me == 0, 0.0, a), jnp.where(me == 0, 0.0, b)
    if i >= rows:
        a, b = jnp.where(me == n - 1, 0.0, a), jnp.where(me == n - 1, 0.0, b)
    return lower + 1, a, b


class DecoderRefs(typing.NamedTuple):
    offsets: object
    feat: object
    point: object
    atrous_hbm: object
    pool_w: object
    low_rows: object
    low_w: object
    w_proj: object
    w_dec1: object
    w_side: object
    w_dec2: object
    w_cls: object
    own_gain: object
    own_shift: object
    low_gain: object
    low_shift: object
    bias: object
    d_logits: object
    logits_hbm: object
    branch_hbm: object
    low_hbm: object
    pack_hbm: object
    dec2_hbm: object
    wgrads_hbm: object
    src_all: object
    low_flat: object
    dlog: object
    near: object
    low_in: object
    atrous: object
    src_own: object
    logits: object
    branch_out: object
    low_out: object
    pack: object
    dec2_w: object
    wgrads: object
    low_ext: object
    low_push: object
    lowx: object
    merged_ext: object
    merged_part: object
    dec1: object
    dec2: object
    pushed: object
    pushed1: object
    x1: object
    x2: object
    g2: object
    g1: object
    yt: object
    branch_bf: object
    proj_bf: object
    flip: object
    branch: object
    staged: object
    arrived: object
    low_send: object
    low_pair: object
    low_sum: object
    low_recv: object
    spare: object
    low_spare: object
    gath: object
    norms_all: object
    norms: object
    proj: object
    w1: object
    tail: object
    w1low: object
    w2: object
    w1_back: object
    w2_back: object
    cls_all: object
    cls_t: object
    dmask: object
    columns: object
    own_w: object
    r_first: object
    r_pairs: object
    r_crossed: object
    r_halves: object
    r_lined: object
    r_out: object
    local: object
    f_send: object
    f_recv: object


def rest_groups(crops):
    return -(-15 // crops) * crops


def weight_groups(crops):
    return -(-8 // crops) * crops, -(-9 // crops) * crops


def decoder_kernel(crops, n, samples, *refs):
    ref = DecoderRefs(*refs[: len(DecoderRefs._fields)])
    rest = list(refs[len(DecoderRefs._fields) :])
    (wide_pair, wide_first, wide_second, wide_psem, wide_send, wide_recv) = rest[:6]
    (pair, slots, psem, send, recv, halo_send, halo_recv) = rest[6:13]

    coarse_samples, fine_samples = samples
    my_crop, me = lax.axis_index("crop"), lax.axis_index("chan")
    core = lax.rem(me, 2)
    above = (my_crop, lax.rem(me + n - 1, n))
    below = (my_crop, lax.rem(me + 1, n))
    low_chans, low_width = ref.low_w.shape
    classes = ref.w_cls.shape[0]
    fine = ref.d_logits.shape[1]
    rows = fine // n
    fine_cells = rows * 128
    coarse_cells = ref.branch.shape[0]
    coarse_rows = coarse_cells // FA
    cells = FA * FA
    c_in, c = ref.point.shape
    own = c // n
    chips, chip = n // 2, lax.div(me, 2)
    small, large = weight_groups(crops)
    chunk = min(4, rows)

    other, far = chip_peers(crops, n)
    over_crops = [(lax.rem(my_crop + i, crops), me) for i in range(1, crops)]
    over_chips = [(my_crop, lax.rem(me + 2 * j, n)) for j in range(1, chips)]
    wait_barrier = barrier_with([other, above, below] + far)

    turn_of = lambda i: 0 if i == 6 else (i + 1) % 2
    swaps = [
        Swap(crops, n, pair.at[i], slots.at[i], psem.at[i], send.at[turn_of(i)], recv.at[i])
        for i in range(pair.shape[0])
    ]
    wides = [
        WideSwap(
            crops, n, wide_pair.at[i], wide_first.at[i], wide_second.at[i],
            wide_psem.at[i], wide_send.at[i], wide_recv.at[i],
        )
        for i in range(2)
    ]
    front = Copies(ref.f_send, ref.f_recv)
    for i in range(pair.shape[0]):
        pair[i, core] = jnp.zeros((8, 128), f32)
    for i in range(2):
        wide_pair[i, core] = jnp.zeros(wide_pair.shape[2:], f32)

    def halo(i, first, last, to_above, to_below):
        copies = [
            remote(first, to_above, halo_send.at[i, 0], halo_recv.at[i, 0], above),
            remote(last, to_below, halo_send.at[i, 1], halo_recv.at[i, 1], below),
        ]
        for copy in copies:
            copy.start()
        return copies

    def fine_halo(i, values):
        return halo(
            i,
            values.at[pl.ds(128, 128)],
            values.at[pl.ds(rows * 128, 128)],
            values.at[pl.ds((rows + 1) * 128, 128)],
            values.at[pl.ds(0, 128)],
        )

    def gain(k):
        return ref.norms[k : k + 1]

    def shift(k):
        return ref.norms[8 + k : 9 + k]

    def moments(total, square, count):
        average = total * (1.0 / count)
        return average, lax.rsqrt(square * (1.0 / count) - average * average + epsilon)

    column = lax.broadcasted_iota(jnp.int32, (128, c), 0)

    def put_three(target, base, y):
        target[pl.ds(base, 128), 0:c] = jnp.where(column == 0, 0.0, pltpu.roll(y, 1, 0)).astype(bf16)
        target[pl.ds(base, 128), c : 2 * c] = y.astype(bf16)
        target[pl.ds(base, 128), 2 * c : 3 * c] = jnp.where(
            column == 127, 0.0, pltpu.roll(y, 127, 0)
        ).astype(bf16)

    def inside(i):
        at_top = jnp.logical_and(me == 0, i == 0)
        at_bottom = jnp.logical_and(me == n - 1, i == rows + 1)
        return jnp.where(jnp.logical_or(at_top, at_bottom), 0.0, 1.0)

    def each_row(body, first, last, carry):
        def step(i, kept):
            return body(i, pl.multiple_of(i * 128, 128), kept)

        return lax.fori_loop(first, last, step, carry)

    zero = jnp.zeros((8, c), f32)

    src_all, src_own, gath = ref.src_all, ref.src_own, ref.gath
    local_copies = []

    def local(src, dst):
        copy = pltpu.make_async_copy(src, dst, ref.local.at[len(local_copies)])
        copy.start()
        local_copies.append(copy)

    local(ref.atrous_hbm, ref.atrous)
    group_at = lax.div(me * rows, 16) * 16
    for k in range(3):
        at = jnp.clip(group_at + 16 * (k - 1), 0, fine - 16)
        local(ref.d_logits.at[:, pl.ds(pl.multiple_of(at, 16), 16)], ref.near.at[k])
    for i in range(cells // 256):
        src_own[pl.ds(i * 256, 256)] = ref.feat[:, i * 256 : (i + 1) * 256].T
    local(src_own, src_all.at[my_crop])
    for i in range(0, ref.low_rows.shape[1], 16):
        here = ref.low_rows[:, i : i + 16].astype(f32)
        ref.low_in[:, i * 128 : (i + 16) * 128] = here.reshape(low_chans, 16 * 128).astype(bf16)
    local(ref.low_in, ref.low_flat)
    flip = ref.flip
    flip[...] = jnp.zeros(flip.shape, f32)
    flip[0:classes, 0:own] = ref.w_cls[...].astype(f32)
    own_cls = flip[0:128, 0:128].T[0:own, 0:classes].astype(bf16)
    flip[0:classes, 0:own] = jnp.zeros((classes, own), f32)
    for t in range(9):
        flip[0:own, 128:256] = jnp.zeros((own, 128), f32)
        flip[0:own, 128 : 128 + low_width] = ref.w_side[t].astype(f32)
        flip[t * low_width : (t + 1) * low_width, 0:128] = flip[0:128, 128:256].T[0:low_width]
    for k in range(5):
        gath[me, k] = ref.w_proj[k]
    turned = flip[:, 0:128].T[0:own].astype(bf16)
    gath[me, 5] = turned[:, 0:c]
    gath[me, 6] = turned[:, c : 2 * c]
    gath[me, 7] = jnp.zeros((own, c), bf16)
    gath[me, 7, :, 0:classes] = own_cls
    for k in range(8, small):
        gath[me, k] = jnp.zeros((own, c), bf16)
    for t in range(9, large):
        gath[me, small + t] = jnp.zeros((own, c), bf16)
        gath[me, small + large + t] = jnp.zeros((own, c), bf16)
    for t in range(9):
        gath[me, small + t] = ref.w_dec1[t]
        gath[me, small + large + t] = ref.w_dec2[t]
    columns = ref.columns
    columns[...] = jnp.zeros(columns.shape, f32)
    columns[0:1, 0:low_width] = ref.low_gain[...]
    columns[1:2, 0:low_width] = ref.low_shift[...]
    columns[2:3, 0:classes] = ref.bias[...]
    ref.norms_all[me] = jnp.zeros((16, 128), f32)
    ref.norms_all[me, 0:8, 0:own] = ref.own_gain[...]
    ref.norms_all[me, 8:16, 0:own] = ref.own_shift[...]
    wait_barrier()
    block_of = lambda j: lax.rem(me - 2 * j + n, n)
    crop_of = lambda i: lax.rem(my_crop - i + crops, crops)

    class Spread:
        def __init__(self, first, size):
            per = size // crops
            self.at = lambda b, q: gath.at[b, pl.ds(first + q * per, per)]
            self.first, self.size = first, size

        def start(self):
            here = self.at(me, my_crop)
            self.far = [front.start(here, here, peer) for peer in over_chips]
            here = gath.at[me, pl.ds(self.first, self.size)]
            self.pairs = [front.start(here, here, other)]

        def cross(self):
            self.crossed = []
            for j in range(1, chips):
                self.far[j - 1].wait_recv()
                here = self.at(block_of(j), my_crop)
                for i in range(1, crops):
                    self.crossed.append((i, j, front.start(here, here, over_crops[i - 1])))
                self.pairs.append(front.start(here, here, other))

        def cores(self):
            for i, j, copy in self.crossed:
                copy.wait_recv()
                here = self.at(block_of(j), crop_of(i))
                self.pairs.append(front.start(here, here, other))

        def finish(self):
            for copy in self.pairs:
                copy.wait_recv()

    norm_far = []
    here = ref.norms_all.at[me]
    for peer in over_chips:
        norm_far.append(front.start(here, here, peer))
    norm_pairs = [front.start(here, here, other)]
    spread = [Spread(0, small), Spread(small, large), Spread(small + large, large)]
    spread[0].start()
    spread[1].start()
    feature_copies = [front.start(src_own, src_all.at[my_crop], peer) for peer in over_crops]
    low_send, low_pair = ref.low_send, ref.low_pair

    def low_block(b):
        span = pl.ds(pl.multiple_of(b * fine_cells, fine_cells), fine_cells)
        return dot_tn(ref.low_w[...], ref.low_in[:, span])

    low_copies = []
    for z in range(chips):
        low_send[z] = low_block(2 * z + 1 - core)
        low_copies.append(front.start(low_send.at[z], low_pair.at[z], other))
    for k in range(3):
        local_copies[1 + k].wait()
        here = ref.near[k].astype(f32).reshape(classes, 16 * 128)
        ref.dlog[0:classes, k * 2048 : (k + 1) * 2048] = here.astype(bf16)
        ref.dlog[classes:32, k * 2048 : (k + 1) * 2048] = jnp.zeros((32 - classes, 2048), bf16)

    part, part_in, staged, arrived = ref.pushed, ref.pushed1, ref.staged, ref.arrived
    shifted = ref.g2

    order = (0, 3, 2, 1)

    def branch_partial(k):
        first = k * cells
        if k == 0:
            part[pl.ds(first, cells)] = dot(src_own[...], ref.point[...])
        else:
            rate = atrous_rates[k - 1]
            if k == order[1]:
                local_copies[0].wait()
            shift_three(lambda base: src_own[pl.ds(base, 128)], shifted, rate, -rate, rate)
            part[pl.ds(first, cells)] = dot(shifted[pl.ds(0, cells), 0 : 3 * c_in], ref.atrous[k - 1, 1])
            for a in (0, 2):
                move = (a - 1) * rate
                count = (FA - abs(move)) * FA
                to, off = first + max(-move, 0) * FA, max(move, 0) * FA
                part[pl.ds(to, count)] += dot(shifted[pl.ds(off, count), 0 : 3 * c_in], ref.atrous[k - 1, a])
        copies = []
        for z in range(chips):
            block = pl.multiple_of(first + (2 * z + 1 - core) * coarse_cells, coarse_cells)
            copies.append(
                front.start(
                    part.at[pl.ds(block, coarse_cells)],
                    part_in.at[pl.ds((k * chips + z) * coarse_cells, coarse_cells)],
                    other,
                )
            )
        return copies

    def pair_sum(k, z):
        block = pl.multiple_of(k * cells + (2 * z + core) * coarse_cells, coarse_cells)
        landed = pl.multiple_of((k * chips + z) * coarse_cells, coarse_cells)
        return part[pl.ds(block, coarse_cells)] + part_in[pl.ds(landed, coarse_cells)]

    waited = []
    branch_lines = [
        LineSum(n, front, staged.at[k], arrived.at[k], ref.spare.at[k], functools.partial(pair_sum, k))
        for k in range(4)
    ]

    def branch_out(k, copies):
        for copy in copies:
            copy.wait()
            waited.append(copy)
        for z in range(chips):
            staged[k, z] = pair_sum(k, z).astype(bf16)
        ref.branch[:, k * c : (k + 1) * c] = pair_sum(k, chip)
        branch_lines[k].start()

    before = branch_partial(order[0])
    for at in range(1, 4):
        after = branch_partial(order[at])
        branch_out(order[at - 1], before)
        before = after
        if at == 2:
            spread[0].cross()
        if at == 1:
            for z in range(chips):
                low_copies[z].wait_recv()
                ref.low_sum[z] = (low_block(2 * z + core) + low_pair[z]).astype(bf16)
            low_line = LineSum(
                n, front, ref.low_sum, ref.low_recv, ref.low_spare, lambda z: low_block(2 * z + core) + low_pair[z]
            )
            low_line.start()
        if at == 2:
            branch_lines[order[0]].second()
        if at == 3:
            spread[1].cross()
            low_line.second()
            branch_lines[order[1]].second()
    branch_out(order[3], before)
    branch_lines[order[2]].second()
    for j in range(1, chips):
        norm_far[j - 1].wait_recv()
        here = ref.norms_all.at[block_of(j)]
        norm_pairs.append(front.start(here, here, other))
    pooled = row_of(src_own[...].astype(f32)) * (1.0 / cells)
    pooled = jnp.concatenate([pooled, jnp.zeros((15, c_in), f32)], axis=0).astype(bf16)
    pool_part = dot(pooled, ref.pool_w[...])[0:1]

    branch_lines[order[3]].second()
    for copy in norm_pairs:
        copy.wait_recv()
    for b in range(n):
        ref.norms[:, b * own : (b + 1) * own] = ref.norms_all[b, :, 0:own]

    low_ext = ref.low_ext
    own_low = pl.ds(128, fine_cells)
    low_ext[:, own_low] = low_block(me) + low_pair[chip]

    def add_to_low(value):
        low_ext[:, own_low] += value

    low_line.finish(add_to_low)
    low_edges = halo(
        0,
        low_ext.at[:, pl.ds(128, 128)],
        low_ext.at[:, pl.ds(rows * 128, 128)],
        low_ext.at[:, pl.ds((rows + 1) * 128, 128)],
        low_ext.at[:, pl.ds(0, 128)],
    )

    def add_low(i, base, kept):
        v = low_ext[:, pl.ds(base, 128)]
        return kept[0] + v, kept[1] + v * v

    low_zero = jnp.zeros((low_width, 128), f32)
    low_sum, low_square = each_row(add_low, 1, rows + 1, (low_zero, low_zero))

    def lanes_of(values):
        return row_of(values.T)

    pair[6, core, 0:1, 0:low_width] = lanes_of(low_sum)
    pair[6, core, 1:2, 0:low_width] = lanes_of(low_square)
    swaps[6].start()

    for k in order:

        def add_to_branch(value, k=k):
            ref.branch[:, k * c : (k + 1) * c] += value

        branch_lines[k].finish(add_to_branch)

    spread[0].cores()
    spread[1].cores()
    wide = wide_pair.at[0]
    for k in range(4):
        v = ref.branch[:, k * c : (k + 1) * c]
        wide[core, k : k + 1] = row_of(v)
        wide[core, 4 + k : 5 + k] = row_of(v * v)
    wide[core, 8:16] = jnp.where(
        lax.broadcasted_iota(jnp.int32, (8, c), 0) == my_crop, pool_part, 0.0
    )
    total_a = wides[0].run(spread[2].start)
    spread[0].finish()
    proj, w1, w2, tail = ref.proj, ref.w1, ref.w2, ref.tail
    for b in range(n):
        mine = pl.ds(b * own, own)
        for k in range(5):
            proj[k, mine] = gath[b, k]

    def place_conv(target, back, first):
        for b in range(n):
            for t in range(9):
                a, e = t // 3, t % 3
                here = gath[b, first + t]
                target[a, pl.ds(e * c + b * own, own)] = here
                back[a, pl.ds(b * own, own), (2 - e) * c : (3 - e) * c] = here

    def branch_parts(k):
        average, inverse = moments(total_a[k : k + 1], total_a[4 + k : 5 + k], coarse_samples)
        normed = (ref.branch[:, k * c : (k + 1) * c] - average) * inverse
        return normed, gain(k) * normed + shift(k), inverse

    projected = jnp.zeros((coarse_cells, c), f32)
    for k in range(4):
        y = gelu(branch_parts(k)[1]).astype(bf16)
        ref.branch_bf[:, k * c : (k + 1) * c] = y
        projected = projected + dot(y, ref.proj[k])
    pool_here = lax.broadcasted_iota(jnp.int32, (8, c), 0) < crops
    pool_pre = total_a[8:16]
    pool_average = row_of(pool_pre) * (1.0 / crops)
    pool_spread = jnp.where(pool_here, pool_pre - pool_average, 0.0)
    pool_inverse = lax.rsqrt(row_of(pool_spread * pool_spread) * (1.0 / crops) + epsilon)
    pool_normed = pool_spread * pool_inverse
    pool_before = gain(4) * pool_normed + shift(4)
    pool_bf = gelu(pool_before)
    pool_bf = jnp.concatenate([pool_bf, jnp.zeros((8, c), f32)], axis=0).astype(bf16)
    pool_term = dot(pool_bf, ref.proj[4])
    my_row = lax.broadcasted_iota(jnp.int32, (16, c), 0) == my_crop
    projected = projected + row_of(jnp.where(my_row, pool_term, 0.0))
    merged_ext = ref.merged_ext
    merged_ext[pl.ds(FA, coarse_cells)] = projected
    put_pair(pair.at[0], core, row_of(projected), row_of(projected * projected))
    merged_copies = halo(
        1,
        merged_ext.at[pl.ds(FA, FA)],
        merged_ext.at[pl.ds(coarse_cells, FA)],
        merged_ext.at[pl.ds(FA + coarse_cells, FA)],
        merged_ext.at[pl.ds(0, FA)],
    )
    swaps[0].start()

    total_l = swaps[6].finish()
    for copy in low_edges:
        copy.wait()
    low_average = total_l[0:1] * (1.0 / fine_samples)
    low_variance = total_l[1:2] * (1.0 / fine_samples) - low_average * low_average
    low_inverse_row = lax.rsqrt(low_variance + epsilon)
    low_average = spread_row(low_average)[0:low_width]
    low_inverse = spread_row(low_inverse_row)[0:low_width]
    lane = lax.broadcasted_iota(jnp.int32, (low_width, 128), 1)
    low_gain = spread_row(columns[0:1])[0:low_width]
    low_shift = spread_row(columns[1:2])[0:low_width]

    def low_parts(base):
        normed = (low_ext[:, pl.ds(base, 128)] - low_average) * low_inverse
        return normed, low_gain * normed + low_shift

    def low_row(i, base, kept):
        y = gelu(low_parts(base)[1]) * inside(i)
        lowx = ref.lowx
        lowx[0:low_width, pl.ds(base, 128)] = jnp.where(lane == 0, 0.0, pltpu.roll(y, 1, 1)).astype(bf16)
        lowx[low_width : 2 * low_width, pl.ds(base, 128)] = y.astype(bf16)
        lowx[2 * low_width : 3 * low_width, pl.ds(base, 128)] = jnp.where(
            lane == 127, 0.0, pltpu.roll(y, 127, 1)
        ).astype(bf16)
        return kept

    each_row(low_row, 0, rows + 2, 0)

    for b in range(n):
        mine = pl.ds(b * own, own)
        tail[mine, 0:c] = gath[b, 5]
        tail[mine, c : 2 * c] = gath[b, 6]
        ref.cls_all[mine] = gath[b, 7, :, 0:128]
    turned = tail[...].T
    for a in range(3):
        ref.w1low[a] = turned[a * 3 * low_width : (a + 1) * 3 * low_width]
    cls_lane = lax.broadcasted_iota(jnp.int32, (c, 128), 1)
    cls_clean = jnp.where(cls_lane < classes, ref.cls_all[...].astype(f32), 0.0)
    ref.cls_t[...] = cls_clean.T[0:32].astype(bf16)
    spread[2].cross()
    merged_sum, merged_square = get_pair(swaps[0].finish())
    for copy in merged_copies:
        copy.wait()
    merged_average, merged_inverse = moments(merged_sum, merged_square, coarse_samples)

    def merged_parts(first, count):
        normed = (merged_ext[pl.ds(first, count)] - merged_average) * merged_inverse
        return normed, gain(5) * normed + shift(5)

    fine_at = lax.broadcasted_iota(jnp.int32, (128, FA), 0).astype(f32)
    coarse_at = lax.broadcasted_iota(jnp.int32, (128, FA), 1).astype(f32)
    place = jnp.clip((fine_at + 0.5) / 4.0 - 0.5, 0.0, FA - 1.0)
    up = jnp.maximum(0.0, 1.0 - jnp.abs(place - coarse_at)).astype(bf16)
    coarse_wide = []
    for j in range(coarse_rows + 2):
        coarse_wide.append(dot_exact(up, gelu(merged_parts(j * FA, FA)[1])))
    for i in range(-1, rows + 1):
        lower, a, b = up_weights(i, me, n, rows, coarse_rows)
        put_three(ref.x1, (i + 1) * 128, a * coarse_wide[lower] + b * coarse_wide[lower + 1])
    spread[1].finish()
    place_conv(w1, ref.w1_back, small)
    dec1, dec2, pushed, pushed1 = ref.dec1, ref.dec2, ref.pushed, ref.pushed1

    def conv_piece(source, weight, base):
        total = None
        for a in range(3):
            term = dot(source[pl.ds(base + a * 128, chunk * 128)], weight[a])
            total = term if total is None else total + term
        return total

    def conv_loop(piece, target):
        def step(i, kept):
            base = pl.multiple_of(i * (chunk * 128), 128)
            total = piece(base)
            target[pl.ds(base + 128, chunk * 128)] = total
            return kept[0] + fold(total), kept[1] + fold(total * total)

        return lax.fori_loop(0, rows // chunk, step, (zero, zero))


    def first_piece(base):
        total = conv_piece(ref.x1, w1, base)
        for a in range(3):
            total = total + dot_tn(ref.lowx[:, pl.ds(base + a * 128, chunk * 128)], ref.w1low[a])
        return total

    total, square = conv_loop(first_piece, dec1)
    spread[2].cores()
    put_pair(pair.at[1], core, row_of(total), row_of(square))
    swaps[6].drain()
    swaps[1].start()
    dec1_copies = fine_halo(2, dec1)
    total, square = get_pair(swaps[1].finish())
    for copy in dec1_copies:
        copy.wait()
    first_average, first_inverse = moments(total, square, fine_samples)

    def first_parts(base):
        normed = (dec1[pl.ds(base, 128)] - first_average) * first_inverse
        return normed, gain(6) * normed + shift(6)

    def first_row(i, base, kept):
        put_three(ref.x2, base, gelu(first_parts(base)[1]) * inside(i))
        return kept

    each_row(first_row, 0, rows + 2, 0)
    spread[2].finish()
    place_conv(w2, ref.w2_back, small + large)
    total, square = conv_loop(lambda base: conv_piece(ref.x2, w2, base), dec2)
    put_pair(pair.at[2], core, row_of(total), row_of(square))
    swaps[0].drain()
    swaps[2].start()
    dec2_copies = fine_halo(3, dec2)
    total, square = get_pair(swaps[2].finish())
    for copy in dec2_copies:
        copy.wait()
    second_average, second_inverse = moments(total, square, fine_samples)

    cls_t = ref.cls_t[...]
    bias = spread_row(columns[2:3])[0:32]
    col_here = ref.offsets[0, 1] + 4 * lax.broadcasted_iota(jnp.int32, (1, 128), 1) < SCENE_W
    col_mask = jnp.where(col_here, 1.0, 0.0)

    def scene_mask(i):
        row_here = ref.offsets[0, 0] + 4 * (me * rows + i - 1) < SCENE_H
        return col_mask * jnp.where(row_here, 1.0, 0.0)

    def masked_row(i, base):
        at = pl.multiple_of(base + (15 + me * rows - group_at) * 128, 128)
        return ref.dlog[:, pl.ds(at, 128)] * (scene_mask(i) * inside(i)).astype(bf16)

    def second_parts(base):
        normed = (dec2[pl.ds(base, 128)] - second_average) * second_inverse
        return normed, gain(7) * normed + shift(7)

    def second_row(i, base, kept):
        normed, before = second_parts(base)
        value, slope = gelu_both(before)
        ref.g1[pl.ds(base, 128), 0:c] = value.astype(bf16)
        masked = masked_row(i, base)
        ref.dmask[:, pl.ds(base, 128)] = masked
        grad = dot_tn(masked, cls_t)
        push = slope * grad
        pushed[pl.ds(base, 128)] = push
        own_row = jnp.where(jnp.logical_and(i > 0, i < rows + 1), 1.0, 0.0)
        push = push * own_row
        return kept[0] + fold(push * normed), kept[1] + fold(push)

    along, summed = each_row(second_row, 0, rows + 2, (zero, zero))
    put_pair(pair.at[3], core, row_of(along), row_of(summed))
    swaps[1].drain()
    swaps[3].start()
    second = ref.g1

    def logit_row(i, base, kept):
        out = pl.multiple_of(base - 128, 128)
        value = dot_nt(cls_t, second[pl.ds(base, 128), 0:c]) + bias
        ref.logits[:, pl.ds(out, 128)] = value * scene_mask(i)
        return kept

    each_row(logit_row, 1, rows + 1, 0)
    local(ref.logits, ref.logits_hbm)
    flip[pl.ds(9 * low_width, 32)] = dot(
        ref.dmask[:, 128 : 128 + fine_cells], second[pl.ds(128, fine_cells), 0:c]
    )
    bias_grad = jnp.zeros((32, 128), f32)
    for i in range(1, rows + 1):
        bias_grad = bias_grad + ref.dmask[:, i * 128 : (i + 1) * 128].astype(f32)
    wide_pair[1, core, 16:17, 0:32] = row_of(bias_grad.T)
    second_along, second_summed = get_pair(swaps[3].finish())

    def pull(push, normed, k, inverse, along, summed, count):
        return (gain(k) * inverse) * (push - summed * (1.0 / count) - normed * (along * (1.0 / count)))

    def dec2_row(i, base, kept):
        g = pull(
            pushed[pl.ds(base, 128)], second_parts(base)[0], 7, second_inverse,
            second_along, second_summed, fine_samples,
        )
        put_three(ref.g2, base, g * inside(i))
        return kept

    each_row(dec2_row, 0, rows + 2, 0)

    def back_loop(source, weight, use, carry):
        def step(i, kept):
            base = pl.multiple_of(i * (chunk * 128), 128)
            total = None
            for a in range(3):
                term = dot_nt(source[pl.ds(base + (2 - a) * 128, chunk * 128)], weight[a])
                total = term if total is None else total + term
            return use(base, total, kept)

        return lax.fori_loop(0, rows // chunk, step, carry)

    def first_use(base, grad, kept):
        at = pl.ds(pl.multiple_of(base + 128, 128), chunk * 128)
        normed = (dec1[at] - first_average) * first_inverse
        push = gelu_slope(gain(6) * normed + shift(6)) * grad
        pushed1[at] = push
        return kept[0] + fold(push * normed), kept[1] + fold(push)

    along, summed = back_loop(ref.g2, ref.w2_back, first_use, (zero, zero))
    put_pair(pair.at[4], core, row_of(along), row_of(summed))
    swaps[2].drain()
    swaps[4].start()
    pushed_copies = fine_halo(4, pushed1)

    wgrads = ref.wgrads

    reduce_two = Reduce(
        crops, n, front, ref.own_w, ref.r_first, ref.r_pairs, ref.r_crossed, ref.r_halves, ref.r_lined, ref.r_out
    )

    def weight_grads(target, source, gradient):
        for a in range(3):
            part = dot_tn(
                source[pl.ds(a * 128, fine_cells), c : 2 * c], gradient[pl.ds(128, fine_cells)]
            ).astype(bf16)
            for e in range(3):
                tap = part[:, (2 - e) * c : (3 - e) * c]
                for h in range(n):
                    target[h, 3 * a + e] = tap[h * own : (h + 1) * own]

    weight_grads(ref.own_w, ref.x2, ref.g2)
    for t in range(9, large):
        for h in range(n):
            ref.own_w[h, t] = jnp.zeros((own, c), bf16)
    reduce_two.cores()
    first_along, first_summed = get_pair(swaps[4].finish())
    reduce_two.over_the_crops()
    for copy in pushed_copies:
        copy.wait()

    def dec1_row(i, base, kept):
        g = pull(
            pushed1[pl.ds(base, 128)], first_parts(base)[0], 6, first_inverse,
            first_along, first_summed, fine_samples,
        ) * inside(i)
        put_three(ref.g1, base, g)
        return kept

    each_row(dec1_row, 0, rows + 2, 0)

    def up_use(base, grad, kept):
        dec2[pl.ds(pl.multiple_of(base + 128, 128), chunk * 128)] = grad
        return kept

    back_loop(ref.g1, ref.w1_back, up_use, 0)
    yt = ref.yt

    def low_back_row(i, local, base, kept):
        total = None
        for t in range(9):
            a, e = t // 3, t % 3
            at = pl.ds((local + 2 - a) * 128, 128)
            piece = yt[t * low_width : (t + 1) * low_width, at]
            if e == 0:
                piece = jnp.where(lane == 127, 0.0, pltpu.roll(piece, 127, 1))
            if e == 2:
                piece = jnp.where(lane == 0, 0.0, pltpu.roll(piece, 1, 1))
            total = piece if total is None else total + piece
        normed, before = low_parts(base)
        push = gelu_slope(before) * total
        ref.low_push[:, pl.ds(pl.multiple_of(base - 128, 128), 128)] = push
        return kept[0] + push * normed, kept[1] + push

    def low_back_chunk(i, kept):
        base = pl.multiple_of(i * (chunk * 128), 128)
        here = ref.g1[pl.ds(base, (chunk + 2) * 128), c : 2 * c]
        for a in range(3):
            yt[a * 3 * low_width : (a + 1) * 3 * low_width] = dot_nt(ref.w1low[a], here)
        for local in range(chunk):
            kept = low_back_row(i, local, pl.multiple_of(base + (local + 1) * 128, 128), kept)
        return kept

    low_along, low_summed = lax.fori_loop(0, rows // chunk, low_back_chunk, (low_zero, low_zero))

    part = ref.merged_part
    fine_at = lax.broadcasted_iota(jnp.int32, (FA, 128), 1).astype(f32)
    coarse_at = lax.broadcasted_iota(jnp.int32, (FA, 128), 0).astype(f32)
    place = jnp.clip((fine_at + 0.5) / 4.0 - 0.5, 0.0, FA - 1.0)
    up_t = jnp.maximum(0.0, 1.0 - jnp.abs(place - coarse_at)).astype(bf16)
    row_sums = [None] * (coarse_rows + 2)
    for i in range(rows):
        lower, a, b = up_weights(i, me, n, rows, coarse_rows)
        grad = dec2[pl.ds((i + 1) * 128, 128)]
        for j, weight in ((lower, a), (lower + 1, b)):
            row_sums[j] = weight * grad if row_sums[j] is None else row_sums[j] + weight * grad
    along, summed = zero, zero
    for j in range(coarse_rows + 2):
        grad = dot_exact(up_t, row_sums[j])
        part[pl.ds(j * FA, FA)] = grad
        normed, before = merged_parts(j * FA, FA)
        push = gelu_slope(before) * grad
        along, summed = along + fold(push * normed), summed + fold(push)
    put_pair(pair.at[5], core, row_of(along), row_of(summed))
    pair[5, core, 4:5, 0:low_width] = lanes_of(low_along)
    pair[5, core, 5:6, 0:low_width] = lanes_of(low_summed)
    part_copies = halo(
        5,
        part.at[pl.ds(0, FA)],
        part.at[pl.ds(FA + coarse_cells, FA)],
        part.at[pl.ds((coarse_rows + 3) * FA, FA)],
        part.at[pl.ds((coarse_rows + 2) * FA, FA)],
    )
    swaps[3].drain()
    swaps[5].start()
    reduce_two.over_the_chips()
    weight_grads(wgrads, ref.x1, ref.g1)
    local(wgrads.at[:, pl.ds(0, 9)], ref.wgrads_hbm.at[:, pl.ds(0, 9)])
    total_g = swaps[5].finish()
    for copy in part_copies:
        copy.wait()
    merged_along, merged_summed = get_pair(total_g)
    low_along, low_summed = spread_row(total_g[4:5])[0:low_width], spread_row(total_g[5:6])[0:low_width]
    pack = ref.pack
    pack[17:18, 0:128] = total_g[4:5]
    pack[18:19, 0:128] = total_g[5:6]
    up_here = jnp.where(me == 0, 0.0, 1.0)
    down_here = jnp.where(me == n - 1, 0.0, 1.0)
    proj_bf = ref.proj_bf
    for j in range(1, coarse_rows + 1):
        grad = part[pl.ds(j * FA, FA)]
        if j == 1:
            grad = grad + up_here * part[pl.ds((coarse_rows + 2) * FA, FA)]
        if j == coarse_rows:
            grad = grad + down_here * part[pl.ds((coarse_rows + 3) * FA, FA)]
        normed, before = merged_parts(j * FA, FA)
        push = gelu_slope(before) * grad
        g = pull(push, normed, 5, merged_inverse, merged_along, merged_summed, coarse_samples)
        proj_bf[pl.ds((j - 1) * FA, FA)] = g.astype(bf16)

    push_all = []
    for k in range(4):
        normed, before, _ = branch_parts(k)
        push = gelu_slope(before) * dot_nt(proj_bf[...], ref.proj[k])
        push_all.append(push)
        wide_pair[1, core, k : k + 1] = row_of(push * normed)
        wide_pair[1, core, 4 + k : 5 + k] = row_of(push)
    proj_row = row_of(proj_bf[...].astype(f32))
    wide_pair[1, core, 8:16] = jnp.where(
        lax.broadcasted_iota(jnp.int32, (8, c), 0) == my_crop, proj_row, 0.0
    )
    total_h = wides[1].run()
    reduce_two.to_all_crops()
    for k in range(4):
        normed, _, inverse = branch_parts(k)
        g = pull(
            push_all[k], normed, k, inverse, total_h[k : k + 1], total_h[4 + k : 5 + k], coarse_samples
        )
        ref.branch_out[:, k * c : (k + 1) * c] = g.astype(bf16)

    sums = total_h[8:16]
    sums_high = sums.astype(bf16).astype(f32)
    sums_low = sums - sums_high
    spare = jnp.concatenate([sums_high, sums_low], axis=0)
    spare_mid = spare.astype(bf16)
    spare_rest = (spare - spare_mid.astype(f32)).astype(bf16)
    pieces = dot_nt(spare_mid, ref.proj[4]) + dot_nt(spare_rest, ref.proj[4])
    pool_push = gelu_slope(pool_before) * (pieces[0:8] + pieces[8:16])
    pool_push = jnp.where(pool_here, pool_push, 0.0)
    pool_along, pool_summed = row_of(pool_push * pool_normed), row_of(pool_push)
    pool_grad = pull(pool_push, pool_normed, 4, pool_inverse, pool_along, pool_summed, crops)
    pool_grad = jnp.where(pool_here, pool_grad, 0.0)
    pack[24:32] = pool_grad
    pack[32:40] = jnp.zeros((8, c), f32)

    gain_rows = [total_h[0:4], pool_along, merged_along, first_along, second_along]
    shift_rows = [total_h[4:8], pool_summed, merged_summed, first_summed, second_summed]
    turn = c - me * own
    pack[0:8] = pltpu.roll(jnp.concatenate(gain_rows, axis=0), turn, 1)
    pack[8:16] = pltpu.roll(jnp.concatenate(shift_rows, axis=0), turn, 1)
    pack[16:17] = total_h[16:17]
    pool_rows = jnp.zeros((c, c), f32)
    rest = jnp.concatenate([sums, jnp.zeros((8, c), f32)], axis=0)
    for _ in range(3):
        high = rest.astype(bf16)
        pool_rows = pool_rows + dot_tn(pool_bf, high)
        rest = rest - high.astype(f32)
    dec1[pl.ds(0, c)] = pool_rows
    pack[40 : 40 + own] = dec1[pl.ds(pl.multiple_of(me * own, own), own)]
    local(pack, ref.pack_hbm)

    def low_out_row(i, base, kept):
        at = pl.ds(pl.multiple_of(base - 128, 128), 128)
        normed = low_parts(base)[0]
        g = (low_gain * low_inverse) * (
            ref.low_push[:, at] - low_summed * (1.0 / fine_samples) - normed * (low_along * (1.0 / fine_samples))
        )
        ref.low_out[:, at] = g.astype(bf16)
        return kept

    each_row(low_out_row, 1, rows + 1, 0)
    local(ref.low_out, ref.low_hbm)
    local(ref.branch_out, ref.branch_hbm)

    for a in range(3):
        flip[pl.ds(a * 3 * low_width, 3 * low_width)] = dot(
            ref.lowx[:, a * 128 : a * 128 + fine_cells], ref.g1[pl.ds(128, fine_cells), c : 2 * c]
        )
    flip[pl.ds(9 * low_width + 32, 48)] = jnp.zeros((48, c), f32)
    turned = flip[...].T.astype(bf16)
    for k in range(4):
        product = dot_tn(ref.branch_bf[:, k * c : (k + 1) * c], proj_bf[...]).astype(bf16)
        for h in range(n):
            rows_h = product[h * own : (h + 1) * own]
            wgrads[h, 9 + k] = rows_h
    for h in range(n):
        wgrads[h, 13] = turned[h * own : (h + 1) * own, 0:c]
        wgrads[h, 14] = turned[h * own : (h + 1) * own, c : 2 * c]
        for k in range(15, wgrads.shape[1]):
            wgrads[h, k] = jnp.zeros((own, c), bf16)
    local(wgrads.at[:, pl.ds(9, wgrads.shape[1] - 9)], ref.wgrads_hbm.at[:, pl.ds(9, wgrads.shape[1] - 9)])
    reduce_two.finish()
    for t in range(9):
        ref.dec2_w[t] = ref.r_out[t].astype(f32)
    local(ref.dec2_w, ref.dec2_hbm)
    for copy in feature_copies:
        copy.wait_recv()
    front.drain(waited)
    swaps[4].drain()
    swaps[5].drain()
    for copy in local_copies[4:]:
        copy.wait()


def decoder(crops, n, samples, *args):
    ref = DecoderRefs(*args, *([None] * (len(DecoderRefs._fields) - len(args))))
    c_in, c = ref.point.shape
    low_width = ref.low_w.shape[1]
    classes, fine = ref.d_logits.shape[:2]
    rows = fine // n
    cells = rows * 128
    coarse = FA * FA // n
    own = c // n
    small, large = weight_groups(crops)
    chips = n // 2
    all_chips = crops * chips
    outer = (rows + 2) * 128
    chunk = min(4, rows)
    count = (crops - 1) + 4 * (2 * chips - 1) + 2 * chips - 1
    count += 2 * chips - 1 + 3 * (1 + 2 * crops * (chips - 1)) + reduce_copies(crops, n) + 5
    S = jax.ShapeDtypeStruct
    V = pltpu.VMEM
    D = pltpu.SemaphoreType.DMA
    vmem = pl.BlockSpec(memory_space=pltpu.VMEM)
    hbm = pl.BlockSpec(memory_space=pl.ANY)
    return pl.pallas_call(
        functools.partial(decoder_kernel, crops, n, samples),
        out_shape=[
            S((32, cells), f32),
            S((coarse, 4 * c), bf16),
            S((low_width, cells), bf16),
            S((40 + own, c), f32),
            S((9, own, c), f32),
            S((n, rest_groups(crops), own, c), bf16),
            S((crops, FA * FA, c_in), bf16),
            S((ref.low_rows.shape[0], ref.low_rows.shape[1] * 128), bf16),
        ],
        in_specs=[pl.BlockSpec(memory_space=pltpu.SMEM), vmem, vmem, hbm] + [vmem] * (len(args) - 5) + [hbm],
        out_specs=[hbm] * 8,
        scratch_shapes=[
            V((32, 48 * 128), bf16),
            V((3, classes, 16, 128), bf16),
            V((ref.low_rows.shape[0], ref.low_rows.shape[1] * 128), bf16),
            V(ref.atrous_hbm.shape, bf16),
            V((FA * FA, c_in), bf16),
            V((32, cells), f32),
            V((coarse, 4 * c), bf16),
            V((low_width, cells), bf16),
            V((40 + own, c), f32),
            V((9, own, c), f32),
            V((n, rest_groups(crops), own, c), bf16),
            V((low_width, outer), f32),
            V((low_width, cells), f32),
            V((3 * low_width, outer), bf16),
            V((coarse + 2 * FA, c), f32),
            V((coarse + 4 * FA, c), f32),
            V((outer, c), f32),
            V((outer, c), f32),
            V((max(outer, 4 * FA * FA), c), f32),
            V((max(outer, 2 * FA * FA), c), f32),
            V((outer, 3 * c), bf16),
            V((outer, 3 * c), bf16),
            V((max(outer, FA * FA), 3 * c), bf16),
            V((outer, 3 * c), bf16),
            V((9 * low_width, (chunk + 2) * 128), f32),
            V((coarse, 4 * c), bf16),
            V((coarse, c), bf16),
            V((512, c), f32),
            V((coarse, 4 * c), f32),
            V((4, chips, coarse, c), bf16),
            V((4, chips, coarse, c), bf16),
            V((chips, low_width, cells), f32),
            V((chips, low_width, cells), f32),
            V((chips, low_width, cells), bf16),
            V((chips, low_width, cells), bf16),
            V((4, coarse, c), bf16),
            V((low_width, cells), bf16),
            V((n, small + 2 * large, own, c), bf16),
            V((n, 16, 128), f32),
            V((16, c), f32),
            V((5, c, c), bf16),
            V((3, 3 * c, c), bf16),
            V((c, 2 * c), bf16),
            V((3, 3 * low_width, c), bf16),
            V((3, 3 * c, c), bf16),
            V((3, c, 3 * c), bf16),
            V((3, c, 3 * c), bf16),
            V((c, 128), bf16),
            V((32, c), bf16),
            V((32, outer), bf16),
            V((8, 128), f32),
            V((n, large, own, c), bf16),
            *reduce_scratch(crops, n, large, own, c),
            D((16,)),
            D((count,)),
            D((count,)),
            V((2, 2, 24, c), f32),
            V((2, crops, 24, c), f32),
            V((2, chips, 24, c), f32),
            D((2, 2)),
            D((2, crops + chips)),
            D((2, crops + chips)),
            V((7, 2, 8, 128), f32),
            V((7, all_chips, 8, 128), f32),
            D((7, 2)),
            D((2, all_chips)),
            D((7, all_chips)),
            D((6, 2)),
            D((6, 2)),
        ],
        compiler_params=pltpu.CompilerParams(
            collective_id=0, has_side_effects=True, vmem_limit_bytes=62 * 1024 * 1024
        ),
    )(*args)


class Reduce:
    def __init__(self, crops, n, copies, source, first, pairs, crossed, halves, lined, out, mine=None, mine_sems=None):
        my_crop, me = lax.axis_index("crop"), lax.axis_index("chan")
        self.crops, self.chips, self.copies = crops, n // 2, copies
        self.crop, self.core, self.chip = my_crop, lax.rem(me, 2), lax.div(me, 2)
        self.other = (my_crop, me + 1 - 2 * self.core)
        self.over_crops = [(lax.rem(my_crop + i, crops), me) for i in range(1, crops)]
        self.over_chips = [(my_crop, lax.rem(me + 2 * j, n)) for j in range(1, n // 2)]
        self.source, self.first, self.pairs, self.crossed = source, first, pairs, crossed
        self.halves, self.lined, self.out = halves, lined, out
        self.mine, self.mine_sems = mine, mine_sems
        self.size = source.shape[1]
        self.share = self.size // crops

    def wait(self):
        for copy in self.moving:
            copy.wait_recv()

    def cores(self):
        self.moving = []
        for z in range(self.chips):
            block = self.source.at[2 * z + 1 - self.core]
            self.moving.append(self.copies.start(block, self.first.at[z], self.other))
        self.loads = []
        if self.mine is not None:
            for z in range(self.chips):
                block = self.source.at[2 * z + self.core]
                self.loads.append(pltpu.make_async_copy(block, self.mine.at[z], self.mine_sems.at[z]))
                self.loads[-1].start()

    def over_the_crops(self):
        self.wait()
        for copy in self.loads:
            copy.wait()
        for z in range(self.chips):
            for g in range(self.size):
                here = self.source[2 * z + self.core, g] if self.mine is None else self.mine[z, g]
                both = here.astype(f32) + self.first[z, g].astype(f32)
                self.pairs[z, g] = both.astype(bf16)
        self.moving = []
        for i in range(1, self.crops):
            target = lax.rem(self.crop + i, self.crops)
            block = self.pairs.at[:, pl.ds(target * self.share, self.share)]
            self.moving.append(
                self.copies.start(block, self.crossed.at[self.crop], self.over_crops[i - 1])
            )
        for z in range(self.chips):
            for g in range(self.share):
                self.crossed[self.crop, z, g] = self.pairs[z, self.crop * self.share + g]

    def over_the_chips(self):
        self.wait()
        for z in range(self.chips):
            for g in range(self.share):
                value = self.crossed[0, z, g].astype(f32)
                for i in range(1, self.crops):
                    value = value + self.crossed[i, z, g].astype(f32)
                self.halves[z, g] = value.astype(bf16)
        self.moving = []
        for j in range(1, self.chips):
            target = lax.rem(self.chip + j, self.chips)
            self.moving.append(
                self.copies.start(
                    self.halves.at[target], self.lined.at[self.chip], self.over_chips[j - 1]
                )
            )
        for g in range(self.share):
            self.lined[self.chip, g] = self.halves[self.chip, g]

    def to_all_crops(self):
        self.wait()
        for g in range(self.share):
            value = self.lined[0, g].astype(f32)
            for z in range(1, self.chips):
                value = value + self.lined[z, g].astype(f32)
            self.out[self.crop * self.share + g] = value.astype(bf16)
        here = self.out.at[pl.ds(self.crop * self.share, self.share)]
        self.moving = [self.copies.start(here, here, peer) for peer in self.over_crops]

    def finish(self):
        self.wait()


def reduce_scratch(crops, n, size, own, c):
    chips, share = n // 2, size // crops
    V = pltpu.VMEM
    return [
        V((chips, size, own, c), bf16),
        V((chips, size, own, c), bf16),
        V((crops, chips, share, own, c), bf16),
        V((chips, share, own, c), bf16),
        V((chips, share, own, c), bf16),
        V((size, own, c), bf16),
    ]


def reduce_copies(crops, n):
    return 2 * (n // 2) - 1 + 2 * (crops - 1)


class Gather:
    def __init__(self, n, send, recv):
        my_crop, self.me = lax.axis_index("crop"), lax.axis_index("chan")
        self.n, self.chips = n, n // 2
        self.core = lax.rem(self.me, 2)
        self.other = (my_crop, self.me + 1 - 2 * self.core)
        self.send, self.recv = send, recv
        self.peer = lambda j: (my_crop, lax.rem(self.me + 2 * j, n))

    def block(self, j):
        return lax.rem(self.me - 2 * j + self.n, self.n)

    def other_block(self, j):
        return lax.rem(self.me + 1 - 2 * self.core - 2 * j + self.n, self.n)

    def start(self, at):
        self.at = at
        self.far, self.pairs = [], []
        for j in range(1, self.chips):
            here = at(self.me)
            self.far.append(remote(here, here, self.send.at[j], self.recv.at[j], self.peer(j)))
            self.far[-1].start()
        self.forward(0)

    def forward(self, j):
        here = self.at(self.block(j))
        k = self.chips + j
        self.pairs.append(remote(here, here, self.send.at[k], self.recv.at[k], self.other))
        self.pairs[-1].start()

    def arrive(self, j):
        self.far[j - 1].wait_recv()
        self.forward(j)

    def finish(self):
        for copy in self.pairs:
            copy.wait_recv()

    def drain(self):
        for copy in self.far + self.pairs:
            copy.wait_send()


class LineGather(Gather):
    def __init__(self, n, send, recv):
        super().__init__(n, send, recv)
        my_crop, self.chip = lax.axis_index("crop"), lax.div(self.me, 2)
        self.end = jnp.logical_or(self.chip == 0, self.chip == 3)
        self.inner = jnp.logical_not(self.end)
        beside = self.chip + 1 - 2 * lax.rem(self.chip, 2)
        over, mirror = lax.rem(self.chip + 2, 4), 3 - self.chip
        second = jnp.where(self.end, over, mirror)
        third = jnp.where(self.end, mirror, over)
        self.order = [2 * z + self.core for z in (self.chip, beside, second, third)]
        self.to = lambda z: (my_crop, 2 * z + self.core)
        self.beside, self.over, self.mirror = beside, over, mirror

    def block(self, j):
        return self.order[j]

    def start(self, at):
        self.at = at
        self.pairs = []
        here = at(self.me)
        make = lambda k, block, z, s=None: remote(
            block, block, self.send.at[k if s is None else s], self.recv.at[k], self.to(z)
        )
        self.first = make(0, here, self.beside)
        self.first.start()
        self.middle = make(1, here, self.mirror)
        self.long = make(2, here, self.over, 1)
        pl.when(self.inner)(self.middle.start)
        pl.when(self.end)(self.long.start)
        self.passed = [make(3, at(self.order[2]), self.beside), make(8, at(self.order[3]), self.beside)]
        self.forward(0)

    def arrive(self, j):
        if j == 1:
            self.first.wait_recv()
        else:
            come, on = (self.middle, self.long)[j - 2], self.passed[j - 2]

            def pass_it():
                come.wait_recv()
                on.start()

            pl.when(self.inner)(pass_it)
            pl.when(self.end)(on.wait_recv)
        self.forward(j)

    def drain(self):
        self.first.wait_send()
        self.middle.wait_send()
        for copy in self.pairs:
            copy.wait_send()

        def passed():
            for copy in self.passed:
                copy.wait_send()

        pl.when(self.inner)(passed)


def gather_over(n, send, recv):
    return LineGather(n, send, recv) if n // 2 == 4 else Gather(n, send, recv)


class BackRefs(typing.NamedTuple):
    grad: object
    src_hbm: object
    point: object
    atrous_hbm: object
    pool: object
    pack: object
    low_grad: object
    low_in_hbm: object
    wgrads: object
    features_hbm: object
    point_w: object
    atrous_w_hbm: object
    pool_w: object
    low_w_out: object
    blocks: object
    low_full_hbm: object
    last_grad: object
    last_src: object
    src: object
    atrous: object
    low_in: object
    features: object
    atrous_w: object
    low_full: object
    mine: object
    local: object
    m_sems: object
    w_sems: object
    all_grad: object
    shifted: object
    turned: object
    total: object
    r_first: object
    r_pairs: object
    r_crossed: object
    r_halves: object
    r_lined: object
    r_out: object
    low_parts: object
    g_send: object
    g_recv: object
    l_send: object
    l_recv: object
    c_send: object
    c_recv: object


def back_kernel(crops, n, *refs):
    ref = BackRefs(*refs)
    my_crop, me = lax.axis_index("crop"), lax.axis_index("chan")
    chips = n // 2
    core, chip = lax.rem(me, 2), lax.div(me, 2)
    block, width = ref.grad.shape
    c = width // 4
    half = width // 2
    c_in = ref.src.shape[2]
    cells = FA * FA
    relay = crops == 4
    other = (my_crop, me + 1 - 2 * core)
    over_crops = [(lax.rem(my_crop + i, crops), me) for i in range(1, crops)]
    over_chips = [(my_crop, lax.rem(me + 2 * j, n)) for j in range(1, chips)]
    wait_barrier = barrier_with([other] + over_crops + over_chips)
    all_grad, src = ref.all_grad, ref.src
    if relay:
        along_x = my_crop + 1 - 2 * lax.rem(my_crop, 2)
        along_y = my_crop + 2 - 4 * lax.div(my_crop, 2)
        crop_list = [my_crop, along_x, along_y, 3 - my_crop]
    else:
        crop_list = [my_crop] + [lax.rem(my_crop - i + crops, crops) for i in range(1, crops)]

    def grad_at(crop):
        def at(b):
            return all_grad.at[crop, pl.ds(pl.multiple_of(b * block, block), block)]

        return at

    def lanes_at(crop, b, first):
        return all_grad.at[crop, pl.ds(pl.multiple_of(b * block, block), block), pl.ds(first, half)]

    local_copies = []

    def local(src, dst):
        copy = pltpu.make_async_copy(src, dst, ref.local.at[len(local_copies)])
        copy.start()
        local_copies.append(copy)

    local(ref.src_hbm, src)
    local(ref.src_hbm.at[crop_list[-1]], ref.last_src)
    weight_copies = []
    for k in range(3):
        for t in range(9):
            at = ref.atrous.at[k, t // 3, :, pl.ds(t % 3 * c, c)]
            copy = pltpu.make_async_copy(ref.atrous_hbm.at[k, t], at, ref.w_sems.at[9 * k + t])
            copy.start()
            weight_copies.append(copy)
    local(ref.low_in_hbm, ref.low_in)
    pooled_grad = ref.pack[24:40].astype(bf16)
    all_grad[my_crop, pl.ds(pl.multiple_of(me * block, block), block)] = ref.grad[...]
    ref.low_full[me] = ref.low_grad[...]
    wait_barrier()

    gather = gather_over(n, ref.g_send, ref.g_recv)
    gather.start(grad_at(my_crop))
    moves = Copies(ref.c_send, ref.c_recv)
    crossing = {}

    def cross(j):
        here = grad_at(my_crop)(gather.block(j))
        if relay:
            for i, crop in ((1, along_x), (2, along_y)):
                crossing[i, j] = moves.start(here, here, (crop, me))
        else:
            for i in range(1, crops):
                crossing[i, j] = moves.start(here, here, over_crops[i - 1])

    core_copies = {}

    def pass_on(i, j):
        crossing[i, j].wait_recv()
        b = gather.block(j)
        crop = crop_list[i]
        if relay and i == 1:
            here = lanes_at(crop, b, 0)
            crossing[3, j, 0] = moves.start(here, here, (along_y, me))
        if relay and i == 2:
            here = lanes_at(crop, b, half)
            crossing[3, j, 1] = moves.start(here, here, (along_x, me))
        place = grad_at(crop)(b)
        core_copies[i, j] = moves.start(place, place, other)

    def pass_across(j):
        crossing[3, j, 0].wait_recv()
        crossing[3, j, 1].wait_recv()
        place = grad_at(crop_list[3])(gather.block(j))
        core_copies[3, j] = moves.start(place, place, other)

    cross(0)
    reduce = Reduce(
        crops, n, moves, ref.wgrads, ref.r_first, ref.r_pairs, ref.r_crossed, ref.r_halves, ref.r_lined, ref.r_out,
        ref.mine, ref.m_sems,
    )
    reduce.cores()
    shifted = ref.shifted

    def shift_source(i):
        crop = crop_list[i]
        for k in range(3):
            rate = atrous_rates[k]
            shift_three(lambda base: src[crop, pl.ds(base, 128)], shifted.at[i % 3, k], rate, -rate, rate)

    local_copies[0].wait()
    shift_source(0)
    reduce.over_the_crops()
    for i in range(1, min(3, crops)):
        shift_source(i)
    pooled = []
    for i in range(crops):
        mean = row_of(src[i].astype(f32)) * (1.0 / cells)
        pooled.append(mean)
    pooled = jnp.concatenate(pooled + [jnp.zeros((16 - crops, c_in), f32)], axis=0).astype(bf16)
    ref.pool_w[...] = dot_tn(pooled, pooled_grad)
    for j in range(1, chips):
        gather.arrive(j)
        cross(j)
    reduce.over_the_chips()
    low_gather = Gather(n, ref.l_send, ref.l_recv)
    low_gather.start(lambda b: ref.low_full.at[b])
    if relay:
        pass_on(1, 0)
        pass_on(2, 0)
    gather.finish()

    total, turned = ref.total, ref.turned
    pool_row = dot_nt(pooled_grad, ref.pool[...])
    my_row = lax.broadcasted_iota(jnp.int32, pool_row.shape, 0) == my_crop
    pool_row = row_of(jnp.where(my_row, pool_row, 0.0)) * (1.0 / cells)
    for copy in weight_copies:
        copy.wait()
    total[...] = dot_nt(all_grad[my_crop, :, 0:c], ref.point[...]) + pool_row
    for k in range(3):
        rate = atrous_rates[k]
        shift_three(
            lambda base: all_grad[my_crop, pl.ds(base, 128), (k + 1) * c : (k + 2) * c],
            turned, rate, rate, -rate,
        )
        for a in range(3):
            move = (a - 1) * rate
            count = (FA - abs(move)) * FA
            to, off = max(move, 0) * FA, max(-move, 0) * FA
            total[pl.ds(to, count)] += dot_nt(turned[pl.ds(off, count)], ref.atrous[k, a])

    def weight_part(i):
        crop = crop_list[i]
        part = dot_tn(src[crop], all_grad[crop, :, 0:c])
        ref.point_w[...] = part if i == 0 else ref.point_w[...] + part
        for k in range(3):
            rate = atrous_rates[k]
            for a in range(3):
                move = (a - 1) * rate
                count = (FA - abs(move)) * FA
                from_src, off = max(move, 0) * FA, max(-move, 0) * FA
                part = dot_tn(
                    shifted[i % 3, k, pl.ds(from_src, count)],
                    all_grad[crop, pl.ds(off, count), (k + 1) * c : (k + 2) * c],
                )
                for e in range(3):
                    piece = part[e * c_in : (e + 1) * c_in]
                    if i > 0:
                        piece = ref.atrous_w[k, 3 * a + e] + piece
                    ref.atrous_w[k, 3 * a + e] = piece
            if i == crops - 2:
                local(ref.atrous_w.at[k], ref.atrous_w_hbm.at[k])

    weight_part(0)
    ref.features[...] = total[...].T
    local(ref.features, ref.features_hbm)
    if relay:
        for j in range(1, chips):
            pass_on(1, j)
            pass_on(2, j)

    def low_part():
        for j in range(1, chips):
            low_gather.arrive(j)
        low_gather.finish()
        local(ref.low_full, ref.low_full_hbm)
        local_copies[2].wait()
        rows = ref.low_full.shape[2] // 128
        low_in, low_all = ref.low_in, ref.low_full
        low_total = None
        for b in range(n):
            here = low_all[b]
            span = slice(b * rows * 128, (b + 1) * rows * 128)
            part = dot_nt(low_in[:, span], here)
            low_total = part if low_total is None else low_total + part
        low_parts = ref.low_parts
        low_parts[my_crop] = jnp.zeros(low_parts.shape[1:], f32)
        low_parts[my_crop, :, 0 : low_total.shape[1]] = low_total
        here = low_parts.at[my_crop]
        low_copies = [moves.start(here, here, peer) for peer in over_crops]
        return low_copies

    for i in range(1, crops):
        if i + 2 < crops - 1:
            shift_source(i + 2)
        for j in range(chips):
            if not relay:
                pass_on(i, j)
            elif i == 3:
                pass_across(j)
        for j in range(chips):
            core_copies[i, j].wait_recv()
        if i < crops - 1:
            weight_part(i)
        if i == min(2, crops - 1):
            reduce.to_all_crops()
            low_copies = low_part()

    local(all_grad.at[crop_list[-1]], ref.last_grad)
    reduce.finish()
    for g in range(ref.blocks.shape[0]):
        ref.blocks[g] = ref.r_out[g].astype(f32)
    for copy in low_copies:
        copy.wait_recv()
    ref.low_w_out[...] = jnp.sum(ref.low_parts[...], axis=0)
    gather.drain()
    low_gather.drain()
    moves.drain([])
    for k, copy in enumerate(local_copies):
        if k not in (0, 2):
            copy.wait()


def pyramid_back(crops, n, *args):
    grad, src, low_grad, low_in, wgrads = args[0], args[1], args[6], args[7], args[8]
    block, width = grad.shape
    c = width // 4
    c_in = src.shape[2]
    chips = n // 2
    cells = FA * FA
    low_rows = low_in.shape[0]
    own, lanes = wgrads.shape[2:]
    S = jax.ShapeDtypeStruct
    V = pltpu.VMEM
    D = pltpu.SemaphoreType.DMA
    vmem = pl.BlockSpec(memory_space=pltpu.VMEM)
    hbm = pl.BlockSpec(memory_space=pl.ANY)
    count = 3 * crops * chips + crops - 1 + reduce_copies(crops, n)
    return pl.pallas_call(
        functools.partial(back_kernel, crops, n),
        out_shape=[
            S((c_in, cells), f32),
            S((c_in, c), f32),
            S((3, 9, c_in, c), f32),
            S((c_in, c), f32),
            S((low_rows, 128), f32),
            S((15, own, lanes), f32),
            S((n,) + low_grad.shape, bf16),
            S((cells, width), bf16),
            S((cells, c_in), bf16),
        ],
        in_specs=[vmem, hbm, vmem, hbm, vmem, vmem, vmem, hbm, hbm],
        out_specs=[hbm, vmem, hbm, vmem, vmem, vmem, hbm, hbm, hbm],
        scratch_shapes=[
            V(src.shape, bf16),
            V((3, 3, c_in, 3 * c), bf16),
            V(low_in.shape, bf16),
            V((c_in, cells), f32),
            V((3, 9, c_in, c), f32),
            V((n,) + low_grad.shape, bf16),
            V((chips,) + wgrads.shape[1:], bf16),
            D((12,)),
            D((chips,)),
            D((27,)),
            V((crops, cells, width), bf16),
            V((min(3, crops), 3, cells, 3 * c_in), bf16),
            V((cells, 3 * c), bf16),
            V((cells, c_in), f32),
            *reduce_scratch(crops, n, wgrads.shape[1], own, lanes),
            V((crops, low_rows, 128), f32),
            D((n + 1,)),
            D((n + 1,)),
            D((n + 1,)),
            D((n + 1,)),
            D((count,)),
            D((count,)),
        ],
        compiler_params=pltpu.CompilerParams(
            collective_id=1, has_side_effects=True, vmem_limit_bytes=62 * 1024 * 1024
        ),
    )(*args)


class FinishRefs(typing.NamedTuple):
    atrous_part: object
    point_part: object
    last_grad: object
    last_src: object
    features_in: object
    pool_in: object
    low_full: object
    low_w: object
    low_w_part: object
    logits_in: object
    dec2_in: object
    blocks: object
    pack: object
    logits: object
    features: object
    early: object
    point: object
    atrous: object
    pool: object
    proj: object
    low_w_out: object
    dec1: object
    side: object
    dec2: object
    cls: object
    bias: object
    gain: object
    shift: object
    low_gain: object
    low_shift: object
    v_atrous: object
    v_grad: object
    v_src: object
    v_low: object
    v_logits: object
    v_early: object
    v_point: object
    v_proj: object
    v_low_w: object
    v_side: object
    v_cls: object
    v_bias: object
    v_gain: object
    v_shift: object
    v_low_gain: object
    v_low_shift: object
    turned: object
    sems: object


def finish_kernel(*refs):
    ref = FinishRefs(*refs)
    copies = []

    def move(src, dst):
        copy = pltpu.make_async_copy(src, dst, ref.sems.at[len(copies)])
        copy.start()
        copies.append(copy)
        return copy

    c_in, c = ref.v_point.shape
    classes, rows = ref.v_logits.shape[0], ref.v_logits.shape[1]
    low_width = ref.v_low_w.shape[1]
    own = ref.v_cls.shape[1]
    loaded = [move(ref.last_grad, ref.v_grad), move(ref.last_src, ref.v_src)]
    parts = [move(ref.atrous_part.at[k], ref.v_atrous.at[k]) for k in range(3)]
    low = move(ref.low_full, ref.v_low)
    straight = [
        move(ref.features_in, ref.features),
        move(ref.pool_in, ref.pool),
        move(ref.dec2_in, ref.dec2),
        move(ref.blocks.at[pl.ds(0, 9)], ref.dec1),
        move(ref.blocks.at[pl.ds(9, 4)], ref.proj.at[pl.ds(0, 4)]),
        move(ref.pack.at[pl.ds(40, own)], ref.proj.at[4]),
    ]

    ref.v_logits[...] = ref.logits_in[0:classes].reshape(classes, rows, 128)
    straight.append(move(ref.v_logits, ref.logits))
    pack = ref.pack
    tail = jnp.concatenate([ref.blocks[13], ref.blocks[14]], axis=1)
    width = 2 * c
    for t in range(9):
        ref.v_side[t] = pltpu.roll(tail, (width - t * low_width) % width, 1)[:, 0:low_width]
    cls = pltpu.roll(tail, width - 9 * low_width, 1)[:, 0:128]
    cls = jnp.concatenate([cls, jnp.zeros((128 - own, 128), f32)], axis=0)
    ref.v_cls[...] = cls.T[0:classes, 0:own]
    ref.v_low_w[...] = ref.low_w_part[:, 0:low_width]
    ref.v_gain[...] = pack[0:8, 0:own]
    ref.v_shift[...] = pack[8:16, 0:own]
    ref.v_bias[...] = pack[16:17, 0:classes]
    ref.v_low_gain[...] = pack[17:18, 0:low_width]
    ref.v_low_shift[...] = pack[18:19, 0:low_width]
    for src, dst in (
        (ref.v_side, ref.side),
        (ref.v_cls, ref.cls),
        (ref.v_low_w, ref.low_w_out),
        (ref.v_gain, ref.gain),
        (ref.v_shift, ref.shift),
        (ref.v_bias, ref.bias),
        (ref.v_low_gain, ref.low_gain),
        (ref.v_low_shift, ref.low_shift),
    ):
        straight.append(move(src, dst))

    for copy in loaded:
        copy.wait()
    for k in range(3):
        rate = atrous_rates[k]
        shift_three(lambda base: ref.v_src[pl.ds(base, 128)], ref.turned, rate, -rate, rate)
        parts[k].wait()
        for a in range(3):
            by = (a - 1) * rate
            count = (FA - abs(by)) * FA
            from_src, off = max(by, 0) * FA, max(-by, 0) * FA
            part = dot_tn(
                ref.turned[pl.ds(from_src, count)],
                ref.v_grad[pl.ds(off, count), (k + 1) * c : (k + 2) * c],
            )
            for e in range(3):
                ref.v_atrous[k, 3 * a + e] += part[e * c_in : (e + 1) * c_in]
        straight.append(move(ref.v_atrous.at[k], ref.atrous.at[k]))
        if k == 0:
            low.wait()
            for b in range(ref.low_full.shape[0]):
                value = dot(ref.low_w[...], ref.v_low[b])
                ref.v_early[:, b * rows : (b + 1) * rows] = value.reshape(value.shape[0], rows, 128)
            straight.append(move(ref.v_early, ref.early))
            ref.v_point[...] = ref.point_part[...] + dot_tn(ref.v_src[...], ref.v_grad[:, 0:c])
            straight.append(move(ref.v_point, ref.point))
    for copy in straight:
        copy.wait()


def finish(shapes, *args):
    parts = FinishRefs(*args, *([None] * (len(FinishRefs._fields) - len(args))))
    c_in = parts.point_part.shape[0]
    vmem = pl.BlockSpec(memory_space=pltpu.VMEM)
    hbm = pl.BlockSpec(memory_space=pl.ANY)
    V = pltpu.VMEM
    held = [V(shapes[k], f32) for k in (0, 2, 3)]
    held += [V(shapes[k], f32) for k in (6, 7, 9, 11, 12, 13, 14, 15, 16)]
    return pl.pallas_call(
        finish_kernel,
        out_shape=[jax.ShapeDtypeStruct(shape, f32) for shape in shapes],
        in_specs=[hbm, vmem, hbm, hbm, vmem, vmem, hbm, vmem, vmem, vmem, vmem, vmem, vmem],
        out_specs=[hbm] * len(shapes),
        scratch_shapes=[
            V(parts.atrous_part.shape, f32),
            V(parts.last_grad.shape, bf16),
            V(parts.last_src.shape, bf16),
            V(parts.low_full.shape, bf16),
            *held,
            V((FA * FA, 3 * c_in), bf16),
            pltpu.SemaphoreType.DMA((32,)),
        ],
        compiler_params=pltpu.CompilerParams(vmem_limit_bytes=60 * 1024 * 1024),
    )(*args)


def per_device(
    features,
    low_in,
    offsets,
    d_logits,
    w_point,
    w_atrous,
    w_pool,
    w_proj,
    w_low,
    w_dec1,
    w_dec1_low,
    w_dec2,
    w_cls,
    b_cls,
    bn_gain,
    bn_shift,
    low_gain,
    low_shift,
):
    n = lax.axis_size("chan")
    crops = lax.axis_size("crop")
    fine = low_in.shape[2]
    rows = fine // n
    coarse_rows = FA // n
    channels = w_dec2.shape[2]
    c_in = features.shape[1]
    low_width = w_low.shape[1]
    coarse_samples = FA * FA * crops
    fine_samples = fine * fine * crops

    classes = w_cls.shape[1]
    logits, branch_grad, low_pre_bf, pack, dec2_wgrad, blocks, source_all, low_flat = decoder(
        crops,
        n,
        (coarse_samples, fine_samples),
        offsets,
        features[0],
        w_point,
        w_atrous.reshape(3, 3, 3 * c_in, channels),
        w_pool,
        low_in[0],
        w_low,
        w_proj,
        w_dec1,
        w_dec1_low.transpose(0, 2, 1),
        w_dec2,
        w_cls.T,
        bn_gain,
        bn_shift,
        low_gain[None],
        low_shift[None],
        b_cls[None],
        d_logits[0],
    )
    feature_grad, point_wgrad, atrous_wgrad, pool_wgrad, low_wgrad, blocks, low_full, last_grad, last_src = (
        pyramid_back(
            crops,
            n,
            branch_grad,
            source_all,
            w_point,
            w_atrous,
            w_pool,
            pack,
            low_pre_bf,
            low_flat,
            blocks,
        )
    )
    own = w_dec2.shape[1]
    shapes = [
        (classes, rows, fine),
        (c_in, FA * FA),
        low_in.shape[1:],
        (c_in, channels),
        (3, 9, c_in, channels),
        (c_in, channels),
        (5, own, channels),
        (low_in.shape[1], low_width),
        (9, own, channels),
        (9, own, low_width),
        (9, own, channels),
        (classes, own),
        (1, classes),
        (8, own),
        (8, own),
        (1, low_width),
        (1, low_width),
    ]
    outs = finish(
        shapes,
        atrous_wgrad,
        point_wgrad,
        last_grad,
        last_src,
        feature_grad,
        pool_wgrad,
        low_full,
        w_low,
        low_wgrad,
        logits,
        dec2_wgrad,
        blocks,
        pack,
    )
    outs = list(outs)
    for k in (0, 1, 2):
        outs[k] = outs[k][None]
    for k in (12, 15, 16):
        outs[k] = outs[k][0]
    outs[9] = outs[9].transpose(0, 2, 1)
    outs[11] = outs[11].T
    return tuple(outs)


def solution(mesh):
    placed = (
        P("crop", "chan", None),
        P("crop", "chan", None, None),
        P("crop", None),
        P("crop", None, None, None),
        P("chan", None),
        P(None, None, "chan", None),
        P("chan", None),
        P(None, "chan", None),
        P("chan", None),
        P(None, "chan", None),
        P(None, None, "chan"),
        P(None, "chan", None),
        P("chan", None),
        P(),
        P(None, "chan"),
        P(None, "chan"),
        P(),
        P(),
    )
    return jax.shard_map(
        per_device,
        mesh=mesh,
        in_specs=placed,
        out_specs=(
            P("crop", None, "chan", None),
            P("crop", "chan", None),
            P("crop", "chan", None, None),
            P("chan", None),
            P(None, None, "chan", None),
            P("chan", None),
            P(None, "chan", None),
            P("chan", None),
            P(None, "chan", None),
            P(None, None, "chan"),
            P(None, "chan", None),
            P("chan", None),
            P(),
            P(None, "chan"),
            P(None, "chan"),
            P(),
            P(),
        ),
        check_vma=False,
    )
```

```python
import functools
import typing

import jax
import jax.numpy as jnp
from jax import lax
from jax.experimental import pallas as pl
from jax.experimental.pallas import tpu as pltpu
from jax.sharding import PartitionSpec as P

FA = 32
SCENE_H = 1024
SCENE_W = 2048

epsilon = 1e-05
highest = lax.Precision.HIGHEST
atrous_rates = (6, 12, 18)
f32 = jnp.float32
bf16 = jnp.bfloat16
BOTH = ("crop", "chan")


MESH = pl.DeviceIdType.MESH


def chip_peers(crops, n):
    my_crop, me = lax.axis_index("crop"), lax.axis_index("chan")
    core = lax.rem(me, 2)
    chips = n // 2
    other = (my_crop, me + 1 - 2 * core)
    far = []
    for i in range(crops):
        for j in range(chips):
            if i or j:
                far.append((lax.rem(my_crop + i, crops), lax.rem(me + 2 * j, n)))
    return other, far


GELU_A = 0.7978845608028654
GELU_B = 0.044715


def gelu(x):
    return 0.5 * x * (1.0 + jnp.tanh(GELU_A * (x + GELU_B * x * x * x)))


def gelu_both(x):
    square = x * x
    t = jnp.tanh(GELU_A * x * (1.0 + GELU_B * square))
    upper = 0.5 * (1.0 + t)
    return x * upper, upper + (0.5 * GELU_A) * x * (1.0 - t * t) * (1.0 + (3.0 * GELU_B) * square)


def gelu_slope(x):
    square = x * x
    t = jnp.tanh(GELU_A * x * (1.0 + GELU_B * square))
    return 0.5 * (1.0 + t) + (0.5 * GELU_A) * x * (1.0 - t * t) * (1.0 + (3.0 * GELU_B) * square)


def dot(a, b):
    return jnp.dot(a, b, preferred_element_type=f32)


def dot_nt(a, b):
    return lax.dot_general(a, b, (((1,), (1,)), ((), ())), preferred_element_type=f32)


def dot_tn(a, b):
    return lax.dot_general(a, b, (((0,), (0,)), ((), ())), preferred_element_type=f32)


def dot_exact(table, values):
    high = values.astype(bf16)
    rest = values - high.astype(f32)
    middle = rest.astype(bf16)
    low = (rest - middle.astype(f32)).astype(bf16)
    return dot(table, high) + (dot(table, middle) + dot(table, low))


def fold(values):
    return jnp.sum(values.reshape(values.shape[0] // 8, 8, values.shape[1]), axis=0)


def row_of(values):
    return jnp.sum(values, axis=0, keepdims=True)


def barrier_with(peers):
    barrier = pltpu.get_barrier_semaphore()
    for peer in peers:
        pl.semaphore_signal(barrier, inc=1, device_id=peer, device_id_type=MESH)
    return lambda: pl.semaphore_wait(barrier, len(peers))


def remote(src, dst, send, recv, peer):
    return pltpu.make_async_remote_copy(
        src_ref=src, dst_ref=dst, send_sem=send, recv_sem=recv, device_id=peer, device_id_type=MESH
    )


class Copies:
    def __init__(self, send, recv):
        self.send, self.recv, self.all, self.next = send, recv, [], 0

    def make(self, src, dst, peer, send=None):
        k = self.next
        self.next += 1
        return remote(src, dst, self.send.at[k if send is None else send], self.recv.at[k], peer)

    def start(self, src, dst, peer):
        copy = self.make(src, dst, peer)
        copy.start()
        self.all.append(copy)
        return copy

    def drain(self, kept):
        for copy in self.all:
            if not any(copy is other for other in kept):
                copy.wait_send()


class LineSum:
    def __init__(self, n, copies, staged, arrived, spare, refill):
        my_crop, me = lax.axis_index("crop"), lax.axis_index("chan")
        core, self.chip = lax.rem(me, 2), lax.div(me, 2)
        self.chips, self.copies, self.staged, self.arrived = n // 2, copies, staged, arrived
        self.spare, self.refill = spare, refill
        self.peer = lambda z: (my_crop, 2 * z + core)
        self.line = self.chips == 4
        if self.line:
            self.beside = self.chip + 1 - 2 * lax.rem(self.chip, 2)
            self.over = lax.rem(self.chip + 2, 4)
            self.mirror = 3 - self.chip
            self.end = jnp.logical_or(self.chip == 0, self.chip == 3)
            self.inner = jnp.logical_not(self.end)

    def send(self, z):
        return self.copies.start(self.staged.at[z], self.arrived.at[self.chip], self.peer(z))

    def start(self):
        if not self.line:
            targets = [lax.rem(self.chip + j, self.chips) for j in range(1, self.chips)]
            self.direct = [self.send(z) for z in targets]
            return
        here = self.staged.at[self.mirror]
        k = self.copies.next
        self.passed = self.copies.make(here, self.spare, self.peer(self.beside))
        self.middle = self.copies.make(here, self.arrived.at[self.chip], self.peer(self.mirror), k)
        self.copies.all.append(self.passed)
        pl.when(self.end)(self.passed.start)
        pl.when(self.inner)(self.middle.start)
        self.first = self.send(self.beside)

    def second(self):
        if not self.line:
            return

        def merge():
            self.passed.wait_recv()
            both = self.refill(self.over) + self.spare[...].astype(f32)
            self.staged[self.over] = both.astype(bf16)

        pl.when(self.inner)(merge)
        self.crossed = self.send(self.over)

    def finish(self, add):
        if not self.line:
            for j in range(1, self.chips):
                self.direct[j - 1].wait_recv()
                add(self.arrived[lax.rem(self.chip - j + self.chips, self.chips)].astype(f32))
            return
        self.first.wait_recv()
        add(self.arrived[self.beside].astype(f32))

        def third():
            self.middle.wait_recv()
            add(self.arrived[self.mirror].astype(f32))

        pl.when(self.inner)(third)
        self.crossed.wait_recv()
        add(self.arrived[self.over].astype(f32))


def shift_three(source, target, rate, first, last):
    column = lax.rem(lax.broadcasted_iota(jnp.int32, (128, 1), 0), FA)

    def step(i, kept):
        base = pl.multiple_of(i * 128, 128)
        here = source(base)
        w = here.shape[1]
        wide = here.astype(f32)
        for slot, by in ((0, first), (2, last)):
            ok = jnp.logical_and(column + by >= 0, column + by < FA)
            moved = jnp.where(ok, pltpu.roll(wide, (-by) % 128, 0), 0.0)
            target[pl.ds(base, 128), slot * w : (slot + 1) * w] = moved.astype(bf16)
        target[pl.ds(base, 128), w : 2 * w] = here
        return kept

    lax.fori_loop(0, FA * FA // 128, step, 0)


class Swap:
    def __init__(self, crops, n, pair, slots, pair_sems, send, recv):
        self.other, self.far = chip_peers(crops, n)
        me = lax.axis_index("chan")
        self.core = lax.rem(me, 2)
        self.mine = lax.axis_index("crop") * (n // 2) + lax.div(me, 2)
        self.pair, self.slots, self.pair_sems = pair, slots, pair_sems
        self.send, self.recv = send, recv

    def start(self):
        here = self.pair.at[self.core]
        copy = remote(here, here, self.pair_sems.at[0], self.pair_sems.at[1], self.other)
        copy.start()
        copy.wait()
        self.slots[self.mine] = self.pair[0] + self.pair[1]
        self.copies = []
        for k, peer in enumerate(self.far):
            slot = self.slots.at[self.mine]
            copy = remote(slot, slot, self.send.at[k], self.recv.at[k], peer)
            copy.start()
            self.copies.append(copy)

    def finish(self):
        for copy in self.copies:
            copy.wait_recv()
        return jnp.sum(self.slots[...], axis=0)

    def drain(self):
        for copy in self.copies:
            copy.wait_send()


class WideSwap:
    def __init__(self, crops, n, pair, first, second, pair_sems, send, recv):
        my_crop, me = lax.axis_index("crop"), lax.axis_index("chan")
        self.core, self.crop, self.chip = lax.rem(me, 2), my_crop, lax.div(me, 2)
        self.other = (my_crop, me + 1 - 2 * self.core)
        self.over_crops = [(lax.rem(my_crop + i, crops), me) for i in range(1, crops)]
        self.over_chips = [(my_crop, lax.rem(me + 2 * j, n)) for j in range(1, n // 2)]
        self.pair, self.first, self.second = pair, first, second
        self.pair_sems, self.send, self.recv = pair_sems, send, recv

    def run(self, then=None):
        here = self.pair.at[self.core]
        copy = remote(here, here, self.pair_sems.at[0], self.pair_sems.at[1], self.other)
        copy.start()
        copy.wait()
        self.first[self.crop] = self.pair[0] + self.pair[1]
        k = 0
        copies = []
        for peer in self.over_crops:
            slot = self.first.at[self.crop]
            copies.append(remote(slot, slot, self.send.at[k], self.recv.at[k], peer))
            copies[-1].start()
            k += 1
        for copy in copies:
            copy.wait()
        self.second[self.chip] = jnp.sum(self.first[...], axis=0)
        copies = []
        for peer in self.over_chips:
            slot = self.second.at[self.chip]
            copies.append(remote(slot, slot, self.send.at[k], self.recv.at[k], peer))
            copies[-1].start()
            k += 1
        if then is not None:
            then()
        for copy in copies:
            copy.wait()
        return jnp.sum(self.second[...], axis=0)


def put_pair(ref, core, a, b):
    ref[core, 0:1] = a[:, :128]
    ref[core, 1:2] = a[:, 128:]
    ref[core, 2:3] = b[:, :128]
    ref[core, 3:4] = b[:, 128:]


def get_pair(total):
    return (
        jnp.concatenate([total[0:1], total[1:2]], axis=1),
        jnp.concatenate([total[2:3], total[3:4]], axis=1),
    )


def spread_row(row):
    return jnp.broadcast_to(row, (128, 128)).T


def up_weights(i, me, n, rows, coarse_rows):
    lower = (2 * i - 3) // 8
    upper_weight = (2 * i - 3 - 8 * lower) / 8.0
    a, b = 1.0 - upper_weight, upper_weight
    if lower < 0:
        top = me == 0
        a, b = jnp.where(top, 0.0, a), jnp.where(top, 1.0, b)
    if lower + 1 >= coarse_rows:
        bottom = me == n - 1
        a, b = jnp.where(bottom, 1.0, a), jnp.where(bottom, 0.0, b)
    if i < 0:
        a, b = jnp.where(me == 0, 0.0, a), jnp.where(me == 0, 0.0, b)
    if i >= rows:
        a, b = jnp.where(me == n - 1, 0.0, a), jnp.where(me == n - 1, 0.0, b)
    return lower + 1, a, b


class DecoderRefs(typing.NamedTuple):
    offsets: object
    feat: object
    point: object
    atrous_hbm: object
    pool_w: object
    low_rows: object
    low_w: object
    w_proj: object
    w_dec1: object
    w_side: object
    w_dec2: object
    w_cls: object
    own_gain: object
    own_shift: object
    low_gain: object
    low_shift: object
    bias: object
    d_logits: object
    logits_hbm: object
    branch_hbm: object
    low_hbm: object
    pack_hbm: object
    dec2_hbm: object
    wgrads_hbm: object
    src_all: object
    low_flat: object
    dlog: object
    near: object
    low_in: object
    atrous: object
    src_own: object
    logits: object
    branch_out: object
    low_out: object
    pack: object
    dec2_w: object
    wgrads: object
    low_ext: object
    low_push: object
    lowx: object
    merged_ext: object
    merged_part: object
    dec1: object
    dec2: object
    pushed: object
    pushed1: object
    x1: object
    x2: object
    g2: object
    g1: object
    yt: object
    branch_bf: object
    proj_bf: object
    flip: object
    branch: object
    staged: object
    arrived: object
    low_send: object
    low_pair: object
    low_sum: object
    low_recv: object
    spare: object
    low_spare: object
    gath: object
    norms_all: object
    norms: object
    proj: object
    w1: object
    tail: object
    w1low: object
    w2: object
    w1_back: object
    w2_back: object
    cls_all: object
    cls_t: object
    dmask: object
    columns: object
    own_w: object
    r_first: object
    r_pairs: object
    r_crossed: object
    r_halves: object
    r_lined: object
    r_out: object
    local: object
    f_send: object
    f_recv: object


def rest_groups(crops):
    return -(-15 // crops) * crops


def weight_groups(crops):
    return -(-8 // crops) * crops, -(-9 // crops) * crops


def decoder_kernel(crops, n, samples, *refs):
    ref = DecoderRefs(*refs[: len(DecoderRefs._fields)])
    rest = list(refs[len(DecoderRefs._fields) :])
    (wide_pair, wide_first, wide_second, wide_psem, wide_send, wide_recv) = rest[:6]
    (pair, slots, psem, send, recv, halo_send, halo_recv) = rest[6:13]

    coarse_samples, fine_samples = samples
    my_crop, me = lax.axis_index("crop"), lax.axis_index("chan")
    core = lax.rem(me, 2)
    above = (my_crop, lax.rem(me + n - 1, n))
    below = (my_crop, lax.rem(me + 1, n))
    low_chans, low_width = ref.low_w.shape
    classes = ref.w_cls.shape[0]
    fine = ref.d_logits.shape[1]
    rows = fine // n
    fine_cells = rows * 128
    coarse_cells = ref.branch.shape[0]
    coarse_rows = coarse_cells // FA
    cells = FA * FA
    c_in, c = ref.point.shape
    own = c // n
    chips, chip = n // 2, lax.div(me, 2)
    small, large = weight_groups(crops)
    chunk = min(4, rows)

    other, far = chip_peers(crops, n)
    over_crops = [(lax.rem(my_crop + i, crops), me) for i in range(1, crops)]
    over_chips = [(my_crop, lax.rem(me + 2 * j, n)) for j in range(1, chips)]
    wait_barrier = barrier_with([other, above, below] + far)

    turn_of = lambda i: 0 if i == 6 else (i + 1) % 2
    swaps = [
        Swap(crops, n, pair.at[i], slots.at[i], psem.at[i], send.at[turn_of(i)], recv.at[i])
        for i in range(pair.shape[0])
    ]
    wides = [
        WideSwap(
            crops, n, wide_pair.at[i], wide_first.at[i], wide_second.at[i],
            wide_psem.at[i], wide_send.at[i], wide_recv.at[i],
        )
        for i in range(2)
    ]
    front = Copies(ref.f_send, ref.f_recv)
    for i in range(pair.shape[0]):
        pair[i, core] = jnp.zeros((8, 128), f32)
    for i in range(2):
        wide_pair[i, core] = jnp.zeros(wide_pair.shape[2:], f32)

    def halo(i, first, last, to_above, to_below):
        copies = [
            remote(first, to_above, halo_send.at[i, 0], halo_recv.at[i, 0], above),
            remote(last, to_below, halo_send.at[i, 1], halo_recv.at[i, 1], below),
        ]
        for copy in copies:
            copy.start()
        return copies

    def fine_halo(i, values):
        return halo(
            i,
            values.at[pl.ds(128, 128)],
            values.at[pl.ds(rows * 128, 128)],
            values.at[pl.ds((rows + 1) * 128, 128)],
            values.at[pl.ds(0, 128)],
        )

    def gain(k):
        return ref.norms[k : k + 1]

    def shift(k):
        return ref.norms[8 + k : 9 + k]

    def moments(total, square, count):
        average = total * (1.0 / count)
        return average, lax.rsqrt(jnp.maximum(square * (1.0 / count) - average * average, 0.0) + epsilon)

    column = lax.broadcasted_iota(jnp.int32, (128, c), 0)

    def put_three(target, base, y):
        target[pl.ds(base, 128), 0:c] = jnp.where(column == 0, 0.0, pltpu.roll(y, 1, 0)).astype(bf16)
        target[pl.ds(base, 128), c : 2 * c] = y.astype(bf16)
        target[pl.ds(base, 128), 2 * c : 3 * c] = jnp.where(
            column == 127, 0.0, pltpu.roll(y, 127, 0)
        ).astype(bf16)

    def inside(i):
        at_top = jnp.logical_and(me == 0, i == 0)
        at_bottom = jnp.logical_and(me == n - 1, i == rows + 1)
        return jnp.where(jnp.logical_or(at_top, at_bottom), 0.0, 1.0)

    def each_row(body, first, last, carry):
        def step(i, kept):
            return body(i, pl.multiple_of(i * 128, 128), kept)

        return lax.fori_loop(first, last, step, carry)

    zero = jnp.zeros((8, c), f32)

    src_all, src_own, gath = ref.src_all, ref.src_own, ref.gath
    local_copies = []

    def local(src, dst):
        copy = pltpu.make_async_copy(src, dst, ref.local.at[len(local_copies)])
        copy.start()
        local_copies.append(copy)

    local(ref.atrous_hbm, ref.atrous)
    group_at = lax.div(me * rows, 16) * 16
    for k in range(3):
        at = jnp.clip(group_at + 16 * (k - 1), 0, fine - 16)
        local(ref.d_logits.at[:, pl.ds(pl.multiple_of(at, 16), 16)], ref.near.at[k])
    for i in range(cells // 256):
        src_own[pl.ds(i * 256, 256)] = ref.feat[:, i * 256 : (i + 1) * 256].T
    local(src_own, src_all.at[my_crop])
    flip = ref.flip
    flip[...] = jnp.zeros(flip.shape, f32)
    flip[0:classes, 0:own] = ref.w_cls[...].astype(f32)
    own_cls = flip[0:128, 0:128].T[0:own, 0:classes].astype(bf16)
    flip[0:classes, 0:own] = jnp.zeros((classes, own), f32)
    for t in range(9):
        flip[0:own, 128:256] = jnp.zeros((own, 128), f32)
        flip[0:own, 128 : 128 + low_width] = ref.w_side[t].astype(f32)
        flip[t * low_width : (t + 1) * low_width, 0:128] = flip[0:128, 128:256].T[0:low_width]
    for k in range(5):
        gath[me, k] = ref.w_proj[k]
    turned = flip[:, 0:128].T[0:own].astype(bf16)
    gath[me, 5] = turned[:, 0:c]
    gath[me, 6] = turned[:, c : 2 * c]
    gath[me, 7] = jnp.zeros((own, c), bf16)
    gath[me, 7, :, 0:classes] = own_cls
    for k in range(8, small):
        gath[me, k] = jnp.zeros((own, c), bf16)
    for t in range(9, large):
        gath[me, small + t] = jnp.zeros((own, c), bf16)
        gath[me, small + large + t] = jnp.zeros((own, c), bf16)
    for t in range(9):
        gath[me, small + t] = ref.w_dec1[t]
        gath[me, small + large + t] = ref.w_dec2[t]
    columns = ref.columns
    columns[...] = jnp.zeros(columns.shape, f32)
    columns[0:1, 0:low_width] = ref.low_gain[...]
    columns[1:2, 0:low_width] = ref.low_shift[...]
    columns[2:3, 0:classes] = ref.bias[...]
    ref.norms_all[me] = jnp.zeros((16, 128), f32)
    ref.norms_all[me, 0:8, 0:own] = ref.own_gain[...]
    ref.norms_all[me, 8:16, 0:own] = ref.own_shift[...]
    wait_barrier()
    block_of = lambda j: lax.rem(me - 2 * j + n, n)

    class Spread:
        def __init__(self, first, size):
            per = size // crops
            self.at = lambda b, q: gath.at[b, pl.ds(first + q * per, per)]
            self.first, self.size = first, size

        def start(self):
            here = self.at(me, my_crop)
            self.far = [front.start(here, here, peer) for peer in over_chips]
            here = gath.at[me, pl.ds(self.first, self.size)]
            self.pairs = [front.start(here, here, other)]

        def cross(self):
            self.crossed = []
            for j in range(1, chips):
                self.far[j - 1].wait_recv()
                here = self.at(block_of(j), my_crop)
                for i in range(1, crops):
                    self.crossed.append((j, front.start(here, here, over_crops[i - 1])))

        def cores(self):
            for j in range(1, chips):
                for k, copy in self.crossed:
                    if k == j:
                        copy.wait_recv()
                here = gath.at[block_of(j), pl.ds(self.first, self.size)]
                self.pairs.append(front.start(here, here, other))

        def finish(self):
            for copy in self.pairs:
                copy.wait_recv()

    norm_far = []
    here = ref.norms_all.at[me]
    for peer in over_chips:
        norm_far.append(front.start(here, here, peer))
    norm_pairs = [front.start(here, here, other)]
    spread = [Spread(0, small), Spread(small, large), Spread(small + large, large)]
    spread[0].start()
    spread[1].start()
    feature_copies = [front.start(src_own, src_all.at[my_crop], peer) for peer in over_crops]
    for i in range(0, ref.low_rows.shape[1], 16):
        here = ref.low_rows[:, i : i + 16].astype(f32)
        ref.low_in[:, i * 128 : (i + 16) * 128] = here.reshape(low_chans, 16 * 128).astype(bf16)
    local(ref.low_in, ref.low_flat)

    low_send, low_pair = ref.low_send, ref.low_pair

    def low_block(b):
        span = pl.ds(pl.multiple_of(b * fine_cells, fine_cells), fine_cells)
        return dot_tn(ref.low_w[...], ref.low_in[:, span])

    low_copies = []
    for z in range(chips):
        low_send[z] = low_block(2 * z + 1 - core)
        low_copies.append(front.start(low_send.at[z], low_pair.at[z], other))
    for k in range(3):
        local_copies[1 + k].wait()
        here = ref.near[k].astype(f32).reshape(classes, 16 * 128)
        ref.dlog[0:classes, k * 2048 : (k + 1) * 2048] = here.astype(bf16)
        ref.dlog[classes:32, k * 2048 : (k + 1) * 2048] = jnp.zeros((32 - classes, 2048), bf16)

    part, part_in, staged, arrived = ref.pushed, ref.pushed1, ref.staged, ref.arrived
    shifted = ref.g2

    order = (0, 3, 2, 1)

    def branch_partial(k):
        first = k * cells
        if k == 0:
            part[pl.ds(first, cells)] = dot(src_own[...], ref.point[...])
        else:
            rate = atrous_rates[k - 1]
            if k == order[1]:
                local_copies[0].wait()
            shift_three(lambda base: src_own[pl.ds(base, 128)], shifted, rate, -rate, rate)
            part[pl.ds(first, cells)] = dot(shifted[pl.ds(0, cells), 0 : 3 * c_in], ref.atrous[k - 1, 1])
            for a in (0, 2):
                move = (a - 1) * rate
                count = (FA - abs(move)) * FA
                to, off = first + max(-move, 0) * FA, max(move, 0) * FA
                part[pl.ds(to, count)] += dot(shifted[pl.ds(off, count), 0 : 3 * c_in], ref.atrous[k - 1, a])
        copies = []
        for z in range(chips):
            block = pl.multiple_of(first + (2 * z + 1 - core) * coarse_cells, coarse_cells)
            copies.append(
                front.start(
                    part.at[pl.ds(block, coarse_cells)],
                    part_in.at[pl.ds((k * chips + z) * coarse_cells, coarse_cells)],
                    other,
                )
            )
        return copies

    def pair_sum(k, z):
        block = pl.multiple_of(k * cells + (2 * z + core) * coarse_cells, coarse_cells)
        landed = pl.multiple_of((k * chips + z) * coarse_cells, coarse_cells)
        return part[pl.ds(block, coarse_cells)] + part_in[pl.ds(landed, coarse_cells)]

    waited = []
    branch_lines = [
        LineSum(n, front, staged.at[k], arrived.at[k], ref.spare.at[k], functools.partial(pair_sum, k))
        for k in range(4)
    ]

    def branch_out(k, copies):
        for copy in copies:
            copy.wait()
            waited.append(copy)
        for z in range(chips):
            staged[k, z] = pair_sum(k, z).astype(bf16)
        ref.branch[:, k * c : (k + 1) * c] = pair_sum(k, chip)
        branch_lines[k].start()

    before = branch_partial(order[0])
    for at in range(1, 4):
        after = branch_partial(order[at])
        branch_out(order[at - 1], before)
        before = after
        if at == 2:
            spread[0].cross()
        if at == 1:
            for z in range(chips):
                low_copies[z].wait_recv()
                ref.low_sum[z] = (low_block(2 * z + core) + low_pair[z]).astype(bf16)
            low_line = LineSum(
                n, front, ref.low_sum, ref.low_recv, ref.low_spare, lambda z: low_block(2 * z + core) + low_pair[z]
            )
            low_line.start()
        if at == 2:
            branch_lines[order[0]].second()
        if at == 3:
            spread[1].cross()
            low_line.second()
            branch_lines[order[1]].second()
    branch_out(order[3], before)
    branch_lines[order[2]].second()
    for j in range(1, chips):
        norm_far[j - 1].wait_recv()
        here = ref.norms_all.at[block_of(j)]
        norm_pairs.append(front.start(here, here, other))
    pooled = row_of(src_own[...].astype(f32)) * (1.0 / cells)
    pooled = jnp.concatenate([pooled, jnp.zeros((15, c_in), f32)], axis=0).astype(bf16)
    pool_part = dot(pooled, ref.pool_w[...])[0:1]

    branch_lines[order[3]].second()
    for copy in norm_pairs:
        copy.wait_recv()
    for b in range(n):
        ref.norms[:, b * own : (b + 1) * own] = ref.norms_all[b, :, 0:own]

    low_ext = ref.low_ext
    own_low = pl.ds(128, fine_cells)
    low_ext[:, own_low] = low_block(me) + low_pair[chip]

    def add_to_low(value):
        low_ext[:, own_low] += value

    low_line.finish(add_to_low)
    low_edges = halo(
        0,
        low_ext.at[:, pl.ds(128, 128)],
        low_ext.at[:, pl.ds(rows * 128, 128)],
        low_ext.at[:, pl.ds((rows + 1) * 128, 128)],
        low_ext.at[:, pl.ds(0, 128)],
    )

    def add_low(i, base, kept):
        v = low_ext[:, pl.ds(base, 128)]
        return kept[0] + v, kept[1] + v * v

    low_zero = jnp.zeros((low_width, 128), f32)
    low_sum, low_square = each_row(add_low, 1, rows + 1, (low_zero, low_zero))

    def lanes_of(values):
        return row_of(values.T)

    pair[6, core, 0:1, 0:low_width] = lanes_of(low_sum)
    pair[6, core, 1:2, 0:low_width] = lanes_of(low_square)
    swaps[6].start()

    for k in order:

        def add_to_branch(value, k=k):
            ref.branch[:, k * c : (k + 1) * c] += value

        branch_lines[k].finish(add_to_branch)

    spread[0].cores()
    spread[1].cores()
    wide = wide_pair.at[0]
    for k in range(4):
        v = ref.branch[:, k * c : (k + 1) * c]
        wide[core, k : k + 1] = row_of(v)
        wide[core, 4 + k : 5 + k] = row_of(v * v)
    wide[core, 8:16] = jnp.where(
        lax.broadcasted_iota(jnp.int32, (8, c), 0) == my_crop, pool_part, 0.0
    )
    total_a = wides[0].run(spread[2].start)
    spread[0].finish()
    proj, w1, w2, tail = ref.proj, ref.w1, ref.w2, ref.tail
    for b in range(n):
        mine = pl.ds(b * own, own)
        for k in range(5):
            proj[k, mine] = gath[b, k]

    def place_conv(target, back, first):
        for b in range(n):
            for t in range(9):
                a, e = t // 3, t % 3
                here = gath[b, first + t]
                target[a, pl.ds(e * c + b * own, own)] = here
                back[a, pl.ds(b * own, own), (2 - e) * c : (3 - e) * c] = here

    def branch_parts(k):
        average, inverse = moments(total_a[k : k + 1], total_a[4 + k : 5 + k], coarse_samples)
        normed = (ref.branch[:, k * c : (k + 1) * c] - average) * inverse
        return normed, gain(k) * normed + shift(k), inverse

    projected = jnp.zeros((coarse_cells, c), f32)
    for k in range(4):
        y = gelu(branch_parts(k)[1]).astype(bf16)
        ref.branch_bf[:, k * c : (k + 1) * c] = y
        projected = projected + dot(y, ref.proj[k])
    pool_here = lax.broadcasted_iota(jnp.int32, (8, c), 0) < crops
    pool_pre = total_a[8:16]
    pool_average = row_of(pool_pre) * (1.0 / crops)
    pool_spread = jnp.where(pool_here, pool_pre - pool_average, 0.0)
    pool_inverse = lax.rsqrt(row_of(pool_spread * pool_spread) * (1.0 / crops) + epsilon)
    pool_normed = pool_spread * pool_inverse
    pool_before = gain(4) * pool_normed + shift(4)
    pool_bf = gelu(pool_before)
    pool_bf = jnp.concatenate([pool_bf, jnp.zeros((8, c), f32)], axis=0).astype(bf16)
    pool_term = dot(pool_bf, ref.proj[4])
    my_row = lax.broadcasted_iota(jnp.int32, (16, c), 0) == my_crop
    projected = projected + row_of(jnp.where(my_row, pool_term, 0.0))
    merged_ext = ref.merged_ext
    merged_ext[pl.ds(FA, coarse_cells)] = projected
    put_pair(pair.at[0], core, row_of(projected), row_of(projected * projected))
    merged_copies = halo(
        1,
        merged_ext.at[pl.ds(FA, FA)],
        merged_ext.at[pl.ds(coarse_cells, FA)],
        merged_ext.at[pl.ds(FA + coarse_cells, FA)],
        merged_ext.at[pl.ds(0, FA)],
    )
    swaps[0].start()

    total_l = swaps[6].finish()
    for copy in low_edges:
        copy.wait()
    low_average = total_l[0:1] * (1.0 / fine_samples)
    low_variance = total_l[1:2] * (1.0 / fine_samples) - low_average * low_average
    low_inverse_row = lax.rsqrt(jnp.maximum(low_variance, 0.0) + epsilon)
    low_average = spread_row(low_average)[0:low_width]
    low_inverse = spread_row(low_inverse_row)[0:low_width]
    lane = lax.broadcasted_iota(jnp.int32, (low_width, 128), 1)
    low_gain = spread_row(columns[0:1])[0:low_width]
    low_shift = spread_row(columns[1:2])[0:low_width]

    def low_parts(base):
        normed = (low_ext[:, pl.ds(base, 128)] - low_average) * low_inverse
        return normed, low_gain * normed + low_shift

    def low_row(i, base, kept):
        y = gelu(low_parts(base)[1]) * inside(i)
        lowx = ref.lowx
        lowx[0:low_width, pl.ds(base, 128)] = jnp.where(lane == 0, 0.0, pltpu.roll(y, 1, 1)).astype(bf16)
        lowx[low_width : 2 * low_width, pl.ds(base, 128)] = y.astype(bf16)
        lowx[2 * low_width : 3 * low_width, pl.ds(base, 128)] = jnp.where(
            lane == 127, 0.0, pltpu.roll(y, 127, 1)
        ).astype(bf16)
        return kept

    each_row(low_row, 0, rows + 2, 0)

    for b in range(n):
        mine = pl.ds(b * own, own)
        tail[mine, 0:c] = gath[b, 5]
        tail[mine, c : 2 * c] = gath[b, 6]
        ref.cls_all[mine] = gath[b, 7, :, 0:128]
    turned = tail[...].T
    for a in range(3):
        ref.w1low[a] = turned[a * 3 * low_width : (a + 1) * 3 * low_width]
    cls_lane = lax.broadcasted_iota(jnp.int32, (c, 128), 1)
    cls_clean = jnp.where(cls_lane < classes, ref.cls_all[...].astype(f32), 0.0)
    ref.cls_t[...] = cls_clean.T[0:32].astype(bf16)
    spread[2].cross()
    merged_sum, merged_square = get_pair(swaps[0].finish())
    for copy in merged_copies:
        copy.wait()
    merged_average, merged_inverse = moments(merged_sum, merged_square, coarse_samples)

    def merged_parts(first, count):
        normed = (merged_ext[pl.ds(first, count)] - merged_average) * merged_inverse
        return normed, gain(5) * normed + shift(5)

    fine_at = lax.broadcasted_iota(jnp.int32, (128, FA), 0).astype(f32)
    coarse_at = lax.broadcasted_iota(jnp.int32, (128, FA), 1).astype(f32)
    place = jnp.clip((fine_at + 0.5) / 4.0 - 0.5, 0.0, FA - 1.0)
    up = jnp.maximum(0.0, 1.0 - jnp.abs(place - coarse_at)).astype(bf16)
    coarse_wide = []
    for j in range(coarse_rows + 2):
        coarse_wide.append(dot_exact(up, gelu(merged_parts(j * FA, FA)[1])))
    for i in range(-1, rows + 1):
        lower, a, b = up_weights(i, me, n, rows, coarse_rows)
        put_three(ref.x1, (i + 1) * 128, a * coarse_wide[lower] + b * coarse_wide[lower + 1])
    spread[1].finish()
    place_conv(w1, ref.w1_back, small)
    dec1, dec2, pushed, pushed1 = ref.dec1, ref.dec2, ref.pushed, ref.pushed1

    def conv_piece(source, weight, base):
        total = None
        for a in range(3):
            term = dot(source[pl.ds(base + a * 128, chunk * 128)], weight[a])
            total = term if total is None else total + term
        return total

    def conv_loop(piece, target):
        def step(i, kept):
            base = pl.multiple_of(i * (chunk * 128), 128)
            total = piece(base)
            target[pl.ds(base + 128, chunk * 128)] = total
            return kept[0] + fold(total), kept[1] + fold(total * total)

        return lax.fori_loop(0, rows // chunk, step, (zero, zero))


    def first_piece(base):
        total = conv_piece(ref.x1, w1, base)
        for a in range(3):
            total = total + dot_tn(ref.lowx[:, pl.ds(base + a * 128, chunk * 128)], ref.w1low[a])
        return total

    total, square = conv_loop(first_piece, dec1)
    spread[2].cores()
    put_pair(pair.at[1], core, row_of(total), row_of(square))
    swaps[6].drain()
    swaps[1].start()
    dec1_copies = fine_halo(2, dec1)
    total, square = get_pair(swaps[1].finish())
    for copy in dec1_copies:
        copy.wait()
    first_average, first_inverse = moments(total, square, fine_samples)

    def first_parts(base):
        normed = (dec1[pl.ds(base, 128)] - first_average) * first_inverse
        return normed, gain(6) * normed + shift(6)

    def first_row(i, base, kept):
        put_three(ref.x2, base, gelu(first_parts(base)[1]) * inside(i))
        return kept

    each_row(first_row, 0, rows + 2, 0)
    spread[2].finish()
    place_conv(w2, ref.w2_back, small + large)
    total, square = conv_loop(lambda base: conv_piece(ref.x2, w2, base), dec2)
    put_pair(pair.at[2], core, row_of(total), row_of(square))
    swaps[0].drain()
    swaps[2].start()
    dec2_copies = fine_halo(3, dec2)
    total, square = get_pair(swaps[2].finish())
    for copy in dec2_copies:
        copy.wait()
    second_average, second_inverse = moments(total, square, fine_samples)

    cls_t = ref.cls_t[...]
    bias = spread_row(columns[2:3])[0:32]
    col_here = ref.offsets[0, 1] + 4 * lax.broadcasted_iota(jnp.int32, (1, 128), 1) < SCENE_W
    col_mask = jnp.where(col_here, 1.0, 0.0)

    def scene_mask(i):
        row_here = ref.offsets[0, 0] + 4 * (me * rows + i - 1) < SCENE_H
        return col_mask * jnp.where(row_here, 1.0, 0.0)

    def masked_row(i, base):
        at = pl.multiple_of(base + (15 + me * rows - group_at) * 128, 128)
        return ref.dlog[:, pl.ds(at, 128)] * (scene_mask(i) * inside(i)).astype(bf16)

    def second_parts(base):
        normed = (dec2[pl.ds(base, 128)] - second_average) * second_inverse
        return normed, gain(7) * normed + shift(7)

    def second_row(i, base, kept):
        normed, before = second_parts(base)
        value, slope = gelu_both(before)
        ref.g1[pl.ds(base, 128), 0:c] = value.astype(bf16)
        masked = masked_row(i, base)
        ref.dmask[:, pl.ds(base, 128)] = masked
        grad = dot_tn(masked, cls_t)
        push = slope * grad
        pushed[pl.ds(base, 128)] = push
        own_row = jnp.where(jnp.logical_and(i > 0, i < rows + 1), 1.0, 0.0)
        push = push * own_row
        return kept[0] + fold(push * normed), kept[1] + fold(push)

    along, summed = each_row(second_row, 0, rows + 2, (zero, zero))
    put_pair(pair.at[3], core, row_of(along), row_of(summed))
    swaps[1].drain()
    swaps[3].start()
    second = ref.g1

    def logit_row(i, base, kept):
        out = pl.multiple_of(base - 128, 128)
        value = dot_nt(cls_t, second[pl.ds(base, 128), 0:c]) + bias
        ref.logits[:, pl.ds(out, 128)] = value * scene_mask(i)
        return kept

    each_row(logit_row, 1, rows + 1, 0)
    local(ref.logits, ref.logits_hbm)
    flip[pl.ds(9 * low_width, 32)] = dot(
        ref.dmask[:, 128 : 128 + fine_cells], second[pl.ds(128, fine_cells), 0:c]
    )
    bias_grad = jnp.zeros((32, 128), f32)
    for i in range(1, rows + 1):
        bias_grad = bias_grad + ref.dmask[:, i * 128 : (i + 1) * 128].astype(f32)
    wide_pair[1, core, 16:17, 0:32] = row_of(bias_grad.T)
    second_along, second_summed = get_pair(swaps[3].finish())

    def pull(push, normed, k, inverse, along, summed, count):
        return (gain(k) * inverse) * (push - summed * (1.0 / count) - normed * (along * (1.0 / count)))

    def dec2_row(i, base, kept):
        g = pull(
            pushed[pl.ds(base, 128)], second_parts(base)[0], 7, second_inverse,
            second_along, second_summed, fine_samples,
        )
        put_three(ref.g2, base, g * inside(i))
        return kept

    each_row(dec2_row, 0, rows + 2, 0)

    def back_loop(source, weight, use, carry):
        def step(i, kept):
            base = pl.multiple_of(i * (chunk * 128), 128)
            total = None
            for a in range(3):
                term = dot_nt(source[pl.ds(base + (2 - a) * 128, chunk * 128)], weight[a])
                total = term if total is None else total + term
            return use(base, total, kept)

        return lax.fori_loop(0, rows // chunk, step, carry)

    def first_use(base, grad, kept):
        at = pl.ds(pl.multiple_of(base + 128, 128), chunk * 128)
        normed = (dec1[at] - first_average) * first_inverse
        push = gelu_slope(gain(6) * normed + shift(6)) * grad
        pushed1[at] = push
        return kept[0] + fold(push * normed), kept[1] + fold(push)

    along, summed = back_loop(ref.g2, ref.w2_back, first_use, (zero, zero))
    put_pair(pair.at[4], core, row_of(along), row_of(summed))
    swaps[2].drain()
    swaps[4].start()
    pushed_copies = fine_halo(4, pushed1)

    wgrads = ref.wgrads

    reduce_two = Reduce(
        crops, n, front, ref.own_w, ref.r_first, ref.r_pairs, ref.r_crossed, ref.r_halves, ref.r_lined, ref.r_out
    )

    def weight_grads(target, source, gradient):
        for a in range(3):
            part = dot_tn(
                source[pl.ds(a * 128, fine_cells), c : 2 * c], gradient[pl.ds(128, fine_cells)]
            ).astype(bf16)
            for e in range(3):
                tap = part[:, (2 - e) * c : (3 - e) * c]
                for h in range(n):
                    target[h, 3 * a + e] = tap[h * own : (h + 1) * own]

    weight_grads(ref.own_w, ref.x2, ref.g2)
    for t in range(9, large):
        for h in range(n):
            ref.own_w[h, t] = jnp.zeros((own, c), bf16)
    reduce_two.cores()
    first_along, first_summed = get_pair(swaps[4].finish())
    reduce_two.over_the_crops()
    for copy in pushed_copies:
        copy.wait()

    def dec1_row(i, base, kept):
        g = pull(
            pushed1[pl.ds(base, 128)], first_parts(base)[0], 6, first_inverse,
            first_along, first_summed, fine_samples,
        ) * inside(i)
        put_three(ref.g1, base, g)
        return kept

    each_row(dec1_row, 0, rows + 2, 0)

    def up_use(base, grad, kept):
        dec2[pl.ds(pl.multiple_of(base + 128, 128), chunk * 128)] = grad
        return kept

    back_loop(ref.g1, ref.w1_back, up_use, 0)
    yt = ref.yt

    def low_back_row(i, local, base, kept):
        total = None
        for t in range(9):
            a, e = t // 3, t % 3
            at = pl.ds((local + 2 - a) * 128, 128)
            piece = yt[t * low_width : (t + 1) * low_width, at]
            if e == 0:
                piece = jnp.where(lane == 127, 0.0, pltpu.roll(piece, 127, 1))
            if e == 2:
                piece = jnp.where(lane == 0, 0.0, pltpu.roll(piece, 1, 1))
            total = piece if total is None else total + piece
        normed, before = low_parts(base)
        push = gelu_slope(before) * total
        ref.low_push[:, pl.ds(pl.multiple_of(base - 128, 128), 128)] = push
        return kept[0] + push * normed, kept[1] + push

    def low_back_chunk(i, kept):
        base = pl.multiple_of(i * (chunk * 128), 128)
        here = ref.g1[pl.ds(base, (chunk + 2) * 128), c : 2 * c]
        for a in range(3):
            yt[a * 3 * low_width : (a + 1) * 3 * low_width] = dot_nt(ref.w1low[a], here)
        for local in range(chunk):
            kept = low_back_row(i, local, pl.multiple_of(base + (local + 1) * 128, 128), kept)
        return kept

    low_along, low_summed = lax.fori_loop(0, rows // chunk, low_back_chunk, (low_zero, low_zero))

    part = ref.merged_part
    fine_at = lax.broadcasted_iota(jnp.int32, (FA, 128), 1).astype(f32)
    coarse_at = lax.broadcasted_iota(jnp.int32, (FA, 128), 0).astype(f32)
    place = jnp.clip((fine_at + 0.5) / 4.0 - 0.5, 0.0, FA - 1.0)
    up_t = jnp.maximum(0.0, 1.0 - jnp.abs(place - coarse_at)).astype(bf16)
    row_sums = [None] * (coarse_rows + 2)
    for i in range(rows):
        lower, a, b = up_weights(i, me, n, rows, coarse_rows)
        grad = dec2[pl.ds((i + 1) * 128, 128)]
        for j, weight in ((lower, a), (lower + 1, b)):
            row_sums[j] = weight * grad if row_sums[j] is None else row_sums[j] + weight * grad
    along, summed = zero, zero
    for j in range(coarse_rows + 2):
        grad = dot_exact(up_t, row_sums[j])
        part[pl.ds(j * FA, FA)] = grad
        normed, before = merged_parts(j * FA, FA)
        push = gelu_slope(before) * grad
        along, summed = along + fold(push * normed), summed + fold(push)
    put_pair(pair.at[5], core, row_of(along), row_of(summed))
    pair[5, core, 4:5, 0:low_width] = lanes_of(low_along)
    pair[5, core, 5:6, 0:low_width] = lanes_of(low_summed)
    part_copies = halo(
        5,
        part.at[pl.ds(0, FA)],
        part.at[pl.ds(FA + coarse_cells, FA)],
        part.at[pl.ds((coarse_rows + 3) * FA, FA)],
        part.at[pl.ds((coarse_rows + 2) * FA, FA)],
    )
    swaps[3].drain()
    swaps[5].start()
    reduce_two.over_the_chips()
    weight_grads(wgrads, ref.x1, ref.g1)
    local(wgrads.at[:, pl.ds(0, 9)], ref.wgrads_hbm.at[:, pl.ds(0, 9)])
    total_g = swaps[5].finish()
    for copy in part_copies:
        copy.wait()
    merged_along, merged_summed = get_pair(total_g)
    low_along, low_summed = spread_row(total_g[4:5])[0:low_width], spread_row(total_g[5:6])[0:low_width]
    pack = ref.pack
    pack[17:18, 0:128] = total_g[4:5]
    pack[18:19, 0:128] = total_g[5:6]
    up_here = jnp.where(me == 0, 0.0, 1.0)
    down_here = jnp.where(me == n - 1, 0.0, 1.0)
    proj_bf = ref.proj_bf
    for j in range(1, coarse_rows + 1):
        grad = part[pl.ds(j * FA, FA)]
        if j == 1:
            grad = grad + up_here * part[pl.ds((coarse_rows + 2) * FA, FA)]
        if j == coarse_rows:
            grad = grad + down_here * part[pl.ds((coarse_rows + 3) * FA, FA)]
        normed, before = merged_parts(j * FA, FA)
        push = gelu_slope(before) * grad
        g = pull(push, normed, 5, merged_inverse, merged_along, merged_summed, coarse_samples)
        proj_bf[pl.ds((j - 1) * FA, FA)] = g.astype(bf16)

    push_all = []
    for k in range(4):
        normed, before, _ = branch_parts(k)
        push = gelu_slope(before) * dot_nt(proj_bf[...], ref.proj[k])
        push_all.append(push)
        wide_pair[1, core, k : k + 1] = row_of(push * normed)
        wide_pair[1, core, 4 + k : 5 + k] = row_of(push)
    proj_row = row_of(proj_bf[...].astype(f32))
    wide_pair[1, core, 8:16] = jnp.where(
        lax.broadcasted_iota(jnp.int32, (8, c), 0) == my_crop, proj_row, 0.0
    )
    total_h = wides[1].run()
    reduce_two.to_all_crops()
    for k in range(4):
        normed, _, inverse = branch_parts(k)
        g = pull(
            push_all[k], normed, k, inverse, total_h[k : k + 1], total_h[4 + k : 5 + k], coarse_samples
        )
        ref.branch_out[:, k * c : (k + 1) * c] = g.astype(bf16)

    sums = total_h[8:16]
    sums_high = sums.astype(bf16).astype(f32)
    sums_low = sums - sums_high
    spare = jnp.concatenate([sums_high, sums_low], axis=0)
    spare_mid = spare.astype(bf16)
    spare_rest = (spare - spare_mid.astype(f32)).astype(bf16)
    pieces = dot_nt(spare_mid, ref.proj[4]) + dot_nt(spare_rest, ref.proj[4])
    pool_push = gelu_slope(pool_before) * (pieces[0:8] + pieces[8:16])
    pool_push = jnp.where(pool_here, pool_push, 0.0)
    pool_along, pool_summed = row_of(pool_push * pool_normed), row_of(pool_push)
    pool_grad = pull(pool_push, pool_normed, 4, pool_inverse, pool_along, pool_summed, crops)
    pool_grad = jnp.where(pool_here, pool_grad, 0.0)
    pack[24:32] = pool_grad
    pack[32:40] = jnp.zeros((8, c), f32)

    gain_rows = [total_h[0:4], pool_along, merged_along, first_along, second_along]
    shift_rows = [total_h[4:8], pool_summed, merged_summed, first_summed, second_summed]
    turn = c - me * own
    pack[0:8] = pltpu.roll(jnp.concatenate(gain_rows, axis=0), turn, 1)
    pack[8:16] = pltpu.roll(jnp.concatenate(shift_rows, axis=0), turn, 1)
    pack[16:17] = total_h[16:17]
    pool_rows = jnp.zeros((c, c), f32)
    rest = jnp.concatenate([sums, jnp.zeros((8, c), f32)], axis=0)
    for _ in range(3):
        high = rest.astype(bf16)
        pool_rows = pool_rows + dot_tn(pool_bf, high)
        rest = rest - high.astype(f32)
    dec1[pl.ds(0, c)] = pool_rows
    pack[40 : 40 + own] = dec1[pl.ds(pl.multiple_of(me * own, own), own)]
    local(pack, ref.pack_hbm)

    def low_out_row(i, base, kept):
        at = pl.ds(pl.multiple_of(base - 128, 128), 128)
        normed = low_parts(base)[0]
        g = (low_gain * low_inverse) * (
            ref.low_push[:, at] - low_summed * (1.0 / fine_samples) - normed * (low_along * (1.0 / fine_samples))
        )
        ref.low_out[:, at] = g.astype(bf16)
        return kept

    each_row(low_out_row, 1, rows + 1, 0)
    local(ref.low_out, ref.low_hbm)
    local(ref.branch_out, ref.branch_hbm)

    for a in range(3):
        flip[pl.ds(a * 3 * low_width, 3 * low_width)] = dot(
            ref.lowx[:, a * 128 : a * 128 + fine_cells], ref.g1[pl.ds(128, fine_cells), c : 2 * c]
        )
    flip[pl.ds(9 * low_width + 32, 48)] = jnp.zeros((48, c), f32)
    turned = flip[...].T.astype(bf16)
    for k in range(4):
        product = dot_tn(ref.branch_bf[:, k * c : (k + 1) * c], proj_bf[...]).astype(bf16)
        for h in range(n):
            rows_h = product[h * own : (h + 1) * own]
            wgrads[h, 9 + k] = rows_h
    for h in range(n):
        wgrads[h, 13] = turned[h * own : (h + 1) * own, 0:c]
        wgrads[h, 14] = turned[h * own : (h + 1) * own, c : 2 * c]
        for k in range(15, wgrads.shape[1]):
            wgrads[h, k] = jnp.zeros((own, c), bf16)
    local(wgrads.at[:, pl.ds(9, wgrads.shape[1] - 9)], ref.wgrads_hbm.at[:, pl.ds(9, wgrads.shape[1] - 9)])
    reduce_two.finish()
    for t in range(9):
        ref.dec2_w[t] = ref.r_out[t].astype(f32)
    local(ref.dec2_w, ref.dec2_hbm)
    for copy in feature_copies:
        copy.wait_recv()
    front.drain(waited)
    swaps[4].drain()
    swaps[5].drain()
    for copy in local_copies[4:]:
        copy.wait()


def decoder(crops, n, samples, *args):
    ref = DecoderRefs(*args, *([None] * (len(DecoderRefs._fields) - len(args))))
    c_in, c = ref.point.shape
    low_width = ref.low_w.shape[1]
    classes, fine = ref.d_logits.shape[:2]
    rows = fine // n
    cells = rows * 128
    coarse = FA * FA // n
    own = c // n
    small, large = weight_groups(crops)
    chips = n // 2
    all_chips = crops * chips
    outer = (rows + 2) * 128
    chunk = min(4, rows)
    count = (crops - 1) + 4 * (2 * chips - 1) + 2 * chips - 1
    count += 2 * chips - 1 + 3 * (1 + (crops + 1) * (chips - 1)) + reduce_copies(crops, n) + 5
    S = jax.ShapeDtypeStruct
    V = pltpu.VMEM
    D = pltpu.SemaphoreType.DMA
    vmem = pl.BlockSpec(memory_space=pltpu.VMEM)
    hbm = pl.BlockSpec(memory_space=pl.ANY)
    return pl.pallas_call(
        functools.partial(decoder_kernel, crops, n, samples),
        out_shape=[
            S((32, cells), f32),
            S((coarse, 4 * c), bf16),
            S((low_width, cells), bf16),
            S((40 + own, c), f32),
            S((9, own, c), f32),
            S((n, rest_groups(crops), own, c), bf16),
            S((crops, FA * FA, c_in), bf16),
            S((ref.low_rows.shape[0], ref.low_rows.shape[1] * 128), bf16),
        ],
        in_specs=[pl.BlockSpec(memory_space=pltpu.SMEM), vmem, vmem, hbm] + [vmem] * (len(args) - 5) + [hbm],
        out_specs=[hbm] * 8,
        scratch_shapes=[
            V((32, 48 * 128), bf16),
            V((3, classes, 16, 128), bf16),
            V((ref.low_rows.shape[0], ref.low_rows.shape[1] * 128), bf16),
            V(ref.atrous_hbm.shape, bf16),
            V((FA * FA, c_in), bf16),
            V((32, cells), f32),
            V((coarse, 4 * c), bf16),
            V((low_width, cells), bf16),
            V((40 + own, c), f32),
            V((9, own, c), f32),
            V((n, rest_groups(crops), own, c), bf16),
            V((low_width, outer), f32),
            V((low_width, cells), f32),
            V((3 * low_width, outer), bf16),
            V((coarse + 2 * FA, c), f32),
            V((coarse + 4 * FA, c), f32),
            V((outer, c), f32),
            V((outer, c), f32),
            V((max(outer, 4 * FA * FA), c), f32),
            V((max(outer, 2 * FA * FA), c), f32),
            V((outer, 3 * c), bf16),
            V((outer, 3 * c), bf16),
            V((max(outer, FA * FA), 3 * c), bf16),
            V((outer, 3 * c), bf16),
            V((9 * low_width, (chunk + 2) * 128), f32),
            V((coarse, 4 * c), bf16),
            V((coarse, c), bf16),
            V((512, c), f32),
            V((coarse, 4 * c), f32),
            V((4, chips, coarse, c), bf16),
            V((4, chips, coarse, c), bf16),
            V((chips, low_width, cells), f32),
            V((chips, low_width, cells), f32),
            V((chips, low_width, cells), bf16),
            V((chips, low_width, cells), bf16),
            V((4, coarse, c), bf16),
            V((low_width, cells), bf16),
            V((n, small + 2 * large, own, c), bf16),
            V((n, 16, 128), f32),
            V((16, c), f32),
            V((5, c, c), bf16),
            V((3, 3 * c, c), bf16),
            V((c, 2 * c), bf16),
            V((3, 3 * low_width, c), bf16),
            V((3, 3 * c, c), bf16),
            V((3, c, 3 * c), bf16),
            V((3, c, 3 * c), bf16),
            V((c, 128), bf16),
            V((32, c), bf16),
            V((32, outer), bf16),
            V((8, 128), f32),
            V((n, large, own, c), bf16),
            *reduce_scratch(crops, n, large, own, c),
            D((16,)),
            D((count,)),
            D((count,)),
            V((2, 2, 24, c), f32),
            V((2, crops, 24, c), f32),
            V((2, chips, 24, c), f32),
            D((2, 2)),
            D((2, crops + chips)),
            D((2, crops + chips)),
            V((7, 2, 8, 128), f32),
            V((7, all_chips, 8, 128), f32),
            D((7, 2)),
            D((2, all_chips)),
            D((7, all_chips)),
            D((6, 2)),
            D((6, 2)),
        ],
        compiler_params=pltpu.CompilerParams(
            collective_id=0, has_side_effects=True, vmem_limit_bytes=62 * 1024 * 1024
        ),
    )(*args)


class Reduce:
    def __init__(self, crops, n, copies, source, first, pairs, crossed, halves, lined, out, mine=None, mine_sems=None):
        my_crop, me = lax.axis_index("crop"), lax.axis_index("chan")
        self.crops, self.chips, self.copies = crops, n // 2, copies
        self.crop, self.core, self.chip = my_crop, lax.rem(me, 2), lax.div(me, 2)
        self.other = (my_crop, me + 1 - 2 * self.core)
        self.over_crops = [(lax.rem(my_crop + i, crops), me) for i in range(1, crops)]
        self.over_chips = [(my_crop, lax.rem(me + 2 * j, n)) for j in range(1, n // 2)]
        self.source, self.first, self.pairs, self.crossed = source, first, pairs, crossed
        self.halves, self.lined, self.out = halves, lined, out
        self.mine, self.mine_sems = mine, mine_sems
        self.size = source.shape[1]
        self.share = self.size // crops

    def wait(self):
        for copy in self.moving:
            copy.wait_recv()

    def cores(self):
        self.moving = []
        for z in range(self.chips):
            block = self.source.at[2 * z + 1 - self.core]
            self.moving.append(self.copies.start(block, self.first.at[z], self.other))
        self.loads = []
        if self.mine is not None:
            for z in range(self.chips):
                block = self.source.at[2 * z + self.core]
                self.loads.append(pltpu.make_async_copy(block, self.mine.at[z], self.mine_sems.at[z]))
                self.loads[-1].start()

    def over_the_crops(self):
        self.wait()
        for copy in self.loads:
            copy.wait()
        for z in range(self.chips):
            for g in range(self.size):
                here = self.source[2 * z + self.core, g] if self.mine is None else self.mine[z, g]
                both = here.astype(f32) + self.first[z, g].astype(f32)
                self.pairs[z, g] = both.astype(bf16)
        self.moving = []
        for i in range(1, self.crops):
            target = lax.rem(self.crop + i, self.crops)
            block = self.pairs.at[:, pl.ds(target * self.share, self.share)]
            self.moving.append(
                self.copies.start(block, self.crossed.at[self.crop], self.over_crops[i - 1])
            )
        for z in range(self.chips):
            for g in range(self.share):
                self.crossed[self.crop, z, g] = self.pairs[z, self.crop * self.share + g]

    def over_the_chips(self):
        self.wait()
        for z in range(self.chips):
            for g in range(self.share):
                value = self.crossed[0, z, g].astype(f32)
                for i in range(1, self.crops):
                    value = value + self.crossed[i, z, g].astype(f32)
                self.halves[z, g] = value.astype(bf16)
        self.moving = []
        for j in range(1, self.chips):
            target = lax.rem(self.chip + j, self.chips)
            self.moving.append(
                self.copies.start(
                    self.halves.at[target], self.lined.at[self.chip], self.over_chips[j - 1]
                )
            )
        for g in range(self.share):
            self.lined[self.chip, g] = self.halves[self.chip, g]

    def to_all_crops(self):
        self.wait()
        for g in range(self.share):
            value = self.lined[0, g].astype(f32)
            for z in range(1, self.chips):
                value = value + self.lined[z, g].astype(f32)
            self.out[self.crop * self.share + g] = value.astype(bf16)
        here = self.out.at[pl.ds(self.crop * self.share, self.share)]
        self.moving = [self.copies.start(here, here, peer) for peer in self.over_crops]

    def finish(self):
        self.wait()


def reduce_scratch(crops, n, size, own, c):
    chips, share = n // 2, size // crops
    V = pltpu.VMEM
    return [
        V((chips, size, own, c), bf16),
        V((chips, size, own, c), bf16),
        V((crops, chips, share, own, c), bf16),
        V((chips, share, own, c), bf16),
        V((chips, share, own, c), bf16),
        V((size, own, c), bf16),
    ]


def reduce_copies(crops, n):
    return 2 * (n // 2) - 1 + 2 * (crops - 1)


class Gather:
    def __init__(self, n, send, recv):
        my_crop, self.me = lax.axis_index("crop"), lax.axis_index("chan")
        self.n, self.chips = n, n // 2
        self.core = lax.rem(self.me, 2)
        self.other = (my_crop, self.me + 1 - 2 * self.core)
        self.send, self.recv = send, recv
        self.peer = lambda j: (my_crop, lax.rem(self.me + 2 * j, n))

    def block(self, j):
        return lax.rem(self.me - 2 * j + self.n, self.n)

    def other_block(self, j):
        return lax.rem(self.me + 1 - 2 * self.core - 2 * j + self.n, self.n)

    def start(self, at):
        self.at = at
        self.far, self.pairs = [], []
        for j in range(1, self.chips):
            here = at(self.me)
            self.far.append(remote(here, here, self.send.at[j], self.recv.at[j], self.peer(j)))
            self.far[-1].start()
        self.forward(0)

    def forward(self, j):
        here = self.at(self.block(j))
        k = self.chips + j
        self.pairs.append(remote(here, here, self.send.at[k], self.recv.at[k], self.other))
        self.pairs[-1].start()

    def arrive(self, j):
        self.far[j - 1].wait_recv()
        self.forward(j)

    def finish(self):
        for copy in self.pairs:
            copy.wait_recv()

    def drain(self):
        for copy in self.far + self.pairs:
            copy.wait_send()


class LineGather(Gather):
    def __init__(self, n, send, recv):
        super().__init__(n, send, recv)
        my_crop, self.chip = lax.axis_index("crop"), lax.div(self.me, 2)
        self.end = jnp.logical_or(self.chip == 0, self.chip == 3)
        self.inner = jnp.logical_not(self.end)
        beside = self.chip + 1 - 2 * lax.rem(self.chip, 2)
        over, mirror = lax.rem(self.chip + 2, 4), 3 - self.chip
        second = jnp.where(self.end, over, mirror)
        third = jnp.where(self.end, mirror, over)
        self.order = [2 * z + self.core for z in (self.chip, beside, second, third)]
        self.to = lambda z: (my_crop, 2 * z + self.core)
        self.beside, self.over, self.mirror = beside, over, mirror

    def block(self, j):
        return self.order[j]

    def start(self, at):
        self.at = at
        self.pairs = []
        here = at(self.me)
        make = lambda k, block, z, s=None: remote(
            block, block, self.send.at[k if s is None else s], self.recv.at[k], self.to(z)
        )
        self.first = make(0, here, self.beside)
        self.first.start()
        self.middle = make(1, here, self.mirror)
        self.long = make(2, here, self.over, 1)
        pl.when(self.inner)(self.middle.start)
        pl.when(self.end)(self.long.start)
        self.passed = [make(3, at(self.order[2]), self.beside), make(8, at(self.order[3]), self.beside)]
        self.forward(0)

    def arrive(self, j):
        if j == 1:
            self.first.wait_recv()
        else:
            come, on = (self.middle, self.long)[j - 2], self.passed[j - 2]

            def pass_it():
                come.wait_recv()
                on.start()

            pl.when(self.inner)(pass_it)
            pl.when(self.end)(on.wait_recv)
        self.forward(j)

    def drain(self):
        self.first.wait_send()
        self.middle.wait_send()
        for copy in self.pairs:
            copy.wait_send()

        def passed():
            for copy in self.passed:
                copy.wait_send()

        pl.when(self.inner)(passed)


def gather_over(n, send, recv):
    return LineGather(n, send, recv) if n // 2 == 4 else Gather(n, send, recv)


class BackRefs(typing.NamedTuple):
    grad: object
    src_hbm: object
    point: object
    atrous_hbm: object
    pool: object
    pack: object
    low_grad: object
    low_in_hbm: object
    wgrads: object
    features_hbm: object
    point_w: object
    atrous_w_hbm: object
    pool_w: object
    low_w_out: object
    blocks: object
    low_full_hbm: object
    last_grad: object
    last_src: object
    src: object
    atrous: object
    low_in: object
    features: object
    atrous_w: object
    low_full: object
    mine: object
    local: object
    m_sems: object
    w_sems: object
    all_grad: object
    shifted: object
    turned: object
    total: object
    r_first: object
    r_pairs: object
    r_crossed: object
    r_halves: object
    r_lined: object
    r_out: object
    low_parts: object
    g_send: object
    g_recv: object
    l_send: object
    l_recv: object
    c_send: object
    c_recv: object


def back_kernel(crops, n, *refs):
    ref = BackRefs(*refs)
    my_crop, me = lax.axis_index("crop"), lax.axis_index("chan")
    chips = n // 2
    core, chip = lax.rem(me, 2), lax.div(me, 2)
    block, width = ref.grad.shape
    c = width // 4
    half = width // 2
    c_in = ref.src.shape[2]
    cells = FA * FA
    relay = crops == 4
    other = (my_crop, me + 1 - 2 * core)
    over_crops = [(lax.rem(my_crop + i, crops), me) for i in range(1, crops)]
    over_chips = [(my_crop, lax.rem(me + 2 * j, n)) for j in range(1, chips)]
    wait_barrier = barrier_with([other] + over_crops + over_chips)
    all_grad, src = ref.all_grad, ref.src
    if relay:
        along_x = my_crop + 1 - 2 * lax.rem(my_crop, 2)
        along_y = my_crop + 2 - 4 * lax.div(my_crop, 2)
        crop_list = [my_crop, along_x, along_y, 3 - my_crop]
    else:
        crop_list = [my_crop] + [lax.rem(my_crop - i + crops, crops) for i in range(1, crops)]

    def grad_at(crop):
        def at(b):
            return all_grad.at[crop, pl.ds(pl.multiple_of(b * block, block), block)]

        return at

    def lanes_at(crop, b, first):
        return all_grad.at[crop, pl.ds(pl.multiple_of(b * block, block), block), pl.ds(first, half)]

    local_copies = []

    def local(src, dst):
        copy = pltpu.make_async_copy(src, dst, ref.local.at[len(local_copies)])
        copy.start()
        local_copies.append(copy)

    local(ref.src_hbm, src)
    local(ref.src_hbm.at[crop_list[-1]], ref.last_src)
    weight_copies = []
    for k in range(3):
        for t in range(9):
            at = ref.atrous.at[k, t // 3, :, pl.ds(t % 3 * c, c)]
            copy = pltpu.make_async_copy(ref.atrous_hbm.at[k, t], at, ref.w_sems.at[9 * k + t])
            copy.start()
            weight_copies.append(copy)
    local(ref.low_in_hbm, ref.low_in)
    pooled_grad = ref.pack[24:40].astype(bf16)
    all_grad[my_crop, pl.ds(pl.multiple_of(me * block, block), block)] = ref.grad[...]
    ref.low_full[me] = ref.low_grad[...]
    wait_barrier()

    gather = gather_over(n, ref.g_send, ref.g_recv)
    gather.start(grad_at(my_crop))
    moves = Copies(ref.c_send, ref.c_recv)
    crossing = {}

    def cross(j):
        here = grad_at(my_crop)(gather.block(j))
        if relay:
            for i, crop in ((1, along_x), (2, along_y)):
                crossing[i, j] = moves.start(here, here, (crop, me))
        else:
            for i in range(1, crops):
                crossing[i, j] = moves.start(here, here, over_crops[i - 1])

    core_copies = {}

    def pass_on(i, j):
        crossing[i, j].wait_recv()
        b = gather.block(j)
        crop = crop_list[i]
        if relay and i == 1:
            here = lanes_at(crop, b, 0)
            crossing[3, j, 0] = moves.start(here, here, (along_y, me))
        if relay and i == 2:
            here = lanes_at(crop, b, half)
            crossing[3, j, 1] = moves.start(here, here, (along_x, me))
        place = grad_at(crop)(b)
        core_copies[i, j] = moves.start(place, place, other)

    def pass_across(j):
        crossing[3, j, 0].wait_recv()
        crossing[3, j, 1].wait_recv()
        place = grad_at(crop_list[3])(gather.block(j))
        core_copies[3, j] = moves.start(place, place, other)

    cross(0)
    reduce = Reduce(
        crops, n, moves, ref.wgrads, ref.r_first, ref.r_pairs, ref.r_crossed, ref.r_halves, ref.r_lined, ref.r_out,
        ref.mine, ref.m_sems,
    )
    reduce.cores()
    shifted = ref.shifted

    def shift_source(i):
        crop = crop_list[i]
        for k in range(3):
            rate = atrous_rates[k]
            shift_three(lambda base: src[crop, pl.ds(base, 128)], shifted.at[i % 3, k], rate, -rate, rate)

    local_copies[0].wait()
    shift_source(0)
    reduce.over_the_crops()
    for i in range(1, min(3, crops)):
        shift_source(i)
    pooled = []
    for i in range(crops):
        mean = row_of(src[i].astype(f32)) * (1.0 / cells)
        pooled.append(mean)
    pooled = jnp.concatenate(pooled + [jnp.zeros((16 - crops, c_in), f32)], axis=0).astype(bf16)
    ref.pool_w[...] = dot_tn(pooled, pooled_grad)
    for j in range(1, chips):
        gather.arrive(j)
        cross(j)
    reduce.over_the_chips()
    low_gather = Gather(n, ref.l_send, ref.l_recv)
    low_gather.start(lambda b: ref.low_full.at[b])
    if relay:
        pass_on(1, 0)
        pass_on(2, 0)
    gather.finish()

    total, turned = ref.total, ref.turned
    pool_row = dot_nt(pooled_grad, ref.pool[...])
    my_row = lax.broadcasted_iota(jnp.int32, pool_row.shape, 0) == my_crop
    pool_row = row_of(jnp.where(my_row, pool_row, 0.0)) * (1.0 / cells)
    for copy in weight_copies:
        copy.wait()
    total[...] = dot_nt(all_grad[my_crop, :, 0:c], ref.point[...]) + pool_row
    for k in range(3):
        rate = atrous_rates[k]
        shift_three(
            lambda base: all_grad[my_crop, pl.ds(base, 128), (k + 1) * c : (k + 2) * c],
            turned, rate, rate, -rate,
        )
        for a in range(3):
            move = (a - 1) * rate
            count = (FA - abs(move)) * FA
            to, off = max(move, 0) * FA, max(-move, 0) * FA
            total[pl.ds(to, count)] += dot_nt(turned[pl.ds(off, count)], ref.atrous[k, a])

    def weight_part(i):
        crop = crop_list[i]
        part = dot_tn(src[crop], all_grad[crop, :, 0:c])
        ref.point_w[...] = part if i == 0 else ref.point_w[...] + part
        for k in range(3):
            rate = atrous_rates[k]
            for a in range(3):
                move = (a - 1) * rate
                count = (FA - abs(move)) * FA
                from_src, off = max(move, 0) * FA, max(-move, 0) * FA
                part = dot_tn(
                    shifted[i % 3, k, pl.ds(from_src, count)],
                    all_grad[crop, pl.ds(off, count), (k + 1) * c : (k + 2) * c],
                )
                for e in range(3):
                    piece = part[e * c_in : (e + 1) * c_in]
                    if i > 0:
                        piece = ref.atrous_w[k, 3 * a + e] + piece
                    ref.atrous_w[k, 3 * a + e] = piece
            if i == crops - 2:
                local(ref.atrous_w.at[k], ref.atrous_w_hbm.at[k])

    weight_part(0)
    ref.features[...] = total[...].T
    local(ref.features, ref.features_hbm)
    if relay:
        for j in range(1, chips):
            pass_on(1, j)
            pass_on(2, j)

    def low_part():
        for j in range(1, chips):
            low_gather.arrive(j)
        low_gather.finish()
        local(ref.low_full, ref.low_full_hbm)
        local_copies[2].wait()
        rows = ref.low_full.shape[2] // 128
        low_in, low_all = ref.low_in, ref.low_full
        low_total = None
        for b in range(n):
            here = low_all[b]
            span = slice(b * rows * 128, (b + 1) * rows * 128)
            part = dot_nt(low_in[:, span], here)
            low_total = part if low_total is None else low_total + part
        low_parts = ref.low_parts
        low_parts[my_crop] = jnp.zeros(low_parts.shape[1:], f32)
        low_parts[my_crop, :, 0 : low_total.shape[1]] = low_total
        here = low_parts.at[my_crop]
        low_copies = [moves.start(here, here, peer) for peer in over_crops]
        return low_copies

    for i in range(1, crops):
        if i + 2 < crops - 1:
            shift_source(i + 2)
        for j in range(chips):
            if not relay:
                pass_on(i, j)
            elif i == 3:
                pass_across(j)
        for j in range(chips):
            core_copies[i, j].wait_recv()
        if i < crops - 1:
            weight_part(i)
        if i == min(2, crops - 1):
            reduce.to_all_crops()
            low_copies = low_part()

    local(all_grad.at[crop_list[-1]], ref.last_grad)
    reduce.finish()
    for g in range(ref.blocks.shape[0]):
        ref.blocks[g] = ref.r_out[g].astype(f32)
    for copy in low_copies:
        copy.wait_recv()
    ref.low_w_out[...] = jnp.sum(ref.low_parts[...], axis=0)
    gather.drain()
    low_gather.drain()
    moves.drain([])
    for k, copy in enumerate(local_copies):
        if k not in (0, 2):
            copy.wait()


def pyramid_back(crops, n, *args):
    grad, src, low_grad, low_in, wgrads = args[0], args[1], args[6], args[7], args[8]
    block, width = grad.shape
    c = width // 4
    c_in = src.shape[2]
    chips = n // 2
    cells = FA * FA
    low_rows = low_in.shape[0]
    own, lanes = wgrads.shape[2:]
    S = jax.ShapeDtypeStruct
    V = pltpu.VMEM
    D = pltpu.SemaphoreType.DMA
    vmem = pl.BlockSpec(memory_space=pltpu.VMEM)
    hbm = pl.BlockSpec(memory_space=pl.ANY)
    count = 3 * crops * chips + crops - 1 + reduce_copies(crops, n)
    return pl.pallas_call(
        functools.partial(back_kernel, crops, n),
        out_shape=[
            S((c_in, cells), f32),
            S((c_in, c), f32),
            S((3, 9, c_in, c), f32),
            S((c_in, c), f32),
            S((low_rows, 128), f32),
            S((15, own, lanes), f32),
            S((n,) + low_grad.shape, bf16),
            S((cells, width), bf16),
            S((cells, c_in), bf16),
        ],
        in_specs=[vmem, hbm, vmem, hbm, vmem, vmem, vmem, hbm, hbm],
        out_specs=[hbm, vmem, hbm, vmem, vmem, vmem, hbm, hbm, hbm],
        scratch_shapes=[
            V(src.shape, bf16),
            V((3, 3, c_in, 3 * c), bf16),
            V(low_in.shape, bf16),
            V((c_in, cells), f32),
            V((3, 9, c_in, c), f32),
            V((n,) + low_grad.shape, bf16),
            V((chips,) + wgrads.shape[1:], bf16),
            D((12,)),
            D((chips,)),
            D((27,)),
            V((crops, cells, width), bf16),
            V((min(3, crops), 3, cells, 3 * c_in), bf16),
            V((cells, 3 * c), bf16),
            V((cells, c_in), f32),
            *reduce_scratch(crops, n, wgrads.shape[1], own, lanes),
            V((crops, low_rows, 128), f32),
            D((n + 1,)),
            D((n + 1,)),
            D((n + 1,)),
            D((n + 1,)),
            D((count,)),
            D((count,)),
        ],
        compiler_params=pltpu.CompilerParams(
            collective_id=1, has_side_effects=True, vmem_limit_bytes=62 * 1024 * 1024
        ),
    )(*args)


class FinishRefs(typing.NamedTuple):
    atrous_part: object
    point_part: object
    last_grad: object
    last_src: object
    features_in: object
    pool_in: object
    low_full: object
    low_w: object
    low_w_part: object
    logits_in: object
    dec2_in: object
    blocks: object
    pack: object
    logits: object
    features: object
    early: object
    point: object
    atrous: object
    pool: object
    proj: object
    low_w_out: object
    dec1: object
    side: object
    dec2: object
    cls: object
    bias: object
    gain: object
    shift: object
    low_gain: object
    low_shift: object
    v_atrous: object
    v_grad: object
    v_src: object
    v_low: object
    v_logits: object
    v_early: object
    v_point: object
    v_proj: object
    v_low_w: object
    v_side: object
    v_cls: object
    v_bias: object
    v_gain: object
    v_shift: object
    v_low_gain: object
    v_low_shift: object
    turned: object
    sems: object


def finish_kernel(*refs):
    ref = FinishRefs(*refs)
    copies = []

    def move(src, dst):
        copy = pltpu.make_async_copy(src, dst, ref.sems.at[len(copies)])
        copy.start()
        copies.append(copy)
        return copy

    c_in, c = ref.v_point.shape
    classes, rows = ref.v_logits.shape[0], ref.v_logits.shape[1]
    low_width = ref.v_low_w.shape[1]
    own = ref.v_cls.shape[1]
    loaded = [move(ref.last_grad, ref.v_grad), move(ref.last_src, ref.v_src)]
    parts = [move(ref.atrous_part.at[k], ref.v_atrous.at[k]) for k in range(3)]
    low = move(ref.low_full, ref.v_low)
    straight = [
        move(ref.features_in, ref.features),
        move(ref.pool_in, ref.pool),
        move(ref.dec2_in, ref.dec2),
        move(ref.blocks.at[pl.ds(0, 9)], ref.dec1),
        move(ref.blocks.at[pl.ds(9, 4)], ref.proj.at[pl.ds(0, 4)]),
        move(ref.pack.at[pl.ds(40, own)], ref.proj.at[4]),
    ]

    ref.v_logits[...] = ref.logits_in[0:classes].reshape(classes, rows, 128)
    straight.append(move(ref.v_logits, ref.logits))
    pack = ref.pack
    tail = jnp.concatenate([ref.blocks[13], ref.blocks[14]], axis=1)
    width = 2 * c
    for t in range(9):
        ref.v_side[t] = pltpu.roll(tail, (width - t * low_width) % width, 1)[:, 0:low_width]
    cls = pltpu.roll(tail, width - 9 * low_width, 1)[:, 0:128]
    cls = jnp.concatenate([cls, jnp.zeros((128 - own, 128), f32)], axis=0)
    ref.v_cls[...] = cls.T[0:classes, 0:own]
    ref.v_low_w[...] = ref.low_w_part[:, 0:low_width]
    ref.v_gain[...] = pack[0:8, 0:own]
    ref.v_shift[...] = pack[8:16, 0:own]
    ref.v_bias[...] = pack[16:17, 0:classes]
    ref.v_low_gain[...] = pack[17:18, 0:low_width]
    ref.v_low_shift[...] = pack[18:19, 0:low_width]
    for src, dst in (
        (ref.v_side, ref.side),
        (ref.v_cls, ref.cls),
        (ref.v_low_w, ref.low_w_out),
        (ref.v_gain, ref.gain),
        (ref.v_shift, ref.shift),
        (ref.v_bias, ref.bias),
        (ref.v_low_gain, ref.low_gain),
        (ref.v_low_shift, ref.low_shift),
    ):
        straight.append(move(src, dst))

    for copy in loaded:
        copy.wait()
    for k in range(3):
        rate = atrous_rates[k]
        shift_three(lambda base: ref.v_src[pl.ds(base, 128)], ref.turned, rate, -rate, rate)
        parts[k].wait()
        for a in range(3):
            by = (a - 1) * rate
            count = (FA - abs(by)) * FA
            from_src, off = max(by, 0) * FA, max(-by, 0) * FA
            part = dot_tn(
                ref.turned[pl.ds(from_src, count)],
                ref.v_grad[pl.ds(off, count), (k + 1) * c : (k + 2) * c],
            )
            for e in range(3):
                ref.v_atrous[k, 3 * a + e] += part[e * c_in : (e + 1) * c_in]
        straight.append(move(ref.v_atrous.at[k], ref.atrous.at[k]))
        if k == 0:
            low.wait()
            for b in range(ref.low_full.shape[0]):
                value = dot(ref.low_w[...], ref.v_low[b])
                ref.v_early[:, b * rows : (b + 1) * rows] = value.reshape(value.shape[0], rows, 128)
            straight.append(move(ref.v_early, ref.early))
            ref.v_point[...] = ref.point_part[...] + dot_tn(ref.v_src[...], ref.v_grad[:, 0:c])
            straight.append(move(ref.v_point, ref.point))
    for copy in straight:
        copy.wait()


def finish(shapes, *args):
    parts = FinishRefs(*args, *([None] * (len(FinishRefs._fields) - len(args))))
    c_in = parts.point_part.shape[0]
    vmem = pl.BlockSpec(memory_space=pltpu.VMEM)
    hbm = pl.BlockSpec(memory_space=pl.ANY)
    V = pltpu.VMEM
    held = [V(shapes[k], f32) for k in (0, 2, 3)]
    held += [V(shapes[k], f32) for k in (6, 7, 9, 11, 12, 13, 14, 15, 16)]
    return pl.pallas_call(
        finish_kernel,
        out_shape=[jax.ShapeDtypeStruct(shape, f32) for shape in shapes],
        in_specs=[hbm, vmem, hbm, hbm, vmem, vmem, hbm, vmem, vmem, vmem, vmem, vmem, vmem],
        out_specs=[hbm] * len(shapes),
        scratch_shapes=[
            V(parts.atrous_part.shape, f32),
            V(parts.last_grad.shape, bf16),
            V(parts.last_src.shape, bf16),
            V(parts.low_full.shape, bf16),
            *held,
            V((FA * FA, 3 * c_in), bf16),
            pltpu.SemaphoreType.DMA((32,)),
        ],
        compiler_params=pltpu.CompilerParams(vmem_limit_bytes=60 * 1024 * 1024),
    )(*args)


def per_device(
    features,
    low_in,
    offsets,
    d_logits,
    w_point,
    w_atrous,
    w_pool,
    w_proj,
    w_low,
    w_dec1,
    w_dec1_low,
    w_dec2,
    w_cls,
    b_cls,
    bn_gain,
    bn_shift,
    low_gain,
    low_shift,
):
    n = lax.axis_size("chan")
    crops = lax.axis_size("crop")
    fine = low_in.shape[2]
    rows = fine // n
    coarse_rows = FA // n
    channels = w_dec2.shape[2]
    c_in = features.shape[1]
    low_width = w_low.shape[1]
    coarse_samples = FA * FA * crops
    fine_samples = fine * fine * crops

    classes = w_cls.shape[1]
    logits, branch_grad, low_pre_bf, pack, dec2_wgrad, blocks, source_all, low_flat = decoder(
        crops,
        n,
        (coarse_samples, fine_samples),
        offsets,
        features[0],
        w_point,
        w_atrous.reshape(3, 3, 3 * c_in, channels),
        w_pool,
        low_in[0],
        w_low,
        w_proj,
        w_dec1,
        w_dec1_low.transpose(0, 2, 1),
        w_dec2,
        w_cls.T,
        bn_gain,
        bn_shift,
        low_gain[None],
        low_shift[None],
        b_cls[None],
        d_logits[0],
    )
    feature_grad, point_wgrad, atrous_wgrad, pool_wgrad, low_wgrad, blocks, low_full, last_grad, last_src = (
        pyramid_back(
            crops,
            n,
            branch_grad,
            source_all,
            w_point,
            w_atrous,
            w_pool,
            pack,
            low_pre_bf,
            low_flat,
            blocks,
        )
    )
    own = w_dec2.shape[1]
    shapes = [
        (classes, rows, fine),
        (c_in, FA * FA),
        low_in.shape[1:],
        (c_in, channels),
        (3, 9, c_in, channels),
        (c_in, channels),
        (5, own, channels),
        (low_in.shape[1], low_width),
        (9, own, channels),
        (9, own, low_width),
        (9, own, channels),
        (classes, own),
        (1, classes),
        (8, own),
        (8, own),
        (1, low_width),
        (1, low_width),
    ]
    outs = finish(
        shapes,
        atrous_wgrad,
        point_wgrad,
        last_grad,
        last_src,
        feature_grad,
        pool_wgrad,
        low_full,
        w_low,
        low_wgrad,
        logits,
        dec2_wgrad,
        blocks,
        pack,
    )
    outs = list(outs)
    for k in (0, 1, 2):
        outs[k] = outs[k][None]
    for k in (12, 15, 16):
        outs[k] = outs[k][0]
    outs[9] = outs[9].transpose(0, 2, 1)
    outs[11] = outs[11].T
    return tuple(outs)


def solution(mesh):
    placed = (
        P("crop", "chan", None),
        P("crop", "chan", None, None),
        P("crop", None),
        P("crop", None, None, None),
        P("chan", None),
        P(None, None, "chan", None),
        P("chan", None),
        P(None, "chan", None),
        P("chan", None),
        P(None, "chan", None),
        P(None, None, "chan"),
        P(None, "chan", None),
        P("chan", None),
        P(),
        P(None, "chan"),
        P(None, "chan"),
        P(),
        P(),
    )
    return jax.shard_map(
        per_device,
        mesh=mesh,
        in_specs=placed,
        out_specs=(
            P("crop", None, "chan", None),
            P("crop", "chan", None),
            P("crop", "chan", None, None),
            P("chan", None),
            P(None, None, "chan", None),
            P("chan", None),
            P(None, "chan", None),
            P("chan", None),
            P(None, "chan", None),
            P(None, None, "chan"),
            P(None, "chan", None),
            P("chan", None),
            P(),
            P(None, "chan"),
            P(None, "chan"),
            P(),
            P(),
        ),
        check_vma=False,
    )
```

```python
import functools
import typing

import jax
import jax.numpy as jnp
from jax import lax
from jax.experimental import pallas as pl
from jax.experimental.pallas import tpu as pltpu
from jax.sharding import PartitionSpec as P

FA = 32
SCENE_H = 1024
SCENE_W = 2048

epsilon = 1e-05
highest = lax.Precision.HIGHEST
atrous_rates = (6, 12, 18)
f32 = jnp.float32
bf16 = jnp.bfloat16
BOTH = ("crop", "chan")


MESH = pl.DeviceIdType.MESH


def chip_peers(crops, n):
    my_crop, me = lax.axis_index("crop"), lax.axis_index("chan")
    core = lax.rem(me, 2)
    chips = n // 2
    other = (my_crop, me + 1 - 2 * core)
    far = []
    for i in range(crops):
        for j in range(chips):
            if i or j:
                far.append((lax.rem(my_crop + i, crops), lax.rem(me + 2 * j, n)))
    return other, far


GELU_A = 0.7978845608028654
GELU_B = 0.044715


def gelu(x):
    return 0.5 * x * (1.0 + jnp.tanh(GELU_A * (x + GELU_B * x * x * x)))


def gelu_both(x):
    square = x * x
    t = jnp.tanh(GELU_A * x * (1.0 + GELU_B * square))
    upper = 0.5 * (1.0 + t)
    return x * upper, upper + (0.5 * GELU_A) * x * (1.0 - t * t) * (1.0 + (3.0 * GELU_B) * square)


def gelu_slope(x):
    square = x * x
    t = jnp.tanh(GELU_A * x * (1.0 + GELU_B * square))
    return 0.5 * (1.0 + t) + (0.5 * GELU_A) * x * (1.0 - t * t) * (1.0 + (3.0 * GELU_B) * square)


def dot(a, b):
    return jnp.dot(a, b, preferred_element_type=f32)


def dot_nt(a, b):
    return lax.dot_general(a, b, (((1,), (1,)), ((), ())), preferred_element_type=f32)


def dot_tn(a, b):
    return lax.dot_general(a, b, (((0,), (0,)), ((), ())), preferred_element_type=f32)


def dot_exact(table, values):
    high = values.astype(bf16)
    rest = values - high.astype(f32)
    middle = rest.astype(bf16)
    low = (rest - middle.astype(f32)).astype(bf16)
    return dot(table, high) + (dot(table, middle) + dot(table, low))


def fold(values):
    return jnp.sum(values.reshape(values.shape[0] // 8, 8, values.shape[1]), axis=0)


def row_of(values):
    return jnp.sum(values, axis=0, keepdims=True)


def barrier_with(peers):
    barrier = pltpu.get_barrier_semaphore()
    for peer in peers:
        pl.semaphore_signal(barrier, inc=1, device_id=peer, device_id_type=MESH)
    return lambda: pl.semaphore_wait(barrier, len(peers))


def remote(src, dst, send, recv, peer):
    return pltpu.make_async_remote_copy(
        src_ref=src, dst_ref=dst, send_sem=send, recv_sem=recv, device_id=peer, device_id_type=MESH
    )


class Copies:
    def __init__(self, send, recv):
        self.send, self.recv, self.all, self.next = send, recv, [], 0

    def make(self, src, dst, peer, send=None):
        k = self.next
        self.next += 1
        return remote(src, dst, self.send.at[k if send is None else send], self.recv.at[k], peer)

    def start(self, src, dst, peer):
        copy = self.make(src, dst, peer)
        copy.start()
        self.all.append(copy)
        return copy

    def drain(self, kept):
        for copy in self.all:
            if not any(copy is other for other in kept):
                copy.wait_send()


class LineSum:
    def __init__(self, n, copies, staged, arrived, spare, refill):
        my_crop, me = lax.axis_index("crop"), lax.axis_index("chan")
        core, self.chip = lax.rem(me, 2), lax.div(me, 2)
        self.chips, self.copies, self.staged, self.arrived = n // 2, copies, staged, arrived
        self.spare, self.refill = spare, refill
        self.peer = lambda z: (my_crop, 2 * z + core)
        self.line = self.chips == 4
        if self.line:
            self.beside = self.chip + 1 - 2 * lax.rem(self.chip, 2)
            self.over = lax.rem(self.chip + 2, 4)
            self.mirror = 3 - self.chip
            self.end = jnp.logical_or(self.chip == 0, self.chip == 3)
            self.inner = jnp.logical_not(self.end)

    def send(self, z):
        return self.copies.start(self.staged.at[z], self.arrived.at[self.chip], self.peer(z))

    def start(self):
        if not self.line:
            targets = [lax.rem(self.chip + j, self.chips) for j in range(1, self.chips)]
            self.direct = [self.send(z) for z in targets]
            return
        here = self.staged.at[self.mirror]
        k = self.copies.next
        self.passed = self.copies.make(here, self.spare, self.peer(self.beside))
        self.middle = self.copies.make(here, self.arrived.at[self.chip], self.peer(self.mirror), k)
        self.copies.all.append(self.passed)
        pl.when(self.end)(self.passed.start)
        pl.when(self.inner)(self.middle.start)
        self.first = self.send(self.beside)

    def second(self):
        if not self.line:
            return

        def merge():
            self.passed.wait_recv()
            both = self.refill(self.over) + self.spare[...].astype(f32)
            self.staged[self.over] = both.astype(bf16)

        pl.when(self.inner)(merge)
        self.crossed = self.send(self.over)

    def finish(self, add):
        if not self.line:
            for j in range(1, self.chips):
                self.direct[j - 1].wait_recv()
                add(self.arrived[lax.rem(self.chip - j + self.chips, self.chips)].astype(f32))
            return
        self.first.wait_recv()
        add(self.arrived[self.beside].astype(f32))

        def third():
            self.middle.wait_recv()
            add(self.arrived[self.mirror].astype(f32))

        pl.when(self.inner)(third)
        self.crossed.wait_recv()
        add(self.arrived[self.over].astype(f32))


def shift_three(source, target, rate, first, last):
    column = lax.rem(lax.broadcasted_iota(jnp.int32, (128, 1), 0), FA)

    def step(i, kept):
        base = pl.multiple_of(i * 128, 128)
        here = source(base)
        w = here.shape[1]
        wide = here.astype(f32)
        for slot, by in ((0, first), (2, last)):
            ok = jnp.logical_and(column + by >= 0, column + by < FA)
            moved = jnp.where(ok, pltpu.roll(wide, (-by) % 128, 0), 0.0)
            target[pl.ds(base, 128), slot * w : (slot + 1) * w] = moved.astype(bf16)
        target[pl.ds(base, 128), w : 2 * w] = here
        return kept

    lax.fori_loop(0, FA * FA // 128, step, 0)


class Swap:
    def __init__(self, crops, n, pair, slots, pair_sems, send, recv):
        self.other, self.far = chip_peers(crops, n)
        me = lax.axis_index("chan")
        self.core = lax.rem(me, 2)
        self.mine = lax.axis_index("crop") * (n // 2) + lax.div(me, 2)
        self.pair, self.slots, self.pair_sems = pair, slots, pair_sems
        self.send, self.recv = send, recv

    def start(self):
        here = self.pair.at[self.core]
        copy = remote(here, here, self.pair_sems.at[0], self.pair_sems.at[1], self.other)
        copy.start()
        copy.wait()
        self.slots[self.mine] = self.pair[0] + self.pair[1]
        self.copies = []
        for k, peer in enumerate(self.far):
            slot = self.slots.at[self.mine]
            copy = remote(slot, slot, self.send.at[k], self.recv.at[k], peer)
            copy.start()
            self.copies.append(copy)

    def finish(self):
        for copy in self.copies:
            copy.wait_recv()
        return jnp.sum(self.slots[...], axis=0)

    def drain(self):
        for copy in self.copies:
            copy.wait_send()


class WideSwap:
    def __init__(self, crops, n, pair, first, second, pair_sems, send, recv):
        my_crop, me = lax.axis_index("crop"), lax.axis_index("chan")
        self.core, self.crop, self.chip = lax.rem(me, 2), my_crop, lax.div(me, 2)
        self.other = (my_crop, me + 1 - 2 * self.core)
        self.over_crops = [(lax.rem(my_crop + i, crops), me) for i in range(1, crops)]
        self.over_chips = [(my_crop, lax.rem(me + 2 * j, n)) for j in range(1, n // 2)]
        self.pair, self.first, self.second = pair, first, second
        self.pair_sems, self.send, self.recv = pair_sems, send, recv

    def run(self, then=None):
        here = self.pair.at[self.core]
        copy = remote(here, here, self.pair_sems.at[0], self.pair_sems.at[1], self.other)
        copy.start()
        copy.wait()
        self.first[self.crop] = self.pair[0] + self.pair[1]
        k = 0
        copies = []
        for peer in self.over_crops:
            slot = self.first.at[self.crop]
            copies.append(remote(slot, slot, self.send.at[k], self.recv.at[k], peer))
            copies[-1].start()
            k += 1
        for copy in copies:
            copy.wait()
        self.second[self.chip] = jnp.sum(self.first[...], axis=0)
        copies = []
        for peer in self.over_chips:
            slot = self.second.at[self.chip]
            copies.append(remote(slot, slot, self.send.at[k], self.recv.at[k], peer))
            copies[-1].start()
            k += 1
        if then is not None:
            then()
        for copy in copies:
            copy.wait()
        return jnp.sum(self.second[...], axis=0)


def put_pair(ref, core, a, b):
    ref[core, 0:1] = a[:, :128]
    ref[core, 1:2] = a[:, 128:]
    ref[core, 2:3] = b[:, :128]
    ref[core, 3:4] = b[:, 128:]


def get_pair(total):
    return (
        jnp.concatenate([total[0:1], total[1:2]], axis=1),
        jnp.concatenate([total[2:3], total[3:4]], axis=1),
    )


def spread_row(row):
    return jnp.broadcast_to(row, (128, 128)).T


def up_weights(i, me, n, rows, coarse_rows):
    lower = (2 * i - 3) // 8
    upper_weight = (2 * i - 3 - 8 * lower) / 8.0
    a, b = 1.0 - upper_weight, upper_weight
    if lower < 0:
        top = me == 0
        a, b = jnp.where(top, 0.0, a), jnp.where(top, 1.0, b)
    if lower + 1 >= coarse_rows:
        bottom = me == n - 1
        a, b = jnp.where(bottom, 1.0, a), jnp.where(bottom, 0.0, b)
    if i < 0:
        a, b = jnp.where(me == 0, 0.0, a), jnp.where(me == 0, 0.0, b)
    if i >= rows:
        a, b = jnp.where(me == n - 1, 0.0, a), jnp.where(me == n - 1, 0.0, b)
    return lower + 1, a, b


class DecoderRefs(typing.NamedTuple):
    offsets: object
    feat: object
    point: object
    atrous_hbm: object
    pool_w: object
    low_rows: object
    low_w: object
    w_proj: object
    w_dec1: object
    w_side: object
    w_dec2: object
    w_cls: object
    own_gain: object
    own_shift: object
    low_gain: object
    low_shift: object
    bias: object
    d_logits: object
    logits_hbm: object
    branch_hbm: object
    low_hbm: object
    pack_hbm: object
    dec2_hbm: object
    wgrads_hbm: object
    src_all: object
    low_flat: object
    dlog: object
    near: object
    low_in: object
    atrous: object
    src_own: object
    logits: object
    branch_out: object
    low_out: object
    pack: object
    dec2_w: object
    wgrads: object
    low_ext: object
    low_push: object
    lowx: object
    merged_ext: object
    merged_part: object
    dec1: object
    dec2: object
    pushed: object
    pushed1: object
    x1: object
    x2: object
    g2: object
    g1: object
    yt: object
    branch_bf: object
    proj_bf: object
    flip: object
    branch: object
    staged: object
    arrived: object
    low_send: object
    low_pair: object
    low_sum: object
    low_recv: object
    spare: object
    low_spare: object
    gath: object
    norms_all: object
    norms: object
    proj: object
    w1: object
    tail: object
    w1low: object
    w2: object
    w1_back: object
    w2_back: object
    cls_all: object
    cls_t: object
    dmask: object
    columns: object
    own_w: object
    r_first: object
    r_pairs: object
    r_crossed: object
    r_halves: object
    r_lined: object
    r_out: object
    local: object
    f_send: object
    f_recv: object


def rest_groups(crops):
    return -(-15 // crops) * crops


def weight_groups(crops):
    return -(-8 // crops) * crops, -(-9 // crops) * crops


def decoder_kernel(crops, n, samples, *refs):
    ref = DecoderRefs(*refs[: len(DecoderRefs._fields)])
    rest = list(refs[len(DecoderRefs._fields) :])
    (wide_pair, wide_first, wide_second, wide_psem, wide_send, wide_recv) = rest[:6]
    (pair, slots, psem, send, recv, halo_send, halo_recv) = rest[6:13]

    coarse_samples, fine_samples = samples
    my_crop, me = lax.axis_index("crop"), lax.axis_index("chan")
    core = lax.rem(me, 2)
    above = (my_crop, lax.rem(me + n - 1, n))
    below = (my_crop, lax.rem(me + 1, n))
    low_chans, low_width = ref.low_w.shape
    classes = ref.w_cls.shape[0]
    fine = ref.d_logits.shape[1]
    rows = fine // n
    fine_cells = rows * 128
    coarse_cells = ref.branch.shape[0]
    coarse_rows = coarse_cells // FA
    cells = FA * FA
    c_in, c = ref.point.shape
    own = c // n
    chips, chip = n // 2, lax.div(me, 2)
    small, large = weight_groups(crops)
    chunk = min(4, rows)

    other, far = chip_peers(crops, n)
    over_crops = [(lax.rem(my_crop + i, crops), me) for i in range(1, crops)]
    over_chips = [(my_crop, lax.rem(me + 2 * j, n)) for j in range(1, chips)]
    wait_barrier = barrier_with([other, above, below] + far)

    turn_of = lambda i: 0 if i == 6 else (i + 1) % 2
    swaps = [
        Swap(crops, n, pair.at[i], slots.at[i], psem.at[i], send.at[turn_of(i)], recv.at[i])
        for i in range(pair.shape[0])
    ]
    wides = [
        WideSwap(
            crops, n, wide_pair.at[i], wide_first.at[i], wide_second.at[i],
            wide_psem.at[i], wide_send.at[i], wide_recv.at[i],
        )
        for i in range(2)
    ]
    front = Copies(ref.f_send, ref.f_recv)
    for i in range(pair.shape[0]):
        pair[i, core] = jnp.zeros((8, 128), f32)
    for i in range(2):
        wide_pair[i, core] = jnp.zeros(wide_pair.shape[2:], f32)

    def halo(i, first, last, to_above, to_below):
        copies = [
            remote(first, to_above, halo_send.at[i, 0], halo_recv.at[i, 0], above),
            remote(last, to_below, halo_send.at[i, 1], halo_recv.at[i, 1], below),
        ]
        for copy in copies:
            copy.start()
        return copies

    def fine_halo(i, values):
        return halo(
            i,
            values.at[pl.ds(128, 128)],
            values.at[pl.ds(rows * 128, 128)],
            values.at[pl.ds((rows + 1) * 128, 128)],
            values.at[pl.ds(0, 128)],
        )

    def gain(k):
        return ref.norms[k : k + 1]

    def shift(k):
        return ref.norms[8 + k : 9 + k]

    def moments(total, square, count):
        average = total * (1.0 / count)
        return average, lax.rsqrt(jnp.maximum(square * (1.0 / count) - average * average, 0.0) + epsilon)

    column = lax.broadcasted_iota(jnp.int32, (128, c), 0)

    def put_three(target, base, y):
        target[pl.ds(base, 128), 0:c] = jnp.where(column == 0, 0.0, pltpu.roll(y, 1, 0)).astype(bf16)
        target[pl.ds(base, 128), c : 2 * c] = y.astype(bf16)
        target[pl.ds(base, 128), 2 * c : 3 * c] = jnp.where(
            column == 127, 0.0, pltpu.roll(y, 127, 0)
        ).astype(bf16)

    def inside(i):
        at_top = jnp.logical_and(me == 0, i == 0)
        at_bottom = jnp.logical_and(me == n - 1, i == rows + 1)
        return jnp.where(jnp.logical_or(at_top, at_bottom), 0.0, 1.0)

    def each_row(body, first, last, carry):
        def step(i, kept):
            return body(i, pl.multiple_of(i * 128, 128), kept)

        return lax.fori_loop(first, last, step, carry)

    zero = jnp.zeros((8, c), f32)

    src_all, src_own, gath = ref.src_all, ref.src_own, ref.gath
    local_copies = []

    def local(src, dst):
        copy = pltpu.make_async_copy(src, dst, ref.local.at[len(local_copies)])
        copy.start()
        local_copies.append(copy)

    local(ref.atrous_hbm, ref.atrous)
    group_at = lax.div(me * rows, 16) * 16
    for k in range(3):
        at = jnp.clip(group_at + 16 * (k - 1), 0, fine - 16)
        local(ref.d_logits.at[:, pl.ds(pl.multiple_of(at, 16), 16)], ref.near.at[k])
    for i in range(cells // 256):
        src_own[pl.ds(i * 256, 256)] = ref.feat[:, i * 256 : (i + 1) * 256].T
    local(src_own, src_all.at[my_crop])
    flip = ref.flip
    flip[...] = jnp.zeros(flip.shape, f32)
    flip[0:classes, 0:own] = ref.w_cls[...].astype(f32)
    own_cls = flip[0:128, 0:128].T[0:own, 0:classes].astype(bf16)
    flip[0:classes, 0:own] = jnp.zeros((classes, own), f32)
    for t in range(9):
        flip[0:own, 128:256] = jnp.zeros((own, 128), f32)
        flip[0:own, 128 : 128 + low_width] = ref.w_side[t].astype(f32)
        flip[t * low_width : (t + 1) * low_width, 0:128] = flip[0:128, 128:256].T[0:low_width]
    for k in range(5):
        gath[me, k] = ref.w_proj[k]
    turned = flip[:, 0:128].T[0:own].astype(bf16)
    gath[me, 5] = turned[:, 0:c]
    gath[me, 6] = turned[:, c : 2 * c]
    gath[me, 7] = jnp.zeros((own, c), bf16)
    gath[me, 7, :, 0:classes] = own_cls
    for k in range(8, small):
        gath[me, k] = jnp.zeros((own, c), bf16)
    for t in range(9, large):
        gath[me, small + t] = jnp.zeros((own, c), bf16)
        gath[me, small + large + t] = jnp.zeros((own, c), bf16)
    for t in range(9):
        gath[me, small + t] = ref.w_dec1[t]
        gath[me, small + large + t] = ref.w_dec2[t]
    columns = ref.columns
    columns[...] = jnp.zeros(columns.shape, f32)
    columns[0:1, 0:low_width] = ref.low_gain[...]
    columns[1:2, 0:low_width] = ref.low_shift[...]
    columns[2:3, 0:classes] = ref.bias[...]
    ref.norms_all[me] = jnp.zeros((16, 128), f32)
    ref.norms_all[me, 0:8, 0:own] = ref.own_gain[...]
    ref.norms_all[me, 8:16, 0:own] = ref.own_shift[...]
    wait_barrier()
    block_of = lambda j: lax.rem(me - 2 * j + n, n)

    class Spread:
        def __init__(self, first, size):
            per = size // crops
            self.at = lambda b, q: gath.at[b, pl.ds(first + q * per, per)]
            self.first, self.size = first, size

        def start(self):
            here = self.at(me, my_crop)
            self.far = [front.start(here, here, peer) for peer in over_chips]
            here = gath.at[me, pl.ds(self.first, self.size)]
            self.pairs = [front.start(here, here, other)]

        def cross(self):
            self.crossed = []
            for j in range(1, chips):
                self.far[j - 1].wait_recv()
                here = self.at(block_of(j), my_crop)
                for i in range(1, crops):
                    self.crossed.append((j, front.start(here, here, over_crops[i - 1])))

        def cores(self):
            for j in range(1, chips):
                for k, copy in self.crossed:
                    if k == j:
                        copy.wait_recv()
                here = gath.at[block_of(j), pl.ds(self.first, self.size)]
                self.pairs.append(front.start(here, here, other))

        def finish(self):
            for copy in self.pairs:
                copy.wait_recv()

    norm_far = []
    here = ref.norms_all.at[me]
    for peer in over_chips:
        norm_far.append(front.start(here, here, peer))
    norm_pairs = [front.start(here, here, other)]
    spread = [Spread(0, small), Spread(small, large), Spread(small + large, large)]
    spread[0].start()
    spread[1].start()
    feature_copies = [front.start(src_own, src_all.at[my_crop], peer) for peer in over_crops]
    for i in range(0, ref.low_rows.shape[1], 16):
        here = ref.low_rows[:, i : i + 16].astype(f32)
        ref.low_in[:, i * 128 : (i + 16) * 128] = here.reshape(low_chans, 16 * 128).astype(bf16)
    local(ref.low_in, ref.low_flat)

    low_send, low_pair = ref.low_send, ref.low_pair

    def low_block(b):
        span = pl.ds(pl.multiple_of(b * fine_cells, fine_cells), fine_cells)
        return dot_tn(ref.low_w[...], ref.low_in[:, span])

    low_copies = []
    for z in range(chips):
        low_send[z] = low_block(2 * z + 1 - core)
        low_copies.append(front.start(low_send.at[z], low_pair.at[z], other))
    for k in range(3):
        local_copies[1 + k].wait()
        here = ref.near[k].astype(f32).reshape(classes, 16 * 128)
        ref.dlog[0:classes, k * 2048 : (k + 1) * 2048] = here.astype(bf16)
        ref.dlog[classes:32, k * 2048 : (k + 1) * 2048] = jnp.zeros((32 - classes, 2048), bf16)

    part, part_in, staged, arrived = ref.pushed, ref.pushed1, ref.staged, ref.arrived
    shifted = ref.g2

    order = (0, 3, 2, 1)

    def branch_partial(k):
        first = k * cells
        if k == 0:
            part[pl.ds(first, cells)] = dot(src_own[...], ref.point[...])
        else:
            rate = atrous_rates[k - 1]
            if k == order[1]:
                local_copies[0].wait()
            shift_three(lambda base: src_own[pl.ds(base, 128)], shifted, rate, -rate, rate)
            part[pl.ds(first, cells)] = dot(shifted[pl.ds(0, cells), 0 : 3 * c_in], ref.atrous[k - 1, 1])
            for a in (0, 2):
                move = (a - 1) * rate
                count = (FA - abs(move)) * FA
                to, off = first + max(-move, 0) * FA, max(move, 0) * FA
                part[pl.ds(to, count)] += dot(shifted[pl.ds(off, count), 0 : 3 * c_in], ref.atrous[k - 1, a])
        copies = []
        for z in range(chips):
            block = pl.multiple_of(first + (2 * z + 1 - core) * coarse_cells, coarse_cells)
            copies.append(
                front.start(
                    part.at[pl.ds(block, coarse_cells)],
                    part_in.at[pl.ds((k * chips + z) * coarse_cells, coarse_cells)],
                    other,
                )
            )
        return copies

    def pair_sum(k, z):
        block = pl.multiple_of(k * cells + (2 * z + core) * coarse_cells, coarse_cells)
        landed = pl.multiple_of((k * chips + z) * coarse_cells, coarse_cells)
        return part[pl.ds(block, coarse_cells)] + part_in[pl.ds(landed, coarse_cells)]

    waited = []
    branch_lines = [
        LineSum(n, front, staged.at[k], arrived.at[k], ref.spare.at[k], functools.partial(pair_sum, k))
        for k in range(4)
    ]

    def branch_out(k, copies):
        for copy in copies:
            copy.wait()
            waited.append(copy)
        for z in range(chips):
            staged[k, z] = pair_sum(k, z).astype(bf16)
        ref.branch[:, k * c : (k + 1) * c] = pair_sum(k, chip)
        branch_lines[k].start()

    before = branch_partial(order[0])
    for at in range(1, 4):
        after = branch_partial(order[at])
        branch_out(order[at - 1], before)
        before = after
        if at == 2:
            spread[0].cross()
        if at == 1:
            for z in range(chips):
                low_copies[z].wait_recv()
                ref.low_sum[z] = (low_block(2 * z + core) + low_pair[z]).astype(bf16)
            low_line = LineSum(
                n, front, ref.low_sum, ref.low_recv, ref.low_spare, lambda z: low_block(2 * z + core) + low_pair[z]
            )
            low_line.start()
        if at == 2:
            branch_lines[order[0]].second()
        if at == 3:
            spread[1].cross()
            low_line.second()
            branch_lines[order[1]].second()
    branch_out(order[3], before)
    branch_lines[order[2]].second()
    for j in range(1, chips):
        norm_far[j - 1].wait_recv()
        here = ref.norms_all.at[block_of(j)]
        norm_pairs.append(front.start(here, here, other))
    pooled = row_of(src_own[...].astype(f32)) * (1.0 / cells)
    pooled = jnp.concatenate([pooled, jnp.zeros((15, c_in), f32)], axis=0).astype(bf16)
    pool_part = dot(pooled, ref.pool_w[...])[0:1]

    branch_lines[order[3]].second()
    for copy in norm_pairs:
        copy.wait_recv()
    for b in range(n):
        ref.norms[:, b * own : (b + 1) * own] = ref.norms_all[b, :, 0:own]

    low_ext = ref.low_ext
    own_low = pl.ds(128, fine_cells)
    low_ext[:, own_low] = low_block(me) + low_pair[chip]

    def add_to_low(value):
        low_ext[:, own_low] += value

    low_line.finish(add_to_low)
    low_edges = halo(
        0,
        low_ext.at[:, pl.ds(128, 128)],
        low_ext.at[:, pl.ds(rows * 128, 128)],
        low_ext.at[:, pl.ds((rows + 1) * 128, 128)],
        low_ext.at[:, pl.ds(0, 128)],
    )

    def add_low(i, base, kept):
        v = low_ext[:, pl.ds(base, 128)]
        return kept[0] + v, kept[1] + v * v

    low_zero = jnp.zeros((low_width, 128), f32)
    low_sum, low_square = each_row(add_low, 1, rows + 1, (low_zero, low_zero))

    def lanes_of(values):
        return row_of(values.T)

    pair[6, core, 0:1, 0:low_width] = lanes_of(low_sum)
    pair[6, core, 1:2, 0:low_width] = lanes_of(low_square)
    swaps[6].start()

    for k in order:

        def add_to_branch(value, k=k):
            ref.branch[:, k * c : (k + 1) * c] += value

        branch_lines[k].finish(add_to_branch)

    spread[0].cores()
    spread[1].cores()
    wide = wide_pair.at[0]
    for k in range(4):
        v = ref.branch[:, k * c : (k + 1) * c]
        wide[core, k : k + 1] = row_of(v)
        wide[core, 4 + k : 5 + k] = row_of(v * v)
    wide[core, 8:16] = jnp.where(
        lax.broadcasted_iota(jnp.int32, (8, c), 0) == my_crop, pool_part, 0.0
    )
    total_a = wides[0].run(spread[2].start)
    spread[0].finish()
    proj, w1, w2, tail = ref.proj, ref.w1, ref.w2, ref.tail
    for b in range(n):
        mine = pl.ds(b * own, own)
        for k in range(5):
            proj[k, mine] = gath[b, k]

    def place_conv(target, back, first):
        for b in range(n):
            for t in range(9):
                a, e = t // 3, t % 3
                here = gath[b, first + t]
                target[a, pl.ds(e * c + b * own, own)] = here
                back[a, pl.ds(b * own, own), (2 - e) * c : (3 - e) * c] = here

    def branch_parts(k):
        average, inverse = moments(total_a[k : k + 1], total_a[4 + k : 5 + k], coarse_samples)
        normed = (ref.branch[:, k * c : (k + 1) * c] - average) * inverse
        return normed, gain(k) * normed + shift(k), inverse

    projected = jnp.zeros((coarse_cells, c), f32)
    for k in range(4):
        y = gelu(branch_parts(k)[1]).astype(bf16)
        ref.branch_bf[:, k * c : (k + 1) * c] = y
        projected = projected + dot(y, ref.proj[k])
    pool_here = lax.broadcasted_iota(jnp.int32, (8, c), 0) < crops
    pool_pre = total_a[8:16]
    pool_average = row_of(pool_pre) * (1.0 / crops)
    pool_spread = jnp.where(pool_here, pool_pre - pool_average, 0.0)
    pool_inverse = lax.rsqrt(row_of(pool_spread * pool_spread) * (1.0 / crops) + epsilon)
    pool_normed = pool_spread * pool_inverse
    pool_before = gain(4) * pool_normed + shift(4)
    pool_bf = gelu(pool_before)
    pool_bf = jnp.concatenate([pool_bf, jnp.zeros((8, c), f32)], axis=0).astype(bf16)
    pool_term = dot(pool_bf, ref.proj[4])
    my_row = lax.broadcasted_iota(jnp.int32, (16, c), 0) == my_crop
    projected = projected + row_of(jnp.where(my_row, pool_term, 0.0))
    merged_ext = ref.merged_ext
    merged_ext[pl.ds(FA, coarse_cells)] = projected
    put_pair(pair.at[0], core, row_of(projected), row_of(projected * projected))
    merged_copies = halo(
        1,
        merged_ext.at[pl.ds(FA, FA)],
        merged_ext.at[pl.ds(coarse_cells, FA)],
        merged_ext.at[pl.ds(FA + coarse_cells, FA)],
        merged_ext.at[pl.ds(0, FA)],
    )
    swaps[0].start()

    total_l = swaps[6].finish()
    for copy in low_edges:
        copy.wait()
    low_average = total_l[0:1] * (1.0 / fine_samples)
    low_variance = total_l[1:2] * (1.0 / fine_samples) - low_average * low_average
    low_inverse_row = lax.rsqrt(jnp.maximum(low_variance, 0.0) + epsilon)
    low_average = spread_row(low_average)[0:low_width]
    low_inverse = spread_row(low_inverse_row)[0:low_width]
    lane = lax.broadcasted_iota(jnp.int32, (low_width, 128), 1)
    low_gain = spread_row(columns[0:1])[0:low_width]
    low_shift = spread_row(columns[1:2])[0:low_width]

    def low_parts(base):
        normed = (low_ext[:, pl.ds(base, 128)] - low_average) * low_inverse
        return normed, low_gain * normed + low_shift

    def low_row(i, base, kept):
        y = gelu(low_parts(base)[1]) * inside(i)
        lowx = ref.lowx
        lowx[0:low_width, pl.ds(base, 128)] = jnp.where(lane == 0, 0.0, pltpu.roll(y, 1, 1)).astype(bf16)
        lowx[low_width : 2 * low_width, pl.ds(base, 128)] = y.astype(bf16)
        lowx[2 * low_width : 3 * low_width, pl.ds(base, 128)] = jnp.where(
            lane == 127, 0.0, pltpu.roll(y, 127, 1)
        ).astype(bf16)
        return kept

    each_row(low_row, 0, rows + 2, 0)

    for b in range(n):
        mine = pl.ds(b * own, own)
        tail[mine, 0:c] = gath[b, 5]
        tail[mine, c : 2 * c] = gath[b, 6]
        ref.cls_all[mine] = gath[b, 7, :, 0:128]
    turned = tail[...].T
    for a in range(3):
        ref.w1low[a] = turned[a * 3 * low_width : (a + 1) * 3 * low_width]
    cls_lane = lax.broadcasted_iota(jnp.int32, (c, 128), 1)
    cls_clean = jnp.where(cls_lane < classes, ref.cls_all[...].astype(f32), 0.0)
    ref.cls_t[...] = cls_clean.T[0:32].astype(bf16)
    spread[2].cross()
    merged_sum, merged_square = get_pair(swaps[0].finish())
    for copy in merged_copies:
        copy.wait()
    merged_average, merged_inverse = moments(merged_sum, merged_square, coarse_samples)

    def merged_parts(first, count):
        normed = (merged_ext[pl.ds(first, count)] - merged_average) * merged_inverse
        return normed, gain(5) * normed + shift(5)

    fine_at = lax.broadcasted_iota(jnp.int32, (128, FA), 0).astype(f32)
    coarse_at = lax.broadcasted_iota(jnp.int32, (128, FA), 1).astype(f32)
    place = jnp.clip((fine_at + 0.5) / 4.0 - 0.5, 0.0, FA - 1.0)
    up = jnp.maximum(0.0, 1.0 - jnp.abs(place - coarse_at)).astype(bf16)
    coarse_wide = []
    for j in range(coarse_rows + 2):
        coarse_wide.append(dot_exact(up, gelu(merged_parts(j * FA, FA)[1])))
    for i in range(-1, rows + 1):
        lower, a, b = up_weights(i, me, n, rows, coarse_rows)
        put_three(ref.x1, (i + 1) * 128, a * coarse_wide[lower] + b * coarse_wide[lower + 1])
    spread[1].finish()
    place_conv(w1, ref.w1_back, small)
    dec1, dec2, pushed, pushed1 = ref.dec1, ref.dec2, ref.pushed, ref.pushed1

    def conv_piece(source, weight, base):
        total = None
        for a in range(3):
            term = dot(source[pl.ds(base + a * 128, chunk * 128)], weight[a])
            total = term if total is None else total + term
        return total

    def conv_loop(piece, target):
        def step(i, kept):
            base = pl.multiple_of(i * (chunk * 128), 128)
            total = piece(base)
            target[pl.ds(base + 128, chunk * 128)] = total
            return kept[0] + fold(total), kept[1] + fold(total * total)

        return lax.fori_loop(0, rows // chunk, step, (zero, zero))


    def first_piece(base):
        total = conv_piece(ref.x1, w1, base)
        for a in range(3):
            total = total + dot_tn(ref.lowx[:, pl.ds(base + a * 128, chunk * 128)], ref.w1low[a])
        return total

    total, square = conv_loop(first_piece, dec1)
    spread[2].cores()
    put_pair(pair.at[1], core, row_of(total), row_of(square))
    swaps[6].drain()
    swaps[1].start()
    dec1_copies = fine_halo(2, dec1)
    total, square = get_pair(swaps[1].finish())
    for copy in dec1_copies:
        copy.wait()
    first_average, first_inverse = moments(total, square, fine_samples)

    def first_parts(base):
        normed = (dec1[pl.ds(base, 128)] - first_average) * first_inverse
        return normed, gain(6) * normed + shift(6)

    def first_row(i, base, kept):
        put_three(ref.x2, base, gelu(first_parts(base)[1]) * inside(i))
        return kept

    each_row(first_row, 0, rows + 2, 0)
    spread[2].finish()
    place_conv(w2, ref.w2_back, small + large)
    total, square = conv_loop(lambda base: conv_piece(ref.x2, w2, base), dec2)
    put_pair(pair.at[2], core, row_of(total), row_of(square))
    swaps[0].drain()
    swaps[2].start()
    dec2_copies = fine_halo(3, dec2)
    total, square = get_pair(swaps[2].finish())
    for copy in dec2_copies:
        copy.wait()
    second_average, second_inverse = moments(total, square, fine_samples)

    cls_t = ref.cls_t[...]
    bias = spread_row(columns[2:3])[0:32]
    col_here = ref.offsets[0, 1] + 4 * lax.broadcasted_iota(jnp.int32, (1, 128), 1) < SCENE_W
    col_mask = jnp.where(col_here, 1.0, 0.0)

    def scene_mask(i):
        row_here = ref.offsets[0, 0] + 4 * (me * rows + i - 1) < SCENE_H
        return col_mask * jnp.where(row_here, 1.0, 0.0)

    def masked_row(i, base):
        at = pl.multiple_of(base + (15 + me * rows - group_at) * 128, 128)
        return ref.dlog[:, pl.ds(at, 128)] * (scene_mask(i) * inside(i)).astype(bf16)

    def second_parts(base):
        normed = (dec2[pl.ds(base, 128)] - second_average) * second_inverse
        return normed, gain(7) * normed + shift(7)

    def second_row(i, base, kept):
        normed, before = second_parts(base)
        value, slope = gelu_both(before)
        ref.g1[pl.ds(base, 128), 0:c] = value.astype(bf16)
        masked = masked_row(i, base)
        ref.dmask[:, pl.ds(base, 128)] = masked
        grad = dot_tn(masked, cls_t)
        push = slope * grad
        pushed[pl.ds(base, 128)] = push
        own_row = jnp.where(jnp.logical_and(i > 0, i < rows + 1), 1.0, 0.0)
        push = push * own_row
        return kept[0] + fold(push * normed), kept[1] + fold(push)

    along, summed = each_row(second_row, 0, rows + 2, (zero, zero))
    put_pair(pair.at[3], core, row_of(along), row_of(summed))
    swaps[1].drain()
    swaps[3].start()
    second = ref.g1

    def logit_row(i, base, kept):
        out = pl.multiple_of(base - 128, 128)
        value = dot_nt(cls_t, second[pl.ds(base, 128), 0:c]) + bias
        ref.logits[:, pl.ds(out, 128)] = value * scene_mask(i)
        return kept

    each_row(logit_row, 1, rows + 1, 0)
    local(ref.logits, ref.logits_hbm)
    flip[pl.ds(9 * low_width, 32)] = dot(
        ref.dmask[:, 128 : 128 + fine_cells], second[pl.ds(128, fine_cells), 0:c]
    )
    bias_grad = jnp.zeros((32, 128), f32)
    for i in range(1, rows + 1):
        bias_grad = bias_grad + ref.dmask[:, i * 128 : (i + 1) * 128].astype(f32)
    wide_pair[1, core, 16:17, 0:32] = row_of(bias_grad.T)
    second_along, second_summed = get_pair(swaps[3].finish())

    def pull(push, normed, k, inverse, along, summed, count):
        return (gain(k) * inverse) * (push - summed * (1.0 / count) - normed * (along * (1.0 / count)))

    def dec2_row(i, base, kept):
        g = pull(
            pushed[pl.ds(base, 128)], second_parts(base)[0], 7, second_inverse,
            second_along, second_summed, fine_samples,
        )
        put_three(ref.g2, base, g * inside(i))
        return kept

    each_row(dec2_row, 0, rows + 2, 0)

    def back_loop(source, weight, use, carry):
        def step(i, kept):
            base = pl.multiple_of(i * (chunk * 128), 128)
            total = None
            for a in range(3):
                term = dot_nt(source[pl.ds(base + (2 - a) * 128, chunk * 128)], weight[a])
                total = term if total is None else total + term
            return use(base, total, kept)

        return lax.fori_loop(0, rows // chunk, step, carry)

    def first_use(base, grad, kept):
        at = pl.ds(pl.multiple_of(base + 128, 128), chunk * 128)
        normed = (dec1[at] - first_average) * first_inverse
        push = gelu_slope(gain(6) * normed + shift(6)) * grad
        pushed1[at] = push
        return kept[0] + fold(push * normed), kept[1] + fold(push)

    along, summed = back_loop(ref.g2, ref.w2_back, first_use, (zero, zero))
    put_pair(pair.at[4], core, row_of(along), row_of(summed))
    swaps[2].drain()
    swaps[4].start()
    pushed_copies = fine_halo(4, pushed1)

    wgrads = ref.wgrads

    reduce_two = Reduce(
        crops, n, front, ref.own_w, ref.r_first, ref.r_pairs, ref.r_crossed, ref.r_halves, ref.r_lined, ref.r_out
    )

    def weight_grads(target, source, gradient):
        for a in range(3):
            part = dot_tn(
                source[pl.ds(a * 128, fine_cells), c : 2 * c], gradient[pl.ds(128, fine_cells)]
            ).astype(bf16)
            for e in range(3):
                tap = part[:, (2 - e) * c : (3 - e) * c]
                for h in range(n):
                    target[h, 3 * a + e] = tap[h * own : (h + 1) * own]

    weight_grads(ref.own_w, ref.x2, ref.g2)
    for t in range(9, large):
        for h in range(n):
            ref.own_w[h, t] = jnp.zeros((own, c), bf16)
    reduce_two.cores()
    first_along, first_summed = get_pair(swaps[4].finish())
    reduce_two.over_the_crops()
    for copy in pushed_copies:
        copy.wait()

    def dec1_row(i, base, kept):
        g = pull(
            pushed1[pl.ds(base, 128)], first_parts(base)[0], 6, first_inverse,
            first_along, first_summed, fine_samples,
        ) * inside(i)
        put_three(ref.g1, base, g)
        return kept

    each_row(dec1_row, 0, rows + 2, 0)

    def up_use(base, grad, kept):
        dec2[pl.ds(pl.multiple_of(base + 128, 128), chunk * 128)] = grad
        return kept

    back_loop(ref.g1, ref.w1_back, up_use, 0)
    yt = ref.yt

    def low_back_row(i, local, base, kept):
        total = None
        for t in range(9):
            a, e = t // 3, t % 3
            at = pl.ds((local + 2 - a) * 128, 128)
            piece = yt[t * low_width : (t + 1) * low_width, at]
            if e == 0:
                piece = jnp.where(lane == 127, 0.0, pltpu.roll(piece, 127, 1))
            if e == 2:
                piece = jnp.where(lane == 0, 0.0, pltpu.roll(piece, 1, 1))
            total = piece if total is None else total + piece
        normed, before = low_parts(base)
        push = gelu_slope(before) * total
        ref.low_push[:, pl.ds(pl.multiple_of(base - 128, 128), 128)] = push
        return kept[0] + push * normed, kept[1] + push

    def low_back_chunk(i, kept):
        base = pl.multiple_of(i * (chunk * 128), 128)
        here = ref.g1[pl.ds(base, (chunk + 2) * 128), c : 2 * c]
        for a in range(3):
            yt[a * 3 * low_width : (a + 1) * 3 * low_width] = dot_nt(ref.w1low[a], here)
        for local in range(chunk):
            kept = low_back_row(i, local, pl.multiple_of(base + (local + 1) * 128, 128), kept)
        return kept

    low_along, low_summed = lax.fori_loop(0, rows // chunk, low_back_chunk, (low_zero, low_zero))

    part = ref.merged_part
    fine_at = lax.broadcasted_iota(jnp.int32, (FA, 128), 1).astype(f32)
    coarse_at = lax.broadcasted_iota(jnp.int32, (FA, 128), 0).astype(f32)
    place = jnp.clip((fine_at + 0.5) / 4.0 - 0.5, 0.0, FA - 1.0)
    up_t = jnp.maximum(0.0, 1.0 - jnp.abs(place - coarse_at)).astype(bf16)
    row_sums = [None] * (coarse_rows + 2)
    for i in range(rows):
        lower, a, b = up_weights(i, me, n, rows, coarse_rows)
        grad = dec2[pl.ds((i + 1) * 128, 128)]
        for j, weight in ((lower, a), (lower + 1, b)):
            row_sums[j] = weight * grad if row_sums[j] is None else row_sums[j] + weight * grad
    along, summed = zero, zero
    for j in range(coarse_rows + 2):
        grad = dot_exact(up_t, row_sums[j])
        part[pl.ds(j * FA, FA)] = grad
        normed, before = merged_parts(j * FA, FA)
        push = gelu_slope(before) * grad
        along, summed = along + fold(push * normed), summed + fold(push)
    put_pair(pair.at[5], core, row_of(along), row_of(summed))
    pair[5, core, 4:5, 0:low_width] = lanes_of(low_along)
    pair[5, core, 5:6, 0:low_width] = lanes_of(low_summed)
    part_copies = halo(
        5,
        part.at[pl.ds(0, FA)],
        part.at[pl.ds(FA + coarse_cells, FA)],
        part.at[pl.ds((coarse_rows + 3) * FA, FA)],
        part.at[pl.ds((coarse_rows + 2) * FA, FA)],
    )
    swaps[3].drain()
    swaps[5].start()
    reduce_two.over_the_chips()
    weight_grads(wgrads, ref.x1, ref.g1)
    local(wgrads.at[:, pl.ds(0, 9)], ref.wgrads_hbm.at[:, pl.ds(0, 9)])
    total_g = swaps[5].finish()
    for copy in part_copies:
        copy.wait()
    merged_along, merged_summed = get_pair(total_g)
    low_along, low_summed = spread_row(total_g[4:5])[0:low_width], spread_row(total_g[5:6])[0:low_width]
    pack = ref.pack
    pack[17:18, 0:128] = total_g[4:5]
    pack[18:19, 0:128] = total_g[5:6]
    up_here = jnp.where(me == 0, 0.0, 1.0)
    down_here = jnp.where(me == n - 1, 0.0, 1.0)
    proj_bf = ref.proj_bf
    for j in range(1, coarse_rows + 1):
        grad = part[pl.ds(j * FA, FA)]
        if j == 1:
            grad = grad + up_here * part[pl.ds((coarse_rows + 2) * FA, FA)]
        if j == coarse_rows:
            grad = grad + down_here * part[pl.ds((coarse_rows + 3) * FA, FA)]
        normed, before = merged_parts(j * FA, FA)
        push = gelu_slope(before) * grad
        g = pull(push, normed, 5, merged_inverse, merged_along, merged_summed, coarse_samples)
        proj_bf[pl.ds((j - 1) * FA, FA)] = g.astype(bf16)

    push_all = []
    for k in range(4):
        normed, before, _ = branch_parts(k)
        push = gelu_slope(before) * dot_nt(proj_bf[...], ref.proj[k])
        push_all.append(push)
        wide_pair[1, core, k : k + 1] = row_of(push * normed)
        wide_pair[1, core, 4 + k : 5 + k] = row_of(push)
    proj_row = row_of(proj_bf[...].astype(f32))
    wide_pair[1, core, 8:16] = jnp.where(
        lax.broadcasted_iota(jnp.int32, (8, c), 0) == my_crop, proj_row, 0.0
    )
    total_h = wides[1].run(reduce_two.to_all_crops)
    for k in range(4):
        normed, _, inverse = branch_parts(k)
        g = pull(
            push_all[k], normed, k, inverse, total_h[k : k + 1], total_h[4 + k : 5 + k], coarse_samples
        )
        ref.branch_out[:, k * c : (k + 1) * c] = g.astype(bf16)

    sums = total_h[8:16]
    sums_high = sums.astype(bf16).astype(f32)
    sums_low = sums - sums_high
    spare = jnp.concatenate([sums_high, sums_low], axis=0)
    spare_mid = spare.astype(bf16)
    spare_rest = (spare - spare_mid.astype(f32)).astype(bf16)
    pieces = dot_nt(spare_mid, ref.proj[4]) + dot_nt(spare_rest, ref.proj[4])
    pool_push = gelu_slope(pool_before) * (pieces[0:8] + pieces[8:16])
    pool_push = jnp.where(pool_here, pool_push, 0.0)
    pool_along, pool_summed = row_of(pool_push * pool_normed), row_of(pool_push)
    pool_grad = pull(pool_push, pool_normed, 4, pool_inverse, pool_along, pool_summed, crops)
    pool_grad = jnp.where(pool_here, pool_grad, 0.0)
    pack[24:32] = pool_grad
    pack[32:40] = jnp.zeros((8, c), f32)

    gain_rows = [total_h[0:4], pool_along, merged_along, first_along, second_along]
    shift_rows = [total_h[4:8], pool_summed, merged_summed, first_summed, second_summed]
    turn = c - me * own
    pack[0:8] = pltpu.roll(jnp.concatenate(gain_rows, axis=0), turn, 1)
    pack[8:16] = pltpu.roll(jnp.concatenate(shift_rows, axis=0), turn, 1)
    pack[16:17] = total_h[16:17]
    pool_rows = jnp.zeros((c, c), f32)
    rest = jnp.concatenate([sums, jnp.zeros((8, c), f32)], axis=0)
    for _ in range(3):
        high = rest.astype(bf16)
        pool_rows = pool_rows + dot_tn(pool_bf, high)
        rest = rest - high.astype(f32)
    dec1[pl.ds(0, c)] = pool_rows
    pack[40 : 40 + own] = dec1[pl.ds(pl.multiple_of(me * own, own), own)]
    local(pack, ref.pack_hbm)

    def low_out_row(i, base, kept):
        at = pl.ds(pl.multiple_of(base - 128, 128), 128)
        normed = low_parts(base)[0]
        g = (low_gain * low_inverse) * (
            ref.low_push[:, at] - low_summed * (1.0 / fine_samples) - normed * (low_along * (1.0 / fine_samples))
        )
        ref.low_out[:, at] = g.astype(bf16)
        return kept

    each_row(low_out_row, 1, rows + 1, 0)
    local(ref.low_out, ref.low_hbm)
    local(ref.branch_out, ref.branch_hbm)

    for a in range(3):
        flip[pl.ds(a * 3 * low_width, 3 * low_width)] = dot(
            ref.lowx[:, a * 128 : a * 128 + fine_cells], ref.g1[pl.ds(128, fine_cells), c : 2 * c]
        )
    flip[pl.ds(9 * low_width + 32, 48)] = jnp.zeros((48, c), f32)
    turned = flip[...].T.astype(bf16)
    for k in range(4):
        product = dot_tn(ref.branch_bf[:, k * c : (k + 1) * c], proj_bf[...]).astype(bf16)
        for h in range(n):
            rows_h = product[h * own : (h + 1) * own]
            wgrads[h, 9 + k] = rows_h
    for h in range(n):
        wgrads[h, 13] = turned[h * own : (h + 1) * own, 0:c]
        wgrads[h, 14] = turned[h * own : (h + 1) * own, c : 2 * c]
        for k in range(15, wgrads.shape[1]):
            wgrads[h, k] = jnp.zeros((own, c), bf16)
    local(wgrads.at[:, pl.ds(9, wgrads.shape[1] - 9)], ref.wgrads_hbm.at[:, pl.ds(9, wgrads.shape[1] - 9)])
    reduce_two.finish()
    for t in range(9):
        ref.dec2_w[t] = ref.r_out[t].astype(f32)
    local(ref.dec2_w, ref.dec2_hbm)
    for copy in feature_copies:
        copy.wait_recv()
    front.drain(waited)
    swaps[4].drain()
    swaps[5].drain()
    for copy in local_copies[4:]:
        copy.wait()


def decoder(crops, n, samples, *args):
    ref = DecoderRefs(*args, *([None] * (len(DecoderRefs._fields) - len(args))))
    c_in, c = ref.point.shape
    low_width = ref.low_w.shape[1]
    classes, fine = ref.d_logits.shape[:2]
    rows = fine // n
    cells = rows * 128
    coarse = FA * FA // n
    own = c // n
    small, large = weight_groups(crops)
    chips = n // 2
    all_chips = crops * chips
    outer = (rows + 2) * 128
    chunk = min(4, rows)
    count = (crops - 1) + 4 * (2 * chips - 1) + 2 * chips - 1
    count += 2 * chips - 1 + 3 * (1 + (crops + 1) * (chips - 1)) + reduce_copies(crops, n) + 5
    S = jax.ShapeDtypeStruct
    V = pltpu.VMEM
    D = pltpu.SemaphoreType.DMA
    vmem = pl.BlockSpec(memory_space=pltpu.VMEM)
    hbm = pl.BlockSpec(memory_space=pl.ANY)
    return pl.pallas_call(
        functools.partial(decoder_kernel, crops, n, samples),
        out_shape=[
            S((32, cells), f32),
            S((coarse, 4 * c), bf16),
            S((low_width, cells), bf16),
            S((40 + own, c), f32),
            S((9, own, c), f32),
            S((n, rest_groups(crops), own, c), bf16),
            S((crops, FA * FA, c_in), bf16),
            S((ref.low_rows.shape[0], ref.low_rows.shape[1] * 128), bf16),
        ],
        in_specs=[pl.BlockSpec(memory_space=pltpu.SMEM), vmem, vmem, hbm] + [vmem] * (len(args) - 5) + [hbm],
        out_specs=[hbm] * 8,
        scratch_shapes=[
            V((32, 48 * 128), bf16),
            V((3, classes, 16, 128), bf16),
            V((ref.low_rows.shape[0], ref.low_rows.shape[1] * 128), bf16),
            V(ref.atrous_hbm.shape, bf16),
            V((FA * FA, c_in), bf16),
            V((32, cells), f32),
            V((coarse, 4 * c), bf16),
            V((low_width, cells), bf16),
            V((40 + own, c), f32),
            V((9, own, c), f32),
            V((n, rest_groups(crops), own, c), bf16),
            V((low_width, outer), f32),
            V((low_width, cells), f32),
            V((3 * low_width, outer), bf16),
            V((coarse + 2 * FA, c), f32),
            V((coarse + 4 * FA, c), f32),
            V((outer, c), f32),
            V((outer, c), f32),
            V((max(outer, 4 * FA * FA), c), f32),
            V((max(outer, 2 * FA * FA), c), f32),
            V((outer, 3 * c), bf16),
            V((outer, 3 * c), bf16),
            V((max(outer, FA * FA), 3 * c), bf16),
            V((outer, 3 * c), bf16),
            V((9 * low_width, (chunk + 2) * 128), f32),
            V((coarse, 4 * c), bf16),
            V((coarse, c), bf16),
            V((512, c), f32),
            V((coarse, 4 * c), f32),
            V((4, chips, coarse, c), bf16),
            V((4, chips, coarse, c), bf16),
            V((chips, low_width, cells), f32),
            V((chips, low_width, cells), f32),
            V((chips, low_width, cells), bf16),
            V((chips, low_width, cells), bf16),
            V((4, coarse, c), bf16),
            V((low_width, cells), bf16),
            V((n, small + 2 * large, own, c), bf16),
            V((n, 16, 128), f32),
            V((16, c), f32),
            V((5, c, c), bf16),
            V((3, 3 * c, c), bf16),
            V((c, 2 * c), bf16),
            V((3, 3 * low_width, c), bf16),
            V((3, 3 * c, c), bf16),
            V((3, c, 3 * c), bf16),
            V((3, c, 3 * c), bf16),
            V((c, 128), bf16),
            V((32, c), bf16),
            V((32, outer), bf16),
            V((8, 128), f32),
            V((n, large, own, c), bf16),
            *reduce_scratch(crops, n, large, own, c),
            D((16,)),
            D((count,)),
            D((count,)),
            V((2, 2, 24, c), f32),
            V((2, crops, 24, c), f32),
            V((2, chips, 24, c), f32),
            D((2, 2)),
            D((2, crops + chips)),
            D((2, crops + chips)),
            V((7, 2, 8, 128), f32),
            V((7, all_chips, 8, 128), f32),
            D((7, 2)),
            D((2, all_chips)),
            D((7, all_chips)),
            D((6, 2)),
            D((6, 2)),
        ],
        compiler_params=pltpu.CompilerParams(
            collective_id=0, has_side_effects=True, vmem_limit_bytes=62 * 1024 * 1024
        ),
    )(*args)


class Reduce:
    def __init__(self, crops, n, copies, source, first, pairs, crossed, halves, lined, out, mine=None, mine_sems=None):
        my_crop, me = lax.axis_index("crop"), lax.axis_index("chan")
        self.crops, self.chips, self.copies = crops, n // 2, copies
        self.crop, self.core, self.chip = my_crop, lax.rem(me, 2), lax.div(me, 2)
        self.other = (my_crop, me + 1 - 2 * self.core)
        self.over_crops = [(lax.rem(my_crop + i, crops), me) for i in range(1, crops)]
        self.over_chips = [(my_crop, lax.rem(me + 2 * j, n)) for j in range(1, n // 2)]
        self.source, self.first, self.pairs, self.crossed = source, first, pairs, crossed
        self.halves, self.lined, self.out = halves, lined, out
        self.mine, self.mine_sems = mine, mine_sems
        self.size = source.shape[1]
        self.share = self.size // crops

    def wait(self):
        for copy in self.moving:
            copy.wait_recv()

    def cores(self):
        self.moving = []
        for z in range(self.chips):
            block = self.source.at[2 * z + 1 - self.core]
            self.moving.append(self.copies.start(block, self.first.at[z], self.other))
        self.loads = []
        if self.mine is not None:
            for z in range(self.chips):
                block = self.source.at[2 * z + self.core]
                self.loads.append(pltpu.make_async_copy(block, self.mine.at[z], self.mine_sems.at[z]))
                self.loads[-1].start()

    def over_the_crops(self):
        self.wait()
        for copy in self.loads:
            copy.wait()
        for z in range(self.chips):
            for g in range(self.size):
                here = self.source[2 * z + self.core, g] if self.mine is None else self.mine[z, g]
                both = here.astype(f32) + self.first[z, g].astype(f32)
                self.pairs[z, g] = both.astype(bf16)
        self.moving = []
        for i in range(1, self.crops):
            target = lax.rem(self.crop + i, self.crops)
            block = self.pairs.at[:, pl.ds(target * self.share, self.share)]
            self.moving.append(
                self.copies.start(block, self.crossed.at[self.crop], self.over_crops[i - 1])
            )
        for z in range(self.chips):
            for g in range(self.share):
                self.crossed[self.crop, z, g] = self.pairs[z, self.crop * self.share + g]

    def over_the_chips(self):
        self.wait()
        for z in range(self.chips):
            for g in range(self.share):
                value = self.crossed[0, z, g].astype(f32)
                for i in range(1, self.crops):
                    value = value + self.crossed[i, z, g].astype(f32)
                self.halves[z, g] = value.astype(bf16)
        self.moving = []
        for j in range(1, self.chips):
            target = lax.rem(self.chip + j, self.chips)
            self.moving.append(
                self.copies.start(
                    self.halves.at[target], self.lined.at[self.chip], self.over_chips[j - 1]
                )
            )
        for g in range(self.share):
            self.lined[self.chip, g] = self.halves[self.chip, g]

    def to_all_crops(self):
        self.wait()
        for g in range(self.share):
            value = self.lined[0, g].astype(f32)
            for z in range(1, self.chips):
                value = value + self.lined[z, g].astype(f32)
            self.out[self.crop * self.share + g] = value.astype(bf16)
        here = self.out.at[pl.ds(self.crop * self.share, self.share)]
        self.moving = [self.copies.start(here, here, peer) for peer in self.over_crops]

    def finish(self):
        self.wait()


def reduce_scratch(crops, n, size, own, c):
    chips, share = n // 2, size // crops
    V = pltpu.VMEM
    return [
        V((chips, size, own, c), bf16),
        V((chips, size, own, c), bf16),
        V((crops, chips, share, own, c), bf16),
        V((chips, share, own, c), bf16),
        V((chips, share, own, c), bf16),
        V((size, own, c), bf16),
    ]


def reduce_copies(crops, n):
    return 2 * (n // 2) - 1 + 2 * (crops - 1)


class Gather:
    def __init__(self, n, send, recv):
        my_crop, self.me = lax.axis_index("crop"), lax.axis_index("chan")
        self.n, self.chips = n, n // 2
        self.core = lax.rem(self.me, 2)
        self.other = (my_crop, self.me + 1 - 2 * self.core)
        self.send, self.recv = send, recv
        self.peer = lambda j: (my_crop, lax.rem(self.me + 2 * j, n))

    def block(self, j):
        return lax.rem(self.me - 2 * j + self.n, self.n)

    def other_block(self, j):
        return lax.rem(self.me + 1 - 2 * self.core - 2 * j + self.n, self.n)

    def start(self, at):
        self.at = at
        self.far, self.pairs = [], []
        for j in range(1, self.chips):
            here = at(self.me)
            self.far.append(remote(here, here, self.send.at[j], self.recv.at[j], self.peer(j)))
            self.far[-1].start()
        self.forward(0)

    def forward(self, j):
        here = self.at(self.block(j))
        k = self.chips + j
        self.pairs.append(remote(here, here, self.send.at[k], self.recv.at[k], self.other))
        self.pairs[-1].start()

    def arrive(self, j):
        self.far[j - 1].wait_recv()
        self.forward(j)

    def finish(self):
        for copy in self.pairs:
            copy.wait_recv()

    def drain(self):
        for copy in self.far + self.pairs:
            copy.wait_send()


class LineGather(Gather):
    def __init__(self, n, send, recv):
        super().__init__(n, send, recv)
        my_crop, self.chip = lax.axis_index("crop"), lax.div(self.me, 2)
        self.end = jnp.logical_or(self.chip == 0, self.chip == 3)
        self.inner = jnp.logical_not(self.end)
        beside = self.chip + 1 - 2 * lax.rem(self.chip, 2)
        over, mirror = lax.rem(self.chip + 2, 4), 3 - self.chip
        second = jnp.where(self.end, over, mirror)
        third = jnp.where(self.end, mirror, over)
        self.order = [2 * z + self.core for z in (self.chip, beside, second, third)]
        self.to = lambda z: (my_crop, 2 * z + self.core)
        self.beside, self.over, self.mirror = beside, over, mirror

    def block(self, j):
        return self.order[j]

    def start(self, at):
        self.at = at
        self.pairs = []
        here = at(self.me)
        make = lambda k, block, z, s=None: remote(
            block, block, self.send.at[k if s is None else s], self.recv.at[k], self.to(z)
        )
        self.first = make(0, here, self.beside)
        self.first.start()
        self.middle = make(1, here, self.mirror)
        self.long = make(2, here, self.over, 1)
        pl.when(self.inner)(self.middle.start)
        pl.when(self.end)(self.long.start)
        self.passed = [make(3, at(self.order[2]), self.beside), make(8, at(self.order[3]), self.beside)]
        self.forward(0)

    def arrive(self, j):
        if j == 1:
            self.first.wait_recv()
        else:
            come, on = (self.middle, self.long)[j - 2], self.passed[j - 2]

            def pass_it():
                come.wait_recv()
                on.start()

            pl.when(self.inner)(pass_it)
            pl.when(self.end)(on.wait_recv)
        self.forward(j)

    def drain(self):
        self.first.wait_send()
        self.middle.wait_send()
        for copy in self.pairs:
            copy.wait_send()

        def passed():
            for copy in self.passed:
                copy.wait_send()

        pl.when(self.inner)(passed)


def gather_over(n, send, recv):
    return LineGather(n, send, recv) if n // 2 == 4 else Gather(n, send, recv)


class BackRefs(typing.NamedTuple):
    grad: object
    src_hbm: object
    point: object
    atrous_hbm: object
    pool: object
    pack: object
    low_grad: object
    low_in_hbm: object
    wgrads: object
    features_hbm: object
    point_w: object
    atrous_w_hbm: object
    pool_w: object
    low_w_out: object
    blocks: object
    low_full_hbm: object
    last_grad: object
    last_src: object
    src: object
    atrous: object
    low_in: object
    features: object
    atrous_w: object
    low_full: object
    mine: object
    local: object
    m_sems: object
    w_sems: object
    all_grad: object
    shifted: object
    turned: object
    total: object
    r_first: object
    r_pairs: object
    r_crossed: object
    r_halves: object
    r_lined: object
    r_out: object
    low_parts: object
    g_send: object
    g_recv: object
    l_send: object
    l_recv: object
    c_send: object
    c_recv: object


def back_kernel(crops, n, *refs):
    ref = BackRefs(*refs)
    my_crop, me = lax.axis_index("crop"), lax.axis_index("chan")
    chips = n // 2
    core, chip = lax.rem(me, 2), lax.div(me, 2)
    block, width = ref.grad.shape
    c = width // 4
    half = width // 2
    c_in = ref.src.shape[2]
    cells = FA * FA
    relay = crops == 4
    other = (my_crop, me + 1 - 2 * core)
    over_crops = [(lax.rem(my_crop + i, crops), me) for i in range(1, crops)]
    over_chips = [(my_crop, lax.rem(me + 2 * j, n)) for j in range(1, chips)]
    wait_barrier = barrier_with([other] + over_crops + over_chips)
    all_grad, src = ref.all_grad, ref.src
    if relay:
        along_x = my_crop + 1 - 2 * lax.rem(my_crop, 2)
        along_y = my_crop + 2 - 4 * lax.div(my_crop, 2)
        crop_list = [my_crop, along_x, along_y, 3 - my_crop]
    else:
        crop_list = [my_crop] + [lax.rem(my_crop - i + crops, crops) for i in range(1, crops)]

    def grad_at(crop):
        def at(b):
            return all_grad.at[crop, pl.ds(pl.multiple_of(b * block, block), block)]

        return at

    def lanes_at(crop, b, first):
        return all_grad.at[crop, pl.ds(pl.multiple_of(b * block, block), block), pl.ds(first, half)]

    local_copies = []

    def local(src, dst):
        copy = pltpu.make_async_copy(src, dst, ref.local.at[len(local_copies)])
        copy.start()
        local_copies.append(copy)

    local(ref.src_hbm, src)
    local(ref.src_hbm.at[crop_list[-1]], ref.last_src)
    weight_copies = []
    for k in range(3):
        for t in range(9):
            at = ref.atrous.at[k, t // 3, :, pl.ds(t % 3 * c, c)]
            copy = pltpu.make_async_copy(ref.atrous_hbm.at[k, t], at, ref.w_sems.at[9 * k + t])
            copy.start()
            weight_copies.append(copy)
    local(ref.low_in_hbm, ref.low_in)
    pooled_grad = ref.pack[24:40].astype(bf16)
    all_grad[my_crop, pl.ds(pl.multiple_of(me * block, block), block)] = ref.grad[...]
    ref.low_full[me] = ref.low_grad[...]
    wait_barrier()

    gather = gather_over(n, ref.g_send, ref.g_recv)
    gather.start(grad_at(my_crop))
    moves = Copies(ref.c_send, ref.c_recv)
    crossing = {}

    def cross(j):
        here = grad_at(my_crop)(gather.block(j))
        if relay:
            for i, crop in ((1, along_x), (2, along_y)):
                crossing[i, j] = moves.start(here, here, (crop, me))
        else:
            for i in range(1, crops):
                crossing[i, j] = moves.start(here, here, over_crops[i - 1])

    core_copies = {}

    def pass_on(i, j):
        crossing[i, j].wait_recv()
        b = gather.block(j)
        crop = crop_list[i]
        if relay and i == 1:
            here = lanes_at(crop, b, 0)
            crossing[3, j, 0] = moves.start(here, here, (along_y, me))
        if relay and i == 2:
            here = lanes_at(crop, b, half)
            crossing[3, j, 1] = moves.start(here, here, (along_x, me))
        place = grad_at(crop)(b)
        core_copies[i, j] = moves.start(place, place, other)

    def pass_across(j):
        crossing[3, j, 0].wait_recv()
        crossing[3, j, 1].wait_recv()
        place = grad_at(crop_list[3])(gather.block(j))
        core_copies[3, j] = moves.start(place, place, other)

    cross(0)
    reduce = Reduce(
        crops, n, moves, ref.wgrads, ref.r_first, ref.r_pairs, ref.r_crossed, ref.r_halves, ref.r_lined, ref.r_out,
        ref.mine, ref.m_sems,
    )
    reduce.cores()
    shifted = ref.shifted

    def shift_source(i):
        crop = crop_list[i]
        for k in range(3):
            rate = atrous_rates[k]
            shift_three(lambda base: src[crop, pl.ds(base, 128)], shifted.at[i % 3, k], rate, -rate, rate)

    local_copies[0].wait()
    shift_source(0)
    reduce.over_the_crops()
    for i in range(1, min(3, crops)):
        shift_source(i)
    pooled = []
    for i in range(crops):
        mean = row_of(src[i].astype(f32)) * (1.0 / cells)
        pooled.append(mean)
    pooled = jnp.concatenate(pooled + [jnp.zeros((16 - crops, c_in), f32)], axis=0).astype(bf16)
    ref.pool_w[...] = dot_tn(pooled, pooled_grad)
    for j in range(1, chips):
        gather.arrive(j)
        cross(j)
    reduce.over_the_chips()
    low_gather = Gather(n, ref.l_send, ref.l_recv)
    low_gather.start(lambda b: ref.low_full.at[b])
    if relay:
        pass_on(1, 0)
        pass_on(2, 0)
    gather.finish()

    total, turned = ref.total, ref.turned
    pool_row = dot_nt(pooled_grad, ref.pool[...])
    my_row = lax.broadcasted_iota(jnp.int32, pool_row.shape, 0) == my_crop
    pool_row = row_of(jnp.where(my_row, pool_row, 0.0)) * (1.0 / cells)
    for copy in weight_copies:
        copy.wait()
    total[...] = dot_nt(all_grad[my_crop, :, 0:c], ref.point[...]) + pool_row
    for k in range(3):
        rate = atrous_rates[k]
        shift_three(
            lambda base: all_grad[my_crop, pl.ds(base, 128), (k + 1) * c : (k + 2) * c],
            turned, rate, rate, -rate,
        )
        for a in range(3):
            move = (a - 1) * rate
            count = (FA - abs(move)) * FA
            to, off = max(move, 0) * FA, max(-move, 0) * FA
            total[pl.ds(to, count)] += dot_nt(turned[pl.ds(off, count)], ref.atrous[k, a])

    def weight_part(i):
        crop = crop_list[i]
        part = dot_tn(src[crop], all_grad[crop, :, 0:c])
        ref.point_w[...] = part if i == 0 else ref.point_w[...] + part
        for k in range(3):
            rate = atrous_rates[k]
            for a in range(3):
                move = (a - 1) * rate
                count = (FA - abs(move)) * FA
                from_src, off = max(move, 0) * FA, max(-move, 0) * FA
                part = dot_tn(
                    shifted[i % 3, k, pl.ds(from_src, count)],
                    all_grad[crop, pl.ds(off, count), (k + 1) * c : (k + 2) * c],
                )
                for e in range(3):
                    piece = part[e * c_in : (e + 1) * c_in]
                    if i > 0:
                        piece = ref.atrous_w[k, 3 * a + e] + piece
                    ref.atrous_w[k, 3 * a + e] = piece
            if i == crops - 2:
                local(ref.atrous_w.at[k], ref.atrous_w_hbm.at[k])

    weight_part(0)
    ref.features[...] = total[...].T
    local(ref.features, ref.features_hbm)
    if relay:
        for j in range(1, chips):
            pass_on(1, j)
            pass_on(2, j)

    def low_part():
        for j in range(1, chips):
            low_gather.arrive(j)
        low_gather.finish()
        local(ref.low_full, ref.low_full_hbm)
        local_copies[2].wait()
        rows = ref.low_full.shape[2] // 128
        low_in, low_all = ref.low_in, ref.low_full
        low_total = None
        for b in range(n):
            here = low_all[b]
            span = slice(b * rows * 128, (b + 1) * rows * 128)
            part = dot_nt(low_in[:, span], here)
            low_total = part if low_total is None else low_total + part
        low_parts = ref.low_parts
        low_parts[my_crop] = jnp.zeros(low_parts.shape[1:], f32)
        low_parts[my_crop, :, 0 : low_total.shape[1]] = low_total
        here = low_parts.at[my_crop]
        low_copies = [moves.start(here, here, peer) for peer in over_crops]
        return low_copies

    for i in range(1, crops):
        if i + 2 < crops - 1:
            shift_source(i + 2)
        for j in range(chips):
            if not relay:
                pass_on(i, j)
            elif i == 3:
                pass_across(j)
        for j in range(chips):
            core_copies[i, j].wait_recv()
        if i < crops - 1:
            weight_part(i)
        if i == min(2, crops - 1):
            reduce.to_all_crops()
            low_copies = low_part()

    local(all_grad.at[crop_list[-1]], ref.last_grad)
    reduce.finish()
    for g in range(ref.blocks.shape[0]):
        ref.blocks[g] = ref.r_out[g].astype(f32)
    for copy in low_copies:
        copy.wait_recv()
    ref.low_w_out[...] = jnp.sum(ref.low_parts[...], axis=0)
    gather.drain()
    low_gather.drain()
    moves.drain([])
    for k, copy in enumerate(local_copies):
        if k not in (0, 2):
            copy.wait()


def pyramid_back(crops, n, *args):
    grad, src, low_grad, low_in, wgrads = args[0], args[1], args[6], args[7], args[8]
    block, width = grad.shape
    c = width // 4
    c_in = src.shape[2]
    chips = n // 2
    cells = FA * FA
    low_rows = low_in.shape[0]
    own, lanes = wgrads.shape[2:]
    S = jax.ShapeDtypeStruct
    V = pltpu.VMEM
    D = pltpu.SemaphoreType.DMA
    vmem = pl.BlockSpec(memory_space=pltpu.VMEM)
    hbm = pl.BlockSpec(memory_space=pl.ANY)
    count = 3 * crops * chips + crops - 1 + reduce_copies(crops, n)
    return pl.pallas_call(
        functools.partial(back_kernel, crops, n),
        out_shape=[
            S((c_in, cells), f32),
            S((c_in, c), f32),
            S((3, 9, c_in, c), f32),
            S((c_in, c), f32),
            S((low_rows, 128), f32),
            S((15, own, lanes), f32),
            S((n,) + low_grad.shape, bf16),
            S((cells, width), bf16),
            S((cells, c_in), bf16),
        ],
        in_specs=[vmem, hbm, vmem, hbm, vmem, vmem, vmem, hbm, hbm],
        out_specs=[hbm, vmem, hbm, vmem, vmem, vmem, hbm, hbm, hbm],
        scratch_shapes=[
            V(src.shape, bf16),
            V((3, 3, c_in, 3 * c), bf16),
            V(low_in.shape, bf16),
            V((c_in, cells), f32),
            V((3, 9, c_in, c), f32),
            V((n,) + low_grad.shape, bf16),
            V((chips,) + wgrads.shape[1:], bf16),
            D((12,)),
            D((chips,)),
            D((27,)),
            V((crops, cells, width), bf16),
            V((min(3, crops), 3, cells, 3 * c_in), bf16),
            V((cells, 3 * c), bf16),
            V((cells, c_in), f32),
            *reduce_scratch(crops, n, wgrads.shape[1], own, lanes),
            V((crops, low_rows, 128), f32),
            D((n + 1,)),
            D((n + 1,)),
            D((n + 1,)),
            D((n + 1,)),
            D((count,)),
            D((count,)),
        ],
        compiler_params=pltpu.CompilerParams(
            collective_id=1, has_side_effects=True, vmem_limit_bytes=62 * 1024 * 1024
        ),
    )(*args)


class FinishRefs(typing.NamedTuple):
    atrous_part: object
    point_part: object
    last_grad: object
    last_src: object
    features_in: object
    pool_in: object
    low_full: object
    low_w: object
    low_w_part: object
    logits_in: object
    dec2_in: object
    blocks: object
    pack: object
    logits: object
    features: object
    early: object
    point: object
    atrous: object
    pool: object
    proj: object
    low_w_out: object
    dec1: object
    side: object
    dec2: object
    cls: object
    bias: object
    gain: object
    shift: object
    low_gain: object
    low_shift: object
    v_atrous: object
    v_grad: object
    v_src: object
    v_low: object
    v_logits: object
    v_early: object
    v_point: object
    v_proj: object
    v_low_w: object
    v_side: object
    v_cls: object
    v_bias: object
    v_gain: object
    v_shift: object
    v_low_gain: object
    v_low_shift: object
    turned: object
    sems: object


def finish_kernel(*refs):
    ref = FinishRefs(*refs)
    copies = []

    def move(src, dst):
        copy = pltpu.make_async_copy(src, dst, ref.sems.at[len(copies)])
        copy.start()
        copies.append(copy)
        return copy

    c_in, c = ref.v_point.shape
    classes, rows = ref.v_logits.shape[0], ref.v_logits.shape[1]
    low_width = ref.v_low_w.shape[1]
    own = ref.v_cls.shape[1]
    loaded = [move(ref.last_grad, ref.v_grad), move(ref.last_src, ref.v_src)]
    parts = [move(ref.atrous_part.at[k], ref.v_atrous.at[k]) for k in range(3)]
    low = move(ref.low_full, ref.v_low)
    straight = [
        move(ref.features_in, ref.features),
        move(ref.pool_in, ref.pool),
        move(ref.dec2_in, ref.dec2),
        move(ref.blocks.at[pl.ds(0, 9)], ref.dec1),
        move(ref.blocks.at[pl.ds(9, 4)], ref.proj.at[pl.ds(0, 4)]),
        move(ref.pack.at[pl.ds(40, own)], ref.proj.at[4]),
    ]

    ref.v_logits[...] = ref.logits_in[0:classes].reshape(classes, rows, 128)
    straight.append(move(ref.v_logits, ref.logits))
    pack = ref.pack
    tail = jnp.concatenate([ref.blocks[13], ref.blocks[14]], axis=1)
    width = 2 * c
    for t in range(9):
        ref.v_side[t] = pltpu.roll(tail, (width - t * low_width) % width, 1)[:, 0:low_width]
    cls = pltpu.roll(tail, width - 9 * low_width, 1)[:, 0:128]
    cls = jnp.concatenate([cls, jnp.zeros((128 - own, 128), f32)], axis=0)
    ref.v_cls[...] = cls.T[0:classes, 0:own]
    ref.v_low_w[...] = ref.low_w_part[:, 0:low_width]
    ref.v_gain[...] = pack[0:8, 0:own]
    ref.v_shift[...] = pack[8:16, 0:own]
    ref.v_bias[...] = pack[16:17, 0:classes]
    ref.v_low_gain[...] = pack[17:18, 0:low_width]
    ref.v_low_shift[...] = pack[18:19, 0:low_width]
    for src, dst in (
        (ref.v_side, ref.side),
        (ref.v_cls, ref.cls),
        (ref.v_low_w, ref.low_w_out),
        (ref.v_gain, ref.gain),
        (ref.v_shift, ref.shift),
        (ref.v_bias, ref.bias),
        (ref.v_low_gain, ref.low_gain),
        (ref.v_low_shift, ref.low_shift),
    ):
        straight.append(move(src, dst))

    for copy in loaded:
        copy.wait()
    for k in range(3):
        rate = atrous_rates[k]
        shift_three(lambda base: ref.v_src[pl.ds(base, 128)], ref.turned, rate, -rate, rate)
        parts[k].wait()
        for a in range(3):
            by = (a - 1) * rate
            count = (FA - abs(by)) * FA
            from_src, off = max(by, 0) * FA, max(-by, 0) * FA
            part = dot_tn(
                ref.turned[pl.ds(from_src, count)],
                ref.v_grad[pl.ds(off, count), (k + 1) * c : (k + 2) * c],
            )
            for e in range(3):
                ref.v_atrous[k, 3 * a + e] += part[e * c_in : (e + 1) * c_in]
        straight.append(move(ref.v_atrous.at[k], ref.atrous.at[k]))
        if k == 0:
            low.wait()
            for b in range(ref.low_full.shape[0]):
                value = dot(ref.low_w[...], ref.v_low[b])
                ref.v_early[:, b * rows : (b + 1) * rows] = value.reshape(value.shape[0], rows, 128)
            straight.append(move(ref.v_early, ref.early))
            ref.v_point[...] = ref.point_part[...] + dot_tn(ref.v_src[...], ref.v_grad[:, 0:c])
            straight.append(move(ref.v_point, ref.point))
    for copy in straight:
        copy.wait()


def finish(shapes, *args):
    parts = FinishRefs(*args, *([None] * (len(FinishRefs._fields) - len(args))))
    c_in = parts.point_part.shape[0]
    vmem = pl.BlockSpec(memory_space=pltpu.VMEM)
    hbm = pl.BlockSpec(memory_space=pl.ANY)
    V = pltpu.VMEM
    held = [V(shapes[k], f32) for k in (0, 2, 3)]
    held += [V(shapes[k], f32) for k in (6, 7, 9, 11, 12, 13, 14, 15, 16)]
    return pl.pallas_call(
        finish_kernel,
        out_shape=[jax.ShapeDtypeStruct(shape, f32) for shape in shapes],
        in_specs=[hbm, vmem, hbm, hbm, vmem, vmem, hbm, vmem, vmem, vmem, vmem, vmem, vmem],
        out_specs=[hbm] * len(shapes),
        scratch_shapes=[
            V(parts.atrous_part.shape, f32),
            V(parts.last_grad.shape, bf16),
            V(parts.last_src.shape, bf16),
            V(parts.low_full.shape, bf16),
            *held,
            V((FA * FA, 3 * c_in), bf16),
            pltpu.SemaphoreType.DMA((32,)),
        ],
        compiler_params=pltpu.CompilerParams(vmem_limit_bytes=60 * 1024 * 1024),
    )(*args)


def per_device(
    features,
    low_in,
    offsets,
    d_logits,
    w_point,
    w_atrous,
    w_pool,
    w_proj,
    w_low,
    w_dec1,
    w_dec1_low,
    w_dec2,
    w_cls,
    b_cls,
    bn_gain,
    bn_shift,
    low_gain,
    low_shift,
):
    n = lax.axis_size("chan")
    crops = lax.axis_size("crop")
    fine = low_in.shape[2]
    rows = fine // n
    coarse_rows = FA // n
    channels = w_dec2.shape[2]
    c_in = features.shape[1]
    low_width = w_low.shape[1]
    coarse_samples = FA * FA * crops
    fine_samples = fine * fine * crops

    classes = w_cls.shape[1]
    logits, branch_grad, low_pre_bf, pack, dec2_wgrad, blocks, source_all, low_flat = decoder(
        crops,
        n,
        (coarse_samples, fine_samples),
        offsets,
        features[0],
        w_point,
        w_atrous.reshape(3, 3, 3 * c_in, channels),
        w_pool,
        low_in[0],
        w_low,
        w_proj,
        w_dec1,
        w_dec1_low.transpose(0, 2, 1),
        w_dec2,
        w_cls.T,
        bn_gain,
        bn_shift,
        low_gain[None],
        low_shift[None],
        b_cls[None],
        d_logits[0],
    )
    feature_grad, point_wgrad, atrous_wgrad, pool_wgrad, low_wgrad, blocks, low_full, last_grad, last_src = (
        pyramid_back(
            crops,
            n,
            branch_grad,
            source_all,
            w_point,
            w_atrous,
            w_pool,
            pack,
            low_pre_bf,
            low_flat,
            blocks,
        )
    )
    own = w_dec2.shape[1]
    shapes = [
        (classes, rows, fine),
        (c_in, FA * FA),
        low_in.shape[1:],
        (c_in, channels),
        (3, 9, c_in, channels),
        (c_in, channels),
        (5, own, channels),
        (low_in.shape[1], low_width),
        (9, own, channels),
        (9, own, low_width),
        (9, own, channels),
        (classes, own),
        (1, classes),
        (8, own),
        (8, own),
        (1, low_width),
        (1, low_width),
    ]
    outs = finish(
        shapes,
        atrous_wgrad,
        point_wgrad,
        last_grad,
        last_src,
        feature_grad,
        pool_wgrad,
        low_full,
        w_low,
        low_wgrad,
        logits,
        dec2_wgrad,
        blocks,
        pack,
    )
    outs = list(outs)
    for k in (0, 1, 2):
        outs[k] = outs[k][None]
    for k in (12, 15, 16):
        outs[k] = outs[k][0]
    outs[9] = outs[9].transpose(0, 2, 1)
    outs[11] = outs[11].T
    return tuple(outs)


def solution(mesh):
    placed = (
        P("crop", "chan", None),
        P("crop", "chan", None, None),
        P("crop", None),
        P("crop", None, None, None),
        P("chan", None),
        P(None, None, "chan", None),
        P("chan", None),
        P(None, "chan", None),
        P("chan", None),
        P(None, "chan", None),
        P(None, None, "chan"),
        P(None, "chan", None),
        P("chan", None),
        P(),
        P(None, "chan"),
        P(None, "chan"),
        P(),
        P(),
    )
    return jax.shard_map(
        per_device,
        mesh=mesh,
        in_specs=placed,
        out_specs=(
            P("crop", None, "chan", None),
            P("crop", "chan", None),
            P("crop", "chan", None, None),
            P("chan", None),
            P(None, None, "chan", None),
            P("chan", None),
            P(None, "chan", None),
            P("chan", None),
            P(None, "chan", None),
            P(None, None, "chan"),
            P(None, "chan", None),
            P("chan", None),
            P(),
            P(None, "chan"),
            P(None, "chan"),
            P(),
            P(),
        ),
        check_vma=False,
    )
```
